128 devices in a mesh: dp: 32 (over y_lo, x, z), mp: 4 (over y_hi, core).
Axes of the slice: x: 4, y: 4 (y_hi: 2, y_lo: 2; y = y_hi * 2 + y_lo), z: 4, core: 2. Of those that a mesh axis runs over, the one named last changes fastest.
Arguments:
- stream: bfloat16 [32, 512, 2048], P('dp'), may hold values from -6 to 6
- code_ids: int32 [32, 512], P('dp'), may hold values from 0 to 4095
- segment_ids: int32 [32, 512], P('dp'), may hold values from 0 to 3, never falling along the last dimension, each value on 1 to 256 neighbouring positions
- padding: int32 [32, 512], P('dp'), may hold values from 0 to 1, as said below
- codebook: bfloat16 [4096, 2048], replicated, may hold values from -6 to 6
- norm1_gain: bfloat16 [2048], P('dp'), may hold values from 0.099609375 to 1.8984375
- norm1_shift: bfloat16 [2048], P('dp'), may hold values from -3 to 3
- w_qkv: bfloat16 [2048, 3, 2048], P('dp', None, 'mp'), may hold values from -0.125 to 0.125
- w_out: bfloat16 [2048, 2048], P('dp', 'mp'), may hold values from -0.75 to 0.75
- norm2_gain: bfloat16 [2048], P('dp'), may hold values from 0.099609375 to 1.8984375
- norm2_shift: bfloat16 [2048], P('dp'), may hold values from -3 to 3
- w_up: bfloat16 [2048, 8192], P('dp', 'mp'), may hold values from -0.125 to 0.125
- w_down: bfloat16 [2048, 8192], P('dp', 'mp'), may hold values from -0.0625 to 0.0625
- cotangent: bfloat16 [32, 512, 2048], P('dp'), may hold values from -6 to 6
Outputs:
- layer_out: float32 [32, 512, 2048], P('dp')
- input_grad: float32 [32, 512, 2048], P('dp')
- grad_norm1_gain: float32 [2048], P('dp')
- grad_norm1_shift: float32 [2048], P('dp')
- grad_w_qkv: float32 [2048, 3, 2048], P('dp', None, 'mp')
- grad_w_out: float32 [2048, 2048], P('dp', 'mp')
- grad_norm2_gain: float32 [2048], P('dp')
- grad_norm2_shift: float32 [2048], P('dp')
- grad_w_up: float32 [2048, 8192], P('dp', 'mp')
- grad_w_down: float32 [2048, 8192], P('dp', 'mp')
The draws below stay inside these ranges and needn't reach their ends.
Inputs may be any that keep to these rules, and one draw needn't show every extreme that they name: In each row the real tokens come first and the last 1 to 128 positions are padding. `segment_ids`: episode numbers never fall along a row; an episode spans at most 256 positions.
All inputs are finite; a program needn't handle non-finite values.
Results may differ from the reference program's by a relative error of at most 0.028.
Values may be sent and summed in bfloat16 or wider, within the bound.
A program may use at most 192 MiB of HBM per device.

```python
import math
import jax
import jax.numpy as jnp
import numpy as np
from jax import lax

D = 2048
HEADS = 16
HEAD = 128
FF = 8192
CODES = 4096
SEQ = 512
ROWS = 32


def draw_padding(key, part):
    key = jax.random.fold_in(key, 7)
    cut = jax.random.randint(key, (ROWS, 1), 1, SEQ // 4 + 1)
    position = jnp.arange(SEQ)[None, :]
    return (position < SEQ - cut).astype(jnp.int32)


def place_ends(entries, stream_key, low, top_value):
    longest = entries.shape.index(max(entries.shape))
    spots = []
    for shift in (0, 1):
        where = [jax.random.randint(jax.random.fold_in(stream_key, axis), (), 0, length) for axis, length in enumerate(entries.shape)]
        where[longest] = (where[longest] + shift) % entries.shape[longest]
        spots.append(tuple(where))
    return entries.at[spots[0]].set(low).at[spots[1]].set(top_value)


def steps_of(own_key, extent, split, smallest, high):
    def one(dim, shards_of):
        steps = jax.random.uniform(jax.random.fold_in(jax.random.fold_in(own_key, 6), dim), (shards_of,), jnp.float32, smallest / len(split), high / len(split))
        return jnp.repeat(jnp.exp(steps), extent[dim] // shards_of).reshape((-1,) + (1,) * (len(extent) - dim - 1))

    level = one(*split[0])
    for cut in split[1:]:
        level = level * one(*cut)
    return level


def split_up(number_of, total, bound, slope):
    weights = [(1 << 20) // math.isqrt(standing ** slope) + 1 for standing in range(2, number_of + 1)]
    surplus, holding = total - bound - (number_of - 1), [1] * (number_of - 1)
    while surplus > 0:
        movable = [i for i in range(number_of - 1) if holding[i] < bound]
        mass, remaining = sum([weights[i] for i in movable]), surplus
        for i in movable:
            more = min(bound - holding[i], max(1, remaining * weights[i] // mass), surplus)
            holding[i] = holding[i] + more
            surplus = surplus - more
    return np.array([bound] + holding)


def uneven(stream_key, count, total, reach, slope):
    if count == 2:
        one = jax.random.randint(stream_key, (), max(1, total - reach), min(reach, total - 1) + 1)
        return jnp.stack([one, total - one])
    lengths = jnp.asarray(split_up(count, total, reach, slope), jnp.int32)
    pairs = (count - 1) // 2
    donor, sink = lengths[1:1 + 2 * pairs:2], lengths[2:2 + 2 * pairs:2]
    room = jnp.minimum(donor - 1, reach - sink)
    shifted = jax.random.randint(jax.random.fold_in(stream_key, 1), (pairs,), 0, 1 << 20) % (room + 1)
    lengths = lengths.at[1:1 + 2 * pairs:2].set(donor - shifted).at[2:2 + 2 * pairs:2].set(sink + shifted)
    return lengths[jax.random.permutation(jax.random.fold_in(stream_key, 2), count)]


def bell_draw(own_key, extent, scale, most, split=(), dtype=jnp.bfloat16):
    entries = scale * jax.random.normal(own_key, extent, jnp.float32)
    if split:
        entries = entries * steps_of(own_key, extent, split, -0.22, 0.18)
    return jnp.clip(entries, -most, most).astype(dtype)


def setup_inputs(seed: int = 0) -> dict:
    splits = jax.random.split(jax.random.key(seed), 15)
    return {
        "stream": bell_draw(splits[0], (ROWS, SEQ, D), 1.0, 6.0, ((0, 32),)),
        "code_ids": place_ends(jax.random.randint(splits[1], (ROWS, SEQ), 0, CODES), jax.random.fold_in(splits[1], 1), 0, CODES - 1).astype(jnp.int32),
        "segment_ids": jax.vmap(lambda own: jnp.searchsorted(jnp.cumsum(uneven(own, 4, SEQ, SEQ // 2, 0)), jnp.arange(SEQ), side="right"))(jax.random.split(splits[2], ROWS)).reshape((ROWS, SEQ)).astype(jnp.int32),
        "padding": draw_padding(jax.random.fold_in(splits[14], 71), 0),
        "codebook": bell_draw(splits[4], (CODES, D), 1.0, 6.0),
        "norm1_gain": jnp.clip(1.0 + 0.18 * jax.random.normal(splits[5], (D,), jnp.float32), 0.099609375, 1.8984375).astype(jnp.bfloat16),
        "norm1_shift": bell_draw(splits[6], (D,), 0.5, 3.0, ((0, 32),)),
        "w_qkv": bell_draw(splits[7], (D, 3, D), D ** -0.5, 0.125, ((0, 32), (2, 4))),
        "w_out": bell_draw(splits[8], (D, D), (D // 32) ** -0.5, 0.75, ((0, 32), (1, 4))),
        "norm2_gain": jnp.clip(1.0 + 0.18 * jax.random.normal(splits[9], (D,), jnp.float32), 0.099609375, 1.8984375).astype(jnp.bfloat16),
        "norm2_shift": bell_draw(splits[10], (D,), 0.5, 3.0, ((0, 32),)),
        "w_up": bell_draw(splits[11], (D, FF), D ** -0.5, 0.125, ((0, 32), (1, 4))),
        "w_down": bell_draw(splits[12], (D, FF), FF ** -0.5, 0.0625, ((0, 32), (1, 4))),
        "cotangent": bell_draw(splits[13], (ROWS, SEQ, D), 1.0, 6.0, ((0, 32),)),
    }


@jax.custom_vjp
def low(v):
    return lax.optimization_barrier(v.astype(jnp.bfloat16)).astype(jnp.float32)

@jax.custom_vjp
def low_back(v):
    return v

def low_keep(v):
    return (low(v), None)

def low_pass(kept, grad):
    return (grad,)

def back_keep(v):
    return (v, None)

def back_low(kept, grad):
    return (low(grad),)
low.defvjp(low_keep, low_pass)
low_back.defvjp(back_keep, back_low)
highest = lax.Precision.HIGHEST
masked_score = -1000000000.0
epsilon = 1e-05

def layer_norm(value, gain, shift):
    mean = lax.optimization_barrier(jnp.mean(value, axis=-1, keepdims=True))
    centered = value - mean
    variance = lax.optimization_barrier(jnp.mean(centered * centered, axis=-1, keepdims=True))
    return centered * lax.rsqrt(variance + epsilon) * gain + shift

def block_row(param_list, row_input, allowed):
    gain_one, shift_one, qkv_weight, out_weight, gain_two, shift_two, up_weight, down_weight = param_list
    attn_in = low(layer_norm(row_input, gain_one, shift_one))
    projected = jnp.einsum('sd,dtf->tsf', attn_in, qkv_weight, precision=highest)
    projected = low_back(low(projected))
    split_heads = projected.reshape(3, SEQ, HEADS, HEAD)
    scores = jnp.einsum('qhe,khe->hqk', split_heads[0], split_heads[1], precision=highest) * HEAD ** (-0.5)
    scores = low_back(scores)
    scores = jnp.where(allowed[None], scores, masked_score)
    prob_low = low(jax.nn.softmax(scores, axis=-1))
    attended = jnp.einsum('hqk,khe->qhe', prob_low, split_heads[2], precision=highest).reshape(SEQ, D)
    attended = low_back(low(attended))
    branch = low_back(jnp.dot(attended, out_weight.T, precision=highest))
    middle = row_input + branch
    ffn_in = low(layer_norm(middle, gain_two, shift_two))
    up_proj = low_back(jnp.dot(ffn_in, up_weight, precision=highest))
    hidden = low(jax.nn.gelu(up_proj, approximate=True))
    ffn_out = low_back(jnp.dot(hidden, down_weight.T, precision=highest))
    return middle + ffn_out

def reference(stream, code_ids, segment_ids, padding, codebook, norm1_gain, norm1_shift, w_qkv, w_out, norm2_gain, norm2_shift, w_up, w_down, cotangent):
    param_list = tuple((item.astype(jnp.float32) for item in (norm1_gain, norm1_shift, w_qkv, w_out, norm2_gain, norm2_shift, w_up, w_down)))
    inputs = stream.astype(jnp.float32) + codebook.astype(jnp.float32)[code_ids]
    position = jnp.arange(SEQ)
    causal = position[None, :] <= position[:, None]
    itself = position[None, :] == position[:, None]

    def one_row(totals, row_items):
        row_input, row_segments, row_live, row_cot = row_items
        allowed = (row_segments[:, None] == row_segments[None, :]) & causal & ((row_live[None, :] == 1) | itself)

        def forward(params_now, input_now):
            return block_row(params_now, input_now, allowed)
        row_out, pull = jax.vjp(forward, param_list, row_input)
        grads, grad_input = pull(row_cot)
        totals = jax.tree.map(jnp.add, totals, grads)
        return (totals, (row_out, grad_input))
    zeros = jax.tree.map(jnp.zeros_like, param_list)
    totals, (layer_out, input_grad) = lax.scan(one_row, zeros, (inputs, segment_ids, padding, cotangent.astype(jnp.float32)))
    return (layer_out, input_grad, totals[0], totals[1], totals[2], totals[3], totals[4], totals[5], totals[6], totals[7])
```

```python
import functools

import jax
import jax.numpy as jnp
from jax import lax
from jax.experimental import pallas as pl
from jax.experimental.pallas import tpu as pltpu
from jax.sharding import PartitionSpec as P

HEAD = 128
WIDTH = 2048
SHARE = 128
PART = 1024
MESH = pl.DeviceIdType.MESH
ANY = pl.BlockSpec(memory_space=pl.ANY)
VMEM = pl.BlockSpec(memory_space=pltpu.VMEM)
masked_score = -1000000000.0
epsilon = 1e-05
f32 = jnp.float32
bf16 = jnp.bfloat16


def place():
    dp, mp = lax.axis_index("dp"), lax.axis_index("mp")
    return lax.div(dp, 16), lax.rem(lax.div(dp, 4), 4), lax.rem(dp, 4), lax.div(mp, 2), lax.rem(mp, 2)


def ring(position, step):
    return lax.rem(position + step + 4, 4)


def xz_neighbour(axis, step):
    ylo, x, z, yhi, core = place()
    if axis == 0:
        x = ring(x, step)
    else:
        z = ring(z, step)
    return (ylo * 16 + x * 4 + z, yhi * 2 + core)


def y_peer(step):
    ylo, x, z, yhi, core = place()
    y = ring(yhi * 2 + ylo, step)
    return (lax.rem(y, 2) * 16 + x * 4 + z, lax.div(y, 2) * 2 + core)


def lo_partner():
    ylo, x, z, yhi, core = place()
    return ((1 - ylo) * 16 + x * 4 + z, yhi * 2 + core)


def core_partner():
    ylo, x, z, yhi, core = place()
    return (ylo * 16 + x * 4 + z, yhi * 2 + 1 - core)


def greet(peers):
    barrier = pltpu.get_barrier_semaphore()
    for peer in peers:
        pl.semaphore_signal(barrier, inc=1, device_id=peer, device_id_type=MESH)
    pl.semaphore_wait(barrier, len(peers))


def remote(src, dst, send_sem, recv_sem, peer):
    return pltpu.make_async_remote_copy(
        src_ref=src,
        dst_ref=dst,
        send_sem=send_sem,
        recv_sem=recv_sem,
        device_id=peer,
        device_id_type=MESH,
    )


def sems(*shape):
    return pltpu.SemaphoreType.DMA(shape)


def params(collective_id, mib=48):
    return pltpu.CompilerParams(
        collective_id=collective_id, has_side_effects=True, vmem_limit_bytes=mib << 20
    )


def small_gather_kernel(own, mask, everyone, mask_out, send, recv, mask_send, mask_recv):
    dp, mp = lax.axis_index("dp"), lax.axis_index("mp")
    barrier = pltpu.get_barrier_semaphore()

    def greet_one(k, carry):
        pl.semaphore_signal(
            barrier, inc=1, device_id=(lax.rem(dp + k, 32), mp), device_id_type=MESH
        )
        return carry

    lax.fori_loop(1, 32, greet_one, 0)
    pl.semaphore_wait(barrier, 31)

    def move(k):
        peer = lax.rem(dp + k, 32)
        return remote(own, everyone.at[dp], send.at[k], recv.at[dp], (peer, mp))

    def start(k, carry):
        move(k).start()
        return carry

    def finish(k, carry):
        source = lax.rem(dp + k, 32)
        move(k).wait_send()
        remote(own, everyone.at[source], send.at[k], recv.at[source], (source, mp)).wait_recv()
        return carry

    swap = remote(mask, mask_out, mask_send, mask_recv, lo_partner())
    swap.start()
    lax.fori_loop(1, 32, start, 0)
    everyone[dp] = own[...]
    lax.fori_loop(1, 32, finish, 0)
    swap.wait()


def small_gather(own, mask, collective_id):
    return pl.pallas_call(
        small_gather_kernel,
        out_shape=(
            jax.ShapeDtypeStruct((32, 8, 128), f32),
            jax.ShapeDtypeStruct((8, 128), f32),
        ),
        in_specs=[VMEM, VMEM],
        out_specs=(VMEM, VMEM),
        scratch_shapes=[sems(32), sems(32), pltpu.SemaphoreType.DMA, pltpu.SemaphoreType.DMA],
        compiler_params=params(collective_id, 8),
    )(own, mask)


def small_reduce_kernel(pieces, out, arrived, summed, more, send, recv, send_two, recv_two):
    dp, mp = lax.axis_index("dp"), lax.axis_index("mp")
    barrier = pltpu.get_barrier_semaphore()

    def greet_one(k, carry):
        pl.semaphore_signal(
            barrier, inc=1, device_id=(lax.rem(dp + k, 32), mp), device_id_type=MESH
        )
        return carry

    lax.fori_loop(1, 32, greet_one, 0)
    for k in (1, 2, 3):
        pl.semaphore_signal(
            barrier, inc=1, device_id=(dp, lax.rem(mp + k, 4)), device_id_type=MESH
        )
    pl.semaphore_wait(barrier, 34)

    def move(k):
        peer = lax.rem(dp + k, 32)
        return remote(pieces.at[peer], arrived.at[k], send.at[k], recv.at[k], (peer, mp))

    def start(k, carry):
        move(k).start()
        return carry

    def finish(k, total):
        move(k).wait()
        return total + arrived[k]

    lax.fori_loop(1, 32, start, 0)
    summed[...] = lax.fori_loop(1, 32, finish, pieces[dp])
    copies = [
        remote(summed, more.at[k - 1], send_two.at[k], recv_two.at[k], (dp, lax.rem(mp + k, 4)))
        for k in (1, 2, 3)
    ]
    for copy in copies:
        copy.start()
    for copy in copies:
        copy.wait()
    out[...] = summed[...] + more[0] + more[1] + more[2]


def small_reduce(pieces, collective_id):
    return pl.pallas_call(
        small_reduce_kernel,
        out_shape=jax.ShapeDtypeStruct((8, 128), f32),
        in_specs=[VMEM],
        out_specs=VMEM,
        scratch_shapes=[
            pltpu.VMEM((32, 8, 128), f32),
            pltpu.VMEM((8, 128), f32),
            pltpu.VMEM((3, 8, 128), f32),
            sems(32),
            sems(32),
            sems(4),
            sems(4),
        ],
        compiler_params=params(collective_id, 8),
    )(pieces)


def row_exchange_kernel(count, halves, full, local_sem, send, recv):
    ylo, x, z, yhi, core = place()
    up, down, other = y_peer(1), y_peer(-1), core_partner()
    greet([up, down, other])
    first = []
    for n in range(count):
        first.append(remote(halves.at[n, 0], full.at[n, ylo, core, 0], send.at[n, 0], recv.at[n, 0], up))
        first.append(remote(halves.at[n, 1], full.at[n, ylo, core, 1], send.at[n, 1], recv.at[n, 1], down))
    for n in range(count):
        first.append(remote(halves.at[n], full.at[n, ylo, core], send.at[n, 2], recv.at[n, 2], other))
    for copy in first:
        copy.start()
    local = [pltpu.make_async_copy(halves.at[n], full.at[n, ylo, core], local_sem.at[n]) for n in range(count)]
    for copy in local:
        copy.start()
    second = []
    for n in range(count):
        for u in range(2):
            here = full.at[n, 1 - ylo, core, u]
            remote(halves.at[n, u], here, send.at[n, u], recv.at[n, u], up).wait_recv()
            copy = remote(here, here, send.at[n, 3 + u], recv.at[n, 3 + u], other)
            copy.start()
            second.append(copy)
    for n in range(count):
        remote(halves.at[n], full.at[n, ylo, 1 - core], send.at[n, 2], recv.at[n, 2], other).wait_recv()
        for u in range(2):
            here = full.at[n, 1 - ylo, 1 - core, u]
            remote(here, here, send.at[n, 3 + u], recv.at[n, 3 + u], other).wait_recv()
    for copy in first + second:
        copy.wait_send()
    for copy in local:
        copy.wait()


def row_exchange(halves, collective_id):
    count = halves.shape[0]
    return pl.pallas_call(
        functools.partial(row_exchange_kernel, count),
        out_shape=jax.ShapeDtypeStruct((count, 2, 2, 2, SHARE, WIDTH), bf16),
        in_specs=[ANY],
        out_specs=ANY,
        scratch_shapes=[sems(count), sems(count, 5), sems(count, 5)],
        compiler_params=params(collective_id),
    )(halves)


def share_gather_kernel(share, full, local_sem, send, recv):
    ylo, x, z, yhi, core = place()
    y = yhi * 2 + ylo
    other = core_partner()
    greet([y_peer(1), y_peer(2), y_peer(3), other])
    mine = full.at[ylo, core, yhi]
    local = pltpu.make_async_copy(share, mine, local_sem)
    local.start()
    first = [remote(share, mine, send.at[k], recv.at[k], y_peer(k) if k else other) for k in (2, 1, 3, 0)]
    for copy in first:
        copy.start()
    second = []
    for k in (1, 3, 2):
        source = ring(y, -k)
        here = full.at[lax.rem(source, 2), core, lax.div(source, 2)]
        remote(share, here, send.at[k], recv.at[k], y_peer(-k)).wait_recv()
        copy = remote(here, here, send.at[3 + k], recv.at[3 + k], other)
        copy.start()
        second.append(copy)
    remote(share, full.at[ylo, 1 - core, yhi], send.at[0], recv.at[0], other).wait_recv()
    for k in (1, 3, 2):
        source = ring(y, -k)
        here = full.at[lax.rem(source, 2), 1 - core, lax.div(source, 2)]
        remote(here, here, send.at[3 + k], recv.at[3 + k], other).wait_recv()
    for copy in first + second:
        copy.wait_send()
    local.wait()


def share_gather(share, collective_id):
    return pl.pallas_call(
        share_gather_kernel,
        out_shape=jax.ShapeDtypeStruct((2, 2, 2, SHARE, WIDTH), bf16),
        in_specs=[ANY],
        out_specs=ANY,
        scratch_shapes=[pltpu.SemaphoreType.DMA, sems(7), sems(7)],
        compiler_params=params(collective_id),
    )(share)


CHUNK = 16


def share_sum_kernel(partial, out, from_core, turned, arrived, send, recv, send_two, recv_two):
    ylo, x, z, yhi, core = place()
    y = yhi * 2 + ylo
    other = core_partner()
    greet([y_peer(1), y_peer(2), y_peer(3), other])

    def block(k, half):
        target = ring(y, k)
        return partial.at[lax.rem(target, 2), half, lax.div(target, 2)]

    first = {}
    for k in (2, 1, 3, 0):
        first[k] = remote(block(k, 1 - core), from_core.at[k], send.at[k], recv.at[k], other)
        first[k].start()
    second = {}
    for k in (2, 1, 3):
        first[k].wait_recv()
        mine = block(k, core)

        def add(i, carry):
            rows = pl.ds(pl.multiple_of(i * CHUNK, CHUNK), CHUNK)
            turned[k, rows] = (mine[rows].astype(f32) + from_core[k, rows].astype(f32)).astype(bf16)
            return carry

        lax.fori_loop(0, SHARE // CHUNK, add, 0)
        second[k] = remote(turned.at[k], arrived.at[k], send_two.at[k], recv_two.at[k], y_peer(k))
        second[k].start()
    first[0].wait_recv()
    for k in (1, 3, 2):
        second[k].wait_recv()
    mine_own = block(0, core)

    def total(i, carry):
        rows = pl.ds(pl.multiple_of(i * CHUNK, CHUNK), CHUNK)
        value = mine_own[rows].astype(f32) + from_core[0, rows].astype(f32)
        for k in (1, 2, 3):
            value += arrived[k, rows].astype(f32)
        out[rows] = value
        return carry

    lax.fori_loop(0, SHARE // CHUNK, total, 0)
    for k in range(4):
        first[k].wait_send()
    for k in (1, 2, 3):
        second[k].wait_send()


def share_sum(partial, collective_id):
    return pl.pallas_call(
        share_sum_kernel,
        out_shape=jax.ShapeDtypeStruct((SHARE, WIDTH), f32),
        in_specs=[VMEM],
        out_specs=VMEM,
        scratch_shapes=[
            pltpu.VMEM((4, SHARE, WIDTH), bf16),
            pltpu.VMEM((4, SHARE, WIDTH), bf16),
            pltpu.VMEM((4, SHARE, WIDTH), bf16),
            sems(4),
            sems(4),
            sems(4),
            sems(4),
        ],
        compiler_params=params(collective_id),
    )(partial.reshape(2, 2, 2, SHARE, WIDTH))


def row_gather_kernel(share, full, local_sem, send, recv):
    ylo, x, z, yhi, core = place()
    across, other = y_peer(2), core_partner()
    greet([across, other])
    mine = full.at[:, core, yhi]
    far = full.at[:, core, 1 - yhi]
    local = pltpu.make_async_copy(share, mine, local_sem)
    local.start()
    one = remote(share, mine, send.at[0], recv.at[0], across)
    two = remote(share, mine, send.at[1], recv.at[1], other)
    one.start()
    two.start()
    remote(share, far, send.at[0], recv.at[0], across).wait_recv()
    three = remote(far, far, send.at[2], recv.at[2], other)
    three.start()
    remote(share, full.at[:, 1 - core, yhi], send.at[1], recv.at[1], other).wait_recv()
    last = full.at[:, 1 - core, 1 - yhi]
    remote(last, last, send.at[2], recv.at[2], other).wait_recv()
    for copy in (one, two, three):
        copy.wait_send()
    local.wait()


def row_gather(share, collective_id):
    count = share.shape[0]
    return pl.pallas_call(
        row_gather_kernel,
        out_shape=jax.ShapeDtypeStruct((count, 2, 2, SHARE, WIDTH), bf16),
        in_specs=[ANY],
        out_specs=ANY,
        scratch_shapes=[pltpu.SemaphoreType.DMA, sems(3), sems(3)],
        compiler_params=params(collective_id),
    )(share)


SIGNS = (1, -1)


def weight_gather_kernel(own, full, local_sem, swap_send, swap_recv, send, recv):
    ylo, x, z, yhi, core = place()
    partner = lo_partner()
    near = [[xz_neighbour(axis, d) for d in SIGNS] for axis in (0, 1)]
    greet([partner] + near[0] + near[1])
    here = (x, z)
    arrays = own.shape[0]

    def number(s, r, stage, d):
        return ((s * 2 + r) * 4 + stage) * 2 + d

    def move(src, dst, s, r, stage, d, axis):
        n = number(s, r, stage, d)
        return remote(src, dst, send.at[n], recv.at[n], near[axis][d])

    def locate(s):
        a, o = lax.div(s, 2), lax.rem(s, 2)
        return a, ylo + o - 2 * o * ylo

    def block(s, r, step, rows):
        a, yl = locate(s)
        if r == 0:
            return full.at[a, yl, ring(x, step), z, rows]
        return full.at[a, yl, x, ring(z, step), rows]

    def line(s, r, step, part):
        a, yl = locate(s)
        if r == 0:
            return full.at[a, yl, part, ring(z, step), pl.ds(0, 32)]
        return full.at[a, yl, ring(x, step), part, pl.ds(32, 32)]

    def local(a):
        return pltpu.make_async_copy(own.at[a, ylo], full.at[a, ylo, x, z], local_sem.at[a])

    def swap(a):
        return remote(own.at[a, 1 - ylo], full.at[a, ylo, x, z], swap_send.at[a], swap_recv.at[a], partner)

    def swap_arrived(a):
        return remote(own.at[a, 1 - ylo], full.at[a, 1 - ylo, x, z], swap_send.at[a], swap_recv.at[a], partner)

    def begin(a, carry):
        swap(a).start()
        local(a).start()
        for r in range(2):
            rows = pl.ds(32 * r, 32)
            for d in range(2):
                move(own.at[a, ylo, rows], block(2 * a, r, 0, rows), 2 * a, r, 0, d, r).start()
        return carry

    lax.fori_loop(0, arrays, begin, 0)

    def begin_other(a, carry):
        swap_arrived(a).wait_recv()
        for r in range(2):
            rows = pl.ds(32 * r, 32)
            for d in range(2):
                mine = block(2 * a + 1, r, 0, rows)
                move(mine, mine, 2 * a + 1, r, 0, d, r).start()
        return carry

    lax.fori_loop(0, arrays, begin_other, 0)

    def forward(s, carry):
        for r in range(2):
            for d in range(2):
                rows = pl.ds(32 * r, 32)
                came = block(s, r, -SIGNS[d], rows)
                move(came, came, s, r, 0, d, r).wait_recv()
                piece = block(s, r, -SIGNS[d], pl.ds(32 * r + 16 * d, 16))
                move(piece, piece, s, r, 1, d, r).start()
        return carry

    lax.fori_loop(0, 2 * arrays, forward, 0)

    def wait_local(a, carry):
        local(a).wait()
        return carry

    lax.fori_loop(0, arrays, wait_local, 0)

    def lines(s, carry):
        for r in range(2):
            for d in range(2):
                piece = block(s, r, 2, pl.ds(32 * r + 16 * d, 16))
                move(piece, piece, s, r, 1, d, r).wait_recv()
            for d in range(2):
                mine = line(s, r, 0, slice(None))
                move(mine, mine, s, r, 2, d, 1 - r).start()
        return carry

    lax.fori_loop(0, 2 * arrays, lines, 0)

    def forward_lines(s, carry):
        for r in range(2):
            for d in range(2):
                came = line(s, r, -SIGNS[d], slice(None))
                move(came, came, s, r, 2, d, 1 - r).wait_recv()
                piece = line(s, r, -SIGNS[d], pl.ds(2 * d, 2))
                move(piece, piece, s, r, 3, d, 1 - r).start()
        return carry

    lax.fori_loop(0, 2 * arrays, forward_lines, 0)

    def finish(s, carry):
        for r in range(2):
            for d in range(2):
                piece = line(s, r, 2, pl.ds(2 * d, 2))
                move(piece, piece, s, r, 3, d, 1 - r).wait_recv()
                rows = pl.ds(32 * r, 32)
                mine = block(s, r, 0, rows)
                move(mine, mine, s, r, 0, d, r).wait_send()
                piece = block(s, r, -SIGNS[d], pl.ds(32 * r + 16 * d, 16))
                move(piece, piece, s, r, 1, d, r).wait_send()
                mine = line(s, r, 0, slice(None))
                move(mine, mine, s, r, 2, d, 1 - r).wait_send()
                piece = line(s, r, -SIGNS[d], pl.ds(2 * d, 2))
                move(piece, piece, s, r, 3, d, 1 - r).wait_send()
        return carry

    lax.fori_loop(0, 2 * arrays, finish, 0)

    def finish_swap(a, carry):
        swap(a).wait_send()
        return carry

    lax.fori_loop(0, arrays, finish_swap, 0)


def weight_gather(own, collective_id):
    arrays = own.shape[0]
    return pl.pallas_call(
        weight_gather_kernel,
        out_shape=jax.ShapeDtypeStruct((arrays, 2, 4, 4, 64, PART), bf16),
        in_specs=[ANY],
        out_specs=ANY,
        scratch_shapes=[sems(arrays), sems(arrays), sems(arrays), sems(arrays * 32), sems(arrays * 32)],
        compiler_params=params(collective_id),
    )(own)


def add_rows(count, one):
    def body(i, carry):
        one(pl.ds(pl.multiple_of(i * 16, 16), 16))
        return carry

    lax.fori_loop(0, count // 16, body, 0)


def weight_sum_kernel(
    grads, out, wide, wide_out, middle, thin, thin_out, total, swap_send, swap_recv, send, recv
):
    ylo, x, z, yhi, core = place()
    partner = lo_partner()
    near = [[xz_neighbour(axis, d) for d in SIGNS] for axis in (0, 1)]
    greet([partner] + near[0] + near[1])
    streams = grads.shape[0] * 2

    def number(s, r, stage, d):
        return ((s * 2 + r) * 6 + stage) * 2 + d

    def move(src, dst, s, r, stage, d, axis):
        n = number(s, r, stage, d)
        return remote(src, dst, send.at[n], recv.at[n], near[axis][d])

    def line(s, r, step, part):
        a, yl = lax.div(s, 2), lax.rem(s, 2)
        if r == 0:
            return grads.at[a, yl, part, ring(z, step), pl.ds(0, 32)]
        return grads.at[a, yl, ring(x, step), part, pl.ds(32, 32)]

    def at(r):
        return x if r == 0 else z

    def wide_move(s, r, d, kind):
        if kind == 0:
            src = line(s, r, 2, pl.ds(2 * d, 2))
        elif kind == 1:
            src = line(s, r, SIGNS[d], pl.ds(2 - 2 * d, 2))
        else:
            src = wide_out.at[s, r, d]
        return move(src, wide.at[s, r, kind, d], s, r, kind, d, 1 - r)

    def thin_move(s, r, d, kind):
        if kind == 0:
            src = middle.at[s, r, ring(at(r), 2), pl.ds(16 * d, 16)]
        elif kind == 1:
            src = middle.at[s, r, ring(at(r), SIGNS[d]), pl.ds(16 - 16 * d, 16)]
        else:
            src = thin_out.at[s, r, d]
        return move(src, thin.at[s, r, kind, d], s, r, 3 + kind, d, r)

    def step_one(s, carry):
        for r in range(2):
            for d in range(2):
                wide_move(s, r, d, 0).start()
        for r in range(2):
            for d in range(2):
                wide_move(s, r, d, 1).start()
        return carry

    lax.fori_loop(0, streams, step_one, 0)

    def step_two(s, carry):
        for r in range(2):
            for d in range(2):
                wide_move(s, r, d, 0).wait_recv()
                for p in range(2):
                    mine = line(s, r, SIGNS[d], 2 * d + p)

                    def one(rows):
                        wide_out[s, r, d, p, rows] = (
                            mine[rows].astype(f32) + wide[s, r, 0, d, p, rows].astype(f32)
                        ).astype(bf16)

                    add_rows(32, one)
                wide_move(s, r, d, 2).start()
        return carry

    lax.fori_loop(0, streams, step_two, 0)

    def step_three(s, carry):
        for r in range(2):
            for d in range(2):
                wide_move(s, r, d, 1).wait_recv()
                wide_move(s, r, d, 2).wait_recv()
            for p in range(4):
                mine = line(s, r, 0, p)
                d = p // 2

                def one(rows):
                    value = mine[rows].astype(f32) + wide[s, r, 2, d, p % 2, rows].astype(f32)
                    value += wide[s, r, 1, 1 - d, p % 2, rows].astype(f32)
                    middle[s, r, p, rows] = value.astype(bf16)

                add_rows(32, one)
            for d in range(2):
                thin_move(s, r, d, 0).start()
            for d in range(2):
                thin_move(s, r, d, 1).start()
        return carry

    lax.fori_loop(0, streams, step_three, 0)

    def step_four(s, carry):
        for r in range(2):
            for d in range(2):
                thin_move(s, r, d, 0).wait_recv()
                mine = middle[s, r, ring(at(r), SIGNS[d]), pl.ds(16 * d, 16)]
                thin_out[s, r, d] = (mine.astype(f32) + thin[s, r, 0, d].astype(f32)).astype(bf16)
                thin_move(s, r, d, 2).start()
        return carry

    lax.fori_loop(0, streams, step_four, 0)

    def step_five(s, carry):
        for r in range(2):
            for d in range(2):
                thin_move(s, r, d, 1).wait_recv()
                thin_move(s, r, d, 2).wait_recv()
            for d in range(2):
                rows = pl.ds(16 * d, 16)
                value = middle[s, r, at(r), rows].astype(f32) + thin[s, r, 2, d].astype(f32)
                value += thin[s, r, 1, 1 - d].astype(f32)
                total[s, pl.ds(32 * r + 16 * d, 16)] = value.astype(bf16)
        return carry

    lax.fori_loop(0, streams, step_five, 0)

    def swap(a):
        return remote(
            total.at[2 * a + 1 - ylo], out.at[a, ylo], swap_send.at[a], swap_recv.at[a], partner
        )

    def start_swap(a, carry):
        swap(a).start()
        return carry

    def finish_swap(a, carry):
        out[a, ylo] = total[2 * a + ylo]
        remote(
            total.at[2 * a], out.at[a, 1 - ylo], swap_send.at[a], swap_recv.at[a], partner
        ).wait_recv()
        swap(a).wait_send()
        return carry

    lax.fori_loop(0, streams // 2, start_swap, 0)

    def sent(s, carry):
        for r in range(2):
            for d in range(2):
                for kind in range(3):
                    wide_move(s, r, d, kind).wait_send()
                    thin_move(s, r, d, kind).wait_send()
        return carry

    lax.fori_loop(0, streams, sent, 0)
    lax.fori_loop(0, streams // 2, finish_swap, 0)


def weight_sum(grads, collective_id):
    arrays = grads.shape[0]
    n = arrays * 2
    return pl.pallas_call(
        weight_sum_kernel,
        out_shape=jax.ShapeDtypeStruct((arrays, 2, 64, PART), bf16),
        in_specs=[VMEM],
        out_specs=VMEM,
        scratch_shapes=[
            pltpu.VMEM((n, 2, 3, 2, 2, 32, PART), bf16),
            pltpu.VMEM((n, 2, 2, 2, 32, PART), bf16),
            pltpu.VMEM((n, 2, 4, 32, PART), bf16),
            pltpu.VMEM((n, 2, 3, 2, 16, PART), bf16),
            pltpu.VMEM((n, 2, 2, 16, PART), bf16),
            pltpu.VMEM((n, 64, PART), bf16),
            sems(arrays),
            sems(arrays),
            sems(n * 24),
            sems(n * 24),
        ],
        compiler_params=params(collective_id, 56),
    )(grads.reshape(arrays, 2, 4, 4, 64, PART))


def standardize(value):
    mean = jnp.mean(value, axis=-1, keepdims=True)
    centered = value - mean
    scale_inv = lax.rsqrt(jnp.mean(centered * centered, axis=-1, keepdims=True) + epsilon)
    return (centered * scale_inv, scale_inv)


def norm_back(grad_normed_out, normed, scale_inv, gain):
    scaled = grad_normed_out * gain
    mean_one = jnp.mean(scaled, axis=-1, keepdims=True)
    mean_two = jnp.mean(scaled * normed, axis=-1, keepdims=True)
    grad_value = scale_inv * (scaled - mean_one - normed * mean_two)
    grad_gain = jnp.sum(grad_normed_out * normed, axis=0)
    grad_shift = jnp.sum(grad_normed_out, axis=0)
    return (grad_value, grad_gain, grad_shift)


def visible(segment_ids, padding):
    seq_len = segment_ids.shape[1]
    position = jnp.arange(seq_len)
    causal = position[None, :] <= position[:, None]
    itself = position[None, :] == position[:, None]
    same = segment_ids[:, :, None] == segment_ids[:, None, :]
    live = (padding[:, None, :] == 1) | itself[None]
    return same & causal[None] & live


def score_block(query_heads, key_heads, allowed):
    scores = jnp.einsum(
        "rqhe,rkhe->rhqk", query_heads, key_heads, preferred_element_type=f32
    ) * HEAD ** (-0.5)
    return jnp.where(allowed[:, None], scores, masked_score)


def on_device(
    stream,
    code_ids,
    segment_ids,
    padding,
    codebook,
    norm1_gain,
    norm1_shift,
    w_qkv,
    w_out,
    norm2_gain,
    norm2_shift,
    w_up,
    w_down,
    cotangent,
):
    ylo, x, z, yhi, core = place()

    mine = jnp.stack(
        [
            jnp.concatenate(
                [
                    w_qkv.reshape(64, 3, 2, 256).transpose(2, 0, 1, 3).reshape(2, 64, 768),
                    w_out.reshape(64, 2, 256).transpose(1, 0, 2),
                ],
                axis=2,
            ),
            w_up.reshape(64, 2, PART).transpose(1, 0, 2),
            w_down.reshape(64, 2, PART).transpose(1, 0, 2),
        ]
    )
    weights = weight_gather(mine, 0).reshape(3, WIDTH, PART)
    qkv_full, out_full = weights[0, :, :768], weights[0, :, 768:]
    up_full, down_full = weights[1], weights[2]

    norms = jnp.stack([norm1_gain, norm1_shift, norm2_gain, norm2_shift]).astype(f32)
    masks = jnp.concatenate([segment_ids.reshape(4, 128), padding.reshape(4, 128)]).astype(f32)
    norms_all, masks_other = small_gather(jnp.pad(norms, ((0, 4), (0, 64))), masks, 1)
    norms_all = norms_all[:, :4, :64].transpose(1, 0, 2).reshape(4, WIDTH)
    gain_one, shift_one, gain_two, shift_two = norms_all
    both = jnp.where(ylo == 0, jnp.stack([masks, masks_other]), jnp.stack([masks_other, masks]))
    allowed = visible(both[:, :4].reshape(2, 512), both[:, 4:].reshape(2, 512))

    ids_half = lax.dynamic_slice_in_dim(code_ids[0], core * 256, 256, 0)
    stream_half = lax.dynamic_slice_in_dim(stream[0], core * 256, 256, 0)
    cot_half = lax.dynamic_slice_in_dim(cotangent[0], core * 256, 256, 0)
    inputs_half = stream_half.astype(f32) + jnp.take(codebook, ids_half, axis=0).astype(f32)
    normed_half, inv_half = standardize(inputs_half)
    attn_half = (normed_half * gain_one + shift_one).astype(bf16)

    def share_of(value):
        return lax.dynamic_slice_in_dim(value, yhi * SHARE, SHARE, 0)

    inputs_share, normed_one, inv_one = (share_of(v) for v in (inputs_half, normed_half, inv_half))
    cot_share = share_of(cot_half).astype(f32)

    rows = row_exchange(jnp.stack([attn_half, cot_half]).reshape(2, 2, SHARE, WIDTH), 2)
    attn_in, cot = rows[0].reshape(1024, WIDTH), rows[1].reshape(1024, WIDTH)

    projected = jnp.dot(attn_in, qkv_full, preferred_element_type=f32).astype(bf16)
    query_heads, key_heads, value_heads = (
        projected[:, 256 * t : 256 * t + 256].reshape(2, 512, 2, HEAD) for t in range(3)
    )
    scores = score_block(query_heads, key_heads, allowed)
    row_max = jnp.max(scores, axis=-1, keepdims=True)
    expd = jnp.exp(scores - row_max)
    row_sum = jnp.sum(expd, axis=-1, keepdims=True)
    log_total = row_max + jnp.log(row_sum)
    prob_low = (expd / row_sum).astype(bf16)
    attended = jnp.einsum("rhqk,rkhe->rqhe", prob_low, value_heads, preferred_element_type=f32)
    attended = attended.reshape(1024, 256).astype(bf16)
    partial_branch = jnp.einsum("sf,df->sd", attended, out_full, preferred_element_type=f32)
    middle = inputs_share + share_sum(partial_branch.astype(bf16), 3)
    normed_two, inv_two = standardize(middle)
    ffn_share = (normed_two * gain_two + shift_two).astype(bf16)
    ffn_in = share_gather(ffn_share, 4).reshape(1024, WIDTH)
    up_proj = jnp.dot(ffn_in, up_full, preferred_element_type=f32)
    hidden = jax.nn.gelu(up_proj, approximate=True).astype(bf16)
    partial_ffn = jnp.einsum("sf,df->sd", hidden, down_full, preferred_element_type=f32)
    layer_out = middle + share_sum(partial_ffn.astype(bf16), 5)

    grad_w_down = jnp.einsum("sd,sf->df", cot, hidden, preferred_element_type=f32).astype(bf16)
    grad_hidden = jnp.dot(cot, down_full, preferred_element_type=f32)
    _, gelu_pull = jax.vjp(lambda value: jax.nn.gelu(value, approximate=True), up_proj)
    grad_up = gelu_pull(grad_hidden)[0].astype(bf16)
    grad_w_up = jnp.einsum("sd,sf->df", ffn_in, grad_up, preferred_element_type=f32).astype(bf16)
    partial_ffn_in = jnp.einsum("sf,df->sd", grad_up, up_full, preferred_element_type=f32)
    grad_ffn_in = share_sum(partial_ffn_in.astype(bf16), 6)
    grad_norm_mid, grad_gain_two, grad_shift_two = norm_back(
        grad_ffn_in, normed_two, inv_two, gain_two
    )
    grad_middle = cot_share + grad_norm_mid
    grad_branch = share_gather(grad_middle.astype(bf16), 7).reshape(1024, WIDTH)
    grad_w_out = jnp.einsum("sd,sf->df", grad_branch, attended, preferred_element_type=f32)
    grad_attended = jnp.dot(grad_branch, out_full, preferred_element_type=f32).astype(bf16)
    grad_att_heads = grad_attended.reshape(2, 512, 2, HEAD)
    again_scores = score_block(query_heads, key_heads, allowed)
    probs = jnp.exp(again_scores - log_total)
    probs_low = probs.astype(bf16)
    grad_probs = jnp.einsum(
        "rqhe,rkhe->rhqk", grad_att_heads, value_heads, preferred_element_type=f32
    )
    inner = jnp.sum(grad_probs * probs, axis=-1, keepdims=True)
    grad_scores = (probs * (grad_probs - inner)).astype(bf16)
    grad_query = jnp.einsum(
        "rhqk,rkhe->rqhe", grad_scores, key_heads, preferred_element_type=f32
    ) * HEAD ** (-0.5)
    grad_key = jnp.einsum(
        "rhqk,rqhe->rkhe", grad_scores, query_heads, preferred_element_type=f32
    ) * HEAD ** (-0.5)
    grad_value = jnp.einsum(
        "rhqk,rqhe->rkhe", probs_low, grad_att_heads, preferred_element_type=f32
    )
    grad_projected = jnp.concatenate(
        [g.reshape(1024, 256) for g in (grad_query, grad_key, grad_value)], axis=1
    ).astype(bf16)
    grad_w_qkv = jnp.einsum("sd,sf->df", attn_in, grad_projected, preferred_element_type=f32)
    partial_attn_in = jnp.einsum("sf,df->sd", grad_projected, qkv_full, preferred_element_type=f32)
    grad_attn_in = share_sum(partial_attn_in.astype(bf16), 8)
    grad_norm_in, grad_gain_one, grad_shift_one = norm_back(
        grad_attn_in, normed_one, inv_one, gain_one
    )
    input_grad = grad_middle + grad_norm_in

    grads = jnp.stack(
        [
            jnp.concatenate([grad_w_qkv.astype(bf16), grad_w_out.astype(bf16)], axis=1),
            grad_w_up,
            grad_w_down,
        ]
    )
    summed = weight_sum(grads, 9).astype(f32)
    out_qkv = summed[0, :, :, :768].reshape(2, 64, 3, 256).transpose(1, 2, 0, 3).reshape(64, 3, 512)
    out_out = summed[0, :, :, 768:].transpose(1, 0, 2).reshape(64, 512)
    out_up = summed[1].transpose(1, 0, 2).reshape(64, WIDTH)
    out_down = summed[2].transpose(1, 0, 2).reshape(64, WIDTH)

    small = jnp.stack([grad_gain_one, grad_shift_one, grad_gain_two, grad_shift_two])
    small = jnp.pad(small.reshape(4, 32, 64).transpose(1, 0, 2), ((0, 0), (0, 4), (0, 64)))
    small = small_reduce(small, 10)[:4, :64]

    tokens = row_gather(jnp.stack([layer_out.astype(bf16), input_grad.astype(bf16)]), 11)
    tokens = tokens.reshape(2, 1, 512, WIDTH).astype(f32)
    return (
        tokens[0],
        tokens[1],
        small[0],
        small[1],
        out_qkv,
        out_out,
        small[2],
        small[3],
        out_up,
        out_down,
    )


def solution(mesh):
    in_specs = (
        P("dp", None, None),
        P("dp", None),
        P("dp", None),
        P("dp", None),
        P(),
        P("dp"),
        P("dp"),
        P("dp", None, "mp"),
        P("dp", "mp"),
        P("dp"),
        P("dp"),
        P("dp", "mp"),
        P("dp", "mp"),
        P("dp", None, None),
    )
    out_specs = (
        P("dp", None, None),
        P("dp", None, None),
        P("dp"),
        P("dp"),
        P("dp", None, "mp"),
        P("dp", "mp"),
        P("dp"),
        P("dp"),
        P("dp", "mp"),
        P("dp", "mp"),
    )
    return jax.shard_map(
        on_device, mesh=mesh, in_specs=in_specs, out_specs=out_specs, check_vma=False
    )
```

```python
import functools

import jax
import jax.numpy as jnp
from jax import lax
from jax.experimental import pallas as pl
from jax.experimental.pallas import tpu as pltpu
from jax.sharding import PartitionSpec as P

HEAD = 128
WIDTH = 2048
SHARE = 128
PART = 1024
MESH = pl.DeviceIdType.MESH
ANY = pl.BlockSpec(memory_space=pl.ANY)
VMEM = pl.BlockSpec(memory_space=pltpu.VMEM)
masked_score = -1000000000.0
epsilon = 1e-05
f32 = jnp.float32
bf16 = jnp.bfloat16


def place():
    dp, mp = lax.axis_index("dp"), lax.axis_index("mp")
    return lax.div(dp, 16), lax.rem(lax.div(dp, 4), 4), lax.rem(dp, 4), lax.div(mp, 2), lax.rem(mp, 2)


def ring(position, step):
    return lax.rem(position + step + 4, 4)


def xz_neighbour(axis, step):
    ylo, x, z, yhi, core = place()
    if axis == 0:
        x = ring(x, step)
    else:
        z = ring(z, step)
    return (ylo * 16 + x * 4 + z, yhi * 2 + core)


def y_peer(step):
    ylo, x, z, yhi, core = place()
    y = ring(yhi * 2 + ylo, step)
    return (lax.rem(y, 2) * 16 + x * 4 + z, lax.div(y, 2) * 2 + core)


def lo_partner():
    ylo, x, z, yhi, core = place()
    return ((1 - ylo) * 16 + x * 4 + z, yhi * 2 + core)


def core_partner():
    ylo, x, z, yhi, core = place()
    return (ylo * 16 + x * 4 + z, yhi * 2 + 1 - core)


def greet(peers):
    barrier = pltpu.get_barrier_semaphore()
    for peer in peers:
        pl.semaphore_signal(barrier, inc=1, device_id=peer, device_id_type=MESH)
    pl.semaphore_wait(barrier, len(peers))


def remote(src, dst, send_sem, recv_sem, peer):
    return pltpu.make_async_remote_copy(
        src_ref=src,
        dst_ref=dst,
        send_sem=send_sem,
        recv_sem=recv_sem,
        device_id=peer,
        device_id_type=MESH,
    )


def sems(*shape):
    return pltpu.SemaphoreType.DMA(shape)


def params(collective_id, mib=48):
    return pltpu.CompilerParams(
        collective_id=collective_id, has_side_effects=True, vmem_limit_bytes=mib << 20
    )


PEERS = {
    "core": core_partner,
    "x+": lambda: xz_neighbour(0, 1),
    "x-": lambda: xz_neighbour(0, -1),
    "z+": lambda: xz_neighbour(1, 1),
    "z-": lambda: xz_neighbour(1, -1),
    "y1": lambda: y_peer(1),
    "y2": lambda: y_peer(2),
    "y3": lambda: y_peer(3),
}


def fused_kernel(jobs, schedule, *refs):
    taken = 0

    def take(count):
        nonlocal taken
        taken += count
        return refs[taken - count : taken]

    ins = [take(len(job["ins"])) for job in jobs]
    outs = [take(len(job["outs"])) for job in jobs]
    scratch = [take(len(job["scratch"])) for job in jobs]
    greet([PEERS[name]() for name in sorted({name for job in jobs for name in job["peers"]})])
    runs = [job["steps"](*i, *o, *s) for job, i, o, s in zip(jobs, ins, outs, scratch)]
    for which in schedule:
        next(runs[int(which)], None)
    for run in runs:
        for _ in run:
            pass


def fused(jobs, schedule, collective_id, mib=48):
    results = pl.pallas_call(
        functools.partial(fused_kernel, jobs, schedule),
        out_shape=[shape for job in jobs for shape, _ in job["outs"]],
        in_specs=[spec for job in jobs for _, spec in job["ins"]],
        out_specs=[spec for job in jobs for _, spec in job["outs"]],
        scratch_shapes=[one for job in jobs for one in job["scratch"]],
        compiler_params=params(collective_id, mib),
    )(*[array for job in jobs for array, _ in job["ins"]])
    return results


def shaped(dtype, *shape):
    return jax.ShapeDtypeStruct(shape, dtype)


def small_gather_kernel(own, mask, everyone, mask_out, send, recv, mask_send, mask_recv):
    dp, mp = lax.axis_index("dp"), lax.axis_index("mp")
    barrier = pltpu.get_barrier_semaphore()

    def greet_one(k, carry):
        pl.semaphore_signal(
            barrier, inc=1, device_id=(lax.rem(dp + k, 32), mp), device_id_type=MESH
        )
        return carry

    lax.fori_loop(1, 32, greet_one, 0)
    pl.semaphore_wait(barrier, 31)

    def move(k):
        peer = lax.rem(dp + k, 32)
        return remote(own, everyone.at[dp], send.at[k], recv.at[dp], (peer, mp))

    def start(k, carry):
        move(k).start()
        return carry

    def finish(k, carry):
        source = lax.rem(dp + k, 32)
        move(k).wait_send()
        remote(own, everyone.at[source], send.at[k], recv.at[source], (source, mp)).wait_recv()
        return carry

    swap = remote(mask, mask_out, mask_send, mask_recv, lo_partner())
    swap.start()
    lax.fori_loop(1, 32, start, 0)
    everyone[dp] = own[...]
    lax.fori_loop(1, 32, finish, 0)
    swap.wait()


def small_gather(own, mask, collective_id):
    return pl.pallas_call(
        small_gather_kernel,
        out_shape=(
            jax.ShapeDtypeStruct((32, 8, 128), f32),
            jax.ShapeDtypeStruct((8, 128), f32),
        ),
        in_specs=[VMEM, VMEM],
        out_specs=(VMEM, VMEM),
        scratch_shapes=[sems(32), sems(32), pltpu.SemaphoreType.DMA, pltpu.SemaphoreType.DMA],
        compiler_params=params(collective_id, 8),
    )(own, mask)


def small_reduce_kernel(pieces, out, arrived, summed, more, send, recv, send_two, recv_two):
    dp, mp = lax.axis_index("dp"), lax.axis_index("mp")
    barrier = pltpu.get_barrier_semaphore()

    def greet_one(k, carry):
        pl.semaphore_signal(
            barrier, inc=1, device_id=(lax.rem(dp + k, 32), mp), device_id_type=MESH
        )
        return carry

    lax.fori_loop(1, 32, greet_one, 0)
    for k in (1, 2, 3):
        pl.semaphore_signal(
            barrier, inc=1, device_id=(dp, lax.rem(mp + k, 4)), device_id_type=MESH
        )
    pl.semaphore_wait(barrier, 34)

    def move(k):
        peer = lax.rem(dp + k, 32)
        return remote(pieces.at[peer], arrived.at[k], send.at[k], recv.at[k], (peer, mp))

    def start(k, carry):
        move(k).start()
        return carry

    def finish(k, total):
        move(k).wait()
        return total + arrived[k]

    lax.fori_loop(1, 32, start, 0)
    summed[...] = lax.fori_loop(1, 32, finish, pieces[dp])
    copies = [
        remote(summed, more.at[k - 1], send_two.at[k], recv_two.at[k], (dp, lax.rem(mp + k, 4)))
        for k in (1, 2, 3)
    ]
    for copy in copies:
        copy.start()
    for copy in copies:
        copy.wait()
    out[...] = summed[...] + more[0] + more[1] + more[2]


def small_reduce(pieces, collective_id):
    return pl.pallas_call(
        small_reduce_kernel,
        out_shape=jax.ShapeDtypeStruct((8, 128), f32),
        in_specs=[VMEM],
        out_specs=VMEM,
        scratch_shapes=[
            pltpu.VMEM((32, 8, 128), f32),
            pltpu.VMEM((8, 128), f32),
            pltpu.VMEM((3, 8, 128), f32),
            sems(32),
            sems(32),
            sems(4),
            sems(4),
        ],
        compiler_params=params(collective_id, 8),
    )(pieces)


def row_exchange(halves):
    count = halves.shape[0]

    def steps(halves, full, local_sem, send, recv):
        ylo, x, z, yhi, core = place()
        up, down, other = y_peer(1), y_peer(3), core_partner()
        first = []
        for n in range(count):
            for u, peer in ((0, up), (1, down)):
                here = full.at[n, ylo, core, u]
                first.append(remote(halves.at[n, u], here, send.at[n, u], recv.at[n, u], peer))
        for n in range(count):
            here = full.at[n, ylo, core]
            first.append(remote(halves.at[n], here, send.at[n, 2], recv.at[n, 2], other))
        for copy in first:
            copy.start()
        local = [
            pltpu.make_async_copy(halves.at[n], full.at[n, ylo, core], local_sem.at[n])
            for n in range(count)
        ]
        for copy in local:
            copy.start()
        yield
        second = []
        for n in range(count):
            for u in range(2):
                here = full.at[n, 1 - ylo, core, u]
                remote(halves.at[n, u], here, send.at[n, u], recv.at[n, u], up).wait_recv()
                copy = remote(here, here, send.at[n, 3 + u], recv.at[n, 3 + u], other)
                copy.start()
                second.append(copy)
        yield
        for n in range(count):
            here = full.at[n, ylo, 1 - core]
            remote(halves.at[n], here, send.at[n, 2], recv.at[n, 2], other).wait_recv()
            for u in range(2):
                here = full.at[n, 1 - ylo, 1 - core, u]
                remote(here, here, send.at[n, 3 + u], recv.at[n, 3 + u], other).wait_recv()
        for copy in first + second:
            copy.wait_send()
        for copy in local:
            copy.wait()

    return {
        "ins": [(halves, ANY)],
        "outs": [(shaped(bf16, count, 2, 2, 2, SHARE, WIDTH), ANY)],
        "scratch": [sems(count), sems(count, 5), sems(count, 5)],
        "peers": ["y1", "y3", "core"],
        "steps": steps,
    }


def share_gather(share):
    def steps(share, full, local_sem, send, recv):
        ylo, x, z, yhi, core = place()
        y = yhi * 2 + ylo
        other = core_partner()
        mine = full.at[ylo, core, yhi]
        local = pltpu.make_async_copy(share, mine, local_sem)
        first = [
            remote(share, mine, send.at[k], recv.at[k], y_peer(k) if k else other)
            for k in (2, 1, 3, 0)
        ]
        for copy in first:
            copy.start()
        local.start()
        yield
        second = []
        for k in (1, 3, 2):
            source = ring(y, -k)
            here = full.at[lax.rem(source, 2), core, lax.div(source, 2)]
            remote(share, here, send.at[k], recv.at[k], y_peer(4 - k)).wait_recv()
            copy = remote(here, here, send.at[3 + k], recv.at[3 + k], other)
            copy.start()
            second.append(copy)
        yield
        remote(share, full.at[ylo, 1 - core, yhi], send.at[0], recv.at[0], other).wait_recv()
        for k in (1, 3, 2):
            source = ring(y, -k)
            here = full.at[lax.rem(source, 2), 1 - core, lax.div(source, 2)]
            remote(here, here, send.at[3 + k], recv.at[3 + k], other).wait_recv()
        for copy in first + second:
            copy.wait_send()
        local.wait()

    return {
        "ins": [(share, ANY)],
        "outs": [(shaped(bf16, 2, 2, 2, SHARE, WIDTH), ANY)],
        "scratch": [pltpu.SemaphoreType.DMA, sems(7), sems(7)],
        "peers": ["y1", "y2", "y3", "core"],
        "steps": steps,
    }


def add_rows(count, one):
    def body(i, carry):
        one(pl.ds(pl.multiple_of(i * 16, 16), 16))
        return carry

    lax.fori_loop(0, count // 16, body, 0)


def share_sum(partial):
    def steps(partial, out, from_core, turned, arrived, send, recv, send_two, recv_two):
        ylo, x, z, yhi, core = place()
        y = yhi * 2 + ylo
        other = core_partner()

        def block(k, half):
            target = ring(y, k)
            return partial.at[lax.rem(target, 2), half, lax.div(target, 2)]

        first = {}
        for k in (2, 1, 3, 0):
            first[k] = remote(block(k, 1 - core), from_core.at[k], send.at[k], recv.at[k], other)
            first[k].start()
        yield
        second = {}
        for k in (2, 1, 3):
            first[k].wait_recv()
            mine = block(k, core)

            def add(rows):
                value = mine[rows].astype(f32) + from_core[k, rows].astype(f32)
                turned[k, rows] = value.astype(bf16)

            add_rows(SHARE, add)
            second[k] = remote(turned.at[k], arrived.at[k], send_two.at[k], recv_two.at[k], y_peer(k))
            second[k].start()
        yield
        first[0].wait_recv()
        for k in (1, 3, 2):
            second[k].wait_recv()
        mine_own = block(0, core)

        def total(rows):
            value = mine_own[rows].astype(f32) + from_core[0, rows].astype(f32)
            for k in (1, 2, 3):
                value += arrived[k, rows].astype(f32)
            out[rows] = value

        add_rows(SHARE, total)
        for k in range(4):
            first[k].wait_send()
        for k in (1, 2, 3):
            second[k].wait_send()

    return {
        "ins": [(partial.reshape(2, 2, 2, SHARE, WIDTH), VMEM)],
        "outs": [(shaped(f32, SHARE, WIDTH), VMEM)],
        "scratch": [pltpu.VMEM((4, SHARE, WIDTH), bf16)] * 3 + [sems(4)] * 4,
        "peers": ["y1", "y2", "y3", "core"],
        "steps": steps,
    }


def row_gather(share):
    count = share.shape[0]

    def steps(share, full, local_sem, send, recv):
        ylo, x, z, yhi, core = place()
        across, other = y_peer(2), core_partner()
        mine = full.at[:, core, yhi]
        far = full.at[:, core, 1 - yhi]
        local = pltpu.make_async_copy(share, mine, local_sem)
        one = remote(share, mine, send.at[0], recv.at[0], across)
        two = remote(share, mine, send.at[1], recv.at[1], other)
        one.start()
        two.start()
        local.start()
        yield
        remote(share, far, send.at[0], recv.at[0], across).wait_recv()
        three = remote(far, far, send.at[2], recv.at[2], other)
        three.start()
        yield
        remote(share, full.at[:, 1 - core, yhi], send.at[1], recv.at[1], other).wait_recv()
        last = full.at[:, 1 - core, 1 - yhi]
        remote(last, last, send.at[2], recv.at[2], other).wait_recv()
        for copy in (one, two, three):
            copy.wait_send()
        local.wait()

    return {
        "ins": [(share, ANY)],
        "outs": [(shaped(bf16, count, 2, 2, SHARE, WIDTH), ANY)],
        "scratch": [pltpu.SemaphoreType.DMA, sems(3), sems(3)],
        "peers": ["y2", "core"],
        "steps": steps,
    }


SIGNS = (1, -1)
XZ = ["x+", "x-", "z+", "z-"]


def xz_near():
    return [[xz_neighbour(axis, d) for d in SIGNS] for axis in (0, 1)]


def weight_gather(own):
    def steps(own, full, local_sem, swap_send, swap_recv, send, recv):
        ylo, x, z, yhi, core = place()
        near = xz_near()
        partner = lo_partner()
        offsets = (0, -1, 1, 2)

        def move(src, dst, s, r, stage, d, axis):
            n = ((s * 2 + r) * 8 + stage) * 2 + d
            return remote(src, dst, send.at[n], recv.at[n], near[axis][d])

        def block(s, r, one, two, rows):
            yl = ylo if s == 0 else 1 - ylo
            if r == 0:
                return full.at[yl, ring(x, one), ring(z, two), rows]
            return full.at[yl, ring(x, two), ring(z, one), rows]

        def rows_of(r, d=None):
            return pl.ds(32 * r, 32) if d is None else pl.ds(32 * r + 16 * d, 16)

        local = pltpu.make_async_copy(own.at[ylo], full.at[ylo, x, z], local_sem)
        swap = remote(own.at[1 - ylo], full.at[ylo, x, z], swap_send, swap_recv, partner)
        swap.start()
        sent = []

        def go(*args):
            copy = move(*args)
            copy.start()
            sent.append(copy)

        def begin(s, source):
            for r in range(2):
                for d in range(2):
                    src = source.at[rows_of(r)]
                    go(src, block(s, r, 0, 0, rows_of(r)), s, r, 0, d, r)
            for r in range(2):
                for d in range(2):
                    src = source.at[rows_of(r)]
                    go(src, block(s, r, 0, 0, rows_of(r)), s, r, 2, d, 1 - r)

        begin(0, own.at[ylo])
        local.start()
        yield
        remote(own.at[1 - ylo], full.at[1 - ylo, x, z], swap_send, swap_recv, partner).wait_recv()
        begin(1, full.at[1 - ylo, x, z])
        yield
        for s in range(2):
            for r in range(2):
                for d in range(2):
                    came = block(s, r, -SIGNS[d], 0, rows_of(r))
                    move(came, came, s, r, 0, d, r).wait_recv()
                    piece = block(s, r, -SIGNS[d], 0, rows_of(r, d))
                    go(piece, piece, s, r, 1, d, r)
                for part in (1, 2):
                    for d in range(2):
                        mine = block(s, r, offsets[part], 0, rows_of(r))
                        go(mine, mine, s, r, 2 + part, d, 1 - r)
            yield
        for s in range(2):
            for r in range(2):
                for d in range(2):
                    piece = block(s, r, 2, 0, rows_of(r, d))
                    move(piece, piece, s, r, 1, d, r).wait_recv()
                for d in range(2):
                    mine = block(s, r, 2, 0, rows_of(r))
                    go(mine, mine, s, r, 5, d, 1 - r)
            yield
        for part in (0, 2, 1, 3):
            d = part // 2
            for s in range(2):
                for r in range(2):
                    came = block(s, r, offsets[part], -SIGNS[d], rows_of(r))
                    move(came, came, s, r, 2 + part, d, 1 - r).wait_recv()
                    go(came, came, s, r, 6 + part % 2, d, 1 - r)
            yield
        for s in range(2):
            for r in range(2):
                for part in range(4):
                    d = 1 - part // 2
                    came = block(s, r, offsets[part], -SIGNS[d], rows_of(r))
                    move(came, came, s, r, 2 + part, d, 1 - r).wait_recv()
                for part in range(4):
                    d = part // 2
                    came = block(s, r, offsets[part], 2, rows_of(r))
                    move(came, came, s, r, 6 + part % 2, d, 1 - r).wait_recv()
        for copy in sent:
            copy.wait_send()
        swap.wait_send()
        local.wait()

    return {
        "ins": [(own, ANY)],
        "outs": [(shaped(bf16, 2, 4, 4, 64, PART), ANY)],
        "scratch": [pltpu.SemaphoreType.DMA] * 3 + [sems(64), sems(64)],
        "peers": XZ + ["y1", "y3"],
        "steps": steps,
    }


def weight_sum(grads):
    def steps(grads, out, wide, wide_out, middle, thin, thin_out, total, swap_send, swap_recv, send, recv):
        ylo, x, z, yhi, core = place()
        near = xz_near()
        partner = lo_partner()

        def move(src, dst, s, r, stage, d, axis):
            n = ((s * 2 + r) * 6 + stage) * 2 + d
            return remote(src, dst, send.at[n], recv.at[n], near[axis][d])

        def line(s, r, step, part):
            if r == 0:
                return grads.at[s, part, ring(z, step), pl.ds(0, 32)]
            return grads.at[s, ring(x, step), part, pl.ds(32, 32)]

        def at(r):
            return x if r == 0 else z

        def wide_move(s, r, d, kind):
            if kind == 0:
                src = line(s, r, 2, pl.ds(2 * d, 2))
            elif kind == 1:
                src = line(s, r, SIGNS[d], pl.ds(2 - 2 * d, 2))
            else:
                src = wide_out.at[s, r, d]
            return move(src, wide.at[s, r, kind, d], s, r, kind, d, 1 - r)

        def thin_move(s, r, d, kind):
            if kind == 0:
                src = middle.at[s, r, ring(at(r), 2), pl.ds(16 * d, 16)]
            elif kind == 1:
                src = middle.at[s, r, ring(at(r), SIGNS[d]), pl.ds(16 - 16 * d, 16)]
            else:
                src = thin_out.at[s, r, d]
            return move(src, thin.at[s, r, kind, d], s, r, 3 + kind, d, r)

        for s in range(2):
            for kind in range(2):
                for r in range(2):
                    for d in range(2):
                        wide_move(s, r, d, kind).start()
        yield

        def step_two(s, carry):
            for r in range(2):
                for d in range(2):
                    wide_move(s, r, d, 0).wait_recv()
                    for p in range(2):
                        mine = line(s, r, SIGNS[d], 2 * d + p)

                        def one(rows):
                            value = mine[rows].astype(f32) + wide[s, r, 0, d, p, rows].astype(f32)
                            wide_out[s, r, d, p, rows] = value.astype(bf16)

                        add_rows(32, one)
                    wide_move(s, r, d, 2).start()
            return carry

        lax.fori_loop(0, 2, step_two, 0)
        yield

        def step_three(s, carry):
            for r in range(2):
                for d in range(2):
                    wide_move(s, r, d, 1).wait_recv()
                    wide_move(s, r, d, 2).wait_recv()
                for p in range(4):
                    mine = line(s, r, 0, p)
                    d = p // 2

                    def one(rows):
                        value = mine[rows].astype(f32) + wide[s, r, 2, d, p % 2, rows].astype(f32)
                        value += wide[s, r, 1, 1 - d, p % 2, rows].astype(f32)
                        middle[s, r, p, rows] = value.astype(bf16)

                    add_rows(32, one)
                for kind in range(2):
                    for d in range(2):
                        thin_move(s, r, d, kind).start()
            return carry

        lax.fori_loop(0, 2, step_three, 0)
        yield

        def step_four(s, carry):
            for r in range(2):
                for d in range(2):
                    thin_move(s, r, d, 0).wait_recv()
                    mine = middle[s, r, ring(at(r), SIGNS[d]), pl.ds(16 * d, 16)]
                    value = mine.astype(f32) + thin[s, r, 0, d].astype(f32)
                    thin_out[s, r, d] = value.astype(bf16)
                    thin_move(s, r, d, 2).start()
            return carry

        lax.fori_loop(0, 2, step_four, 0)
        yield

        def step_five(s, carry):
            for r in range(2):
                for d in range(2):
                    thin_move(s, r, d, 1).wait_recv()
                    thin_move(s, r, d, 2).wait_recv()
                for d in range(2):
                    rows = pl.ds(16 * d, 16)
                    value = middle[s, r, at(r), rows].astype(f32) + thin[s, r, 2, d].astype(f32)
                    value += thin[s, r, 1, 1 - d].astype(f32)
                    total[s, pl.ds(32 * r + 16 * d, 16)] = value.astype(bf16)
            return carry

        lax.fori_loop(0, 2, step_five, 0)
        swap = remote(total.at[1 - ylo], out.at[ylo], swap_send, swap_recv, partner)
        swap.start()
        out[ylo] = total[ylo]
        yield
        for s in range(2):
            for r in range(2):
                for d in range(2):
                    for kind in range(3):
                        wide_move(s, r, d, kind).wait_send()
                        thin_move(s, r, d, kind).wait_send()
        remote(total.at[0], out.at[1 - ylo], swap_send, swap_recv, partner).wait_recv()
        swap.wait_send()

    return {
        "ins": [(grads.reshape(2, 4, 4, 64, PART), VMEM)],
        "outs": [(shaped(bf16, 2, 64, PART), VMEM)],
        "scratch": [
            pltpu.VMEM((2, 2, 3, 2, 2, 32, PART), bf16),
            pltpu.VMEM((2, 2, 2, 2, 32, PART), bf16),
            pltpu.VMEM((2, 2, 4, 32, PART), bf16),
            pltpu.VMEM((2, 2, 3, 2, 16, PART), bf16),
            pltpu.VMEM((2, 2, 2, 16, PART), bf16),
            pltpu.VMEM((2, 64, PART), bf16),
            pltpu.SemaphoreType.DMA,
            pltpu.SemaphoreType.DMA,
            sems(48),
            sems(48),
        ],
        "peers": XZ + ["y1", "y3"],
        "steps": steps,
    }


def standardize(value):
    mean = jnp.mean(value, axis=-1, keepdims=True)
    centered = value - mean
    scale_inv = lax.rsqrt(jnp.mean(centered * centered, axis=-1, keepdims=True) + epsilon)
    return (centered * scale_inv, scale_inv)


def norm_back(grad_normed_out, normed, scale_inv, gain):
    scaled = grad_normed_out * gain
    mean_one = jnp.mean(scaled, axis=-1, keepdims=True)
    mean_two = jnp.mean(scaled * normed, axis=-1, keepdims=True)
    grad_value = scale_inv * (scaled - mean_one - normed * mean_two)
    grad_gain = jnp.sum(grad_normed_out * normed, axis=0)
    grad_shift = jnp.sum(grad_normed_out, axis=0)
    return (grad_value, grad_gain, grad_shift)


def visible(segment_ids, padding):
    seq_len = segment_ids.shape[1]
    position = jnp.arange(seq_len)
    causal = position[None, :] <= position[:, None]
    itself = position[None, :] == position[:, None]
    same = segment_ids[:, :, None] == segment_ids[:, None, :]
    live = (padding[:, None, :] == 1) | itself[None]
    return same & causal[None] & live


def score_block(query_heads, key_heads, allowed):
    scores = jnp.einsum(
        "rqhe,rkhe->rhqk", query_heads, key_heads, preferred_element_type=f32
    ) * HEAD ** (-0.5)
    return jnp.where(allowed[:, None], scores, masked_score)


def on_device(
    stream,
    code_ids,
    segment_ids,
    padding,
    codebook,
    norm1_gain,
    norm1_shift,
    w_qkv,
    w_out,
    norm2_gain,
    norm2_shift,
    w_up,
    w_down,
    cotangent,
):
    ylo, x, z, yhi, core = place()

    own_attn = jnp.concatenate(
        [
            w_qkv.reshape(64, 3, 2, 256).transpose(2, 0, 1, 3).reshape(2, 64, 768),
            w_out.reshape(64, 2, 256).transpose(1, 0, 2),
        ],
        axis=2,
    )
    own_up = w_up.reshape(64, 2, PART).transpose(1, 0, 2)
    own_down = w_down.reshape(64, 2, PART).transpose(1, 0, 2)

    norms = jnp.stack([norm1_gain, norm1_shift, norm2_gain, norm2_shift]).astype(f32)
    masks = jnp.concatenate([segment_ids.reshape(4, 128), padding.reshape(4, 128)]).astype(f32)
    norms_all, masks_other = small_gather(jnp.pad(norms, ((0, 4), (0, 64))), masks, 1)
    norms_all = norms_all[:, :4, :64].transpose(1, 0, 2).reshape(4, WIDTH)
    gain_one, shift_one, gain_two, shift_two = norms_all
    both = jnp.where(ylo == 0, jnp.stack([masks, masks_other]), jnp.stack([masks_other, masks]))
    allowed = visible(both[:, :4].reshape(2, 512), both[:, 4:].reshape(2, 512))

    ids_half = lax.dynamic_slice_in_dim(code_ids[0], core * 256, 256, 0)
    stream_half = lax.dynamic_slice_in_dim(stream[0], core * 256, 256, 0)
    cot_half = lax.dynamic_slice_in_dim(cotangent[0], core * 256, 256, 0)
    inputs_half = stream_half.astype(f32) + jnp.take(codebook, ids_half, axis=0).astype(f32)
    normed_half, inv_half = standardize(inputs_half)
    attn_half = (normed_half * gain_one + shift_one).astype(bf16)

    def share_of(value):
        return lax.dynamic_slice_in_dim(value, yhi * SHARE, SHARE, 0)

    inputs_share, normed_one, inv_one = (share_of(v) for v in (inputs_half, normed_half, inv_half))
    cot_share = share_of(cot_half).astype(f32)

    halves = jnp.stack([attn_half, cot_half]).reshape(2, 2, SHARE, WIDTH)
    rows, attn_full = fused([row_exchange(halves), weight_gather(own_attn)], "0111101111", 2)
    attn_full = attn_full.reshape(WIDTH, PART)
    qkv_full, out_full = attn_full[:, :768], attn_full[:, 768:]
    attn_in, cot = rows[0].reshape(1024, WIDTH), rows[1].reshape(1024, WIDTH)

    projected = jnp.dot(attn_in, qkv_full, preferred_element_type=f32).astype(bf16)
    query_heads, key_heads, value_heads = (
        projected[:, 256 * t : 256 * t + 256].reshape(2, 512, 2, HEAD) for t in range(3)
    )
    scores = score_block(query_heads, key_heads, allowed)
    row_max = jnp.max(scores, axis=-1, keepdims=True)
    expd = jnp.exp(scores - row_max)
    row_sum = jnp.sum(expd, axis=-1, keepdims=True)
    log_total = row_max + jnp.log(row_sum)
    prob_low = (expd / row_sum).astype(bf16)
    attended = jnp.einsum("rhqk,rkhe->rqhe", prob_low, value_heads, preferred_element_type=f32)
    attended = attended.reshape(1024, 256).astype(bf16)
    partial_branch = jnp.einsum("sf,df->sd", attended, out_full, preferred_element_type=f32)
    branch, up_full = fused(
        [share_sum(partial_branch.astype(bf16)), weight_gather(own_up)], "0101111111", 3
    )
    up_full = up_full.reshape(WIDTH, PART)
    middle = inputs_share + branch
    normed_two, inv_two = standardize(middle)
    ffn_share = (normed_two * gain_two + shift_two).astype(bf16)
    ffn_in, down_full = fused([share_gather(ffn_share), weight_gather(own_down)], "0111101111", 4)
    ffn_in = ffn_in.reshape(1024, WIDTH)
    down_full = down_full.reshape(WIDTH, PART)
    up_proj = jnp.dot(ffn_in, up_full, preferred_element_type=f32)
    hidden = jax.nn.gelu(up_proj, approximate=True).astype(bf16)
    partial_ffn = jnp.einsum("sf,df->sd", hidden, down_full, preferred_element_type=f32)
    grad_w_down = jnp.einsum("sd,sf->df", cot, hidden, preferred_element_type=f32).astype(bf16)
    grad_hidden = jnp.dot(cot, down_full, preferred_element_type=f32)
    _, gelu_pull = jax.vjp(lambda value: jax.nn.gelu(value, approximate=True), up_proj)
    grad_up = gelu_pull(grad_hidden)[0].astype(bf16)
    grad_w_up = jnp.einsum("sd,sf->df", ffn_in, grad_up, preferred_element_type=f32).astype(bf16)
    partial_ffn_in = jnp.einsum("sf,df->sd", grad_up, up_full, preferred_element_type=f32)
    grad_ffn_in, ffn_out, sum_down = fused(
        [
            share_sum(partial_ffn_in.astype(bf16)),
            share_sum(partial_ffn.astype(bf16)),
            weight_sum(grad_w_down),
        ],
        "0201222011222",
        5,
        56,
    )
    layer_out = middle + ffn_out
    grad_norm_mid, grad_gain_two, grad_shift_two = norm_back(
        grad_ffn_in, normed_two, inv_two, gain_two
    )
    grad_middle = cot_share + grad_norm_mid
    grad_branch, sum_up = fused(
        [share_gather(grad_middle.astype(bf16)), weight_sum(grad_w_up)], "01111011", 6
    )
    grad_branch = grad_branch.reshape(1024, WIDTH)
    grad_w_out = jnp.einsum("sd,sf->df", grad_branch, attended, preferred_element_type=f32)
    grad_attended = jnp.dot(grad_branch, out_full, preferred_element_type=f32).astype(bf16)
    grad_att_heads = grad_attended.reshape(2, 512, 2, HEAD)
    again_scores = score_block(query_heads, key_heads, allowed)
    probs = jnp.exp(again_scores - log_total)
    probs_low = probs.astype(bf16)
    grad_probs = jnp.einsum(
        "rqhe,rkhe->rhqk", grad_att_heads, value_heads, preferred_element_type=f32
    )
    inner = jnp.sum(grad_probs * probs, axis=-1, keepdims=True)
    grad_scores = (probs * (grad_probs - inner)).astype(bf16)
    grad_query = jnp.einsum(
        "rhqk,rkhe->rqhe", grad_scores, key_heads, preferred_element_type=f32
    ) * HEAD ** (-0.5)
    grad_key = jnp.einsum(
        "rhqk,rqhe->rkhe", grad_scores, query_heads, preferred_element_type=f32
    ) * HEAD ** (-0.5)
    grad_value = jnp.einsum(
        "rhqk,rqhe->rkhe", probs_low, grad_att_heads, preferred_element_type=f32
    )
    grad_projected = jnp.concatenate(
        [g.reshape(1024, 256) for g in (grad_query, grad_key, grad_value)], axis=1
    ).astype(bf16)
    grad_w_qkv = jnp.einsum("sd,sf->df", attn_in, grad_projected, preferred_element_type=f32)
    partial_attn_in = jnp.einsum("sf,df->sd", grad_projected, qkv_full, preferred_element_type=f32)
    grad_w_attn = jnp.concatenate([grad_w_qkv.astype(bf16), grad_w_out.astype(bf16)], axis=1)
    grad_attn_in, sum_attn = fused(
        [share_sum(partial_attn_in.astype(bf16)), weight_sum(grad_w_attn)], "01011011", 7
    )
    grad_norm_in, grad_gain_one, grad_shift_one = norm_back(
        grad_attn_in, normed_one, inv_one, gain_one
    )
    input_grad = grad_middle + grad_norm_in

    sum_attn, sum_up, sum_down = (g.astype(f32) for g in (sum_attn, sum_up, sum_down))
    out_qkv = sum_attn[:, :, :768].reshape(2, 64, 3, 256).transpose(1, 2, 0, 3).reshape(64, 3, 512)
    out_out = sum_attn[:, :, 768:].transpose(1, 0, 2).reshape(64, 512)
    out_up = sum_up.transpose(1, 0, 2).reshape(64, WIDTH)
    out_down = sum_down.transpose(1, 0, 2).reshape(64, WIDTH)

    small = jnp.stack([grad_gain_one, grad_shift_one, grad_gain_two, grad_shift_two])
    small = jnp.pad(small.reshape(4, 32, 64).transpose(1, 0, 2), ((0, 0), (0, 4), (0, 64)))
    small = small_reduce(small, 10)[:4, :64]

    ends = jnp.stack([layer_out.astype(bf16), input_grad.astype(bf16)])
    (tokens,) = fused([row_gather(ends)], "000", 8)
    tokens = tokens.reshape(2, 1, 512, WIDTH).astype(f32)
    return (
        tokens[0],
        tokens[1],
        small[0],
        small[1],
        out_qkv,
        out_out,
        small[2],
        small[3],
        out_up,
        out_down,
    )


def solution(mesh):
    in_specs = (
        P("dp", None, None),
        P("dp", None),
        P("dp", None),
        P("dp", None),
        P(),
        P("dp"),
        P("dp"),
        P("dp", None, "mp"),
        P("dp", "mp"),
        P("dp"),
        P("dp"),
        P("dp", "mp"),
        P("dp", "mp"),
        P("dp", None, None),
    )
    out_specs = (
        P("dp", None, None),
        P("dp", None, None),
        P("dp"),
        P("dp"),
        P("dp", None, "mp"),
        P("dp", "mp"),
        P("dp"),
        P("dp"),
        P("dp", "mp"),
        P("dp", "mp"),
    )
    return jax.shard_map(
        on_device, mesh=mesh, in_specs=in_specs, out_specs=out_specs, check_vma=False
    )
```

```python
import functools

import jax
import jax.numpy as jnp
from jax import lax
from jax.experimental import pallas as pl
from jax.experimental.pallas import tpu as pltpu
from jax.sharding import PartitionSpec as P

HEAD = 128
WIDTH = 2048
SHARE = 128
PART = 1024
MESH = pl.DeviceIdType.MESH
ANY = pl.BlockSpec(memory_space=pl.ANY)
VMEM = pl.BlockSpec(memory_space=pltpu.VMEM)
masked_score = -1000000000.0
epsilon = 1e-05
f32 = jnp.float32
bf16 = jnp.bfloat16


def place():
    dp, mp = lax.axis_index("dp"), lax.axis_index("mp")
    return lax.div(dp, 16), lax.rem(lax.div(dp, 4), 4), lax.rem(dp, 4), lax.div(mp, 2), lax.rem(mp, 2)


def ring(position, step):
    return lax.rem(position + step + 4, 4)


def xz_neighbour(axis, step):
    ylo, x, z, yhi, core = place()
    if axis == 0:
        x = ring(x, step)
    else:
        z = ring(z, step)
    return (ylo * 16 + x * 4 + z, yhi * 2 + core)


def y_peer(step):
    ylo, x, z, yhi, core = place()
    y = ring(yhi * 2 + ylo, step)
    return (lax.rem(y, 2) * 16 + x * 4 + z, lax.div(y, 2) * 2 + core)


def lo_partner():
    ylo, x, z, yhi, core = place()
    return ((1 - ylo) * 16 + x * 4 + z, yhi * 2 + core)


def core_partner():
    ylo, x, z, yhi, core = place()
    return (ylo * 16 + x * 4 + z, yhi * 2 + 1 - core)


def greet(peers):
    barrier = pltpu.get_barrier_semaphore()
    for peer in peers:
        pl.semaphore_signal(barrier, inc=1, device_id=peer, device_id_type=MESH)
    pl.semaphore_wait(barrier, len(peers))


def remote(src, dst, send_sem, recv_sem, peer):
    return pltpu.make_async_remote_copy(
        src_ref=src,
        dst_ref=dst,
        send_sem=send_sem,
        recv_sem=recv_sem,
        device_id=peer,
        device_id_type=MESH,
    )


def sems(*shape):
    return pltpu.SemaphoreType.DMA(shape)


def params(collective_id, mib=48):
    return pltpu.CompilerParams(
        collective_id=collective_id, has_side_effects=True, vmem_limit_bytes=mib << 20
    )


PEERS = {
    "core": core_partner,
    "x+": lambda: xz_neighbour(0, 1),
    "x-": lambda: xz_neighbour(0, -1),
    "z+": lambda: xz_neighbour(1, 1),
    "z-": lambda: xz_neighbour(1, -1),
    "y1": lambda: y_peer(1),
    "y2": lambda: y_peer(2),
    "y3": lambda: y_peer(3),
}


def dp_peer(step):
    return (lax.rem(lax.axis_index("dp") + step, 32), lax.axis_index("mp"))


def mp_peer(step):
    return (lax.axis_index("dp"), lax.rem(lax.axis_index("mp") + step, 4))


PEERS.update({f"dp{k}": functools.partial(dp_peer, k) for k in range(1, 32)})
PEERS.update({f"mp{k}": functools.partial(mp_peer, k) for k in range(1, 4)})
DP = [f"dp{k}" for k in range(1, 32)]
MP = ["mp1", "mp2", "mp3"]


def kernel_call(body, jobs, peers, ins, outs, scratch, collective_id, mib=56):
    def kernel(*refs):
        taken = 0

        def take(count):
            nonlocal taken
            taken += count
            return refs[taken - count : taken]

        groups = [take(len(ins)), take(len(outs)), take(len(scratch))]
        makers = []
        for job in jobs:
            own = take(len(job["scratch"]))
            makers.append(lambda *given, job=job, own=own: job["steps"](*given, *own))
        greet([PEERS[name]() for name in peers])
        body(*groups, makers)

    return pl.pallas_call(
        kernel,
        out_shape=[shape for shape, _ in outs],
        in_specs=[spec for _, spec in ins],
        out_specs=[spec for _, spec in outs],
        scratch_shapes=scratch + [one for job in jobs for one in job["scratch"]],
        compiler_params=params(collective_id, mib),
    )(*[array for array, _ in ins])


def finish(*runs):
    for run in runs:
        for _ in run:
            pass


def step(*runs):
    for run in runs:
        next(run, None)


def fused_kernel(jobs, schedule, *refs):
    taken = 0

    def take(count):
        nonlocal taken
        taken += count
        return refs[taken - count : taken]

    ins = [take(len(job["ins"])) for job in jobs]
    outs = [take(len(job["outs"])) for job in jobs]
    scratch = [take(len(job["scratch"])) for job in jobs]
    greet([PEERS[name]() for name in sorted({name for job in jobs for name in job["peers"]})])
    runs = [job["steps"](*i, *o, *s) for job, i, o, s in zip(jobs, ins, outs, scratch)]
    for which in schedule:
        next(runs[int(which)], None)
    for run in runs:
        for _ in run:
            pass


def fused(jobs, schedule, collective_id, mib=48):
    results = pl.pallas_call(
        functools.partial(fused_kernel, jobs, schedule),
        out_shape=[shape for job in jobs for shape, _ in job["outs"]],
        in_specs=[spec for job in jobs for _, spec in job["ins"]],
        out_specs=[spec for job in jobs for _, spec in job["outs"]],
        scratch_shapes=[one for job in jobs for one in job["scratch"]],
        compiler_params=params(collective_id, mib),
    )(*[array for job in jobs for array, _ in job["ins"]])
    return results


def shaped(dtype, *shape):
    return jax.ShapeDtypeStruct(shape, dtype)


def small_gather():
    def steps(own, mask, everyone, mask_out, mask_send, mask_recv, send, recv):
        dp, mp = lax.axis_index("dp"), lax.axis_index("mp")

        def move(k):
            return remote(own, everyone.at[dp], send.at[k], recv.at[dp], dp_peer(k))

        def start(k, carry):
            move(k).start()
            return carry

        swap = remote(mask, mask_out, mask_send, mask_recv, lo_partner())
        swap.start()
        lax.fori_loop(1, 32, start, 0)
        everyone[dp] = own[...]
        yield

        def end(k, carry):
            source = lax.rem(dp + k, 32)
            move(k).wait_send()
            remote(own, everyone.at[source], send.at[k], recv.at[source], dp_peer(k)).wait_recv()
            return carry

        lax.fori_loop(1, 32, end, 0)
        swap.wait()

    return {
        "scratch": [pltpu.SemaphoreType.DMA] * 2 + [sems(32), sems(32)],
        "peers": DP,
        "steps": steps,
    }


def small_reduce(rows):
    def steps(rows, out, arrived, summed, more, send, recv, send_two, recv_two):
        dp = lax.axis_index("dp")

        def move(k):
            tile = lax.div(lax.rem(dp + k, 32), 2)
            src = rows.at[:, pl.ds(pl.multiple_of(tile * 128, 128), 128)]
            return remote(src, arrived.at[k], send.at[k], recv.at[k], dp_peer(k))

        def start(k, carry):
            move(k).start()
            return carry

        def add(k, total):
            move(k).wait()
            return total + arrived[k]

        lax.fori_loop(1, 32, start, 0)
        yield
        mine = rows[:, pl.ds(pl.multiple_of(lax.div(dp, 2) * 128, 128), 128)]
        summed[...] = lax.fori_loop(1, 32, add, mine)
        copies = [
            remote(summed, more.at[k - 1], send_two.at[k], recv_two.at[k], mp_peer(k))
            for k in (1, 2, 3)
        ]
        for copy in copies:
            copy.start()
        yield
        for copy in copies:
            copy.wait()
        out[...] = summed[...] + more[0] + more[1] + more[2]

    return {
        "ins": [(rows, VMEM)],
        "outs": [(shaped(f32, 8, 128), VMEM)],
        "scratch": [
            pltpu.VMEM((32, 8, 128), f32),
            pltpu.VMEM((8, 128), f32),
            pltpu.VMEM((3, 8, 128), f32),
            sems(32),
            sems(32),
            sems(4),
            sems(4),
        ],
        "peers": DP + MP,
        "steps": steps,
    }


def row_exchange(halves=None, count=1):
    if halves is not None:
        count = halves.shape[0]

    def steps(halves, full, local_sem, send, recv):
        ylo, x, z, yhi, core = place()
        up, down, other = y_peer(1), y_peer(3), core_partner()
        first = []
        for n in range(count):
            for u, peer in ((0, up), (1, down)):
                here = full.at[n, ylo, core, u]
                first.append(remote(halves.at[n, u], here, send.at[n, u], recv.at[n, u], peer))
        for n in range(count):
            here = full.at[n, ylo, core]
            first.append(remote(halves.at[n], here, send.at[n, 2], recv.at[n, 2], other))
        for copy in first:
            copy.start()
        local = [
            pltpu.make_async_copy(halves.at[n], full.at[n, ylo, core], local_sem.at[n])
            for n in range(count)
        ]
        for copy in local:
            copy.start()
        yield
        second = []
        for n in range(count):
            for u in range(2):
                here = full.at[n, 1 - ylo, core, u]
                remote(halves.at[n, u], here, send.at[n, u], recv.at[n, u], up).wait_recv()
                copy = remote(here, here, send.at[n, 3 + u], recv.at[n, 3 + u], other)
                copy.start()
                second.append(copy)
        yield
        for n in range(count):
            here = full.at[n, ylo, 1 - core]
            remote(halves.at[n], here, send.at[n, 2], recv.at[n, 2], other).wait_recv()
            for u in range(2):
                here = full.at[n, 1 - ylo, 1 - core, u]
                remote(here, here, send.at[n, 3 + u], recv.at[n, 3 + u], other).wait_recv()
        for copy in first + second:
            copy.wait_send()
        for copy in local:
            copy.wait()

    return {
        "ins": [(halves, VMEM)],
        "outs": [(shaped(bf16, count, 2, 2, 2, SHARE, WIDTH), ANY)],
        "scratch": [sems(count), sems(count, 5), sems(count, 5)],
        "peers": ["y1", "y3", "core"],
        "steps": steps,
    }


def share_gather(share=None):
    def steps(share, full, local_sem, send, recv):
        ylo, x, z, yhi, core = place()
        y = yhi * 2 + ylo
        other = core_partner()
        mine = full.at[ylo, core, yhi]
        local = pltpu.make_async_copy(share, mine, local_sem)
        first = [
            remote(share, mine, send.at[k], recv.at[k], y_peer(k) if k else other)
            for k in (2, 1, 3, 0)
        ]
        for copy in first:
            copy.start()
        local.start()
        yield
        second = []
        for k in (1, 3, 2):
            source = ring(y, -k)
            here = full.at[lax.rem(source, 2), core, lax.div(source, 2)]
            remote(share, here, send.at[k], recv.at[k], y_peer(4 - k)).wait_recv()
            copy = remote(here, here, send.at[3 + k], recv.at[3 + k], other)
            copy.start()
            second.append(copy)
        yield
        remote(share, full.at[ylo, 1 - core, yhi], send.at[0], recv.at[0], other).wait_recv()
        for k in (1, 3, 2):
            source = ring(y, -k)
            here = full.at[lax.rem(source, 2), 1 - core, lax.div(source, 2)]
            remote(here, here, send.at[3 + k], recv.at[3 + k], other).wait_recv()
        for copy in first + second:
            copy.wait_send()
        local.wait()

    return {
        "ins": [(share, VMEM)],
        "outs": [(shaped(bf16, 2, 2, 2, SHARE, WIDTH), ANY)],
        "scratch": [pltpu.SemaphoreType.DMA, sems(7), sems(7)],
        "peers": ["y1", "y2", "y3", "core"],
        "steps": steps,
    }


def add_rows(count, one):
    def body(i, carry):
        one(pl.ds(pl.multiple_of(i * 16, 16), 16))
        return carry

    lax.fori_loop(0, count // 16, body, 0)


def share_sum(partial=None, split=False):
    def steps(partial, out, from_core, turned, arrived, send, recv, send_two, recv_two):
        ylo, x, z, yhi, core = place()
        y = yhi * 2 + ylo
        other = core_partner()

        def block(k, half):
            target = ring(y, k)
            return partial.at[lax.rem(target, 2), half, lax.div(target, 2)]

        first, second = {}, {}

        def to_core(order):
            for k in order:
                first[k] = remote(block(k, 1 - core), from_core.at[k], send.at[k], recv.at[k], other)
                first[k].start()

        def to_owner(order):
            for k in order:
                first[k].wait_recv()
                mine = block(k, core)

                def add(rows):
                    value = mine[rows].astype(f32) + from_core[k, rows].astype(f32)
                    turned[k, rows] = value.astype(bf16)

                add_rows(SHARE, add)
                second[k] = remote(
                    turned.at[k], arrived.at[k], send_two.at[k], recv_two.at[k], y_peer(k)
                )
                second[k].start()

        to_core((1, 3))
        if not split:
            to_core((2, 0))
        yield
        to_owner((1, 3))
        yield
        if split:
            to_core((2, 0))
            yield
        to_owner((2,))
        yield
        first[0].wait_recv()
        for k in (1, 3, 2):
            second[k].wait_recv()
        mine_own = block(0, core)

        def total(rows):
            value = mine_own[rows].astype(f32) + from_core[0, rows].astype(f32)
            for k in (1, 2, 3):
                value += arrived[k, rows].astype(f32)
            out[rows] = value

        add_rows(SHARE, total)
        for k in range(4):
            first[k].wait_send()
        for k in (1, 2, 3):
            second[k].wait_send()

    return {
        "ins": [(None if partial is None else partial.reshape(2, 2, 2, SHARE, WIDTH), VMEM)],
        "outs": [(shaped(f32, SHARE, WIDTH), VMEM)],
        "scratch": [pltpu.VMEM((4, SHARE, WIDTH), bf16)] * 3 + [sems(4)] * 4,
        "peers": ["y1", "y2", "y3", "core"],
        "steps": steps,
    }


def row_gather(share):
    count = share.shape[0]

    def steps(share, full, local_sem, send, recv):
        ylo, x, z, yhi, core = place()
        across, other = y_peer(2), core_partner()
        mine = full.at[:, core, yhi]
        far = full.at[:, core, 1 - yhi]
        local = pltpu.make_async_copy(share, mine, local_sem)
        one = remote(share, mine, send.at[0], recv.at[0], across)
        two = remote(share, mine, send.at[1], recv.at[1], other)
        one.start()
        two.start()
        local.start()
        yield
        remote(share, far, send.at[0], recv.at[0], across).wait_recv()
        three = remote(far, far, send.at[2], recv.at[2], other)
        three.start()
        yield
        remote(share, full.at[:, 1 - core, yhi], send.at[1], recv.at[1], other).wait_recv()
        last = full.at[:, 1 - core, 1 - yhi]
        remote(last, last, send.at[2], recv.at[2], other).wait_recv()
        for copy in (one, two, three):
            copy.wait_send()
        local.wait()

    return {
        "ins": [(share, VMEM)],
        "outs": [(shaped(bf16, count, 2, 2, SHARE, WIDTH), ANY)],
        "scratch": [pltpu.SemaphoreType.DMA, sems(3), sems(3)],
        "peers": ["y2", "core"],
        "steps": steps,
    }


SIGNS = (1, -1)
XZ = ["x+", "x-", "z+", "z-"]


def xz_near():
    return [[xz_neighbour(axis, d) for d in SIGNS] for axis in (0, 1)]


def weight_gather(own=None):
    def steps(own, full, local_sem, swap_send, swap_recv, send, recv):
        ylo, x, z, yhi, core = place()
        near = xz_near()
        partner = lo_partner()
        offsets = (0, -1, 1, 2)

        def move(src, dst, s, r, stage, d, axis):
            n = ((s * 2 + r) * 8 + stage) * 2 + d
            return remote(src, dst, send.at[n], recv.at[n], near[axis][d])

        def block(s, r, one, two, rows):
            yl = ylo if s == 0 else 1 - ylo
            if r == 0:
                return full.at[yl, ring(x, one), ring(z, two), rows]
            return full.at[yl, ring(x, two), ring(z, one), rows]

        def rows_of(r, d=None):
            return pl.ds(32 * r, 32) if d is None else pl.ds(32 * r + 16 * d, 16)

        local = pltpu.make_async_copy(own.at[ylo], full.at[ylo, x, z], local_sem)
        swap = remote(own.at[1 - ylo], full.at[ylo, x, z], swap_send, swap_recv, partner)
        swap.start()
        sent = []

        def go(*args):
            copy = move(*args)
            copy.start()
            sent.append(copy)

        def begin(s, source):
            for r in range(2):
                for d in range(2):
                    src = source.at[rows_of(r)]
                    go(src, block(s, r, 0, 0, rows_of(r)), s, r, 0, d, r)
            for r in range(2):
                for d in range(2):
                    src = source.at[rows_of(r)]
                    go(src, block(s, r, 0, 0, rows_of(r)), s, r, 2, d, 1 - r)

        begin(0, own.at[ylo])
        local.start()
        yield
        remote(own.at[1 - ylo], full.at[1 - ylo, x, z], swap_send, swap_recv, partner).wait_recv()
        begin(1, full.at[1 - ylo, x, z])
        yield
        for s in range(2):
            for r in range(2):
                for d in range(2):
                    came = block(s, r, -SIGNS[d], 0, rows_of(r))
                    move(came, came, s, r, 0, d, r).wait_recv()
                    piece = block(s, r, -SIGNS[d], 0, rows_of(r, d))
                    go(piece, piece, s, r, 1, d, r)
                for part in (1, 2):
                    for d in range(2):
                        mine = block(s, r, offsets[part], 0, rows_of(r))
                        go(mine, mine, s, r, 2 + part, d, 1 - r)
            yield
        for s in range(2):
            for r in range(2):
                for d in range(2):
                    piece = block(s, r, 2, 0, rows_of(r, d))
                    move(piece, piece, s, r, 1, d, r).wait_recv()
                for d in range(2):
                    mine = block(s, r, 2, 0, rows_of(r))
                    go(mine, mine, s, r, 5, d, 1 - r)
            yield
        for part in (0, 2, 1, 3):
            d = part // 2
            for s in range(2):
                for r in range(2):
                    came = block(s, r, offsets[part], -SIGNS[d], rows_of(r))
                    move(came, came, s, r, 2 + part, d, 1 - r).wait_recv()
                    go(came, came, s, r, 6 + part % 2, d, 1 - r)
            yield
        for s in range(2):
            for r in range(2):
                for part in range(4):
                    d = 1 - part // 2
                    came = block(s, r, offsets[part], -SIGNS[d], rows_of(r))
                    move(came, came, s, r, 2 + part, d, 1 - r).wait_recv()
                for part in range(4):
                    d = part // 2
                    came = block(s, r, offsets[part], 2, rows_of(r))
                    move(came, came, s, r, 6 + part % 2, d, 1 - r).wait_recv()
        for copy in sent:
            copy.wait_send()
        swap.wait_send()
        local.wait()

    return {
        "ins": [(own, VMEM)],
        "outs": [(shaped(bf16, 2, 4, 4, 64, PART), ANY)],
        "scratch": [pltpu.SemaphoreType.DMA] * 3 + [sems(64), sems(64)],
        "peers": XZ + ["y1", "y3"],
        "steps": steps,
    }


def weight_sum(grads):
    def steps(grads, out, wide, wide_out, middle, thin, thin_out, total, swap_send, swap_recv, send, recv):
        ylo, x, z, yhi, core = place()
        near = xz_near()
        partner = lo_partner()

        def move(src, dst, s, r, stage, d, axis):
            n = ((s * 2 + r) * 6 + stage) * 2 + d
            return remote(src, dst, send.at[n], recv.at[n], near[axis][d])

        def line(s, r, step, part):
            if r == 0:
                return grads.at[s, part, ring(z, step), pl.ds(0, 32)]
            return grads.at[s, ring(x, step), part, pl.ds(32, 32)]

        def at(r):
            return x if r == 0 else z

        def wide_move(s, r, d, kind):
            if kind == 0:
                src = line(s, r, 2, pl.ds(2 * d, 2))
            elif kind == 1:
                src = line(s, r, SIGNS[d], pl.ds(2 - 2 * d, 2))
            else:
                src = wide_out.at[s, r, d]
            return move(src, wide.at[s, r, kind, d], s, r, kind, d, 1 - r)

        def thin_move(s, r, d, kind):
            if kind == 0:
                src = middle.at[s, r, ring(at(r), 2), pl.ds(16 * d, 16)]
            elif kind == 1:
                src = middle.at[s, r, ring(at(r), SIGNS[d]), pl.ds(16 - 16 * d, 16)]
            else:
                src = thin_out.at[s, r, d]
            return move(src, thin.at[s, r, kind, d], s, r, 3 + kind, d, r)

        for s in range(2):
            for kind in range(2):
                for r in range(2):
                    for d in range(2):
                        wide_move(s, r, d, kind).start()
        yield

        def step_two(s, carry):
            for r in range(2):
                for d in range(2):
                    wide_move(s, r, d, 0).wait_recv()
                    for p in range(2):
                        mine = line(s, r, SIGNS[d], 2 * d + p)

                        def one(rows):
                            value = mine[rows].astype(f32) + wide[s, r, 0, d, p, rows].astype(f32)
                            wide_out[s, r, d, p, rows] = value.astype(bf16)

                        add_rows(32, one)
                    wide_move(s, r, d, 2).start()
            return carry

        lax.fori_loop(0, 2, step_two, 0)
        yield

        def step_three(s, carry):
            for r in range(2):
                for d in range(2):
                    wide_move(s, r, d, 1).wait_recv()
                    wide_move(s, r, d, 2).wait_recv()
                for p in range(4):
                    mine = line(s, r, 0, p)
                    d = p // 2

                    def one(rows):
                        value = mine[rows].astype(f32) + wide[s, r, 2, d, p % 2, rows].astype(f32)
                        value += wide[s, r, 1, 1 - d, p % 2, rows].astype(f32)
                        middle[s, r, p, rows] = value.astype(bf16)

                    add_rows(32, one)
                for kind in range(2):
                    for d in range(2):
                        thin_move(s, r, d, kind).start()
            return carry

        lax.fori_loop(0, 2, step_three, 0)
        yield

        def step_four(s, carry):
            for r in range(2):
                for d in range(2):
                    thin_move(s, r, d, 0).wait_recv()
                    mine = middle[s, r, ring(at(r), SIGNS[d]), pl.ds(16 * d, 16)]
                    value = mine.astype(f32) + thin[s, r, 0, d].astype(f32)
                    thin_out[s, r, d] = value.astype(bf16)
                    thin_move(s, r, d, 2).start()
            return carry

        lax.fori_loop(0, 2, step_four, 0)
        yield

        def step_five(s, carry):
            for r in range(2):
                for d in range(2):
                    thin_move(s, r, d, 1).wait_recv()
                    thin_move(s, r, d, 2).wait_recv()
                for d in range(2):
                    rows = pl.ds(16 * d, 16)
                    value = middle[s, r, at(r), rows].astype(f32) + thin[s, r, 2, d].astype(f32)
                    value += thin[s, r, 1, 1 - d].astype(f32)
                    total[s, pl.ds(32 * r + 16 * d, 16)] = value.astype(bf16)
            return carry

        lax.fori_loop(0, 2, step_five, 0)
        swap = remote(total.at[1 - ylo], out.at[ylo], swap_send, swap_recv, partner)
        swap.start()
        out[ylo] = total[ylo]
        yield
        for s in range(2):
            for r in range(2):
                for d in range(2):
                    for kind in range(3):
                        wide_move(s, r, d, kind).wait_send()
                        thin_move(s, r, d, kind).wait_send()
        remote(total.at[0], out.at[1 - ylo], swap_send, swap_recv, partner).wait_recv()
        swap.wait_send()

    return {
        "ins": [(grads.reshape(2, 4, 4, 64, PART), VMEM)],
        "outs": [(shaped(bf16, 2, 64, PART), VMEM)],
        "scratch": [
            pltpu.VMEM((2, 2, 3, 2, 2, 32, PART), bf16),
            pltpu.VMEM((2, 2, 2, 2, 32, PART), bf16),
            pltpu.VMEM((2, 2, 4, 32, PART), bf16),
            pltpu.VMEM((2, 2, 3, 2, 16, PART), bf16),
            pltpu.VMEM((2, 2, 2, 16, PART), bf16),
            pltpu.VMEM((2, 64, PART), bf16),
            pltpu.SemaphoreType.DMA,
            pltpu.SemaphoreType.DMA,
            sems(48),
            sems(48),
        ],
        "peers": XZ + ["y1", "y3"],
        "steps": steps,
    }


CODES = 4096
CODE_CHUNK = 512


def embed_body(ins, outs, scratch, makers):
    ids, stream, cot, codebook, own_attn, norms, masks = ins
    attn_full, cot_full, inputs_share, gains, masks_out, attn_weight = outs
    everyone, chunk, total, halves, chunk_sem = scratch
    make_small, make_gather, make_cot, make_attn = makers
    ylo, x, z, yhi, core = place()
    small = make_small(norms, masks, everyone, masks_out)
    gather = make_gather(own_attn, attn_weight)
    cot_move = make_cot(cot, cot_full)
    attn_move = make_attn(halves, attn_full)

    def fetch(j):
        rows = pl.ds(j * CODE_CHUNK, CODE_CHUNK)
        return pltpu.make_async_copy(codebook.at[rows], chunk.at[j % 2], chunk_sem.at[j % 2])

    step(small, gather)
    fetch(0).start()
    step(cot_move)
    total[...] = stream[...].astype(f32)
    count = CODES // CODE_CHUNK
    for j in range(count):
        if j + 1 < count:
            fetch(j + 1).start()
        fetch(j).wait()
        code = lax.broadcasted_iota(jnp.int32, (256, CODE_CHUNK), 1) + j * CODE_CHUNK
        pick = jnp.where(ids[...] == code, 1.0, 0.0).astype(bf16)
        for part in range(2):
            columns = pl.ds(part * 1024, 1024)
            total[:, columns] += jnp.dot(
                pick, chunk[j % 2, :, columns], preferred_element_type=f32
            )
        if j in (2, 4, 6):
            step(gather)
    step(small)
    for t in range(16):
        for k in range(4):
            pair = everyone[2 * t, pl.ds(k, 1)] + everyone[2 * t + 1, pl.ds(k, 1)]
            gains[pl.ds(k, 1), pl.ds(128 * t, 128)] = pair
    gain, shift = gains[pl.ds(0, 1)], gains[pl.ds(1, 1)]
    for u in range(2):

        def norm(i, carry):
            at = pl.multiple_of(i * 16, 16)
            value = total[pl.ds(u * SHARE + at, 16)]
            normed, _ = standardize(value)
            halves[0, u, pl.ds(at, 16)] = (normed * gain + shift).astype(bf16)
            return carry

        lax.fori_loop(0, SHARE // 16, norm, 0)
    step(attn_move, gather)

    def keep(i, carry):
        at = pl.multiple_of(i * 16, 16)
        inputs_share[pl.ds(at, 16)] = total[pl.ds(pl.multiple_of(yhi * SHARE + at, 16), 16)]
        return carry

    lax.fori_loop(0, SHARE // 16, keep, 0)
    step(gather, gather, cot_move, gather, gather, attn_move, gather)
    finish(attn_move, cot_move, gather)


def embed(ids, stream, cot, codebook, own_attn, norms, masks, collective_id):
    return kernel_call(
        embed_body,
        [small_gather(), weight_gather(), row_exchange(), row_exchange()],
        DP + ["y1", "y3", "core"],
        [
            (ids, VMEM),
            (stream, VMEM),
            (cot, VMEM),
            (codebook, ANY),
            (own_attn, VMEM),
            (norms, VMEM),
            (masks, VMEM),
        ],
        [
            (shaped(bf16, 1, 2, 2, 2, SHARE, WIDTH), ANY),
            (shaped(bf16, 1, 2, 2, 2, SHARE, WIDTH), ANY),
            (shaped(f32, SHARE, WIDTH), VMEM),
            (shaped(f32, 8, WIDTH), VMEM),
            (shaped(f32, 8, 128), VMEM),
            (shaped(bf16, 2, 4, 4, 64, PART), ANY),
        ],
        [
            pltpu.VMEM((32, 8, 128), f32),
            pltpu.VMEM((2, CODE_CHUNK, WIDTH), bf16),
            pltpu.VMEM((256, WIDTH), f32),
            pltpu.VMEM((1, 2, SHARE, WIDTH), bf16),
            sems(2),
        ],
        collective_id,
    )


TURNED = (((1,), (1,)), ((), ()))


def turned_dot(a, b):
    return lax.dot_general(a, b, TURNED, preferred_element_type=f32)


def attention_body(ins, outs, scratch, makers):
    attn_in, weight, mask, inputs_share, gains, own_up, own_down = ins
    projected, attended, middle, ffn_full, up_full, down_full = outs
    partial, branch, ffn_share = scratch
    make_up, make_down, make_sum, make_share = makers
    ylo, x, z, yhi, core = place()
    up, down = make_up(own_up, up_full), make_down(own_down, down_full)
    total = make_sum(partial, branch)
    spread = make_share(ffn_share, ffn_full)

    def project(r):
        def one(t, carry):
            columns = pl.ds(pl.multiple_of(t * 256, 256), 256)
            projected[pl.ds(r * 512, 512), columns] = jnp.dot(
                attn_in[pl.ds(r * 512, 512)], weight[:, columns], preferred_element_type=f32
            ).astype(bf16)
            return carry

        lax.fori_loop(0, 3, one, 0)

    def attend(r):
        for h in range(2):
            key = projected[pl.ds(r * 512, 512), pl.ds(256 + h * HEAD, HEAD)]
            value = projected[pl.ds(r * 512, 512), pl.ds(512 + h * HEAD, HEAD)]

            def one(q, carry):
                rows = pl.ds(pl.multiple_of(r * 512 + q * 128, 128), 128)
                query = projected[rows, pl.ds(h * HEAD, HEAD)]
                scores = turned_dot(query, key) * HEAD ** (-0.5)
                seen = mask[r, pl.ds(pl.multiple_of(q * 128, 128), 128)].astype(f32)
                scores = jnp.where(seen > 0.5, scores, masked_score)
                expd = jnp.exp(scores - jnp.max(scores, axis=-1, keepdims=True))
                probs = expd / jnp.sum(expd, axis=-1, keepdims=True)
                attended[rows, pl.ds(h * HEAD, HEAD)] = jnp.dot(
                    probs.astype(bf16), value, preferred_element_type=f32
                ).astype(bf16)
                return carry

            lax.fori_loop(0, 4, one, 0)

    def send_out(r):
        def one(n, carry):
            columns = pl.ds(pl.multiple_of(n * 512, 512), 512)
            out_weight = weight[columns, pl.ds(768, 256)]
            for q in range(4):
                rows = pl.ds(pl.multiple_of(r * 512 + q * 128, 128), 128)
                partial[r, q // 2, q % 2, :, columns] = turned_dot(
                    attended[rows], out_weight
                ).astype(bf16)
            return carry

        lax.fori_loop(0, 4, one, 0)

    step(up, down)
    project(1 - ylo)
    step(up, down)
    attend(1 - ylo)
    step(up, down)
    send_out(1 - ylo)
    step(total)
    step(up, down)
    project(ylo)
    step(total)
    step(up, down)
    attend(ylo)
    step(up, down)
    send_out(ylo)
    step(total)
    step(up, down)
    step(total)
    step(up, down)
    step(up, down)
    finish(total)
    gain, shift = gains[pl.ds(2, 1)], gains[pl.ds(3, 1)]

    def norm(i, carry):
        rows = pl.ds(pl.multiple_of(i * 16, 16), 16)
        value = inputs_share[rows] + branch[rows]
        middle[rows] = value
        normed, _ = standardize(value)
        ffn_share[rows] = (normed * gain + shift).astype(bf16)
        return carry

    lax.fori_loop(0, SHARE // 16, norm, 0)
    step(spread)
    step(up, down)
    step(spread)
    finish(spread, up, down)


def attention(attn_in, weight, mask, inputs_share, gains, own_up, own_down, collective_id):
    return kernel_call(
        attention_body,
        [weight_gather(), weight_gather(), share_sum(split=True), share_gather()],
        XZ + ["y1", "y2", "y3", "core"],
        [
            (attn_in, VMEM),
            (weight, VMEM),
            (mask, VMEM),
            (inputs_share, VMEM),
            (gains, VMEM),
            (own_up, VMEM),
            (own_down, VMEM),
        ],
        [
            (shaped(bf16, 1024, 768), VMEM),
            (shaped(bf16, 1024, 256), VMEM),
            (shaped(f32, SHARE, WIDTH), VMEM),
            (shaped(bf16, 2, 2, 2, SHARE, WIDTH), ANY),
            (shaped(bf16, 2, 4, 4, 64, PART), ANY),
            (shaped(bf16, 2, 4, 4, 64, PART), ANY),
        ],
        [
            pltpu.VMEM((2, 2, 2, SHARE, WIDTH), bf16),
            pltpu.VMEM((SHARE, WIDTH), f32),
            pltpu.VMEM((SHARE, WIDTH), bf16),
        ],
        collective_id,
    )


def standardize(value):
    mean = jnp.mean(value, axis=-1, keepdims=True)
    centered = value - mean
    scale_inv = lax.rsqrt(jnp.mean(centered * centered, axis=-1, keepdims=True) + epsilon)
    return (centered * scale_inv, scale_inv)


def norm_back(grad_normed_out, normed, scale_inv, gain):
    scaled = grad_normed_out * gain
    mean_one = jnp.mean(scaled, axis=-1, keepdims=True)
    mean_two = jnp.mean(scaled * normed, axis=-1, keepdims=True)
    grad_value = scale_inv * (scaled - mean_one - normed * mean_two)
    grad_gain = jnp.sum(grad_normed_out * normed, axis=0)
    grad_shift = jnp.sum(grad_normed_out, axis=0)
    return (grad_value, grad_gain, grad_shift)


def visible(segment_ids, padding):
    seq_len = segment_ids.shape[1]
    position = jnp.arange(seq_len)
    causal = position[None, :] <= position[:, None]
    itself = position[None, :] == position[:, None]
    same = segment_ids[:, :, None] == segment_ids[:, None, :]
    live = (padding[:, None, :] == 1) | itself[None]
    return same & causal[None] & live


def score_block(query_heads, key_heads, allowed):
    scores = jnp.einsum(
        "rqhe,rkhe->rhqk", query_heads, key_heads, preferred_element_type=f32
    ) * HEAD ** (-0.5)
    return jnp.where(allowed[:, None], scores, masked_score)


def on_device(
    stream,
    code_ids,
    segment_ids,
    padding,
    codebook,
    norm1_gain,
    norm1_shift,
    w_qkv,
    w_out,
    norm2_gain,
    norm2_shift,
    w_up,
    w_down,
    cotangent,
):
    ylo, x, z, yhi, core = place()

    own_attn = jnp.concatenate(
        [
            w_qkv.reshape(64, 3, 2, 256).transpose(2, 0, 1, 3).reshape(2, 64, 768),
            w_out.reshape(64, 2, 256).transpose(1, 0, 2),
        ],
        axis=2,
    )
    own_up = w_up.reshape(64, 2, PART).transpose(1, 0, 2)
    own_down = w_down.reshape(64, 2, PART).transpose(1, 0, 2)

    norms = jnp.stack([norm1_gain, norm1_shift, norm2_gain, norm2_shift]).astype(f32)
    none = jnp.zeros_like(norms)
    odd = lax.rem(z, 2) == 1
    norms = jnp.concatenate([jnp.where(odd, none, norms), jnp.where(odd, norms, none)], axis=1)
    masks = jnp.concatenate([segment_ids.reshape(4, 128), padding.reshape(4, 128)]).astype(f32)
    ids_half = lax.dynamic_slice_in_dim(code_ids[0], core * 256, 256, 0)
    stream_half = lax.dynamic_slice_in_dim(stream[0], core * 256, 256, 0)
    cot_half = lax.dynamic_slice_in_dim(cotangent[0], core * 256, 256, 0)
    attn_in, cot, inputs_share, gains, masks_other, attn_full = embed(
        ids_half[:, None],
        stream_half,
        cot_half.reshape(1, 2, SHARE, WIDTH),
        codebook,
        own_attn,
        jnp.pad(norms, ((0, 4), (0, 0))),
        masks,
        0,
    )
    gain_one, shift_one, gain_two, shift_two = (gains[k] for k in range(4))
    attn_in, cot = attn_in.reshape(1024, WIDTH), cot.reshape(1024, WIDTH)
    attn_full = attn_full.reshape(WIDTH, PART)
    qkv_full, out_full = attn_full[:, :768], attn_full[:, 768:]
    both = jnp.where(ylo == 0, jnp.stack([masks, masks_other]), jnp.stack([masks_other, masks]))
    allowed = visible(both[:, :4].reshape(2, 512), both[:, 4:].reshape(2, 512))
    cot_share = lax.dynamic_slice_in_dim(cot_half, yhi * SHARE, SHARE, 0).astype(f32)
    normed_one, inv_one = standardize(inputs_share)

    projected, attended, middle, ffn_in, up_full, down_full = attention(
        attn_in, attn_full, allowed.astype(bf16), inputs_share, gains, own_up, own_down, 1
    )
    query_heads, key_heads, value_heads = (
        projected[:, 256 * t : 256 * t + 256].reshape(2, 512, 2, HEAD) for t in range(3)
    )
    normed_two, inv_two = standardize(middle)
    ffn_in = ffn_in.reshape(1024, WIDTH)
    up_full, down_full = up_full.reshape(WIDTH, PART), down_full.reshape(WIDTH, PART)
    up_proj = jnp.dot(ffn_in, up_full, preferred_element_type=f32)
    hidden = jax.nn.gelu(up_proj, approximate=True).astype(bf16)
    partial_ffn = jnp.einsum("sf,df->sd", hidden, down_full, preferred_element_type=f32)
    grad_w_down = jnp.einsum("sd,sf->df", cot, hidden, preferred_element_type=f32).astype(bf16)
    grad_hidden = jnp.dot(cot, down_full, preferred_element_type=f32)
    _, gelu_pull = jax.vjp(lambda value: jax.nn.gelu(value, approximate=True), up_proj)
    grad_up = gelu_pull(grad_hidden)[0].astype(bf16)
    grad_w_up = jnp.einsum("sd,sf->df", ffn_in, grad_up, preferred_element_type=f32).astype(bf16)
    partial_ffn_in = jnp.einsum("sf,df->sd", grad_up, up_full, preferred_element_type=f32)
    grad_ffn_in, ffn_out, sum_down = fused(
        [
            share_sum(partial_ffn_in.astype(bf16)),
            share_sum(partial_ffn.astype(bf16)),
            weight_sum(grad_w_down),
        ],
        "200122222",
        5,
        56,
    )
    layer_out = middle + ffn_out
    grad_norm_mid, grad_gain_two, grad_shift_two = norm_back(
        grad_ffn_in, normed_two, inv_two, gain_two
    )
    grad_middle = cot_share + grad_norm_mid
    grad_branch, sum_up = fused(
        [share_gather(grad_middle.astype(bf16)), weight_sum(grad_w_up)], "10111111", 6
    )
    grad_branch = grad_branch.reshape(1024, WIDTH)
    grad_w_out = jnp.einsum("sd,sf->df", grad_branch, attended, preferred_element_type=f32)
    grad_attended = jnp.dot(grad_branch, out_full, preferred_element_type=f32).astype(bf16)
    grad_att_heads = grad_attended.reshape(2, 512, 2, HEAD)
    again_scores = score_block(query_heads, key_heads, allowed)
    probs = jax.nn.softmax(again_scores, axis=-1)
    probs_low = probs.astype(bf16)
    grad_probs = jnp.einsum(
        "rqhe,rkhe->rhqk", grad_att_heads, value_heads, preferred_element_type=f32
    )
    inner = jnp.sum(grad_probs * probs, axis=-1, keepdims=True)
    grad_scores = (probs * (grad_probs - inner)).astype(bf16)
    grad_query = jnp.einsum(
        "rhqk,rkhe->rqhe", grad_scores, key_heads, preferred_element_type=f32
    ) * HEAD ** (-0.5)
    grad_key = jnp.einsum(
        "rhqk,rqhe->rkhe", grad_scores, query_heads, preferred_element_type=f32
    ) * HEAD ** (-0.5)
    grad_value = jnp.einsum(
        "rhqk,rqhe->rkhe", probs_low, grad_att_heads, preferred_element_type=f32
    )
    grad_projected = jnp.concatenate(
        [g.reshape(1024, 256) for g in (grad_query, grad_key, grad_value)], axis=1
    ).astype(bf16)
    grad_w_qkv = jnp.einsum("sd,sf->df", attn_in, grad_projected, preferred_element_type=f32)
    partial_attn_in = jnp.einsum("sf,df->sd", grad_projected, qkv_full, preferred_element_type=f32)
    grad_w_attn = jnp.concatenate([grad_w_qkv.astype(bf16), grad_w_out.astype(bf16)], axis=1)
    grad_attn_in, sum_attn = fused(
        [share_sum(partial_attn_in.astype(bf16)), weight_sum(grad_w_attn)], "1001111111", 7
    )
    grad_norm_in, grad_gain_one, grad_shift_one = norm_back(
        grad_attn_in, normed_one, inv_one, gain_one
    )
    input_grad = grad_middle + grad_norm_in

    sum_attn, sum_up, sum_down = (g.astype(f32) for g in (sum_attn, sum_up, sum_down))
    out_qkv = sum_attn[:, :, :768].reshape(2, 64, 3, 256).transpose(1, 2, 0, 3).reshape(64, 3, 512)
    out_out = sum_attn[:, :, 768:].transpose(1, 0, 2).reshape(64, 512)
    out_up = sum_up.transpose(1, 0, 2).reshape(64, WIDTH)
    out_down = sum_down.transpose(1, 0, 2).reshape(64, WIDTH)

    small = jnp.stack([grad_gain_one, grad_shift_one, grad_gain_two, grad_shift_two])
    ends = jnp.stack([layer_out.astype(bf16), input_grad.astype(bf16)])
    tokens, small = fused(
        [row_gather(ends), small_reduce(jnp.pad(small, ((0, 4), (0, 0))))], "10101010", 8
    )
    small = jnp.where(odd, small[:4, 64:], small[:4, :64])
    tokens = tokens.reshape(2, 1, 512, WIDTH).astype(f32)
    return (
        tokens[0],
        tokens[1],
        small[0],
        small[1],
        out_qkv,
        out_out,
        small[2],
        small[3],
        out_up,
        out_down,
    )


def solution(mesh):
    in_specs = (
        P("dp", None, None),
        P("dp", None),
        P("dp", None),
        P("dp", None),
        P(),
        P("dp"),
        P("dp"),
        P("dp", None, "mp"),
        P("dp", "mp"),
        P("dp"),
        P("dp"),
        P("dp", "mp"),
        P("dp", "mp"),
        P("dp", None, None),
    )
    out_specs = (
        P("dp", None, None),
        P("dp", None, None),
        P("dp"),
        P("dp"),
        P("dp", None, "mp"),
        P("dp", "mp"),
        P("dp"),
        P("dp"),
        P("dp", "mp"),
        P("dp", "mp"),
    )
    return jax.shard_map(
        on_device, mesh=mesh, in_specs=in_specs, out_specs=out_specs, check_vma=False
    )
```

```python
import functools

import jax
import jax.numpy as jnp
from jax import lax
from jax.experimental import pallas as pl
from jax.experimental.pallas import tpu as pltpu
from jax.sharding import PartitionSpec as P

HEAD = 128
WIDTH = 2048
SHARE = 128
PART = 1024
MESH = pl.DeviceIdType.MESH
ANY = pl.BlockSpec(memory_space=pl.ANY)
VMEM = pl.BlockSpec(memory_space=pltpu.VMEM)
masked_score = -1000000000.0
epsilon = 1e-05
f32 = jnp.float32
bf16 = jnp.bfloat16


def place():
    dp, mp = lax.axis_index("dp"), lax.axis_index("mp")
    return lax.div(dp, 16), lax.rem(lax.div(dp, 4), 4), lax.rem(dp, 4), lax.div(mp, 2), lax.rem(mp, 2)


def ring(position, step):
    return lax.rem(position + step + 4, 4)


def xz_neighbour(axis, step):
    ylo, x, z, yhi, core = place()
    if axis == 0:
        x = ring(x, step)
    else:
        z = ring(z, step)
    return (ylo * 16 + x * 4 + z, yhi * 2 + core)


def y_peer(step):
    ylo, x, z, yhi, core = place()
    y = ring(yhi * 2 + ylo, step)
    return (lax.rem(y, 2) * 16 + x * 4 + z, lax.div(y, 2) * 2 + core)


def lo_partner():
    ylo, x, z, yhi, core = place()
    return ((1 - ylo) * 16 + x * 4 + z, yhi * 2 + core)


def core_partner():
    ylo, x, z, yhi, core = place()
    return (ylo * 16 + x * 4 + z, yhi * 2 + 1 - core)


def greet(peers):
    barrier = pltpu.get_barrier_semaphore()
    for peer in peers:
        pl.semaphore_signal(barrier, inc=1, device_id=peer, device_id_type=MESH)
    pl.semaphore_wait(barrier, len(peers))


def remote(src, dst, send_sem, recv_sem, peer):
    return pltpu.make_async_remote_copy(
        src_ref=src,
        dst_ref=dst,
        send_sem=send_sem,
        recv_sem=recv_sem,
        device_id=peer,
        device_id_type=MESH,
    )


def sems(*shape):
    return pltpu.SemaphoreType.DMA(shape)


def params(collective_id, mib=48):
    return pltpu.CompilerParams(
        collective_id=collective_id, has_side_effects=True, vmem_limit_bytes=mib << 20
    )


PEERS = {
    "core": core_partner,
    "x+": lambda: xz_neighbour(0, 1),
    "x-": lambda: xz_neighbour(0, -1),
    "z+": lambda: xz_neighbour(1, 1),
    "z-": lambda: xz_neighbour(1, -1),
    "y1": lambda: y_peer(1),
    "y2": lambda: y_peer(2),
    "y3": lambda: y_peer(3),
}


def dp_peer(step):
    return (lax.rem(lax.axis_index("dp") + step, 32), lax.axis_index("mp"))


def diagonal_peer(step):
    dp, mp = y_peer(step)
    return (dp, mp + 1 - 2 * lax.rem(mp, 2))


def mp_peer(step):
    return (lax.axis_index("dp"), lax.rem(lax.axis_index("mp") + step, 4))


PEERS.update({f"dp{k}": functools.partial(dp_peer, k) for k in range(1, 32)})
PEERS.update({f"mp{k}": functools.partial(mp_peer, k) for k in range(1, 4)})
PEERS.update({f"d{k}": functools.partial(diagonal_peer, k) for k in range(1, 4)})
GROUP = ["y1", "y2", "y3", "core", "d1", "d2", "d3"]
DP = [f"dp{k}" for k in range(1, 32)]
MP = ["mp1", "mp2", "mp3"]


def kernel_call(body, jobs, peers, ins, outs, scratch, collective_id, mib=56):
    def kernel(*refs):
        taken = 0

        def take(count):
            nonlocal taken
            taken += count
            return refs[taken - count : taken]

        groups = [take(len(ins)), take(len(outs)), take(len(scratch))]
        makers = []
        for job in jobs:
            own = take(len(job["scratch"]))
            makers.append(lambda *given, job=job, own=own: job["steps"](*given, *own))
        greet([PEERS[name]() for name in peers])
        body(*groups, makers)

    return pl.pallas_call(
        kernel,
        out_shape=[shape for shape, _ in outs],
        in_specs=[spec for _, spec in ins],
        out_specs=[spec for _, spec in outs],
        scratch_shapes=scratch + [one for job in jobs for one in job["scratch"]],
        compiler_params=params(collective_id, mib),
    )(*[array for array, _ in ins])


def finish(*runs):
    for run in runs:
        for _ in run:
            pass


def step(*runs):
    for run in runs:
        next(run, None)


def shaped(dtype, *shape):
    return jax.ShapeDtypeStruct(shape, dtype)


def small_gather():
    def steps(own, mask, everyone, mask_out, mask_send, mask_recv, send, recv):
        dp, mp = lax.axis_index("dp"), lax.axis_index("mp")

        def move(k):
            return remote(own, everyone.at[dp], send.at[k], recv.at[dp], dp_peer(k))

        def start(k, carry):
            move(k).start()
            return carry

        swap = remote(mask, mask_out, mask_send, mask_recv, lo_partner())
        swap.start()
        lax.fori_loop(1, 32, start, 0)
        everyone[dp] = own[...]
        yield

        def end(k, carry):
            source = lax.rem(dp + k, 32)
            move(k).wait_send()
            remote(own, everyone.at[source], send.at[k], recv.at[source], dp_peer(k)).wait_recv()
            return carry

        lax.fori_loop(1, 32, end, 0)
        swap.wait()

    return {
        "scratch": [pltpu.SemaphoreType.DMA] * 2 + [sems(32), sems(32)],
        "steps": steps,
    }


def small_reduce():
    def steps(rows, out, arrived, summed, more, send, recv, send_two, recv_two):
        dp = lax.axis_index("dp")

        def move(k):
            tile = lax.div(lax.rem(dp + k, 32), 2)
            src = rows.at[:, pl.ds(pl.multiple_of(tile * 128, 128), 128)]
            return remote(src, arrived.at[k], send.at[k], recv.at[k], dp_peer(k))

        def start(k, carry):
            move(k).start()
            return carry

        def add(k, total):
            move(k).wait()
            return total + arrived[k]

        lax.fori_loop(1, 32, start, 0)
        yield
        mine = rows[:, pl.ds(pl.multiple_of(lax.div(dp, 2) * 128, 128), 128)]
        summed[...] = lax.fori_loop(1, 32, add, mine)
        copies = [
            remote(summed, more.at[k - 1], send_two.at[k], recv_two.at[k], mp_peer(k))
            for k in (1, 2, 3)
        ]
        for copy in copies:
            copy.start()
        yield
        for copy in copies:
            copy.wait()
        out[...] = summed[...] + more[0] + more[1] + more[2]

    return {
        "scratch": [
            pltpu.VMEM((32, 8, 128), f32),
            pltpu.VMEM((8, 128), f32),
            pltpu.VMEM((3, 8, 128), f32),
            sems(32),
            sems(32),
            sems(4),
            sems(4),
        ],
        "steps": steps,
    }


def row_exchange(count=1):
    def steps(halves, full, local_sem, send, recv):
        ylo, x, z, yhi, core = place()
        up, down, other = y_peer(1), y_peer(3), core_partner()
        first = []
        for n in range(count):
            for u, peer in ((0, up), (1, down)):
                here = full.at[n, ylo, core, u]
                first.append(remote(halves.at[n, u], here, send.at[n, u], recv.at[n, u], peer))
        for n in range(count):
            here = full.at[n, ylo, core]
            first.append(remote(halves.at[n], here, send.at[n, 2], recv.at[n, 2], other))
        for copy in first:
            copy.start()
        local = [
            pltpu.make_async_copy(halves.at[n], full.at[n, ylo, core], local_sem.at[n])
            for n in range(count)
        ]
        for copy in local:
            copy.start()
        yield
        second = []
        for n in range(count):
            for u in range(2):
                here = full.at[n, 1 - ylo, core, u]
                remote(halves.at[n, u], here, send.at[n, u], recv.at[n, u], up).wait_recv()
                copy = remote(here, here, send.at[n, 3 + u], recv.at[n, 3 + u], other)
                copy.start()
                second.append(copy)
        yield
        for n in range(count):
            here = full.at[n, ylo, 1 - core]
            remote(halves.at[n], here, send.at[n, 2], recv.at[n, 2], other).wait_recv()
            for u in range(2):
                here = full.at[n, 1 - ylo, 1 - core, u]
                remote(here, here, send.at[n, 3 + u], recv.at[n, 3 + u], other).wait_recv()
        for copy in first + second:
            copy.wait_send()
        for copy in local:
            copy.wait()

    return {
        "scratch": [sems(count), sems(count, 5), sems(count, 5)],
        "steps": steps,
    }


def share_gather():
    def steps(share, full, local_sem, send, recv):
        ylo, x, z, yhi, core = place()
        y = yhi * 2 + ylo
        other = core_partner()
        mine = full.at[ylo, core, yhi]
        local = pltpu.make_async_copy(share, mine, local_sem)
        first = [
            remote(share, mine, send.at[k], recv.at[k], y_peer(k) if k else other)
            for k in (2, 1, 3, 0)
        ]
        for copy in first:
            copy.start()
        local.start()
        yield
        second = []
        for k in (1, 3, 2):
            source = ring(y, -k)
            here = full.at[lax.rem(source, 2), core, lax.div(source, 2)]
            remote(share, here, send.at[k], recv.at[k], y_peer(4 - k)).wait_recv()
            copy = remote(here, here, send.at[3 + k], recv.at[3 + k], other)
            copy.start()
            second.append(copy)
        yield
        remote(share, full.at[ylo, 1 - core, yhi], send.at[0], recv.at[0], other).wait_recv()
        for k in (1, 3, 2):
            source = ring(y, -k)
            here = full.at[lax.rem(source, 2), 1 - core, lax.div(source, 2)]
            remote(here, here, send.at[3 + k], recv.at[3 + k], other).wait_recv()
        for copy in first + second:
            copy.wait_send()
        local.wait()

    return {
        "scratch": [pltpu.SemaphoreType.DMA, sems(7), sems(7)],
        "steps": steps,
    }


def add_rows(count, one):
    def body(i, carry):
        one(pl.ds(pl.multiple_of(i * 16, 16), 16))
        return carry

    lax.fori_loop(0, count // 16, body, 0)


def share_sum():
    def steps(partial, out, from_core, arrived, send, recv, send_two, recv_two):
        ylo, x, z, yhi, core = place()
        y = yhi * 2 + ylo
        other = core_partner()

        def block(k, half):
            target = ring(y, k)
            return partial.at[lax.rem(target, 2), half, lax.div(target, 2)]

        first, second = {}, {}

        def to_core(order):
            for k in order:
                first[k] = remote(block(k, 1 - core), from_core.at[k], send.at[k], recv.at[k], other)
                first[k].start()

        def to_owner(order):
            for k in order:
                first[k].wait_recv()
                mine = block(k, core)

                def add(rows):
                    value = mine[rows].astype(f32) + from_core[k, rows].astype(f32)
                    mine[rows] = value.astype(bf16)

                add_rows(SHARE, add)
                second[k] = remote(
                    mine, arrived.at[k - 1], send_two.at[k], recv_two.at[k], y_peer(k)
                )
                second[k].start()

        to_core((1, 3))
        yield
        to_owner((1, 3))
        yield
        to_core((2, 0))
        yield
        to_owner((2,))
        yield
        first[0].wait_recv()
        for k in (1, 3, 2):
            second[k].wait_recv()
        mine_own = block(0, core)

        def total(rows):
            value = mine_own[rows].astype(f32) + from_core[0, rows].astype(f32)
            for k in (1, 2, 3):
                value += arrived[k - 1, rows].astype(f32)
            out[rows] = value

        add_rows(SHARE, total)
        for k in range(4):
            first[k].wait_send()
        for k in (1, 2, 3):
            second[k].wait_send()

    return {
        "scratch": [pltpu.VMEM((4, SHARE, WIDTH), bf16), pltpu.VMEM((3, SHARE, WIDTH), bf16)]
        + [sems(4)] * 4,
        "steps": steps,
    }


def feature_start(ylo, yhi, core):
    return pl.multiple_of((yhi * 2 + core) * 512 + ylo * 256, 256)


def heads_to_tokens():
    def steps(heads, tokens, send, recv):
        ylo, x, z, yhi, core = place()
        y = yhi * 2 + ylo
        mine = tokens.at[:, pl.ds(feature_start(ylo, yhi, core), 256)]
        sent = []

        def go(k, flip):
            target = ring(y, k)
            half = 1 - core if flip else core
            peer = diagonal_peer(k) if flip else y_peer(k)
            src = heads.at[lax.rem(target, 2), half, lax.div(target, 2)]
            copy = remote(src, mine, send.at[2 * k + flip], recv.at[2 * k + flip], peer)
            copy.start()
            sent.append(copy)

        for k in (1, 3):
            for flip in (0, 1):
                go(k, flip)
        yield
        for k, flip in ((2, 0), (2, 1), (0, 1)):
            go(k, flip)
        tokens[:, pl.ds(feature_start(ylo, yhi, core), 256)] = heads[ylo, core, yhi]
        yield
        for k, flip in ((1, 0), (1, 1), (3, 0), (3, 1), (2, 0), (2, 1), (0, 1)):
            source = ring(y, -k)
            half = 1 - core if flip else core
            start = feature_start(lax.rem(source, 2), lax.div(source, 2), half)
            here = tokens.at[:, pl.ds(start, 256)]
            remote(heads.at[0, 0, 0], here, send.at[2 * k + flip], recv.at[2 * k + flip], y_peer(1)).wait_recv()
        for copy in sent:
            copy.wait_send()

    return {"scratch": [sems(8), sems(8)], "steps": steps}


def tokens_to_heads():
    def steps(tokens, heads, send, recv):
        ylo, x, z, yhi, core = place()
        y = yhi * 2 + ylo
        mine = heads.at[ylo, core, yhi]
        sent = []
        order = ((1, 0), (1, 1), (3, 0), (3, 1), (2, 0), (2, 1), (0, 1))
        for k, flip in order:
            target = ring(y, k)
            half = 1 - core if flip else core
            peer = diagonal_peer(k) if flip else y_peer(k)
            start = feature_start(lax.rem(target, 2), lax.div(target, 2), half)
            src = tokens.at[:, pl.ds(start, 256)]
            copy = remote(src, mine, send.at[2 * k + flip], recv.at[2 * k + flip], peer)
            copy.start()
            sent.append(copy)
        heads[ylo, core, yhi] = tokens[:, pl.ds(feature_start(ylo, yhi, core), 256)]
        yield
        for k, flip in order:
            source = ring(y, -k)
            half = 1 - core if flip else core
            here = heads.at[lax.rem(source, 2), half, lax.div(source, 2)]
            remote(here, here, send.at[2 * k + flip], recv.at[2 * k + flip], y_peer(1)).wait_recv()
        for copy in sent:
            copy.wait_send()

    return {"scratch": [sems(8), sems(8)], "steps": steps}


def row_gather():
    def steps(share, full, local_sem, send, recv):
        ylo, x, z, yhi, core = place()
        across, other = y_peer(2), core_partner()
        mine = full.at[:, core, yhi]
        far = full.at[:, core, 1 - yhi]
        local = pltpu.make_async_copy(share, mine, local_sem)
        one = remote(share, mine, send.at[0], recv.at[0], across)
        two = remote(share, mine, send.at[1], recv.at[1], other)
        one.start()
        two.start()
        local.start()
        yield
        remote(share, far, send.at[0], recv.at[0], across).wait_recv()
        three = remote(far, far, send.at[2], recv.at[2], other)
        three.start()
        yield
        remote(share, full.at[:, 1 - core, yhi], send.at[1], recv.at[1], other).wait_recv()
        last = full.at[:, 1 - core, 1 - yhi]
        remote(last, last, send.at[2], recv.at[2], other).wait_recv()
        for copy in (one, two, three):
            copy.wait_send()
        local.wait()

    return {
        "scratch": [pltpu.SemaphoreType.DMA, sems(3), sems(3)],
        "steps": steps,
    }


SIGNS = (1, -1)
XZ = ["x+", "x-", "z+", "z-"]


def xz_near():
    return [[xz_neighbour(axis, d) for d in SIGNS] for axis in (0, 1)]


def weight_gather(columns, spread=False):
    count = 4 if spread else 2

    def steps(own, full, local_sem, swap_send, swap_recv, send, recv):
        ylo, x, z, yhi, core = place()
        y = yhi * 2 + ylo
        near = xz_near()
        offsets = (0, -1, 1, 2)

        def move(src, dst, s, r, stage, d, axis):
            n = ((s * 2 + r) * 8 + stage) * 2 + d
            return remote(src, dst, send.at[n], recv.at[n], near[axis][d])

        def origin(s):
            if spread:
                return ring(y, offsets[s])
            return ylo if s == 0 else 1 - ylo

        def block(s, r, one, two, rows):
            if r == 0:
                return full.at[origin(s), ring(x, one), ring(z, two), rows]
            return full.at[origin(s), ring(x, two), ring(z, one), rows]

        def rows_of(r, d=None):
            return pl.ds(32 * r, 32) if d is None else pl.ds(32 * r + 16 * d, 16)

        mine = own if spread else own.at[ylo]
        here = full.at[origin(0), x, z]
        local = pltpu.make_async_copy(mine, here, local_sem)
        swaps = []
        for s in range(1, count):
            peer = y_peer((4 - offsets[s]) % 4) if spread else lo_partner()
            src = own if spread else own.at[1 - ylo]
            swaps.append(remote(src, here, swap_send.at[s], swap_recv.at[s], peer))
        for swap in swaps:
            swap.start()
        sent = []

        def go(*args):
            copy = move(*args)
            copy.start()
            sent.append(copy)

        def begin(s, source):
            for r in range(2):
                for d in range(2):
                    src = source.at[rows_of(r)]
                    go(src, block(s, r, 0, 0, rows_of(r)), s, r, 0, d, r)
            for r in range(2):
                for d in range(2):
                    src = source.at[rows_of(r)]
                    go(src, block(s, r, 0, 0, rows_of(r)), s, r, 2, d, 1 - r)

        begin(0, mine)
        local.start()
        yield
        for s in range(1, count):
            came = full.at[origin(s), x, z]
            remote(came, came, swap_send.at[s], swap_recv.at[s], lo_partner()).wait_recv()
            begin(s, came)
        yield
        for s in range(count):
            for r in range(2):
                for d in range(2):
                    came = block(s, r, -SIGNS[d], 0, rows_of(r))
                    move(came, came, s, r, 0, d, r).wait_recv()
                    piece = block(s, r, -SIGNS[d], 0, rows_of(r, d))
                    go(piece, piece, s, r, 1, d, r)
                for part in (1, 2):
                    for d in range(2):
                        came = block(s, r, offsets[part], 0, rows_of(r))
                        go(came, came, s, r, 2 + part, d, 1 - r)
            if s % 2:
                yield
        for s in range(count):
            for r in range(2):
                for d in range(2):
                    piece = block(s, r, 2, 0, rows_of(r, d))
                    move(piece, piece, s, r, 1, d, r).wait_recv()
                for d in range(2):
                    came = block(s, r, 2, 0, rows_of(r))
                    go(came, came, s, r, 5, d, 1 - r)
            if s % 2:
                yield
        for part in (0, 2, 1, 3):
            d = part // 2
            for s in range(count):
                for r in range(2):
                    came = block(s, r, offsets[part], -SIGNS[d], rows_of(r))
                    move(came, came, s, r, 2 + part, d, 1 - r).wait_recv()
                    go(came, came, s, r, 6 + part % 2, d, 1 - r)
            yield
        for s in range(count):
            for r in range(2):
                for part in range(4):
                    d = 1 - part // 2
                    came = block(s, r, offsets[part], -SIGNS[d], rows_of(r))
                    move(came, came, s, r, 2 + part, d, 1 - r).wait_recv()
                for part in range(4):
                    d = part // 2
                    came = block(s, r, offsets[part], 2, rows_of(r))
                    move(came, came, s, r, 6 + part % 2, d, 1 - r).wait_recv()
        for copy in sent + swaps:
            copy.wait_send()
        local.wait()

    return {
        "scratch": [pltpu.SemaphoreType.DMA, sems(count), sems(count), sems(32 * count), sems(32 * count)],
        "steps": steps,
    }


def gathered(columns, count=2):
    return (shaped(bf16, count, 4, 4, 64, columns), ANY)


def weight_sum():
    def steps(grads, out, wide, thin, total, swap_send, swap_recv, send, recv):
        ylo, x, z, yhi, core = place()
        near = xz_near()
        partner = lo_partner()

        def move(src, dst, s, r, stage, d, axis):
            n = ((s * 2 + r) * 6 + stage) * 2 + d
            return remote(src, dst, send.at[n], recv.at[n], near[axis][d])

        def line(s, r, step, part):
            if r == 0:
                return grads.at[s, part, ring(z, step), pl.ds(0, 32)]
            return grads.at[s, ring(x, step), part, pl.ds(32, 32)]

        def block(s, r, step, rows):
            if r == 0:
                return grads.at[s, ring(x, step), z, rows]
            return grads.at[s, x, ring(z, step), rows]

        def wide_move(s, r, d, kind):
            if kind == 0:
                src = line(s, r, 2, pl.ds(2 * d, 2))
            elif kind == 1:
                src = line(s, r, SIGNS[d], pl.ds(2 - 2 * d, 2))
            else:
                src = line(s, r, SIGNS[d], pl.ds(2 * d, 2))
            return move(src, wide.at[s, r, kind, d], s, r, kind, d, 1 - r)

        def thin_move(s, r, d, kind):
            if kind == 0:
                src = block(s, r, 2, pl.ds(32 * r + 16 * d, 16))
            elif kind == 1:
                src = block(s, r, SIGNS[d], pl.ds(32 * r + 16 - 16 * d, 16))
            else:
                src = block(s, r, SIGNS[d], pl.ds(32 * r + 16 * d, 16))
            return move(src, thin.at[s, r, kind, d], s, r, 3 + kind, d, r)

        for s in range(2):
            for kind in range(2):
                for r in range(2):
                    for d in range(2):
                        wide_move(s, r, d, kind).start()
        yield

        for s in range(2):
            for r in range(2):
                for d in range(2):
                    wide_move(s, r, d, 0).wait_recv()
                    for p in range(2):
                        mine = line(s, r, SIGNS[d], 2 * d + p)

                        def one(rows):
                            value = mine[rows].astype(f32) + wide[s, r, 0, d, p, rows].astype(f32)
                            mine[rows] = value.astype(bf16)

                        add_rows(32, one)
                    wide_move(s, r, d, 2).start()
            yield

        for s in range(2):
            for r in range(2):
                for d in range(2):
                    wide_move(s, r, d, 1).wait_recv()
                    wide_move(s, r, d, 2).wait_recv()
                for p in range(4):
                    mine = line(s, r, 0, p)
                    d = p // 2

                    def one(rows):
                        value = mine[rows].astype(f32) + wide[s, r, 2, d, p % 2, rows].astype(f32)
                        value += wide[s, r, 1, 1 - d, p % 2, rows].astype(f32)
                        mine[rows] = value.astype(bf16)

                    add_rows(32, one)
                for kind in range(2):
                    for d in range(2):
                        thin_move(s, r, d, kind).start()
            yield

        for s in range(2):
            for r in range(2):
                for d in range(2):
                    thin_move(s, r, d, 0).wait_recv()
                    mine = block(s, r, SIGNS[d], pl.ds(32 * r + 16 * d, 16))
                    value = mine[...].astype(f32) + thin[s, r, 0, d].astype(f32)
                    mine[...] = value.astype(bf16)
                    thin_move(s, r, d, 2).start()
        yield

        for s in range(2):
            for r in range(2):
                for d in range(2):
                    thin_move(s, r, d, 1).wait_recv()
                    thin_move(s, r, d, 2).wait_recv()
                for d in range(2):
                    rows = pl.ds(32 * r + 16 * d, 16)
                    value = block(s, r, 0, rows)[...].astype(f32) + thin[s, r, 2, d].astype(f32)
                    value += thin[s, r, 1, 1 - d].astype(f32)
                    total[s, rows] = value.astype(bf16)
        swap = remote(total.at[1 - ylo], out.at[ylo], swap_send, swap_recv, partner)
        swap.start()
        out[ylo] = total[ylo]
        yield
        for s in range(2):
            for r in range(2):
                for d in range(2):
                    for kind in range(3):
                        wide_move(s, r, d, kind).wait_send()
                        thin_move(s, r, d, kind).wait_send()
        remote(total.at[0], out.at[1 - ylo], swap_send, swap_recv, partner).wait_recv()
        swap.wait_send()

    return {
        "scratch": [
            pltpu.VMEM((2, 2, 3, 2, 2, 32, PART), bf16),
            pltpu.VMEM((2, 2, 3, 2, 16, PART), bf16),
            pltpu.VMEM((2, 64, PART), bf16),
            pltpu.SemaphoreType.DMA,
            pltpu.SemaphoreType.DMA,
            sems(48),
            sems(48),
        ],
        "steps": steps,
    }


def standardize(value):
    mean = jnp.mean(value, axis=-1, keepdims=True)
    centered = value - mean
    scale_inv = lax.rsqrt(jnp.mean(centered * centered, axis=-1, keepdims=True) + epsilon)
    return (centered * scale_inv, scale_inv)


def norm_back(grad_normed_out, normed, scale_inv, gain):
    scaled = grad_normed_out * gain
    mean_one = jnp.mean(scaled, axis=-1, keepdims=True)
    mean_two = jnp.mean(scaled * normed, axis=-1, keepdims=True)
    grad_value = scale_inv * (scaled - mean_one - normed * mean_two)
    grad_gain = jnp.sum(grad_normed_out * normed, axis=0, keepdims=True)
    grad_shift = jnp.sum(grad_normed_out, axis=0, keepdims=True)
    return (grad_value, grad_gain, grad_shift)


def dot(a, b):
    return jnp.dot(a, b, preferred_element_type=f32)


def turned_dot(a, b):
    return lax.dot_general(a, b, (((1,), (1,)), ((), ())), preferred_element_type=f32)


def outer_dot(a, b):
    return lax.dot_general(a, b, (((0,), (0,)), ((), ())), preferred_element_type=f32)


def some_rows(count, size, one):
    def body(i, carry):
        one(pl.ds(pl.multiple_of(i * size, size), size))
        return carry

    lax.fori_loop(0, count // size, body, 0)


def fetched(src, dst, sem):
    copy = pltpu.make_async_copy(src, dst, sem)
    copy.start()
    return copy


CODES = 4096
CODE_CHUNK = 512


def embed_body(ins, outs, scratch, makers):
    ids, stream, cot, codebook, own_qkv, own_out, norms, masks = ins
    attn_full, cot_full, inputs_share, gains, masks_out, qkv_full, out_half = outs
    everyone, chunk, total, halves, chunk_sem = scratch
    make_small, make_qkv, make_out, make_cot, make_attn = makers
    ylo, x, z, yhi, core = place()
    small = make_small(norms, masks, everyone, masks_out)
    qkv = make_qkv(own_qkv, qkv_full)
    out = make_out(own_out, out_half)
    cot_move = make_cot(cot, cot_full)
    attn_move = make_attn(halves, attn_full)

    def fetch(j):
        rows = pl.ds(j * CODE_CHUNK, CODE_CHUNK)
        return pltpu.make_async_copy(codebook.at[rows], chunk.at[j % 2], chunk_sem.at[j % 2])

    fetch(0).start()
    step(small, qkv, out, cot_move)
    total[...] = stream[...].astype(f32)
    count = CODES // CODE_CHUNK
    for j in range(count):
        if j + 1 < count:
            fetch(j + 1).start()
        fetch(j).wait()
        code = lax.broadcasted_iota(jnp.int32, (256, CODE_CHUNK), 1) + j * CODE_CHUNK
        pick = jnp.where(ids[...] == code, 1.0, 0.0).astype(bf16)
        for part in range(2):
            columns = pl.ds(part * 1024, 1024)
            total[:, columns] += dot(pick, chunk[j % 2, :, columns])
        if j in (2, 5):
            step(qkv, out)
    step(small)
    for t in range(16):
        for k in range(4):
            pair = everyone[2 * t, pl.ds(k, 1)] + everyone[2 * t + 1, pl.ds(k, 1)]
            gains[pl.ds(k, 1), pl.ds(128 * t, 128)] = pair
    gain, shift = gains[pl.ds(0, 1)], gains[pl.ds(1, 1)]
    for u in range(2):

        def norm(rows):
            value = total[pl.ds(pl.multiple_of(u * SHARE + rows.start, 16), 16)]
            normed, _ = standardize(value)
            halves[0, u, rows] = (normed * gain + shift).astype(bf16)

        some_rows(SHARE, 16, norm)
    step(attn_move)

    def keep(rows):
        inputs_share[rows] = total[pl.ds(pl.multiple_of(yhi * SHARE + rows.start, 16), 16)]

    some_rows(SHARE, 16, keep)
    step(qkv, out, qkv, out, out)
    step(qkv, qkv, cot_move, out, out, qkv, qkv)
    step(attn_move)
    step(out, out)
    finish(cot_move, attn_move, qkv, out)


def embed(ids, stream, cot, codebook, own_qkv, own_out, norms, masks):
    return kernel_call(
        embed_body,
        [
            small_gather(),
            weight_gather(768),
            weight_gather(512, spread=True),
            row_exchange(),
            row_exchange(),
        ],
        DP + ["y1", "y2", "y3", "core"],
        [
            (ids, VMEM),
            (stream, VMEM),
            (cot, VMEM),
            (codebook, ANY),
            (own_qkv, VMEM),
            (own_out, VMEM),
            (norms, VMEM),
            (masks, VMEM),
        ],
        [
            (shaped(bf16, 1, 2, 2, 2, SHARE, WIDTH), ANY),
            (shaped(bf16, 1, 2, 2, 2, SHARE, WIDTH), ANY),
            (shaped(f32, SHARE, WIDTH), VMEM),
            (shaped(f32, 8, WIDTH), VMEM),
            (shaped(f32, 8, 128), VMEM),
            gathered(768),
            gathered(512, 4),
        ],
        [
            pltpu.VMEM((32, 8, 128), f32),
            pltpu.VMEM((2, CODE_CHUNK, WIDTH), bf16),
            pltpu.VMEM((256, WIDTH), f32),
            pltpu.VMEM((1, 2, SHARE, WIDTH), bf16),
            sems(2),
        ],
        0,
    )


def attention_body(ins, outs, scratch, makers):
    attn_hbm, weight_hbm, mask, inputs_share, gains, own_up, own_down, out_half = ins
    projected, attended, middle, ffn_full, up_full, down_full, out_other = outs
    attn_in, weight, out_weight, tokens, ffn_share, load_sem, swap_send, swap_recv = scratch
    make_up, make_down, make_heads, make_share = makers
    ylo, x, z, yhi, core = place()
    up, down = make_up(own_up, up_full), make_down(own_down, down_full)
    heads = make_heads(attended, tokens)
    spread = make_share(ffn_share, ffn_full)

    loads = [
        fetched(attn_hbm.at[1 - ylo], attn_in.at[1 - ylo], load_sem.at[0]),
        fetched(weight_hbm, weight, load_sem.at[1]),
        fetched(attn_hbm.at[ylo], attn_in.at[ylo], load_sem.at[2]),
        fetched(out_half, out_weight.at[core], load_sem.at[3]),
    ]
    swap = remote(out_half, out_other, swap_send, swap_recv, core_partner())
    swap.start()

    def project(r):
        def one(t, carry):
            columns = pl.ds(pl.multiple_of(t * 256, 256), 256)
            projected[r, :, columns] = dot(attn_in[r], weight[:, columns]).astype(bf16)
            return carry

        lax.fori_loop(0, 3, one, 0)

    def attend(r):
        for h in range(2):
            key = projected[r, :, pl.ds(256 + h * HEAD, HEAD)]
            value = projected[r, :, pl.ds(512 + h * HEAD, HEAD)]
            for c in range(2):
                rows = pl.ds(c * 256, 256)
                query = projected[r, rows, pl.ds(h * HEAD, HEAD)]
                scores = turned_dot(query, key) * HEAD ** (-0.5)
                scores = jnp.where(mask[r, rows].astype(f32) > 0.5, scores, masked_score)
                expd = jnp.exp(scores - jnp.max(scores, axis=-1, keepdims=True))
                probs = expd / jnp.sum(expd, axis=-1, keepdims=True)
                result = dot(probs.astype(bf16), value).astype(bf16)
                for u in range(2):
                    attended[r, c, u, :, pl.ds(h * HEAD, HEAD)] = result[u * SHARE : (u + 1) * SHARE]

    step(up, down)
    loads[0].wait()
    loads[1].wait()
    project(1 - ylo)
    step(up, down)
    attend(1 - ylo)
    step(heads)
    step(up, down)
    loads[2].wait()
    project(ylo)
    step(up, down)
    attend(ylo)
    step(heads)
    remote(out_half, out_other, swap_send, swap_recv, core_partner()).wait_recv()
    other_load = fetched(out_other, out_weight.at[1 - core], load_sem.at[4])
    step(up, down)
    finish(heads)
    loads[3].wait()
    other_load.wait()

    def branch(n, carry):
        columns = pl.ds(pl.multiple_of(n * 256, 256), 256)
        value = inputs_share[:, columns]
        for c in range(2):
            for h in range(2):
                features = pl.ds((h * 2 + c) * 512, 512)
                value += turned_dot(tokens[:, features], out_weight[c, h, columns])
        middle[:, columns] = value
        return carry

    lax.fori_loop(0, WIDTH // 256, branch, 0)
    gain, shift = gains[pl.ds(2, 1)], gains[pl.ds(3, 1)]

    def norm(rows):
        normed, _ = standardize(middle[rows])
        ffn_share[rows] = (normed * gain + shift).astype(bf16)

    some_rows(SHARE, 16, norm)
    step(spread)
    step(up, down)
    step(up, down)
    step(up, down)
    step(spread)
    finish(spread, up, down)
    swap.wait_send()


def attention(attn_in, weight, mask, inputs_share, gains, own_up, own_down, out_half):
    return kernel_call(
        attention_body,
        [weight_gather(PART), weight_gather(PART), heads_to_tokens(), share_gather()],
        XZ + GROUP,
        [
            (attn_in, ANY),
            (weight, ANY),
            (mask, VMEM),
            (inputs_share, VMEM),
            (gains, VMEM),
            (own_up, VMEM),
            (own_down, VMEM),
            (out_half, ANY),
        ],
        [
            (shaped(bf16, 2, 512, 768), VMEM),
            (shaped(bf16, 2, 2, 2, SHARE, 256), VMEM),
            (shaped(f32, SHARE, WIDTH), VMEM),
            (shaped(bf16, 2, 2, 2, SHARE, WIDTH), ANY),
            gathered(PART),
            gathered(PART),
            (shaped(bf16, 2, WIDTH, 512), ANY),
        ],
        [
            pltpu.VMEM((2, 512, WIDTH), bf16),
            pltpu.VMEM((WIDTH, 768), bf16),
            pltpu.VMEM((2, 2, WIDTH, 512), bf16),
            pltpu.VMEM((SHARE, WIDTH), bf16),
            pltpu.VMEM((SHARE, WIDTH), bf16),
            sems(5),
            pltpu.SemaphoreType.DMA,
            pltpu.SemaphoreType.DMA,
        ],
        1,
    )


SLOPE = 0.7978845608028654
CUBIC = 0.044715


def ffn_body(ins, outs, scratch, makers):
    ffn_hbm, cot_hbm, up_hbm, down_hbm, middle, gains = ins
    sum_down, grad_up_weight, layer_out, grad_middle, small = outs
    (
        ffn_in,
        cot,
        up_weight,
        down_weight,
        hidden,
        grad_up,
        back,
        ahead,
        grad_down_weight,
        back_share,
        ahead_share,
        load_sem,
    ) = scratch
    make_back, make_ahead, make_down = makers
    ylo, x, z, yhi, core = place()
    back_sum = make_back(back, back_share)
    ahead_sum = make_ahead(ahead, ahead_share)
    down_sum = make_down(grad_down_weight, sum_down)
    loads = [
        fetched(ffn_hbm.at[1 - ylo], ffn_in.at[1 - ylo], load_sem.at[0]),
        fetched(up_hbm, up_weight, load_sem.at[1]),
        fetched(cot_hbm.at[1 - ylo], cot.at[1 - ylo], load_sem.at[2]),
        fetched(down_hbm, down_weight, load_sem.at[3]),
        fetched(ffn_hbm.at[ylo], ffn_in.at[ylo], load_sem.at[4]),
        fetched(cot_hbm.at[ylo], cot.at[ylo], load_sem.at[5]),
    ]

    def units(r):
        def one(n, carry):
            columns = pl.ds(pl.multiple_of(n * 256, 256), 256)
            value = dot(ffn_in[r], up_weight[:, columns])
            grad = dot(cot[r], down_weight[:, columns])
            square = value * value
            bend = jnp.tanh(SLOPE * value * (1.0 + CUBIC * square))
            half = 0.5 * (1.0 + bend)
            hidden[r, :, columns] = (value * half).astype(bf16)
            slope = half + 0.5 * value * (1.0 - bend * bend) * SLOPE * (1.0 + 3.0 * CUBIC * square)
            grad_up[r, :, columns] = (grad * slope).astype(bf16)
            return carry

        lax.fori_loop(0, PART // 256, one, 0)

    def spread_out(r, source, weight, target):
        def one(n, carry):
            columns = pl.ds(pl.multiple_of(n * 256, 256), 256)
            value = turned_dot(source[r], weight[columns]).astype(bf16)
            for c in range(2):
                for u in range(2):
                    at = (2 * c + u) * SHARE
                    target[r, c, u, :, columns] = value[at : at + SHARE]
            return carry

        lax.fori_loop(0, WIDTH // 256, one, 0)

    for load in loads[:4]:
        load.wait()
    units(1 - ylo)
    spread_out(1 - ylo, grad_up, up_weight, back)
    step(back_sum)
    for load in loads[4:]:
        load.wait()
    units(ylo)
    step(back_sum)
    spread_out(ylo, grad_up, up_weight, back)
    step(back_sum)

    def weight_grad(left, right, target):
        for n in range(WIDTH // 256):
            columns = pl.ds(n * 256, 256)
            value = outer_dot(left[0, :, columns], right[0]) + outer_dot(left[1, :, columns], right[1])
            target(n, value.astype(bf16))

    def keep_down(n, value):
        for j in range(4):
            grad_down_weight[n // 4, n % 4, j] = value[64 * j : 64 * j + 64]

    def keep_up(n, value):
        for j in range(4):
            grad_up_weight[n // 4, n % 4, j] = value[64 * j : 64 * j + 64]

    weight_grad(cot, hidden, keep_down)
    step(down_sum)
    step(back_sum)
    spread_out(1 - ylo, hidden, down_weight, ahead)
    step(ahead_sum)
    spread_out(ylo, hidden, down_weight, ahead)
    step(ahead_sum)
    step(ahead_sum)
    step(down_sum)
    step(ahead_sum)
    step(down_sum)
    weight_grad(ffn_in, grad_up, keep_up)
    finish(back_sum)
    step(down_sum)
    gain = gains[pl.ds(2, 1)]
    small[...] = jnp.zeros_like(small)

    def back_norm(i, carry):
        at = pl.multiple_of(i * 16, 16)
        rows = pl.ds(at, 16)
        normed, inverse = standardize(middle[rows])
        value, grad_gain, grad_shift = norm_back(back_share[rows], normed, inverse, gain)
        grad_middle[rows] = value + cot[ylo, pl.ds(pl.multiple_of(core * 256 + yhi * SHARE + at, 16), 16)].astype(f32)
        small[pl.ds(2, 1)] += grad_gain
        small[pl.ds(3, 1)] += grad_shift
        return carry

    lax.fori_loop(0, SHARE // 16, back_norm, 0)
    step(down_sum, down_sum)
    finish(ahead_sum)

    def end(rows):
        layer_out[0, rows] = (middle[rows] + ahead_share[rows]).astype(bf16)

    some_rows(SHARE, 16, end)
    finish(down_sum)


def feed_forward(ffn_in, cot, up, down, middle, gains):
    return kernel_call(
        ffn_body,
        [share_sum(), share_sum(), weight_sum()],
        XZ + ["y1", "y2", "y3", "core"],
        [(ffn_in, ANY), (cot, ANY), (up, ANY), (down, ANY), (middle, VMEM), (gains, VMEM)],
        [
            (shaped(bf16, 2, 64, PART), VMEM),
            (shaped(bf16, 2, 4, 4, 64, PART), VMEM),
            (shaped(bf16, 1, SHARE, WIDTH), VMEM),
            (shaped(f32, SHARE, WIDTH), VMEM),
            (shaped(f32, 8, WIDTH), VMEM),
        ],
        [
            pltpu.VMEM((2, 512, WIDTH), bf16),
            pltpu.VMEM((2, 512, WIDTH), bf16),
            pltpu.VMEM((WIDTH, PART), bf16),
            pltpu.VMEM((WIDTH, PART), bf16),
            pltpu.VMEM((2, 512, PART), bf16),
            pltpu.VMEM((2, 512, PART), bf16),
            pltpu.VMEM((2, 2, 2, SHARE, WIDTH), bf16),
            pltpu.VMEM((2, 2, 2, SHARE, WIDTH), bf16),
            pltpu.VMEM((2, 4, 4, 64, PART), bf16),
            pltpu.VMEM((SHARE, WIDTH), f32),
            pltpu.VMEM((SHARE, WIDTH), f32),
            sems(6),
        ],
        2,
        62,
    )


def back_body(ins, outs, scratch, makers):
    (
        attn_hbm,
        weight_hbm,
        out_half,
        out_other,
        up_hbm,
        projected,
        attended,
        mask,
        grad_middle,
        inputs_share,
        layer_out,
        small_in,
        gains,
    ) = ins
    layer_full, input_full, sum_up, sum_attn, small_out, branch_full = outs
    (
        attn_in,
        weight,
        out_weight,
        grad_up_weight,
        grad_attn_weight,
        grad_branch,
        branch_share,
        grad_tokens,
        grad_heads,
        grad_projected,
        back,
        back_share,
        input_share,
        small,
        load_sem,
    ) = scratch
    make_up, make_attn, make_heads, make_branch, make_back, make_layer, make_input, make_small = makers
    ylo, x, z, yhi, core = place()
    up_sum = make_up(grad_up_weight, sum_up)
    attn_sum = make_attn(grad_attn_weight, sum_attn)
    heads = make_heads(grad_tokens, grad_heads)
    branch = make_branch(branch_share, branch_full)
    back_sum = make_back(back, back_share)
    layer_move = make_layer(layer_out, layer_full)
    input_move = make_input(input_share, input_full)
    small_sum = make_small(small, small_out)
    loads = [
        fetched(out_half, out_weight.at[core], load_sem.at[0]),
        fetched(out_other, out_weight.at[1 - core], load_sem.at[1]),
        fetched(up_hbm, grad_up_weight, load_sem.at[2]),
        fetched(weight_hbm, weight, load_sem.at[3]),
        fetched(attn_hbm, attn_in, load_sem.at[4]),
    ]

    def low(rows):
        branch_share[rows] = grad_middle[rows].astype(bf16)

    some_rows(SHARE, 16, low)
    loads[0].wait()
    loads[1].wait()
    for h in range(2):
        for c in range(2):
            grad_tokens[:, pl.ds((h * 2 + c) * 512, 512)] = dot(
                branch_share[...], out_weight[c, h]
            ).astype(bf16)
    step(heads)
    loads[2].wait()
    step(up_sum)
    step(branch)
    finish(heads)

    def attend(r):
        for h in range(2):
            query = projected[r, :, pl.ds(h * HEAD, HEAD)]
            key = projected[r, :, pl.ds(256 + h * HEAD, HEAD)]
            value = projected[r, :, pl.ds(512 + h * HEAD, HEAD)]
            grad = grad_heads[r, :, :, :, pl.ds(h * HEAD, HEAD)].reshape(512, HEAD)
            scores = turned_dot(query, key) * HEAD ** (-0.5)
            scores = jnp.where(mask[r].astype(f32) > 0.5, scores, masked_score)
            expd = jnp.exp(scores - jnp.max(scores, axis=-1, keepdims=True))
            probs = expd / jnp.sum(expd, axis=-1, keepdims=True)
            grad_probs = turned_dot(grad, value)
            inner = jnp.sum(grad_probs * probs, axis=-1, keepdims=True)
            grad_scores = (probs * (grad_probs - inner)).astype(bf16)
            parts = (
                dot(grad_scores, key) * HEAD ** (-0.5),
                outer_dot(grad_scores, query) * HEAD ** (-0.5),
                outer_dot(probs.astype(bf16), grad),
            )
            for t in range(3):
                grad_projected[r, :, pl.ds(t * 256 + h * HEAD, HEAD)] = parts[t].astype(bf16)

    def spread_out(r):
        def one(n, carry):
            columns = pl.ds(pl.multiple_of(n * 256, 256), 256)
            value = turned_dot(grad_projected[r], weight[columns]).astype(bf16)
            for c in range(2):
                for u in range(2):
                    at = (2 * c + u) * SHARE
                    back[r, c, u, :, columns] = value[at : at + SHARE]
            return carry

        lax.fori_loop(0, WIDTH // 256, one, 0)

    attend(1 - ylo)
    loads[3].wait()
    step(up_sum)
    spread_out(1 - ylo)
    step(back_sum)
    attend(ylo)
    step(back_sum)
    step(up_sum)
    spread_out(ylo)
    step(back_sum)
    step(branch)
    loads[4].wait()
    for n in range(WIDTH // 256):
        columns = pl.ds(n * 256, 256)
        value = outer_dot(attn_in[0, :, columns], grad_projected[0])
        value += outer_dot(attn_in[1, :, columns], grad_projected[1])
        value = value.astype(bf16)
        for j in range(4):
            grad_attn_weight[n // 4, n % 4, j, :, pl.ds(0, 768)] = value[64 * j : 64 * j + 64]
        if n == 2:
            step(back_sum)
    step(layer_move)
    step(up_sum)
    finish(branch)
    gather_load = fetched(branch_full, grad_branch, load_sem.at[5])
    step(up_sum)
    gather_load.wait()
    for n in range(WIDTH // 256):
        columns = pl.ds(n * 256, 256)
        value = sum(
            outer_dot(grad_branch[r, :, :, :, columns].reshape(512, 256), attended[r].reshape(512, 256))
            for r in range(2)
        )
        value = value.astype(bf16)
        for j in range(4):
            grad_attn_weight[n // 4, n % 4, j, :, pl.ds(768, 256)] = value[64 * j : 64 * j + 64]
    step(attn_sum)
    step(up_sum)
    finish(back_sum)
    gain = gains[pl.ds(0, 1)]
    small[...] = small_in[...]

    def back_norm(i, carry):
        rows = pl.ds(pl.multiple_of(i * 16, 16), 16)
        normed, inverse = standardize(inputs_share[rows])
        value, grad_gain, grad_shift = norm_back(back_share[rows], normed, inverse, gain)
        input_share[0, rows] = (grad_middle[rows] + value).astype(bf16)
        small[pl.ds(0, 1)] += grad_gain
        small[pl.ds(1, 1)] += grad_shift
        return carry

    lax.fori_loop(0, SHARE // 16, back_norm, 0)
    step(input_move, small_sum)
    step(up_sum, up_sum)
    step(attn_sum, layer_move, attn_sum, small_sum, input_move)
    step(attn_sum, attn_sum, attn_sum)
    finish(layer_move, input_move, small_sum, up_sum, attn_sum)


def attention_back(
    attn_in,
    weight,
    out_half,
    out_other,
    grad_up_weight,
    projected,
    attended,
    mask,
    grad_middle,
    inputs_share,
    layer_out,
    small,
    gains,
):
    return kernel_call(
        back_body,
        [
            weight_sum(),
            weight_sum(),
            tokens_to_heads(),
            share_gather(),
            share_sum(),
            row_gather(),
            row_gather(),
            small_reduce(),
        ],
        DP + MP + GROUP,
        [
            (attn_in, ANY),
            (weight, ANY),
            (out_half, ANY),
            (out_other, ANY),
            (grad_up_weight, ANY),
            (projected, VMEM),
            (attended, VMEM),
            (mask, VMEM),
            (grad_middle, VMEM),
            (inputs_share, VMEM),
            (layer_out, VMEM),
            (small, VMEM),
            (gains, VMEM),
        ],
        [
            (shaped(bf16, 1, 2, 2, SHARE, WIDTH), ANY),
            (shaped(bf16, 1, 2, 2, SHARE, WIDTH), ANY),
            (shaped(bf16, 2, 64, PART), VMEM),
            (shaped(bf16, 2, 64, PART), VMEM),
            (shaped(f32, 8, 128), VMEM),
            (shaped(bf16, 2, 2, 2, SHARE, WIDTH), ANY),
        ],
        [
            pltpu.VMEM((2, 512, WIDTH), bf16),
            pltpu.VMEM((WIDTH, 768), bf16),
            pltpu.VMEM((2, 2, WIDTH, 512), bf16),
            pltpu.VMEM((2, 4, 4, 64, PART), bf16),
            pltpu.VMEM((2, 4, 4, 64, PART), bf16),
            pltpu.VMEM((2, 2, 2, SHARE, WIDTH), bf16),
            pltpu.VMEM((SHARE, WIDTH), bf16),
            pltpu.VMEM((SHARE, WIDTH), bf16),
            pltpu.VMEM((2, 2, 2, SHARE, 256), bf16),
            pltpu.VMEM((2, 512, 768), bf16),
            pltpu.VMEM((2, 2, 2, SHARE, WIDTH), bf16),
            pltpu.VMEM((SHARE, WIDTH), f32),
            pltpu.VMEM((1, SHARE, WIDTH), bf16),
            pltpu.VMEM((8, WIDTH), f32),
            sems(6),
        ],
        3,
        62,
    )


def visible(segment_ids, padding):
    seq_len = segment_ids.shape[1]
    position = jnp.arange(seq_len)
    causal = position[None, :] <= position[:, None]
    itself = position[None, :] == position[:, None]
    same = segment_ids[:, :, None] == segment_ids[:, None, :]
    live = (padding[:, None, :] == 1) | itself[None]
    return same & causal[None] & live


def on_device(
    stream,
    code_ids,
    segment_ids,
    padding,
    codebook,
    norm1_gain,
    norm1_shift,
    w_qkv,
    w_out,
    norm2_gain,
    norm2_shift,
    w_up,
    w_down,
    cotangent,
):
    ylo, x, z, yhi, core = place()
    own_qkv = w_qkv.reshape(64, 3, 2, 256).transpose(2, 0, 1, 3).reshape(2, 64, 768)
    own_up = w_up.reshape(64, 2, PART).transpose(1, 0, 2)
    own_down = w_down.reshape(64, 2, PART).transpose(1, 0, 2)

    odd = lax.rem(z, 2) == 1
    norms = jnp.stack([norm1_gain, norm1_shift, norm2_gain, norm2_shift]).astype(f32)
    none = jnp.zeros_like(norms)
    norms = jnp.concatenate([jnp.where(odd, none, norms), jnp.where(odd, norms, none)], axis=1)
    masks = jnp.concatenate([segment_ids.reshape(4, 128), padding.reshape(4, 128)]).astype(f32)
    ids_half = lax.dynamic_slice_in_dim(code_ids[0], core * 256, 256, 0)
    stream_half = lax.dynamic_slice_in_dim(stream[0], core * 256, 256, 0)
    cot_half = lax.dynamic_slice_in_dim(cotangent[0], core * 256, 256, 0)

    attn_in, cot, inputs_share, gains, masks_other, qkv_full, out_half = embed(
        ids_half[:, None],
        stream_half,
        cot_half.reshape(1, 2, SHARE, WIDTH),
        codebook,
        own_qkv,
        w_out,
        jnp.pad(norms, ((0, 4), (0, 0))),
        masks,
    )
    attn_in, cot = attn_in.reshape(2, 512, WIDTH), cot.reshape(2, 512, WIDTH)
    qkv_full, out_half = qkv_full.reshape(WIDTH, 768), out_half.reshape(2, WIDTH, 512)
    both = jnp.where(ylo == 0, jnp.stack([masks, masks_other]), jnp.stack([masks_other, masks]))
    allowed = visible(both[:, :4].reshape(2, 512), both[:, 4:].reshape(2, 512)).astype(bf16)

    projected, attended, middle, ffn_in, up_full, down_full, out_other = attention(
        attn_in, qkv_full, allowed, inputs_share, gains, own_up, own_down, out_half
    )
    sum_down, grad_up_weight, layer_out, grad_middle, small = feed_forward(
        ffn_in.reshape(2, 512, WIDTH),
        cot,
        up_full.reshape(WIDTH, PART),
        down_full.reshape(WIDTH, PART),
        middle,
        gains,
    )
    layer_out, input_grad, sum_up, sum_attn, small, _ = attention_back(
        attn_in,
        qkv_full,
        out_half,
        out_other,
        grad_up_weight,
        projected,
        attended,
        allowed,
        grad_middle,
        inputs_share,
        layer_out,
        small,
        gains,
    )

    sum_attn, sum_up, sum_down = (g.astype(f32) for g in (sum_attn, sum_up, sum_down))
    out_qkv = sum_attn[:, :, :768].reshape(2, 64, 3, 256).transpose(1, 2, 0, 3).reshape(64, 3, 512)
    out_out = sum_attn[:, :, 768:].transpose(1, 0, 2).reshape(64, 512)
    out_up = sum_up.transpose(1, 0, 2).reshape(64, WIDTH)
    out_down = sum_down.transpose(1, 0, 2).reshape(64, WIDTH)
    small = jnp.where(odd, small[:4, 64:], small[:4, :64])
    return (
        layer_out.reshape(1, 512, WIDTH).astype(f32),
        input_grad.reshape(1, 512, WIDTH).astype(f32),
        small[0],
        small[1],
        out_qkv,
        out_out,
        small[2],
        small[3],
        out_up,
        out_down,
    )


def solution(mesh):
    in_specs = (
        P("dp", None, None),
        P("dp", None),
        P("dp", None),
        P("dp", None),
        P(),
        P("dp"),
        P("dp"),
        P("dp", None, "mp"),
        P("dp", "mp"),
        P("dp"),
        P("dp"),
        P("dp", "mp"),
        P("dp", "mp"),
        P("dp", None, None),
    )
    out_specs = (
        P("dp", None, None),
        P("dp", None, None),
        P("dp"),
        P("dp"),
        P("dp", None, "mp"),
        P("dp", "mp"),
        P("dp"),
        P("dp"),
        P("dp", "mp"),
        P("dp", "mp"),
    )
    return jax.shard_map(
        on_device, mesh=mesh, in_specs=in_specs, out_specs=out_specs, check_vma=False
    )
```

```python
import functools

import jax
import jax.numpy as jnp
from jax import lax
from jax.experimental import pallas as pl
from jax.experimental.pallas import tpu as pltpu
from jax.sharding import PartitionSpec as P

HEAD = 128
WIDTH = 2048
SHARE = 128
PART = 1024
MESH = pl.DeviceIdType.MESH
ANY = pl.BlockSpec(memory_space=pl.ANY)
VMEM = pl.BlockSpec(memory_space=pltpu.VMEM)
masked_score = -1000000000.0
epsilon = 1e-05
f32 = jnp.float32
bf16 = jnp.bfloat16


def place():
    dp, mp = lax.axis_index("dp"), lax.axis_index("mp")
    return lax.div(dp, 16), lax.rem(lax.div(dp, 4), 4), lax.rem(dp, 4), lax.div(mp, 2), lax.rem(mp, 2)


def ring(position, step):
    return lax.rem(position + step + 4, 4)


def xz_neighbour(axis, step):
    ylo, x, z, yhi, core = place()
    if axis == 0:
        x = ring(x, step)
    else:
        z = ring(z, step)
    return (ylo * 16 + x * 4 + z, yhi * 2 + core)


def y_peer(step):
    ylo, x, z, yhi, core = place()
    y = ring(yhi * 2 + ylo, step)
    return (lax.rem(y, 2) * 16 + x * 4 + z, lax.div(y, 2) * 2 + core)


def lo_partner():
    ylo, x, z, yhi, core = place()
    return ((1 - ylo) * 16 + x * 4 + z, yhi * 2 + core)


def core_partner():
    ylo, x, z, yhi, core = place()
    return (ylo * 16 + x * 4 + z, yhi * 2 + 1 - core)


def greet(peers):
    barrier = pltpu.get_barrier_semaphore()
    for peer in peers:
        pl.semaphore_signal(barrier, inc=1, device_id=peer, device_id_type=MESH)
    pl.semaphore_wait(barrier, len(peers))


def remote(src, dst, send_sem, recv_sem, peer):
    return pltpu.make_async_remote_copy(
        src_ref=src,
        dst_ref=dst,
        send_sem=send_sem,
        recv_sem=recv_sem,
        device_id=peer,
        device_id_type=MESH,
    )


def sems(*shape):
    return pltpu.SemaphoreType.DMA(shape)


def params(collective_id, mib=48):
    return pltpu.CompilerParams(
        collective_id=collective_id, has_side_effects=True, vmem_limit_bytes=mib << 20
    )


PEERS = {
    "core": core_partner,
    "x+": lambda: xz_neighbour(0, 1),
    "x-": lambda: xz_neighbour(0, -1),
    "z+": lambda: xz_neighbour(1, 1),
    "z-": lambda: xz_neighbour(1, -1),
    "y1": lambda: y_peer(1),
    "y2": lambda: y_peer(2),
    "y3": lambda: y_peer(3),
}


def dp_peer(step):
    return (lax.rem(lax.axis_index("dp") + step, 32), lax.axis_index("mp"))


def diagonal_peer(step):
    dp, mp = y_peer(step)
    return (dp, mp + 1 - 2 * lax.rem(mp, 2))


def mp_peer(step):
    return (lax.axis_index("dp"), lax.rem(lax.axis_index("mp") + step, 4))


PEERS.update({f"dp{k}": functools.partial(dp_peer, k) for k in range(1, 32)})
PEERS.update({f"mp{k}": functools.partial(mp_peer, k) for k in range(1, 4)})
PEERS.update({f"d{k}": functools.partial(diagonal_peer, k) for k in range(1, 4)})
GROUP = ["y1", "y2", "y3", "core", "d1", "d2", "d3"]
DP = [f"dp{k}" for k in range(1, 32)]
MP = ["mp1", "mp2", "mp3"]


def kernel_call(body, jobs, peers, ins, outs, scratch, collective_id, mib=56):
    def kernel(*refs):
        taken = 0

        def take(count):
            nonlocal taken
            taken += count
            return refs[taken - count : taken]

        groups = [take(len(ins)), take(len(outs)), take(len(scratch))]
        makers = []
        for job in jobs:
            own = take(len(job["scratch"]))
            makers.append(lambda *given, job=job, own=own: job["steps"](*given, *own))
        greet([PEERS[name]() for name in peers])
        body(*groups, makers)

    return pl.pallas_call(
        kernel,
        out_shape=[shape for shape, _ in outs],
        in_specs=[spec for _, spec in ins],
        out_specs=[spec for _, spec in outs],
        scratch_shapes=scratch + [one for job in jobs for one in job["scratch"]],
        compiler_params=params(collective_id, mib),
    )(*[array for array, _ in ins])


def finish(*runs):
    for run in runs:
        for _ in run:
            pass


def step(*runs):
    for run in runs:
        next(run, None)


def shaped(dtype, *shape):
    return jax.ShapeDtypeStruct(shape, dtype)


def small_gather():
    def steps(own, everyone, send, recv):
        dp, mp = lax.axis_index("dp"), lax.axis_index("mp")

        def move(k):
            return remote(own, everyone.at[dp], send.at[k], recv.at[dp], dp_peer(k))

        def start(k, carry):
            move(k).start()
            return carry

        lax.fori_loop(1, 32, start, 0)
        everyone[dp] = own[...]
        yield

        def end(k, carry):
            source = lax.rem(dp + k, 32)
            move(k).wait_send()
            remote(own, everyone.at[source], send.at[k], recv.at[source], dp_peer(k)).wait_recv()
            return carry

        lax.fori_loop(1, 32, end, 0)

    return {"scratch": [sems(32), sems(32)], "steps": steps}


def small_reduce():
    def steps(rows, out, arrived, summed, more, send, recv, send_two, recv_two):
        dp = lax.axis_index("dp")

        def move(k):
            tile = lax.div(lax.rem(dp + k, 32), 2)
            src = rows.at[:, pl.ds(pl.multiple_of(tile * 128, 128), 128)]
            return remote(src, arrived.at[k], send.at[k], recv.at[k], dp_peer(k))

        def start(k, carry):
            move(k).start()
            return carry

        def add(k, total):
            move(k).wait()
            return total + arrived[k]

        lax.fori_loop(1, 32, start, 0)
        yield
        mine = rows[:, pl.ds(pl.multiple_of(lax.div(dp, 2) * 128, 128), 128)]
        summed[...] = lax.fori_loop(1, 32, add, mine)
        copies = [
            remote(summed, more.at[k - 1], send_two.at[k], recv_two.at[k], mp_peer(k))
            for k in (1, 2, 3)
        ]
        for copy in copies:
            copy.start()
        yield
        for copy in copies:
            copy.wait()
        out[...] = summed[...] + more[0] + more[1] + more[2]

    return {
        "scratch": [
            pltpu.VMEM((32, 8, 128), f32),
            pltpu.VMEM((8, 128), f32),
            pltpu.VMEM((3, 8, 128), f32),
            sems(32),
            sems(32),
            sems(4),
            sems(4),
        ],
        "steps": steps,
    }


def row_exchange(count=1):
    def steps(halves, full, local_sem, send, recv):
        ylo, x, z, yhi, core = place()
        up, down, other = y_peer(1), y_peer(3), core_partner()
        first = []
        for n in range(count):
            for u, peer in ((0, up), (1, down)):
                here = full.at[n, ylo, core, u]
                first.append(remote(halves.at[n, u], here, send.at[n, u], recv.at[n, u], peer))
        for n in range(count):
            here = full.at[n, ylo, core]
            first.append(remote(halves.at[n], here, send.at[n, 2], recv.at[n, 2], other))
        for copy in first:
            copy.start()
        local = [
            pltpu.make_async_copy(halves.at[n], full.at[n, ylo, core], local_sem.at[n])
            for n in range(count)
        ]
        for copy in local:
            copy.start()
        yield
        second = []
        for n in range(count):
            for u in range(2):
                here = full.at[n, 1 - ylo, core, u]
                remote(halves.at[n, u], here, send.at[n, u], recv.at[n, u], up).wait_recv()
                copy = remote(here, here, send.at[n, 3 + u], recv.at[n, 3 + u], other)
                copy.start()
                second.append(copy)
        yield
        for n in range(count):
            here = full.at[n, ylo, 1 - core]
            remote(halves.at[n], here, send.at[n, 2], recv.at[n, 2], other).wait_recv()
            for u in range(2):
                here = full.at[n, 1 - ylo, 1 - core, u]
                remote(here, here, send.at[n, 3 + u], recv.at[n, 3 + u], other).wait_recv()
        for copy in first + second:
            copy.wait_send()
        for copy in local:
            copy.wait()

    return {
        "scratch": [sems(count), sems(count, 5), sems(count, 5)],
        "steps": steps,
    }


def share_gather():
    def steps(share, full, local_sem, send, recv):
        ylo, x, z, yhi, core = place()
        y = yhi * 2 + ylo
        other = core_partner()
        half = SHARE // 2
        sent = []

        def of(step, half_core):
            source = ring(y, step)
            return full.at[lax.rem(source, 2), half_core, lax.div(source, 2)]

        def go(src, dst, n, peer):
            copy = remote(src, dst, send.at[n], recv.at[n], peer)
            copy.start()
            sent.append(copy)

        def came(dst, n):
            remote(dst, dst, send.at[n], recv.at[n], other).wait_recv()

        local = pltpu.make_async_copy(share, of(0, core), local_sem)
        go(share, of(0, core), 0, y_peer(1))
        go(share, of(0, core), 1, y_peer(3))
        go(share, of(0, core), 2, other)
        local.start()
        yield
        for n, step_back, rows, onward in ((0, 3, pl.ds(0, half), 1), (1, 1, pl.ds(half, half), 3)):
            here = of(step_back, core)
            came(here, n)
            go(here.at[rows], here.at[rows], 3 + n, y_peer(onward))
            go(here, here, 5 + n, other)
        yield
        far = of(2, core)
        came(far.at[pl.ds(0, half)], 3)
        came(far.at[pl.ds(half, half)], 4)
        go(far, far, 7, other)
        yield
        came(of(0, 1 - core), 2)
        came(of(3, 1 - core), 5)
        came(of(1, 1 - core), 6)
        came(of(2, 1 - core), 7)
        for copy in sent:
            copy.wait_send()
        local.wait()

    return {"scratch": [pltpu.SemaphoreType.DMA, sems(8), sems(8)], "steps": steps}


def add_rows(count, one):
    def body(i, carry):
        one(pl.ds(pl.multiple_of(i * 16, 16), 16))
        return carry

    lax.fori_loop(0, count // 16, body, 0)


def share_sum():
    def steps(partial, out, from_core, via, arrived, send, recv, send_two, recv_two):
        ylo, x, z, yhi, core = place()
        y = yhi * 2 + ylo
        other = core_partner()
        half = SHARE // 2

        def block(k, half_core):
            target = ring(y, k)
            return partial.at[lax.rem(target, 2), half_core, lax.div(target, 2)]

        first, second = {}, {}

        def to_core(order):
            for k in order:
                first[k] = remote(block(k, 1 - core), from_core.at[k], send.at[k], recv.at[k], other)
                first[k].start()

        to_core((2, 0))
        yield
        first[2].wait_recv()
        far = block(2, core)

        def add_far(rows):
            far[rows] = (far[rows].astype(f32) + from_core[2, rows].astype(f32)).astype(bf16)

        add_rows(SHARE, add_far)
        for n, k in ((0, 1), (1, 3)):
            second[n] = remote(
                far.at[pl.ds(half * n, half)], via.at[n], send_two.at[n], recv_two.at[n], y_peer(k)
            )
            second[n].start()
        yield
        to_core((1, 3))
        yield
        for n, k in ((0, 1), (1, 3)):
            first[k].wait_recv()
            second[n].wait_recv()
            near = block(k, core)

            def add_via(i, carry):
                at = pl.multiple_of(i * 16, 16)
                rows, with_via = pl.ds(at, 16), pl.ds(pl.multiple_of(half * n + at, 16), 16)
                value = near[with_via].astype(f32) + from_core[k, with_via].astype(f32)
                near[with_via] = (value + via[n, rows].astype(f32)).astype(bf16)
                plain = pl.ds(pl.multiple_of(half * (1 - n) + at, 16), 16)
                value = near[plain].astype(f32) + from_core[k, plain].astype(f32)
                near[plain] = value.astype(bf16)
                return carry

            lax.fori_loop(0, half // 16, add_via, 0)
            second[2 + n] = remote(near, arrived.at[n], send_two.at[2 + n], recv_two.at[2 + n], y_peer(k))
            second[2 + n].start()
        yield
        first[0].wait_recv()
        second[2].wait_recv()
        second[3].wait_recv()
        mine_own = block(0, core)

        def total(rows):
            value = mine_own[rows].astype(f32) + from_core[0, rows].astype(f32)
            out[rows] = value + arrived[0, rows].astype(f32) + arrived[1, rows].astype(f32)

        add_rows(SHARE, total)
        for k in range(4):
            first[k].wait_send()
            second[k].wait_send()

    return {
        "scratch": [
            pltpu.VMEM((4, SHARE, WIDTH), bf16),
            pltpu.VMEM((2, SHARE // 2, WIDTH), bf16),
            pltpu.VMEM((2, SHARE, WIDTH), bf16),
        ]
        + [sems(4)] * 4,
        "steps": steps,
    }


def feature_start(ylo, yhi, core):
    return pl.multiple_of((yhi * 2 + core) * 512 + ylo * 256, 256)


def heads_to_tokens():
    def steps(heads, tokens, send, recv):
        ylo, x, z, yhi, core = place()
        y = yhi * 2 + ylo
        mine = tokens.at[:, pl.ds(feature_start(ylo, yhi, core), 256)]
        sent = []

        def go(k, flip):
            target = ring(y, k)
            half = 1 - core if flip else core
            peer = diagonal_peer(k) if flip else y_peer(k)
            src = heads.at[lax.rem(target, 2), half, lax.div(target, 2)]
            copy = remote(src, mine, send.at[2 * k + flip], recv.at[2 * k + flip], peer)
            copy.start()
            sent.append(copy)

        for k in (1, 3):
            for flip in (0, 1):
                go(k, flip)
        yield
        for k, flip in ((2, 0), (2, 1), (0, 1)):
            go(k, flip)
        tokens[:, pl.ds(feature_start(ylo, yhi, core), 256)] = heads[ylo, core, yhi]
        yield
        for k, flip in ((1, 0), (1, 1), (3, 0), (3, 1), (2, 0), (2, 1), (0, 1)):
            source = ring(y, -k)
            half = 1 - core if flip else core
            start = feature_start(lax.rem(source, 2), lax.div(source, 2), half)
            here = tokens.at[:, pl.ds(start, 256)]
            remote(heads.at[0, 0, 0], here, send.at[2 * k + flip], recv.at[2 * k + flip], y_peer(1)).wait_recv()
        for copy in sent:
            copy.wait_send()

    return {"scratch": [sems(8), sems(8)], "steps": steps}


def tokens_to_heads():
    def steps(tokens, heads, send, recv):
        ylo, x, z, yhi, core = place()
        y = yhi * 2 + ylo
        mine = heads.at[ylo, core, yhi]
        sent = []
        order = ((1, 0), (1, 1), (3, 0), (3, 1), (2, 0), (2, 1), (0, 1))
        for k, flip in order:
            target = ring(y, k)
            half = 1 - core if flip else core
            peer = diagonal_peer(k) if flip else y_peer(k)
            start = feature_start(lax.rem(target, 2), lax.div(target, 2), half)
            src = tokens.at[:, pl.ds(start, 256)]
            copy = remote(src, mine, send.at[2 * k + flip], recv.at[2 * k + flip], peer)
            copy.start()
            sent.append(copy)
        heads[ylo, core, yhi] = tokens[:, pl.ds(feature_start(ylo, yhi, core), 256)]
        yield
        for k, flip in order:
            source = ring(y, -k)
            half = 1 - core if flip else core
            here = heads.at[lax.rem(source, 2), half, lax.div(source, 2)]
            remote(here, here, send.at[2 * k + flip], recv.at[2 * k + flip], y_peer(1)).wait_recv()
        for copy in sent:
            copy.wait_send()

    return {"scratch": [sems(8), sems(8)], "steps": steps}


def row_gather():
    def steps(share, full, local_sem, send, recv):
        ylo, x, z, yhi, core = place()
        across, other = y_peer(2), core_partner()
        mine = full.at[:, core, yhi]
        far = full.at[:, core, 1 - yhi]
        local = pltpu.make_async_copy(share, mine, local_sem)
        one = remote(share, mine, send.at[0], recv.at[0], across)
        two = remote(share, mine, send.at[1], recv.at[1], other)
        one.start()
        two.start()
        local.start()
        yield
        remote(share, far, send.at[0], recv.at[0], across).wait_recv()
        three = remote(far, far, send.at[2], recv.at[2], other)
        three.start()
        yield
        remote(share, full.at[:, 1 - core, yhi], send.at[1], recv.at[1], other).wait_recv()
        last = full.at[:, 1 - core, 1 - yhi]
        remote(last, last, send.at[2], recv.at[2], other).wait_recv()
        for copy in (one, two, three):
            copy.wait_send()
        local.wait()

    return {
        "scratch": [pltpu.SemaphoreType.DMA, sems(3), sems(3)],
        "steps": steps,
    }


SIGNS = (1, -1)
XZ = ["x+", "x-", "z+", "z-"]


def xz_near():
    return [[xz_neighbour(axis, d) for d in SIGNS] for axis in (0, 1)]


def weight_gather(columns, spread=False, flat=False):
    count = 4 if spread else 2

    def steps(own, full, local_sem, swap_send, swap_recv, send, recv):
        ylo, x, z, yhi, core = place()
        y = yhi * 2 + ylo
        near = xz_near()
        offsets = (0, -1, 1, 2)

        def move(src, dst, s, r, stage, d, axis):
            n = ((s * 2 + r) * 8 + stage) * 2 + d
            return remote(src, dst, send.at[n], recv.at[n], near[axis][d])

        def origin(s):
            if spread:
                return ring(y, offsets[s])
            return ylo if s == 0 else 1 - ylo

        def block(s, r, one, two, rows):
            if r == 0:
                return full.at[origin(s), ring(x, one), ring(z, two), rows]
            return full.at[origin(s), ring(x, two), ring(z, one), rows]

        def rows_of(r, d=None):
            return pl.ds(32 * r, 32) if d is None else pl.ds(32 * r + 16 * d, 16)

        def half(n):
            if flat:
                return own.at[:, pl.ds(pl.multiple_of(n * columns, columns), columns)]
            return own.at[n]

        mine = own if spread else half(ylo)
        here = full.at[origin(0), x, z]
        local = pltpu.make_async_copy(mine, here, local_sem)
        swaps = []
        for s in range(1, count):
            peer = y_peer((4 - offsets[s]) % 4) if spread else lo_partner()
            src = own if spread else half(1 - ylo)
            swaps.append(remote(src, here, swap_send.at[s], swap_recv.at[s], peer))
        for swap in swaps:
            swap.start()
        sent = []

        def go(*args):
            copy = move(*args)
            copy.start()
            sent.append(copy)

        def begin(s, source):
            for r in range(2):
                for d in range(2):
                    src = source.at[rows_of(r)]
                    go(src, block(s, r, 0, 0, rows_of(r)), s, r, 0, d, r)
            for r in range(2):
                for d in range(2):
                    src = source.at[rows_of(r)]
                    go(src, block(s, r, 0, 0, rows_of(r)), s, r, 2, d, 1 - r)

        begin(0, mine)
        local.start()
        yield
        for s in range(1, count):
            came = full.at[origin(s), x, z]
            remote(came, came, swap_send.at[s], swap_recv.at[s], lo_partner()).wait_recv()
            begin(s, came)
        yield
        for s in range(count):
            for r in range(2):
                for d in range(2):
                    came = block(s, r, -SIGNS[d], 0, rows_of(r))
                    move(came, came, s, r, 0, d, r).wait_recv()
                    piece = block(s, r, -SIGNS[d], 0, rows_of(r, d))
                    go(piece, piece, s, r, 1, d, r)
                for part in (1, 2):
                    for d in range(2):
                        came = block(s, r, offsets[part], 0, rows_of(r))
                        go(came, came, s, r, 2 + part, d, 1 - r)
            if s % 2:
                yield
        for s in range(count):
            for r in range(2):
                for d in range(2):
                    piece = block(s, r, 2, 0, rows_of(r, d))
                    move(piece, piece, s, r, 1, d, r).wait_recv()
                for d in range(2):
                    came = block(s, r, 2, 0, rows_of(r))
                    go(came, came, s, r, 5, d, 1 - r)
            if s % 2:
                yield
        for part in (0, 2, 1, 3):
            d = part // 2
            for s in range(count):
                for r in range(2):
                    came = block(s, r, offsets[part], -SIGNS[d], rows_of(r))
                    move(came, came, s, r, 2 + part, d, 1 - r).wait_recv()
                    go(came, came, s, r, 6 + part % 2, d, 1 - r)
            yield
        for s in range(count):
            for r in range(2):
                for part in range(4):
                    d = 1 - part // 2
                    came = block(s, r, offsets[part], -SIGNS[d], rows_of(r))
                    move(came, came, s, r, 2 + part, d, 1 - r).wait_recv()
                for part in range(4):
                    d = part // 2
                    came = block(s, r, offsets[part], 2, rows_of(r))
                    move(came, came, s, r, 6 + part % 2, d, 1 - r).wait_recv()
        for copy in sent + swaps:
            copy.wait_send()
        local.wait()

    return {
        "scratch": [pltpu.SemaphoreType.DMA, sems(count), sems(count), sems(32 * count), sems(32 * count)],
        "steps": steps,
    }


def gathered(columns, count=2):
    return (shaped(bf16, count, 4, 4, 64, columns), ANY)


def weight_sum(columns=PART):
    def steps(grads, out, wide, thin, total, swap_send, swap_recv, send, recv):
        ylo, x, z, yhi, core = place()
        near = xz_near()
        partner = lo_partner()

        def move(src, dst, s, r, stage, d, axis):
            n = ((s * 2 + r) * 6 + stage) * 2 + d
            return remote(src, dst, send.at[n], recv.at[n], near[axis][d])

        def line(s, r, step, part):
            if r == 0:
                return grads.at[s, part, ring(z, step), pl.ds(0, 32)]
            return grads.at[s, ring(x, step), part, pl.ds(32, 32)]

        def block(s, r, step, rows):
            if r == 0:
                return grads.at[s, ring(x, step), z, rows]
            return grads.at[s, x, ring(z, step), rows]

        def wide_move(s, r, d, kind):
            if kind == 0:
                src = line(s, r, 2, pl.ds(2 * d, 2))
            elif kind == 1:
                src = line(s, r, SIGNS[d], pl.ds(2 - 2 * d, 2))
            else:
                src = line(s, r, SIGNS[d], pl.ds(2 * d, 2))
            return move(src, wide.at[s, r, kind, d], s, r, kind, d, 1 - r)

        def thin_move(s, r, d, kind):
            if kind == 0:
                src = block(s, r, 2, pl.ds(32 * r + 16 * d, 16))
            elif kind == 1:
                src = block(s, r, SIGNS[d], pl.ds(32 * r + 16 - 16 * d, 16))
            else:
                src = block(s, r, SIGNS[d], pl.ds(32 * r + 16 * d, 16))
            return move(src, thin.at[s, r, kind, d], s, r, 3 + kind, d, r)

        for s in range(2):
            for kind in range(2):
                for r in range(2):
                    for d in range(2):
                        wide_move(s, r, d, kind).start()
        yield

        for s in range(2):
            for r in range(2):
                for d in range(2):
                    wide_move(s, r, d, 0).wait_recv()
                    for p in range(2):
                        mine = line(s, r, SIGNS[d], 2 * d + p)

                        def one(rows):
                            value = mine[rows].astype(f32) + wide[s, r, 0, d, p, rows].astype(f32)
                            mine[rows] = value.astype(bf16)

                        add_rows(32, one)
                    wide_move(s, r, d, 2).start()
            yield

        for s in range(2):
            for r in range(2):
                for d in range(2):
                    wide_move(s, r, d, 1).wait_recv()
                    wide_move(s, r, d, 2).wait_recv()
                for p in range(4):
                    mine = line(s, r, 0, p)
                    d = p // 2

                    def one(rows):
                        value = mine[rows].astype(f32) + wide[s, r, 2, d, p % 2, rows].astype(f32)
                        value += wide[s, r, 1, 1 - d, p % 2, rows].astype(f32)
                        mine[rows] = value.astype(bf16)

                    add_rows(32, one)
                for kind in range(2):
                    for d in range(2):
                        thin_move(s, r, d, kind).start()
            yield

        for s in range(2):
            for r in range(2):
                for d in range(2):
                    thin_move(s, r, d, 0).wait_recv()
                    mine = block(s, r, SIGNS[d], pl.ds(32 * r + 16 * d, 16))
                    value = mine[...].astype(f32) + thin[s, r, 0, d].astype(f32)
                    mine[...] = value.astype(bf16)
                    thin_move(s, r, d, 2).start()
        yield

        for s in range(2):
            for r in range(2):
                for d in range(2):
                    thin_move(s, r, d, 1).wait_recv()
                    thin_move(s, r, d, 2).wait_recv()
                for d in range(2):
                    rows = pl.ds(32 * r + 16 * d, 16)
                    value = block(s, r, 0, rows)[...].astype(f32) + thin[s, r, 2, d].astype(f32)
                    value += thin[s, r, 1, 1 - d].astype(f32)
                    total[s, rows] = value.astype(bf16)
        swap = remote(total.at[1 - ylo], out.at[ylo], swap_send, swap_recv, partner)
        swap.start()
        out[ylo] = total[ylo]
        yield
        for s in range(2):
            for r in range(2):
                for d in range(2):
                    for kind in range(3):
                        wide_move(s, r, d, kind).wait_send()
                        thin_move(s, r, d, kind).wait_send()
        remote(total.at[0], out.at[1 - ylo], swap_send, swap_recv, partner).wait_recv()
        swap.wait_send()

    return {
        "scratch": [
            pltpu.VMEM((2, 2, 3, 2, 2, 32, columns), bf16),
            pltpu.VMEM((2, 2, 3, 2, 16, columns), bf16),
            pltpu.VMEM((2, 64, columns), bf16),
            pltpu.SemaphoreType.DMA,
            pltpu.SemaphoreType.DMA,
            sems(48),
            sems(48),
        ],
        "steps": steps,
    }


def standardize(value):
    mean = jnp.mean(value, axis=-1, keepdims=True)
    centered = value - mean
    scale_inv = lax.rsqrt(jnp.mean(centered * centered, axis=-1, keepdims=True) + epsilon)
    return (centered * scale_inv, scale_inv)


def norm_back(grad_normed_out, normed, scale_inv, gain):
    scaled = grad_normed_out * gain
    mean_one = jnp.mean(scaled, axis=-1, keepdims=True)
    mean_two = jnp.mean(scaled * normed, axis=-1, keepdims=True)
    grad_value = scale_inv * (scaled - mean_one - normed * mean_two)
    grad_gain = jnp.sum(grad_normed_out * normed, axis=0, keepdims=True)
    grad_shift = jnp.sum(grad_normed_out, axis=0, keepdims=True)
    return (grad_value, grad_gain, grad_shift)


def dot(a, b):
    return jnp.dot(a, b, preferred_element_type=f32)


def turned_dot(a, b):
    return lax.dot_general(a, b, (((1,), (1,)), ((), ())), preferred_element_type=f32)


def outer_dot(a, b):
    return lax.dot_general(a, b, (((0,), (0,)), ((), ())), preferred_element_type=f32)


def some_rows(count, size, one):
    def body(i, carry):
        one(pl.ds(pl.multiple_of(i * size, size), size))
        return carry

    lax.fori_loop(0, count // size, body, 0)


def fetched(src, dst, sem):
    copy = pltpu.make_async_copy(src, dst, sem)
    copy.start()
    return copy


CODES = 4096
CODE_CHUNK = 1024


def forward_body(ins, outs, scratch, makers):
    ids, segments, padding, stream_hbm, cot_hbm, codebook, own_qkv, own_out, own_up, own_down, norms = ins
    (
        attn_out,
        qkv_out,
        out_weight_out,
        cot_full,
        inputs_share,
        gains,
        mask,
        projected,
        attended,
        middle,
        ffn_full,
        up_full,
        down_full,
    ) = outs
    (
        everyone,
        norm_tile,
        other_segments,
        other_padding,
        chunk,
        total,
        stream,
        cot_half,
        halves,
        attn_in,
        weight,
        out_weight,
        tokens,
        ffn_share,
        load_sem,
        swap_send,
        swap_recv,
    ) = scratch
    make_small, make_qkv, make_out, make_up, make_down, make_cot, make_attn, make_heads, make_share = makers
    ylo, x, z, yhi, core = place()
    small = make_small(norm_tile, everyone)
    qkv = make_qkv(own_qkv, weight)
    out = make_out(own_out, out_weight.at[core])
    up, down = make_up(own_up, up_full), make_down(own_down, down_full)
    cot_move = make_cot(cot_half, cot_full)
    attn_move = make_attn(halves, attn_in)
    heads = make_heads(attended, tokens)
    spread = make_share(ffn_share, ffn_full)

    def fetch(j):
        rows = pl.ds(j * CODE_CHUNK, CODE_CHUNK)
        return pltpu.make_async_copy(codebook.at[rows], chunk.at[j % 2], load_sem.at[j % 2])

    mine = pl.ds(pl.multiple_of(core * 256, 256), 256)
    loads = [fetched(stream_hbm.at[mine], stream, load_sem.at[2])]
    for u in range(2):
        rows = pl.ds(pl.multiple_of(core * 256 + u * SHARE, SHARE), SHARE)
        loads.append(fetched(cot_hbm.at[rows], cot_half.at[0, u], load_sem.at[3 + u]))
    fetch(0).start()
    lane = lax.broadcasted_iota(jnp.int32, (8, 128), 1)
    norm_tile[...] = jnp.where(lax.div(lane, 64) == lax.rem(z, 2), norms[...].astype(f32), 0.0)
    step(small, qkv, out)
    row_swaps = [
        remote(segments, other_segments, swap_send.at[0], swap_recv.at[0], lo_partner()),
        remote(padding, other_padding, swap_send.at[1], swap_recv.at[1], lo_partner()),
    ]
    for swap in row_swaps:
        swap.start()
    for load in loads:
        load.wait()
    step(cot_move)
    total[...] = stream[...].astype(f32)
    my_ids = ids[:, mine]
    count = CODES // CODE_CHUNK
    for j in range(count):
        if j + 1 < count:
            fetch(j + 1).start()
        fetch(j).wait()
        code = lax.broadcasted_iota(jnp.int32, (CODE_CHUNK, 256), 0) + j * CODE_CHUNK
        pick = jnp.where(my_ids == code, 1.0, 0.0).astype(bf16)
        for part in range(2):
            columns = pl.ds(part * 1024, 1024)
            total[:, columns] += outer_dot(pick, chunk[j % 2, :, columns])
        step((qkv, out, qkv, out)[j])
    step(small)
    for t in range(16):
        pair = everyone[2 * t, pl.ds(0, 8)] + everyone[2 * t + 1, pl.ds(0, 8)]
        gains[:, pl.ds(128 * t, 128)] = pair
    gain, shift = gains[pl.ds(0, 1)], gains[pl.ds(1, 1)]
    for u in range(2):

        def norm(rows):
            value = total[pl.ds(pl.multiple_of(u * SHARE + rows.start, 32), 32)]
            normed, _ = standardize(value)
            halves[0, u, rows] = (normed * gain + shift).astype(bf16)

        some_rows(SHARE, 32, norm)
    step(attn_move, qkv, out)

    def keep(rows):
        inputs_share[rows] = total[pl.ds(pl.multiple_of(yhi * SHARE + rows.start, 32), 32)]

    some_rows(SHARE, 32, keep)
    step(qkv, qkv)

    def see(r, segment_row, padding_row):
        turned = jnp.broadcast_to(segment_row.astype(f32), (SHARE, 512)).T[:, 0:1]
        query = lax.broadcasted_iota(jnp.int32, (512, 512), 0)
        key = lax.broadcasted_iota(jnp.int32, (512, 512), 1)
        same = turned == segment_row.astype(f32)
        live = (padding_row == 1) | (query == key)
        mask[r] = jnp.where(same & live & (key <= query), 1.0, 0.0).astype(bf16)

    for swap in row_swaps:
        swap.wait()
    see(ylo, segments[...], padding[...])
    see(1 - ylo, other_segments[...], other_padding[...])
    step(qkv, cot_move, qkv, out, out)
    step(attn_move)
    finish(qkv)
    step(out, out, up)
    finish(cot_move, attn_move)
    writes = [
        fetched(attn_in, attn_out, load_sem.at[0]),
        fetched(weight, qkv_out, load_sem.at[1]),
    ]

    def project(r):
        rows = attn_in[0, r].reshape(512, WIDTH)
        for t in range(3):
            columns = pl.ds(t * 256, 256)
            part = weight[:, :, :, :, columns].reshape(WIDTH, 256)
            projected[r, :, columns] = dot(rows, part).astype(bf16)

    def attend(r):
        for h in range(2):
            key = projected[r, :, pl.ds(256 + h * HEAD, HEAD)]
            value = projected[r, :, pl.ds(512 + h * HEAD, HEAD)]
            for c in range(2):
                rows = pl.ds(c * 256, 256)
                query = projected[r, rows, pl.ds(h * HEAD, HEAD)]
                scores = turned_dot(query, key) * HEAD ** (-0.5)
                scores = jnp.where(mask[r, rows].astype(f32) > 0.5, scores, masked_score)
                expd = jnp.exp(scores - jnp.max(scores, axis=-1, keepdims=True))
                probs = expd / jnp.sum(expd, axis=-1, keepdims=True)
                result = dot(probs.astype(bf16), value).astype(bf16)
                for u in range(2):
                    attended[r, c, u, :, pl.ds(h * HEAD, HEAD)] = result[u * SHARE : (u + 1) * SHARE]

    project(1 - ylo)
    step(out, down)
    attend(1 - ylo)
    step(heads)
    step(out, up)
    project(ylo)
    finish(out)
    swap = remote(
        out_weight.at[core], out_weight.at[core], swap_send.at[2], swap_recv.at[2], core_partner()
    )
    swap.start()
    step(down)
    attend(ylo)
    step(heads)
    step(up, down)
    finish(heads)
    there = out_weight.at[1 - core]
    remote(there, there, swap_send.at[2], swap_recv.at[2], core_partner()).wait_recv()
    writes.append(fetched(out_weight, out_weight_out, load_sem.at[2]))

    def branch(n, carry):
        columns = pl.ds(pl.multiple_of(n * 256, 256), 256)
        value = inputs_share[:, columns]
        for c in range(2):
            for h in range(2):
                features = pl.ds((h * 2 + c) * 512, 512)
                part = out_weight[c, h * 2 + lax.div(n, 4), lax.rem(n, 4)].reshape(256, 512)
                value += turned_dot(tokens[:, features], part)
        middle[:, columns] = value
        return carry

    lax.fori_loop(0, WIDTH // 256, branch, 0)
    gain_two, shift_two = gains[pl.ds(2, 1)], gains[pl.ds(3, 1)]

    def norm_two(rows):
        normed, _ = standardize(middle[rows])
        ffn_share[rows] = (normed * gain_two + shift_two).astype(bf16)

    some_rows(SHARE, 32, norm_two)
    step(spread)
    step(up, down)
    step(up, down)
    step(up, down)
    step(spread)
    step(up, down)
    step(spread)
    step(up, down)
    finish(spread, up, down)
    for write in writes:
        write.wait()
    swap.wait_send()


def forward(ids, segments, padding, stream, cot, codebook, own_qkv, own_out, own_up, own_down, norms):
    tokens_full = (shaped(bf16, 1, 2, 2, 2, SHARE, WIDTH), ANY)
    return kernel_call(
        forward_body,
        [
            small_gather(),
            weight_gather(768),
            weight_gather(512, spread=True),
            weight_gather(PART, flat=True),
            weight_gather(PART, flat=True),
            row_exchange(),
            row_exchange(),
            heads_to_tokens(),
            share_gather(),
        ],
        DP + GROUP,
        [
            (ids, VMEM),
            (segments, VMEM),
            (padding, VMEM),
            (stream, ANY),
            (cot, ANY),
            (codebook, ANY),
            (own_qkv, VMEM),
            (own_out, VMEM),
            (own_up, VMEM),
            (own_down, VMEM),
            (norms, VMEM),
        ],
        [
            tokens_full,
            gathered(768),
            (shaped(bf16, 2, 4, 4, 4, 64, 512), ANY),
            tokens_full,
            (shaped(f32, SHARE, WIDTH), VMEM),
            (shaped(f32, 8, WIDTH), VMEM),
            (shaped(bf16, 2, 512, 512), VMEM),
            (shaped(bf16, 2, 512, 768), VMEM),
            (shaped(bf16, 2, 2, 2, SHARE, 256), VMEM),
            (shaped(f32, SHARE, WIDTH), VMEM),
            (shaped(bf16, 2, 2, 2, SHARE, WIDTH), ANY),
            gathered(PART),
            gathered(PART),
        ],
        [
            pltpu.VMEM((32, 8, 128), f32),
            pltpu.VMEM((8, 128), f32),
            pltpu.VMEM((1, 512), jnp.int32),
            pltpu.VMEM((1, 512), jnp.int32),
            pltpu.VMEM((2, CODE_CHUNK, WIDTH), bf16),
            pltpu.VMEM((256, WIDTH), f32),
            pltpu.VMEM((256, WIDTH), bf16),
            pltpu.VMEM((1, 2, SHARE, WIDTH), bf16),
            pltpu.VMEM((1, 2, SHARE, WIDTH), bf16),
            pltpu.VMEM((1, 2, 2, 2, SHARE, WIDTH), bf16),
            pltpu.VMEM((2, 4, 4, 64, 768), bf16),
            pltpu.VMEM((2, 4, 4, 4, 64, 512), bf16),
            pltpu.VMEM((SHARE, WIDTH), bf16),
            pltpu.VMEM((SHARE, WIDTH), bf16),
            sems(5),
            sems(3),
            sems(3),
        ],
        0,
    )


SLOPE = 0.7978845608028654
CUBIC = 0.044715


def ffn_body(ins, outs, scratch, makers):
    ffn_hbm, cot_hbm, up_hbm, down_hbm, middle, gains = ins
    sum_down, grad_down_rest, grad_up_weight, layer_out, grad_middle, small = outs
    (
        ffn_in,
        cot,
        up_weight,
        down_weight,
        hidden,
        grad_up,
        back,
        ahead,
        grad_down_weight,
        back_share,
        ahead_share,
        load_sem,
    ) = scratch
    make_back, make_ahead, make_down = makers
    ylo, x, z, yhi, core = place()
    back_sum = make_back(back, back_share)
    ahead_sum = make_ahead(ahead, ahead_share)
    down_sum = make_down(grad_down_weight, sum_down)
    own, partner = (pl.ds(pl.multiple_of(r * 512, 512), 512) for r in (ylo, 1 - ylo))
    loads = [
        fetched(ffn_hbm.at[own], ffn_in.at[own], load_sem.at[0]),
        fetched(up_hbm, up_weight, load_sem.at[1]),
        fetched(cot_hbm.at[own], cot.at[own], load_sem.at[2]),
        fetched(down_hbm, down_weight, load_sem.at[3]),
        fetched(ffn_hbm.at[partner], ffn_in.at[partner], load_sem.at[4]),
        fetched(cot_hbm.at[partner], cot.at[partner], load_sem.at[5]),
    ]

    def units(rows):
        def one(n, carry):
            columns = pl.ds(pl.multiple_of(n * 512, 512), 512)
            value = dot(ffn_in[rows], up_weight[:, columns])
            grad = dot(cot[rows], down_weight[:, columns])
            square = value * value
            bend = jnp.tanh(SLOPE * value * (1.0 + CUBIC * square))
            half = 0.5 * (1.0 + bend)
            hidden[rows, columns] = (value * half).astype(bf16)
            slope = half + 0.5 * value * (1.0 - bend * bend) * SLOPE * (1.0 + 3.0 * CUBIC * square)
            grad_up[rows, columns] = (grad * slope).astype(bf16)
            return carry

        lax.fori_loop(0, PART // 512, one, 0)

    def spread_out(r, rows, source, weight, target):
        def one(n, carry):
            columns = pl.ds(pl.multiple_of(n * 512, 512), 512)
            value = turned_dot(source[rows], weight[columns]).astype(bf16)
            for c in range(2):
                for u in range(2):
                    at = (2 * c + u) * SHARE
                    target[r, c, u, :, columns] = value[at : at + SHARE]
            return carry

        lax.fori_loop(0, WIDTH // 512, one, 0)

    def weight_grad(left, right, target):
        def one(n, carry):
            columns = pl.ds(pl.multiple_of(n * 256, 256), 256)
            value = outer_dot(left[:, columns], right[...]).astype(bf16)
            for j in range(4):
                target[lax.div(n, 4), lax.rem(n, 4), j] = value[64 * j : 64 * j + 64]
            return carry

        lax.fori_loop(0, WIDTH // 256, one, 0)

    near, rest = pl.ds(0, 512), pl.ds(512, 512)
    for load in loads[:4]:
        load.wait()
    units(own)
    spread_out(ylo, own, grad_up, up_weight, back)
    step(back_sum)
    for load in loads[4:]:
        load.wait()
    units(partner)
    step(back_sum)
    weight_grad(cot, hidden.at[:, near], grad_down_weight)
    step(down_sum)
    spread_out(1 - ylo, partner, grad_up, up_weight, back)
    step(back_sum)
    spread_out(ylo, own, hidden, down_weight, ahead)
    step(back_sum)
    step(ahead_sum)
    step(down_sum)
    spread_out(1 - ylo, partner, hidden, down_weight, ahead)
    step(ahead_sum, ahead_sum)
    step(down_sum)
    weight_grad(cot, hidden.at[:, rest], grad_down_rest)
    step(down_sum)
    step(ahead_sum)
    weight_grad(ffn_in, grad_up, grad_up_weight)
    step(down_sum)
    finish(back_sum)
    gain = gains[pl.ds(2, 1)]
    small[...] = jnp.zeros_like(small)

    def back_norm(i, carry):
        at = pl.multiple_of(i * 32, 32)
        rows = pl.ds(at, 32)
        normed, inverse = standardize(middle[rows])
        value, grad_gain, grad_shift = norm_back(back_share[rows], normed, inverse, gain)
        here = pl.multiple_of(ylo * 512 + core * 256 + yhi * SHARE + at, 32)
        grad_middle[rows] = value + cot[pl.ds(here, 32)].astype(f32)
        small[pl.ds(2, 1)] += grad_gain
        small[pl.ds(3, 1)] += grad_shift
        return carry

    lax.fori_loop(0, SHARE // 32, back_norm, 0)
    step(down_sum, down_sum)
    finish(ahead_sum)

    def end(rows):
        layer_out[0, rows] = (middle[rows] + ahead_share[rows]).astype(bf16)

    some_rows(SHARE, 16, end)
    finish(down_sum)


def feed_forward(ffn_in, cot, up, down, middle, gains):
    return kernel_call(
        ffn_body,
        [share_sum(), share_sum(), weight_sum(512)],
        XZ + ["y1", "y2", "y3", "core"],
        [(ffn_in, ANY), (cot, ANY), (up, ANY), (down, ANY), (middle, VMEM), (gains, VMEM)],
        [
            (shaped(bf16, 2, 64, 512), VMEM),
            (shaped(bf16, 2, 4, 4, 64, 512), VMEM),
            (shaped(bf16, 2, 4, 4, 64, PART), VMEM),
            (shaped(bf16, 1, SHARE, WIDTH), VMEM),
            (shaped(f32, SHARE, WIDTH), VMEM),
            (shaped(f32, 8, WIDTH), VMEM),
        ],
        [
            pltpu.VMEM((1024, WIDTH), bf16),
            pltpu.VMEM((1024, WIDTH), bf16),
            pltpu.VMEM((WIDTH, PART), bf16),
            pltpu.VMEM((WIDTH, PART), bf16),
            pltpu.VMEM((1024, PART), bf16),
            pltpu.VMEM((1024, PART), bf16),
            pltpu.VMEM((2, 2, 2, SHARE, WIDTH), bf16),
            pltpu.VMEM((2, 2, 2, SHARE, WIDTH), bf16),
            pltpu.VMEM((2, 4, 4, 64, 512), bf16),
            pltpu.VMEM((SHARE, WIDTH), f32),
            pltpu.VMEM((SHARE, WIDTH), f32),
            sems(6),
        ],
        2,
        62,
    )


def back_body(ins, outs, scratch, makers):
    (
        attn_hbm,
        weight_hbm,
        out_hbm,
        down_hbm,
        up_hbm,
        projected,
        attended,
        mask,
        grad_middle,
        inputs_share,
        layer_out,
        small_in,
        gains,
    ) = ins
    layer_full, input_full, sum_down, sum_up, sum_qkv, sum_out, small_out, branch_full = outs
    (
        attn_in,
        weight,
        out_weight,
        grad_down_weight,
        grad_up_weight,
        grad_qkv_weight,
        grad_out_weight,
        grad_branch,
        branch_share,
        grad_tokens,
        grad_heads,
        grad_projected,
        back,
        back_share,
        input_share,
        small,
        load_sem,
    ) = scratch
    make_down, make_up, make_qkv, make_out, make_heads, make_branch, make_back, make_layer, make_input, make_small = makers
    ylo, x, z, yhi, core = place()
    down_sum = make_down(grad_down_weight, sum_down)
    up_sum = make_up(grad_up_weight, sum_up)
    qkv_sum = make_qkv(grad_qkv_weight, sum_qkv)
    out_sum = make_out(grad_out_weight, sum_out)
    heads = make_heads(grad_tokens, grad_heads)
    branch = make_branch(branch_share, branch_full)
    back_sum = make_back(back, back_share)
    layer_move = make_layer(layer_out, layer_full)
    input_move = make_input(input_share, input_full)
    small_sum = make_small(small, small_out)
    loads = [
        fetched(out_hbm, out_weight, load_sem.at[0]),
        fetched(down_hbm, grad_down_weight, load_sem.at[1]),
        fetched(up_hbm, grad_up_weight, load_sem.at[2]),
        fetched(weight_hbm, weight, load_sem.at[3]),
        fetched(attn_hbm, attn_in, load_sem.at[4]),
    ]

    def low(rows):
        branch_share[rows] = grad_middle[rows].astype(bf16)

    step(layer_move)
    some_rows(SHARE, 32, low)
    loads[0].wait()
    for h in range(2):
        for c in range(2):
            grad_tokens[:, pl.ds((h * 2 + c) * 512, 512)] = dot(
                branch_share[...], out_weight[c, h]
            ).astype(bf16)
    step(heads)
    step(branch)
    loads[1].wait()
    step(down_sum)
    loads[2].wait()
    step(up_sum)
    step(layer_move)
    finish(heads)

    def attend(r):
        for h in range(2):
            query = projected[r, :, pl.ds(h * HEAD, HEAD)]
            key = projected[r, :, pl.ds(256 + h * HEAD, HEAD)]
            value = projected[r, :, pl.ds(512 + h * HEAD, HEAD)]
            grad = grad_heads[r, :, :, :, pl.ds(h * HEAD, HEAD)].reshape(512, HEAD)
            scores = turned_dot(query, key) * HEAD ** (-0.5)
            scores = jnp.where(mask[r].astype(f32) > 0.5, scores, masked_score)
            expd = jnp.exp(scores - jnp.max(scores, axis=-1, keepdims=True))
            probs = expd / jnp.sum(expd, axis=-1, keepdims=True)
            grad_probs = turned_dot(grad, value)
            inner = jnp.sum(grad_probs * probs, axis=-1, keepdims=True)
            grad_scores = (probs * (grad_probs - inner)).astype(bf16)
            parts = (
                dot(grad_scores, key) * HEAD ** (-0.5),
                outer_dot(grad_scores, query) * HEAD ** (-0.5),
                outer_dot(probs.astype(bf16), grad),
            )
            for t in range(3):
                grad_projected[pl.ds(pl.multiple_of(r * 512, 512), 512), pl.ds(t * 256 + h * HEAD, HEAD)] = parts[
                    t
                ].astype(bf16)

    def spread_out(r):
        def one(n, carry):
            columns = pl.ds(pl.multiple_of(n * 512, 512), 512)
            rows = pl.ds(pl.multiple_of(r * 512, 512), 512)
            value = turned_dot(grad_projected[rows], weight[columns]).astype(bf16)
            for c in range(2):
                for u in range(2):
                    at = (2 * c + u) * SHARE
                    back[r, c, u, :, columns] = value[at : at + SHARE]
            return carry

        lax.fori_loop(0, WIDTH // 512, one, 0)

    def weight_grad(left, right, target):
        def one(n, carry):
            columns = pl.ds(pl.multiple_of(n * 256, 256), 256)
            value = outer_dot(left[..., columns].reshape(1024, 256), right).astype(bf16)
            for j in range(4):
                target[lax.div(n, 4), lax.rem(n, 4), j] = value[64 * j : 64 * j + 64]
            return carry

        lax.fori_loop(0, WIDTH // 256, one, 0)

    attend(ylo)
    step(down_sum)
    loads[3].wait()
    spread_out(ylo)
    step(back_sum)
    step(down_sum)
    attend(1 - ylo)
    step(back_sum)
    step(branch)
    spread_out(1 - ylo)
    step(back_sum)
    step(up_sum)
    loads[4].wait()
    weight_grad(attn_in, grad_projected[...], grad_qkv_weight)
    step(back_sum)
    step(qkv_sum)
    step(down_sum, down_sum, up_sum, down_sum, down_sum)
    finish(branch)
    gather_load = fetched(branch_full, grad_branch, load_sem.at[5])
    step(up_sum)
    gather_load.wait()
    weight_grad(grad_branch, attended[...].reshape(1024, 256), grad_out_weight)
    step(out_sum)
    step(up_sum)
    finish(back_sum)
    gain = gains[pl.ds(0, 1)]
    small[...] = small_in[...]

    def back_norm(i, carry):
        rows = pl.ds(pl.multiple_of(i * 32, 32), 32)
        normed, inverse = standardize(inputs_share[rows])
        value, grad_gain, grad_shift = norm_back(back_share[rows], normed, inverse, gain)
        input_share[0, rows] = (grad_middle[rows] + value).astype(bf16)
        small[pl.ds(0, 1)] += grad_gain
        small[pl.ds(1, 1)] += grad_shift
        return carry

    lax.fori_loop(0, SHARE // 32, back_norm, 0)
    step(input_move, small_sum)
    step(qkv_sum, qkv_sum, up_sum, out_sum, out_sum)
    step(small_sum)
    step(up_sum, qkv_sum, qkv_sum, out_sum, out_sum)
    step(input_move)
    step(qkv_sum, out_sum, qkv_sum, out_sum)
    finish(layer_move, input_move, small_sum, down_sum, up_sum, qkv_sum, out_sum)


def attention_back(
    attn_in,
    weight,
    out_weight,
    grad_down_weight,
    grad_up_weight,
    projected,
    attended,
    mask,
    grad_middle,
    inputs_share,
    layer_out,
    small,
    gains,
):
    return kernel_call(
        back_body,
        [
            weight_sum(512),
            weight_sum(),
            weight_sum(768),
            weight_sum(256),
            tokens_to_heads(),
            share_gather(),
            share_sum(),
            row_gather(),
            row_gather(),
            small_reduce(),
        ],
        DP + MP + GROUP,
        [
            (attn_in, ANY),
            (weight, ANY),
            (out_weight, ANY),
            (grad_down_weight, ANY),
            (grad_up_weight, ANY),
            (projected, VMEM),
            (attended, VMEM),
            (mask, VMEM),
            (grad_middle, VMEM),
            (inputs_share, VMEM),
            (layer_out, VMEM),
            (small, VMEM),
            (gains, VMEM),
        ],
        [
            (shaped(bf16, 1, 2, 2, SHARE, WIDTH), ANY),
            (shaped(bf16, 1, 2, 2, SHARE, WIDTH), ANY),
            (shaped(bf16, 2, 64, 512), VMEM),
            (shaped(bf16, 2, 64, PART), VMEM),
            (shaped(bf16, 2, 64, 768), VMEM),
            (shaped(bf16, 2, 64, 256), VMEM),
            (shaped(f32, 8, 128), VMEM),
            (shaped(bf16, 2, 2, 2, SHARE, WIDTH), ANY),
        ],
        [
            pltpu.VMEM((1024, WIDTH), bf16),
            pltpu.VMEM((WIDTH, 768), bf16),
            pltpu.VMEM((2, 2, WIDTH, 512), bf16),
            pltpu.VMEM((2, 4, 4, 64, 512), bf16),
            pltpu.VMEM((2, 4, 4, 64, PART), bf16),
            pltpu.VMEM((2, 4, 4, 64, 768), bf16),
            pltpu.VMEM((2, 4, 4, 64, 256), bf16),
            pltpu.VMEM((2, 2, 2, SHARE, WIDTH), bf16),
            pltpu.VMEM((SHARE, WIDTH), bf16),
            pltpu.VMEM((SHARE, WIDTH), bf16),
            pltpu.VMEM((2, 2, 2, SHARE, 256), bf16),
            pltpu.VMEM((1024, 768), bf16),
            pltpu.VMEM((2, 2, 2, SHARE, WIDTH), bf16),
            pltpu.VMEM((SHARE, WIDTH), f32),
            pltpu.VMEM((1, SHARE, WIDTH), bf16),
            pltpu.VMEM((8, WIDTH), f32),
            sems(6),
        ],
        3,
        62,
    )


def on_device(
    stream,
    code_ids,
    segment_ids,
    padding,
    codebook,
    norm1_gain,
    norm1_shift,
    w_qkv,
    w_out,
    norm2_gain,
    norm2_shift,
    w_up,
    w_down,
    cotangent,
):
    ylo, x, z, yhi, core = place()
    own_qkv = w_qkv.reshape(64, 3, 2, 256).transpose(2, 0, 1, 3).reshape(2, 64, 768)
    norms = jnp.stack([norm1_gain, norm1_shift, norm2_gain, norm2_shift] * 2)
    norms = jnp.concatenate([norms, norms], axis=1)
    (
        attn_in,
        qkv_full,
        out_full,
        cot,
        inputs_share,
        gains,
        allowed,
        projected,
        attended,
        middle,
        ffn_in,
        up_full,
        down_full,
    ) = forward(
        code_ids,
        segment_ids,
        padding,
        stream[0],
        cotangent[0],
        codebook,
        own_qkv,
        w_out,
        w_up,
        w_down,
        norms,
    )
    sum_down, grad_down_rest, grad_up_weight, layer_out, grad_middle, small = feed_forward(
        ffn_in.reshape(1024, WIDTH),
        cot.reshape(1024, WIDTH),
        up_full.reshape(WIDTH, PART),
        down_full.reshape(WIDTH, PART),
        middle,
        gains,
    )
    layer_out, input_grad, sum_down_rest, sum_up, sum_qkv, sum_out, small, _ = attention_back(
        attn_in.reshape(1024, WIDTH),
        qkv_full.reshape(WIDTH, 768),
        out_full.reshape(2, 2, WIDTH, 512),
        grad_down_rest,
        grad_up_weight,
        projected,
        attended,
        allowed,
        grad_middle,
        inputs_share,
        layer_out,
        small,
        gains,
    )

    sum_down = jnp.concatenate([sum_down, sum_down_rest], axis=2)
    sum_qkv, sum_out, sum_up, sum_down = (g.astype(f32) for g in (sum_qkv, sum_out, sum_up, sum_down))
    out_qkv = sum_qkv.reshape(2, 64, 3, 256).transpose(1, 2, 0, 3).reshape(64, 3, 512)
    out_out = sum_out.transpose(1, 0, 2).reshape(64, 512)
    out_up = sum_up.transpose(1, 0, 2).reshape(64, WIDTH)
    out_down = sum_down.transpose(1, 0, 2).reshape(64, WIDTH)
    odd = lax.rem(z, 2) == 1
    small = jnp.where(odd, small[:4, 64:], small[:4, :64])
    return (
        layer_out.reshape(1, 512, WIDTH).astype(f32),
        input_grad.reshape(1, 512, WIDTH).astype(f32),
        small[0],
        small[1],
        out_qkv,
        out_out,
        small[2],
        small[3],
        out_up,
        out_down,
    )


def solution(mesh):
    in_specs = (
        P("dp", None, None),
        P("dp", None),
        P("dp", None),
        P("dp", None),
        P(),
        P("dp"),
        P("dp"),
        P("dp", None, "mp"),
        P("dp", "mp"),
        P("dp"),
        P("dp"),
        P("dp", "mp"),
        P("dp", "mp"),
        P("dp", None, None),
    )
    out_specs = (
        P("dp", None, None),
        P("dp", None, None),
        P("dp"),
        P("dp"),
        P("dp", None, "mp"),
        P("dp", "mp"),
        P("dp"),
        P("dp"),
        P("dp", "mp"),
        P("dp", "mp"),
    )
    return jax.shard_map(
        on_device, mesh=mesh, in_specs=in_specs, out_specs=out_specs, check_vma=False
    )
```

```python
import functools

import jax
import jax.numpy as jnp
from jax import lax
from jax.experimental import pallas as pl
from jax.experimental.pallas import tpu as pltpu
from jax.sharding import PartitionSpec as P

HEAD = 128
WIDTH = 2048
SHARE = 128
PART = 1024
MESH = pl.DeviceIdType.MESH
ANY = pl.BlockSpec(memory_space=pl.ANY)
VMEM = pl.BlockSpec(memory_space=pltpu.VMEM)
masked_score = -1000000000.0
epsilon = 1e-05
f32 = jnp.float32
bf16 = jnp.bfloat16


def place():
    dp, mp = lax.axis_index("dp"), lax.axis_index("mp")
    return lax.div(dp, 16), lax.rem(lax.div(dp, 4), 4), lax.rem(dp, 4), lax.div(mp, 2), lax.rem(mp, 2)


def ring(position, step):
    return lax.rem(position + step + 4, 4)


def xz_neighbour(axis, step):
    ylo, x, z, yhi, core = place()
    if axis == 0:
        x = ring(x, step)
    else:
        z = ring(z, step)
    return (ylo * 16 + x * 4 + z, yhi * 2 + core)


def y_peer(step):
    ylo, x, z, yhi, core = place()
    y = ring(yhi * 2 + ylo, step)
    return (lax.rem(y, 2) * 16 + x * 4 + z, lax.div(y, 2) * 2 + core)


def lo_partner():
    ylo, x, z, yhi, core = place()
    return ((1 - ylo) * 16 + x * 4 + z, yhi * 2 + core)


def core_partner():
    ylo, x, z, yhi, core = place()
    return (ylo * 16 + x * 4 + z, yhi * 2 + 1 - core)


def greet(peers):
    barrier = pltpu.get_barrier_semaphore()
    for peer in peers:
        pl.semaphore_signal(barrier, inc=1, device_id=peer, device_id_type=MESH)
    return lambda: pl.semaphore_wait(barrier, len(peers))


def remote(src, dst, send_sem, recv_sem, peer):
    return pltpu.make_async_remote_copy(
        src_ref=src,
        dst_ref=dst,
        send_sem=send_sem,
        recv_sem=recv_sem,
        device_id=peer,
        device_id_type=MESH,
    )


def sems(*shape):
    return pltpu.SemaphoreType.DMA(shape)


def params(collective_id, mib=48):
    return pltpu.CompilerParams(
        collective_id=collective_id, has_side_effects=True, vmem_limit_bytes=mib << 20
    )


PEERS = {
    "core": core_partner,
    "x+": lambda: xz_neighbour(0, 1),
    "x-": lambda: xz_neighbour(0, -1),
    "z+": lambda: xz_neighbour(1, 1),
    "z-": lambda: xz_neighbour(1, -1),
    "x2": lambda: xz_neighbour(0, 2),
    "z2": lambda: xz_neighbour(1, 2),
    "y1": lambda: y_peer(1),
    "y2": lambda: y_peer(2),
    "y3": lambda: y_peer(3),
}


def diagonal_peer(step):
    dp, mp = y_peer(step)
    return (dp, mp + 1 - 2 * lax.rem(mp, 2))


PEERS.update({f"d{k}": functools.partial(diagonal_peer, k) for k in range(1, 4)})
GROUP = ["y1", "y2", "y3", "core", "d1", "d2", "d3"]


def kernel_call(body, jobs, peers, ins, outs, scratch, collective_id, mib=56):
    def kernel(*refs):
        taken = 0

        def take(count):
            nonlocal taken
            taken += count
            return refs[taken - count : taken]

        groups = [take(len(ins)), take(len(outs)), take(len(scratch))]
        makers = []
        for job in jobs:
            own = take(len(job["scratch"]))
            makers.append(lambda *given, job=job, own=own: job["steps"](*given, *own))
        ready = greet([PEERS[name]() for name in peers])
        body(*groups, makers, ready)

    return pl.pallas_call(
        kernel,
        out_shape=[shape for shape, _ in outs],
        in_specs=[spec for _, spec in ins],
        out_specs=[spec for _, spec in outs],
        scratch_shapes=scratch + [one for job in jobs for one in job["scratch"]],
        compiler_params=params(collective_id, mib),
    )(*[array for array, _ in ins])


def finish(*runs):
    for run in runs:
        for _ in run:
            pass


def step(*runs):
    for run in runs:
        next(run, None)


def shaped(dtype, *shape):
    return jax.ShapeDtypeStruct(shape, dtype)


def small_gather():
    def steps(own, everyone, send, recv):
        ylo, x, z, yhi, core = place()
        sent = []

        def go(here, n, peer):
            copy = remote(here, here, send.at[n], recv.at[n], peer)
            copy.start()
            sent.append(copy)

        def came(here, n):
            remote(here, here, send.at[n], recv.at[n], lo_partner()).wait_recv()

        everyone[ylo, x, z] = own[...]
        go(everyone.at[ylo, x, z], 0, lo_partner())
        yield
        came(everyone.at[1 - ylo, x, z], 0)
        for k in (1, 2, 3):
            go(everyone.at[:, x, z], k, xz_neighbour(0, k))
        yield
        for k in (1, 2, 3):
            came(everyone.at[:, ring(x, -k), z], k)
        for k in (1, 2, 3):
            go(everyone.at[:, :, z], 3 + k, xz_neighbour(1, k))
        yield
        for k in (1, 2, 3):
            came(everyone.at[:, :, ring(z, -k)], 3 + k)
        for copy in sent:
            copy.wait_send()

    return {"scratch": [sems(7), sems(7)], "steps": steps}


def small_reduce():
    def steps(rows, out, of_group, of_x, of_z, half, quarter, send, recv):
        ylo, x, z, yhi, core = place()
        y = yhi * 2 + ylo
        waits = []

        def go(src, dst, n, peer):
            copy = remote(src, dst, send.at[n], recv.at[n], peer)
            copy.start()
            waits.append(copy)

        def lanes(start, size):
            return pl.ds(pl.multiple_of(start, size), size)

        for n, (k, flip) in enumerate(((1, 0), (1, 1), (2, 0), (2, 1), (3, 0), (3, 1), (0, 1))):
            theirs = lanes(lax.rem(ring(y, k), 2) * 1024, 1024)
            go(rows.at[:, theirs], of_group.at[n], n, diagonal_peer(k) if flip else y_peer(k))
        yield
        for copy in waits:
            copy.wait_recv()
        total = rows[:, lanes(ylo * 1024, 1024)]
        for n in range(7):
            total += of_group[n]
        half[...] = total
        for k in (1, 2, 3):
            go(half.at[:, lanes(ring(x, k) * 256, 256)], of_x.at[k - 1], 6 + k, xz_neighbour(0, k))
        yield
        for copy in waits[7:]:
            copy.wait_recv()
        total = half[:, lanes(x * 256, 256)]
        for n in range(3):
            total += of_x[n]
        quarter[...] = total
        for k in (1, 2, 3):
            theirs = lanes(lax.div(ring(z, k), 2) * 128, 128)
            go(quarter.at[:, theirs], of_z.at[k - 1], 9 + k, xz_neighbour(1, k))
        yield
        for copy in waits[10:]:
            copy.wait_recv()
        total = quarter[:, lanes(lax.div(z, 2) * 128, 128)]
        for n in range(3):
            total += of_z[n]
        out[...] = total
        for copy in waits:
            copy.wait_send()

    return {
        "scratch": [
            pltpu.VMEM((7, 4, 1024), f32),
            pltpu.VMEM((3, 4, 256), f32),
            pltpu.VMEM((3, 4, 128), f32),
            pltpu.VMEM((4, 1024), f32),
            pltpu.VMEM((4, 256), f32),
            sems(13),
            sems(13),
        ],
        "steps": steps,
    }


def row_exchange(count=1):
    def steps(halves, full, local_sem, send, recv):
        ylo, x, z, yhi, core = place()
        up, down, other = y_peer(1), y_peer(3), core_partner()
        first = []
        for n in range(count):
            for u, peer in ((0, up), (1, down)):
                here = full.at[n, ylo, core, u]
                first.append(remote(halves.at[n, u], here, send.at[n, u], recv.at[n, u], peer))
        for n in range(count):
            here = full.at[n, ylo, core]
            first.append(remote(halves.at[n], here, send.at[n, 2], recv.at[n, 2], other))
        for copy in first:
            copy.start()
        local = [
            pltpu.make_async_copy(halves.at[n], full.at[n, ylo, core], local_sem.at[n])
            for n in range(count)
        ]
        for copy in local:
            copy.start()
        yield
        second = []
        for n in range(count):
            for u in range(2):
                here = full.at[n, 1 - ylo, core, u]
                remote(halves.at[n, u], here, send.at[n, u], recv.at[n, u], up).wait_recv()
                copy = remote(here, here, send.at[n, 3 + u], recv.at[n, 3 + u], other)
                copy.start()
                second.append(copy)
        yield
        for n in range(count):
            here = full.at[n, ylo, 1 - core]
            remote(halves.at[n], here, send.at[n, 2], recv.at[n, 2], other).wait_recv()
            for u in range(2):
                here = full.at[n, 1 - ylo, 1 - core, u]
                remote(here, here, send.at[n, 3 + u], recv.at[n, 3 + u], other).wait_recv()
        for copy in first + second:
            copy.wait_send()
        for copy in local:
            copy.wait()

    return {
        "scratch": [sems(count), sems(count, 5), sems(count, 5)],
        "steps": steps,
    }


def share_gather():
    def steps(share, full, local_sem, send, recv):
        ylo, x, z, yhi, core = place()
        y = yhi * 2 + ylo
        other = core_partner()
        half = SHARE // 2
        sent = []

        def of(step, half_core):
            source = ring(y, step)
            return full.at[lax.rem(source, 2), half_core, lax.div(source, 2)]

        def go(src, dst, n, peer):
            copy = remote(src, dst, send.at[n], recv.at[n], peer)
            copy.start()
            sent.append(copy)

        def came(dst, n):
            remote(dst, dst, send.at[n], recv.at[n], other).wait_recv()

        local = pltpu.make_async_copy(share, of(0, core), local_sem)
        go(share, of(0, core), 0, y_peer(1))
        go(share, of(0, core), 1, y_peer(3))
        go(share, of(0, core), 2, other)
        local.start()
        yield
        for n, step_back, rows, onward in ((0, 3, pl.ds(0, half), 1), (1, 1, pl.ds(half, half), 3)):
            here = of(step_back, core)
            came(here, n)
            go(here.at[rows], here.at[rows], 3 + n, y_peer(onward))
            go(here, here, 5 + n, other)
        yield
        far = of(2, core)
        came(far.at[pl.ds(0, half)], 3)
        came(far.at[pl.ds(half, half)], 4)
        go(far, far, 7, other)
        yield
        came(of(0, 1 - core), 2)
        came(of(3, 1 - core), 5)
        came(of(1, 1 - core), 6)
        came(of(2, 1 - core), 7)
        for copy in sent:
            copy.wait_send()
        local.wait()

    return {"scratch": [pltpu.SemaphoreType.DMA, sems(8), sems(8)], "steps": steps}


def add_rows(count, one):
    def body(i, carry):
        one(pl.ds(pl.multiple_of(i * 16, 16), 16))
        return carry

    lax.fori_loop(0, count // 16, body, 0)


def share_sum():
    def steps(partial, out, from_core, via, arrived, send, recv, send_two, recv_two):
        ylo, x, z, yhi, core = place()
        y = yhi * 2 + ylo
        other = core_partner()
        half = SHARE // 2

        def block(k, half_core):
            target = ring(y, k)
            return partial.at[lax.rem(target, 2), half_core, lax.div(target, 2)]

        first, second = {}, {}

        def to_core(order):
            for k in order:
                first[k] = remote(block(k, 1 - core), from_core.at[k], send.at[k], recv.at[k], other)
                first[k].start()

        to_core((2, 0))
        yield
        first[2].wait_recv()
        far = block(2, core)

        def add_far(rows):
            far[rows] = (far[rows].astype(f32) + from_core[2, rows].astype(f32)).astype(bf16)

        add_rows(SHARE, add_far)
        for n, k in ((0, 1), (1, 3)):
            second[n] = remote(
                far.at[pl.ds(half * n, half)], via.at[n], send_two.at[n], recv_two.at[n], y_peer(k)
            )
            second[n].start()
        yield
        to_core((1, 3))
        yield
        for n, k in ((0, 1), (1, 3)):
            first[k].wait_recv()
            second[n].wait_recv()
            near = block(k, core)

            def add_via(i, carry):
                at = pl.multiple_of(i * 16, 16)
                rows, with_via = pl.ds(at, 16), pl.ds(pl.multiple_of(half * n + at, 16), 16)
                value = near[with_via].astype(f32) + from_core[k, with_via].astype(f32)
                near[with_via] = (value + via[n, rows].astype(f32)).astype(bf16)
                plain = pl.ds(pl.multiple_of(half * (1 - n) + at, 16), 16)
                value = near[plain].astype(f32) + from_core[k, plain].astype(f32)
                near[plain] = value.astype(bf16)
                return carry

            lax.fori_loop(0, half // 16, add_via, 0)
            second[2 + n] = remote(near, arrived.at[n], send_two.at[2 + n], recv_two.at[2 + n], y_peer(k))
            second[2 + n].start()
        yield
        first[0].wait_recv()
        second[2].wait_recv()
        second[3].wait_recv()
        mine_own = block(0, core)

        def total(rows):
            value = mine_own[rows].astype(f32) + from_core[0, rows].astype(f32)
            out[rows] = value + arrived[0, rows].astype(f32) + arrived[1, rows].astype(f32)

        add_rows(SHARE, total)
        for k in range(4):
            first[k].wait_send()
            second[k].wait_send()

    return {
        "scratch": [
            pltpu.VMEM((4, SHARE, WIDTH), bf16),
            pltpu.VMEM((2, SHARE // 2, WIDTH), bf16),
            pltpu.VMEM((2, SHARE, WIDTH), bf16),
        ]
        + [sems(4)] * 4,
        "steps": steps,
    }


def feature_start(ylo, yhi, core):
    return pl.multiple_of((yhi * 2 + core) * 512 + ylo * 256, 256)


def heads_to_tokens():
    def steps(heads, tokens, send, recv):
        ylo, x, z, yhi, core = place()
        y = yhi * 2 + ylo
        mine = tokens.at[:, pl.ds(feature_start(ylo, yhi, core), 256)]
        sent = []

        def go(k, flip):
            target = ring(y, k)
            half = 1 - core if flip else core
            peer = diagonal_peer(k) if flip else y_peer(k)
            src = heads.at[lax.rem(target, 2), half, lax.div(target, 2)]
            copy = remote(src, mine, send.at[2 * k + flip], recv.at[2 * k + flip], peer)
            copy.start()
            sent.append(copy)

        for k in (1, 3):
            for flip in (0, 1):
                go(k, flip)
        yield
        for k, flip in ((2, 0), (2, 1), (0, 1)):
            go(k, flip)
        tokens[:, pl.ds(feature_start(ylo, yhi, core), 256)] = heads[ylo, core, yhi]
        yield
        for k, flip in ((1, 0), (1, 1), (3, 0), (3, 1), (2, 0), (2, 1), (0, 1)):
            source = ring(y, -k)
            half = 1 - core if flip else core
            start = feature_start(lax.rem(source, 2), lax.div(source, 2), half)
            here = tokens.at[:, pl.ds(start, 256)]
            remote(heads.at[0, 0, 0], here, send.at[2 * k + flip], recv.at[2 * k + flip], y_peer(1)).wait_recv()
        for copy in sent:
            copy.wait_send()

    return {"scratch": [sems(8), sems(8)], "steps": steps}


def tokens_to_heads():
    def steps(tokens, heads, send, recv):
        ylo, x, z, yhi, core = place()
        y = yhi * 2 + ylo
        mine = heads.at[ylo, core, yhi]
        sent = []
        order = ((1, 0), (1, 1), (3, 0), (3, 1), (2, 0), (2, 1), (0, 1))
        for k, flip in order:
            target = ring(y, k)
            half = 1 - core if flip else core
            peer = diagonal_peer(k) if flip else y_peer(k)
            start = feature_start(lax.rem(target, 2), lax.div(target, 2), half)
            src = tokens.at[:, pl.ds(start, 256)]
            copy = remote(src, mine, send.at[2 * k + flip], recv.at[2 * k + flip], peer)
            copy.start()
            sent.append(copy)
        heads[ylo, core, yhi] = tokens[:, pl.ds(feature_start(ylo, yhi, core), 256)]
        yield
        for k, flip in order:
            source = ring(y, -k)
            half = 1 - core if flip else core
            here = heads.at[lax.rem(source, 2), half, lax.div(source, 2)]
            remote(here, here, send.at[2 * k + flip], recv.at[2 * k + flip], y_peer(1)).wait_recv()
        for copy in sent:
            copy.wait_send()

    return {"scratch": [sems(8), sems(8)], "steps": steps}


def row_gather():
    def steps(share, full, local_sem, send, recv):
        ylo, x, z, yhi, core = place()
        across, other = y_peer(2), core_partner()
        mine = full.at[:, core, yhi]
        far = full.at[:, core, 1 - yhi]
        local = pltpu.make_async_copy(share, mine, local_sem)
        one = remote(share, mine, send.at[0], recv.at[0], across)
        two = remote(share, mine, send.at[1], recv.at[1], other)
        one.start()
        two.start()
        local.start()
        yield
        remote(share, far, send.at[0], recv.at[0], across).wait_recv()
        three = remote(far, far, send.at[2], recv.at[2], other)
        three.start()
        yield
        remote(share, full.at[:, 1 - core, yhi], send.at[1], recv.at[1], other).wait_recv()
        last = full.at[:, 1 - core, 1 - yhi]
        remote(last, last, send.at[2], recv.at[2], other).wait_recv()
        for copy in (one, two, three):
            copy.wait_send()
        local.wait()

    return {
        "scratch": [pltpu.SemaphoreType.DMA, sems(3), sems(3)],
        "steps": steps,
    }


SIGNS = (1, -1)
XZ = ["x+", "x-", "z+", "z-"]


def xz_near():
    return [[xz_neighbour(axis, d) for d in SIGNS] for axis in (0, 1)]


def weight_gather(columns, spread=False, flat=False):
    count = 4 if spread else 2

    def steps(own, full, local_sem, swap_send, swap_recv, send, recv):
        ylo, x, z, yhi, core = place()
        y = yhi * 2 + ylo
        near = xz_near()
        offsets = (0, -1, 1, 2)

        def move(src, dst, s, r, stage, d, axis):
            n = ((s * 2 + r) * 8 + stage) * 2 + d
            return remote(src, dst, send.at[n], recv.at[n], near[axis][d])

        def origin(s):
            if spread:
                return ring(y, offsets[s])
            return ylo if s == 0 else 1 - ylo

        def block(s, r, one, two, rows):
            if r == 0:
                return full.at[origin(s), ring(x, one), ring(z, two), rows]
            return full.at[origin(s), ring(x, two), ring(z, one), rows]

        def rows_of(r, d=None):
            return pl.ds(32 * r, 32) if d is None else pl.ds(32 * r + 16 * d, 16)

        def half(n):
            if flat:
                return own.at[:, pl.ds(pl.multiple_of(n * columns, columns), columns)]
            return own.at[n]

        mine = own if spread else half(ylo)
        here = full.at[origin(0), x, z]
        local = pltpu.make_async_copy(mine, here, local_sem)
        swaps = []
        for s in range(1, count):
            peer = y_peer((4 - offsets[s]) % 4) if spread else lo_partner()
            src = own if spread else half(1 - ylo)
            swaps.append(remote(src, here, swap_send.at[s], swap_recv.at[s], peer))
        for swap in swaps:
            swap.start()
        sent = []

        def go(*args):
            copy = move(*args)
            copy.start()
            sent.append(copy)

        def begin(s, source):
            for r in range(2):
                for d in range(2):
                    src = source.at[rows_of(r)]
                    go(src, block(s, r, 0, 0, rows_of(r)), s, r, 0, d, r)
            for r in range(2):
                for d in range(2):
                    src = source.at[rows_of(r)]
                    go(src, block(s, r, 0, 0, rows_of(r)), s, r, 2, d, 1 - r)

        begin(0, mine)
        local.start()
        yield
        for s in range(1, count):
            came = full.at[origin(s), x, z]
            remote(came, came, swap_send.at[s], swap_recv.at[s], lo_partner()).wait_recv()
            begin(s, came)
        yield
        for s in range(count):
            for r in range(2):
                for d in range(2):
                    came = block(s, r, -SIGNS[d], 0, rows_of(r))
                    move(came, came, s, r, 0, d, r).wait_recv()
                    piece = block(s, r, -SIGNS[d], 0, rows_of(r, d))
                    go(piece, piece, s, r, 1, d, r)
                for part in (1, 2):
                    for d in range(2):
                        came = block(s, r, offsets[part], 0, rows_of(r))
                        go(came, came, s, r, 2 + part, d, 1 - r)
            if s % 2:
                yield
        for s in range(count):
            for r in range(2):
                for d in range(2):
                    piece = block(s, r, 2, 0, rows_of(r, d))
                    move(piece, piece, s, r, 1, d, r).wait_recv()
                for d in range(2):
                    came = block(s, r, 2, 0, rows_of(r))
                    go(came, came, s, r, 5, d, 1 - r)
            if s % 2:
                yield
        for part in (0, 2, 1, 3):
            d = part // 2
            for s in range(count):
                for r in range(2):
                    came = block(s, r, offsets[part], -SIGNS[d], rows_of(r))
                    move(came, came, s, r, 2 + part, d, 1 - r).wait_recv()
                    go(came, came, s, r, 6 + part % 2, d, 1 - r)
            yield
        for s in range(count):
            for r in range(2):
                for part in range(4):
                    d = 1 - part // 2
                    came = block(s, r, offsets[part], -SIGNS[d], rows_of(r))
                    move(came, came, s, r, 2 + part, d, 1 - r).wait_recv()
                for part in range(4):
                    d = part // 2
                    came = block(s, r, offsets[part], 2, rows_of(r))
                    move(came, came, s, r, 6 + part % 2, d, 1 - r).wait_recv()
        for copy in sent + swaps:
            copy.wait_send()
        local.wait()

    return {
        "scratch": [pltpu.SemaphoreType.DMA, sems(count), sems(count), sems(32 * count), sems(32 * count)],
        "steps": steps,
    }


def gathered(columns, count=2):
    return (shaped(bf16, count, 4, 4, 64, columns), ANY)


def weight_sum(columns=PART):
    def steps(grads, out, wide, thin, total, swap_send, swap_recv, send, recv):
        ylo, x, z, yhi, core = place()
        near = xz_near()
        partner = lo_partner()

        def move(src, dst, s, r, stage, d, axis):
            n = ((s * 2 + r) * 6 + stage) * 2 + d
            return remote(src, dst, send.at[n], recv.at[n], near[axis][d])

        def line(s, r, step, part):
            if r == 0:
                return grads.at[s, part, ring(z, step), pl.ds(0, 32)]
            return grads.at[s, ring(x, step), part, pl.ds(32, 32)]

        def block(s, r, step, rows):
            if r == 0:
                return grads.at[s, ring(x, step), z, rows]
            return grads.at[s, x, ring(z, step), rows]

        def wide_move(s, r, d, kind):
            if kind == 0:
                src = line(s, r, 2, pl.ds(2 * d, 2))
            elif kind == 1:
                src = line(s, r, SIGNS[d], pl.ds(2 - 2 * d, 2))
            else:
                src = line(s, r, SIGNS[d], pl.ds(2 * d, 2))
            return move(src, wide.at[s, r, kind, d], s, r, kind, d, 1 - r)

        def thin_move(s, r, d, kind):
            if kind == 0:
                src = block(s, r, 2, pl.ds(32 * r + 16 * d, 16))
            elif kind == 1:
                src = block(s, r, SIGNS[d], pl.ds(32 * r + 16 - 16 * d, 16))
            else:
                src = block(s, r, SIGNS[d], pl.ds(32 * r + 16 * d, 16))
            return move(src, thin.at[s, r, kind, d], s, r, 3 + kind, d, r)

        for s in range(2):
            for kind in range(2):
                for r in range(2):
                    for d in range(2):
                        wide_move(s, r, d, kind).start()
        yield

        for s in range(2):
            for r in range(2):
                for d in range(2):
                    wide_move(s, r, d, 0).wait_recv()
                    for p in range(2):
                        mine = line(s, r, SIGNS[d], 2 * d + p)

                        def one(rows):
                            value = mine[rows].astype(f32) + wide[s, r, 0, d, p, rows].astype(f32)
                            mine[rows] = value.astype(bf16)

                        add_rows(32, one)
                    wide_move(s, r, d, 2).start()
            yield

        for s in range(2):
            for r in range(2):
                for d in range(2):
                    wide_move(s, r, d, 1).wait_recv()
                    wide_move(s, r, d, 2).wait_recv()
                for p in range(4):
                    mine = line(s, r, 0, p)
                    d = p // 2

                    def one(rows):
                        value = mine[rows].astype(f32) + wide[s, r, 2, d, p % 2, rows].astype(f32)
                        value += wide[s, r, 1, 1 - d, p % 2, rows].astype(f32)
                        mine[rows] = value.astype(bf16)

                    add_rows(32, one)
                for kind in range(2):
                    for d in range(2):
                        thin_move(s, r, d, kind).start()
            yield

        for s in range(2):
            for r in range(2):
                for d in range(2):
                    thin_move(s, r, d, 0).wait_recv()
                    mine = block(s, r, SIGNS[d], pl.ds(32 * r + 16 * d, 16))
                    value = mine[...].astype(f32) + thin[s, r, 0, d].astype(f32)
                    mine[...] = value.astype(bf16)
                    thin_move(s, r, d, 2).start()
        yield

        for s in range(2):
            for r in range(2):
                for d in range(2):
                    thin_move(s, r, d, 1).wait_recv()
                    thin_move(s, r, d, 2).wait_recv()
                for d in range(2):
                    rows = pl.ds(32 * r + 16 * d, 16)
                    value = block(s, r, 0, rows)[...].astype(f32) + thin[s, r, 2, d].astype(f32)
                    value += thin[s, r, 1, 1 - d].astype(f32)
                    total[s, rows] = value.astype(bf16)
        swap = remote(total.at[1 - ylo], out.at[ylo], swap_send, swap_recv, partner)
        swap.start()
        out[ylo] = total[ylo]
        yield
        for s in range(2):
            for r in range(2):
                for d in range(2):
                    for kind in range(3):
                        wide_move(s, r, d, kind).wait_send()
                        thin_move(s, r, d, kind).wait_send()
        remote(total.at[0], out.at[1 - ylo], swap_send, swap_recv, partner).wait_recv()
        swap.wait_send()

    return {
        "scratch": [
            pltpu.VMEM((2, 2, 3, 2, 2, 32, columns), bf16),
            pltpu.VMEM((2, 2, 3, 2, 16, columns), bf16),
            pltpu.VMEM((2, 64, columns), bf16),
            pltpu.SemaphoreType.DMA,
            pltpu.SemaphoreType.DMA,
            sems(48),
            sems(48),
        ],
        "steps": steps,
    }


def standardize(value):
    mean = jnp.mean(value, axis=-1, keepdims=True)
    centered = value - mean
    scale_inv = lax.rsqrt(jnp.mean(centered * centered, axis=-1, keepdims=True) + epsilon)
    return (centered * scale_inv, scale_inv)


def norm_back(grad_normed_out, normed, scale_inv, gain):
    scaled = grad_normed_out * gain
    mean_one = jnp.mean(scaled, axis=-1, keepdims=True)
    mean_two = jnp.mean(scaled * normed, axis=-1, keepdims=True)
    grad_value = scale_inv * (scaled - mean_one - normed * mean_two)
    grad_gain = jnp.sum(grad_normed_out * normed, axis=0, keepdims=True)
    grad_shift = jnp.sum(grad_normed_out, axis=0, keepdims=True)
    return (grad_value, grad_gain, grad_shift)


def dot(a, b):
    return jnp.dot(a, b, preferred_element_type=f32)


def turned_dot(a, b):
    return lax.dot_general(a, b, (((1,), (1,)), ((), ())), preferred_element_type=f32)


def outer_dot(a, b):
    return lax.dot_general(a, b, (((0,), (0,)), ((), ())), preferred_element_type=f32)


def some_rows(count, size, one):
    def body(i, carry):
        one(pl.ds(pl.multiple_of(i * size, size), size))
        return carry

    lax.fori_loop(0, count // size, body, 0)


def fetched(src, dst, sem):
    copy = pltpu.make_async_copy(src, dst, sem)
    copy.start()
    return copy


CODES = 4096
CODE_CHUNK = 1024


def forward_body(ins, outs, scratch, makers, ready):
    ids, segments, padding, stream_hbm, cot_hbm, codebook, own_qkv, own_out, own_up, own_down, norms = ins
    (
        attn_out,
        qkv_out,
        out_weight_out,
        cot_full,
        inputs_out,
        gains,
        mask_out,
        projected_out,
        attended_out,
        middle_out,
        ffn_full,
        up_full,
        down_full,
    ) = outs
    (
        inputs_share,
        mask,
        projected,
        attended,
        middle,
        everyone,
        norm_tile,
        other_segments,
        other_padding,
        chunk,
        total,
        stream,
        cot_half,
        halves,
        attn_in,
        weight,
        out_weight,
        tokens,
        ffn_share,
        load_sem,
        swap_send,
        swap_recv,
    ) = scratch
    make_small, make_qkv, make_out, make_up, make_down, make_cot, make_attn, make_heads, make_share = makers
    ylo, x, z, yhi, core = place()
    small = make_small(norm_tile, everyone)
    qkv = make_qkv(own_qkv, weight)
    out = make_out(own_out, out_weight.at[core])
    up, down = make_up(own_up, up_full), make_down(own_down, down_full)
    cot_move = make_cot(cot_half, cot_full)
    attn_move = make_attn(halves, attn_in)
    heads = make_heads(attended, tokens)
    spread = make_share(ffn_share, ffn_full)

    def fetch(j):
        rows = pl.ds(j * CODE_CHUNK, CODE_CHUNK)
        return pltpu.make_async_copy(codebook.at[rows], chunk.at[j % 2], load_sem.at[j % 2])

    mine = pl.ds(pl.multiple_of(core * 256, 256), 256)
    loads = [fetched(stream_hbm.at[mine], stream, load_sem.at[2])]
    for u in range(2):
        rows = pl.ds(pl.multiple_of(core * 256 + u * SHARE, SHARE), SHARE)
        loads.append(fetched(cot_hbm.at[rows], cot_half.at[0, u], load_sem.at[3 + u]))
    fetch(0).start()
    lane = lax.broadcasted_iota(jnp.int32, (8, 128), 1)
    norm_tile[...] = jnp.where(lax.div(lane, 64) == lax.rem(z, 2), norms[...].astype(f32), 0.0)
    ready()
    step(small, qkv, out)
    row_swaps = [
        remote(segments, other_segments, swap_send.at[0], swap_recv.at[0], lo_partner()),
        remote(padding, other_padding, swap_send.at[1], swap_recv.at[1], lo_partner()),
    ]
    for swap in row_swaps:
        swap.start()
    for load in loads:
        load.wait()
    step(cot_move)
    total[...] = stream[...].astype(f32)
    my_ids = ids[:, mine]
    count = CODES // CODE_CHUNK
    for j in range(count):
        if j + 1 < count:
            fetch(j + 1).start()
        fetch(j).wait()
        code = lax.broadcasted_iota(jnp.int32, (CODE_CHUNK, 256), 0) + j * CODE_CHUNK
        pick = jnp.where(my_ids == code, 1.0, 0.0).astype(bf16)
        for part in range(2):
            columns = pl.ds(part * 1024, 1024)
            total[:, columns] += outer_dot(pick, chunk[j % 2, :, columns])
        step(small, (qkv, out, qkv, out)[j])
    finish(small)
    for t in range(16):
        at = (t // 8, t // 2 % 4, t % 2 * 2)
        pair = everyone[at] + everyone[at[0], at[1], at[2] + 1]
        gains[:, pl.ds(128 * t, 128)] = pair
    gain, shift = gains[pl.ds(0, 1)], gains[pl.ds(1, 1)]
    for u in range(2):

        def norm(rows):
            value = total[pl.ds(pl.multiple_of(u * SHARE + rows.start, 32), 32)]
            normed, _ = standardize(value)
            halves[0, u, rows] = (normed * gain + shift).astype(bf16)

        some_rows(SHARE, 32, norm)
    step(attn_move, qkv, out)

    def keep(rows):
        inputs_share[rows] = total[pl.ds(pl.multiple_of(yhi * SHARE + rows.start, 32), 32)]

    some_rows(SHARE, 32, keep)
    step(qkv, qkv)

    def see(r, segment_row, padding_row):
        turned = jnp.broadcast_to(segment_row.astype(f32), (SHARE, 512)).T[:, 0:1]
        query = lax.broadcasted_iota(jnp.int32, (512, 512), 0)
        key = lax.broadcasted_iota(jnp.int32, (512, 512), 1)
        same = turned == segment_row.astype(f32)
        live = (padding_row == 1) | (query == key)
        mask[r] = jnp.where(same & live & (key <= query), 1.0, 0.0).astype(bf16)

    for swap in row_swaps:
        swap.wait()
    see(ylo, segments[...], padding[...])
    see(1 - ylo, other_segments[...], other_padding[...])
    step(qkv, cot_move, qkv, out, out)
    step(attn_move)
    finish(qkv)
    step(out, out, up)
    finish(cot_move, attn_move)
    writes = [
        fetched(attn_in, attn_out, load_sem.at[0]),
        fetched(weight, qkv_out, load_sem.at[1]),
        fetched(inputs_share, inputs_out, load_sem.at[2]),
        fetched(mask, mask_out, load_sem.at[3]),
    ]

    def project(r):
        rows = attn_in[0, r].reshape(512, WIDTH)
        for t in range(3):
            columns = pl.ds(t * 256, 256)
            part = weight[:, :, :, :, columns].reshape(WIDTH, 256)
            projected[r, :, columns] = dot(rows, part).astype(bf16)

    def attend(r):
        for h in range(2):
            key = projected[r, :, pl.ds(256 + h * HEAD, HEAD)]
            value = projected[r, :, pl.ds(512 + h * HEAD, HEAD)]
            for c in range(2):
                rows = pl.ds(c * 256, 256)
                query = projected[r, rows, pl.ds(h * HEAD, HEAD)]
                scores = turned_dot(query, key) * HEAD ** (-0.5)
                scores = jnp.where(mask[r, rows].astype(f32) > 0.5, scores, masked_score)
                expd = jnp.exp(scores - jnp.max(scores, axis=-1, keepdims=True))
                probs = expd / jnp.sum(expd, axis=-1, keepdims=True)
                result = dot(probs.astype(bf16), value).astype(bf16)
                for u in range(2):
                    attended[r, c, u, :, pl.ds(h * HEAD, HEAD)] = result[u * SHARE : (u + 1) * SHARE]

    project(1 - ylo)
    step(out, down)
    attend(1 - ylo)
    step(heads)
    step(out, up)
    project(ylo)
    finish(out)
    swap = remote(
        out_weight.at[core], out_weight.at[core], swap_send.at[2], swap_recv.at[2], core_partner()
    )
    swap.start()
    step(down)
    attend(ylo)
    step(heads)
    step(up, down)
    finish(heads)
    there = out_weight.at[1 - core]
    remote(there, there, swap_send.at[2], swap_recv.at[2], core_partner()).wait_recv()
    writes.append(fetched(out_weight, out_weight_out, load_sem.at[4]))
    writes.append(fetched(projected, projected_out, load_sem.at[5]))
    writes.append(fetched(attended, attended_out, load_sem.at[6]))

    def branch(n, carry):
        columns = pl.ds(pl.multiple_of(n * 256, 256), 256)
        value = inputs_share[:, columns]
        for c in range(2):
            for h in range(2):
                features = pl.ds((h * 2 + c) * 512, 512)
                part = out_weight[c, h * 2 + lax.div(n, 4), lax.rem(n, 4)].reshape(256, 512)
                value += turned_dot(tokens[:, features], part)
        middle[:, columns] = value
        return carry

    lax.fori_loop(0, WIDTH // 256, branch, 0)
    gain_two, shift_two = gains[pl.ds(2, 1)], gains[pl.ds(3, 1)]

    def norm_two(rows):
        normed, _ = standardize(middle[rows])
        ffn_share[rows] = (normed * gain_two + shift_two).astype(bf16)

    some_rows(SHARE, 32, norm_two)
    step(spread)
    writes.append(fetched(middle, middle_out, load_sem.at[7]))
    step(up, down)
    step(up, down)
    step(up, down)
    step(spread)
    step(up, down)
    step(spread)
    step(up, down)
    finish(spread, up, down)
    for write in writes:
        write.wait()
    swap.wait_send()


def forward(ids, segments, padding, stream, cot, codebook, own_qkv, own_out, own_up, own_down, norms):
    tokens_full = (shaped(bf16, 1, 2, 2, 2, SHARE, WIDTH), ANY)
    return kernel_call(
        forward_body,
        [
            small_gather(),
            weight_gather(768),
            weight_gather(512, spread=True),
            weight_gather(PART, flat=True),
            weight_gather(PART, flat=True),
            row_exchange(),
            row_exchange(),
            heads_to_tokens(),
            share_gather(),
        ],
        XZ + ["x2", "z2"] + GROUP,
        [
            (ids, VMEM),
            (segments, VMEM),
            (padding, VMEM),
            (stream, ANY),
            (cot, ANY),
            (codebook, ANY),
            (own_qkv, VMEM),
            (own_out, VMEM),
            (own_up, VMEM),
            (own_down, VMEM),
            (norms, VMEM),
        ],
        [
            tokens_full,
            gathered(768),
            (shaped(bf16, 2, 4, 4, 4, 64, 512), ANY),
            tokens_full,
            (shaped(f32, SHARE, WIDTH), ANY),
            (shaped(f32, 8, WIDTH), VMEM),
            (shaped(bf16, 2, 512, 512), ANY),
            (shaped(bf16, 2, 512, 768), ANY),
            (shaped(bf16, 2, 2, 2, SHARE, 256), ANY),
            (shaped(f32, SHARE, WIDTH), ANY),
            (shaped(bf16, 2, 2, 2, SHARE, WIDTH), ANY),
            gathered(PART),
            gathered(PART),
        ],
        [
            pltpu.VMEM((SHARE, WIDTH), f32),
            pltpu.VMEM((2, 512, 512), bf16),
            pltpu.VMEM((2, 512, 768), bf16),
            pltpu.VMEM((2, 2, 2, SHARE, 256), bf16),
            pltpu.VMEM((SHARE, WIDTH), f32),
            pltpu.VMEM((2, 4, 4, 8, 128), f32),
            pltpu.VMEM((8, 128), f32),
            pltpu.VMEM((1, 512), jnp.int32),
            pltpu.VMEM((1, 512), jnp.int32),
            pltpu.VMEM((2, CODE_CHUNK, WIDTH), bf16),
            pltpu.VMEM((256, WIDTH), f32),
            pltpu.VMEM((256, WIDTH), bf16),
            pltpu.VMEM((1, 2, SHARE, WIDTH), bf16),
            pltpu.VMEM((1, 2, SHARE, WIDTH), bf16),
            pltpu.VMEM((1, 2, 2, 2, SHARE, WIDTH), bf16),
            pltpu.VMEM((2, 4, 4, 64, 768), bf16),
            pltpu.VMEM((2, 4, 4, 4, 64, 512), bf16),
            pltpu.VMEM((SHARE, WIDTH), bf16),
            pltpu.VMEM((SHARE, WIDTH), bf16),
            sems(8),
            sems(3),
            sems(3),
        ],
        0,
    )


SLOPE = 0.7978845608028654
CUBIC = 0.044715


def ffn_body(ins, outs, scratch, makers, ready):
    ffn_hbm, cot_hbm, up_hbm, down_hbm, middle_hbm, out_hbm, gains = ins
    sum_down, grad_up_out, layer_full, grad_middle_out, small, branch_share, grad_heads = outs
    (
        layer_out,
        middle,
        grad_up_weight,
        grad_middle,
        grad_tokens,
        ffn_in,
        cot,
        up_weight,
        down_weight,
        hidden,
        grad_up,
        back,
        ahead,
        grad_down_weight,
        back_share,
        ahead_share,
        load_sem,
    ) = scratch
    make_back, make_ahead, make_down, make_heads, make_layer = makers
    ylo, x, z, yhi, core = place()
    back_sum = make_back(back, back_share)
    ahead_sum = make_ahead(ahead, ahead_share)
    down_sum = make_down(grad_down_weight, sum_down)
    heads = make_heads(grad_tokens, grad_heads)
    layer_move = make_layer(layer_out, layer_full)
    own, partner = (pl.ds(pl.multiple_of(r * 512, 512), 512) for r in (ylo, 1 - ylo))
    loads = [
        fetched(ffn_hbm.at[own], ffn_in.at[own], load_sem.at[0]),
        fetched(up_hbm, up_weight, load_sem.at[1]),
        fetched(ffn_hbm.at[partner], ffn_in.at[partner], load_sem.at[2]),
        fetched(down_hbm, down_weight, load_sem.at[3]),
        fetched(cot_hbm, cot, load_sem.at[4]),
        fetched(middle_hbm, middle, load_sem.at[5]),
    ]

    def units(rows):
        def one(n, carry):
            columns = pl.ds(pl.multiple_of(n * 512, 512), 512)
            value = dot(ffn_in[rows], up_weight[:, columns])
            square = value * value
            bend = jnp.tanh(SLOPE * value * (1.0 + CUBIC * square))
            half = 0.5 * (1.0 + bend)
            hidden[rows, columns] = (value * half).astype(bf16)
            slope = half + 0.5 * value * (1.0 - bend * bend) * SLOPE * (1.0 + 3.0 * CUBIC * square)
            grad_up[rows, columns] = slope.astype(bf16)
            return carry

        lax.fori_loop(0, PART // 512, one, 0)

    def units_back(rows):
        def one(n, carry):
            columns = pl.ds(pl.multiple_of(n * 512, 512), 512)
            grad = dot(cot[rows], down_weight[:, columns])
            grad_up[rows, columns] = (grad * grad_up[rows, columns].astype(f32)).astype(bf16)
            return carry

        lax.fori_loop(0, PART // 512, one, 0)

    def spread_out(r, rows, source, weight, target):
        def one(n, carry):
            columns = pl.ds(pl.multiple_of(n * 512, 512), 512)
            value = turned_dot(source[rows], weight[columns]).astype(bf16)
            for c in range(2):
                for u in range(2):
                    at = (2 * c + u) * SHARE
                    target[r, c, u, :, columns] = value[at : at + SHARE]
            return carry

        lax.fori_loop(0, WIDTH // 512, one, 0)

    def weight_grad(left, right, target, first=0, last=WIDTH // 256):
        def one(n, carry):
            columns = pl.ds(pl.multiple_of(n * 256, 256), 256)
            value = outer_dot(left[:, columns], right[...]).astype(bf16)
            for j in range(4):
                target[lax.div(n, 4), lax.rem(n, 4), j] = value[64 * j : 64 * j + 64]
            return carry

        lax.fori_loop(first, last, one, 0)

    loads[0].wait()
    loads[1].wait()
    units(own)
    loads[2].wait()
    units(partner)
    loads[3].wait()
    spread_out(ylo, own, hidden, down_weight, ahead)
    ready()
    step(ahead_sum)
    spread_out(1 - ylo, partner, hidden, down_weight, ahead)
    step(ahead_sum, ahead_sum)
    loads[4].wait()
    weight_grad(cot, hidden, grad_down_weight)
    step(down_sum)
    step(ahead_sum)
    units_back(own)
    step(down_sum)
    spread_out(ylo, own, grad_up, up_weight, back)
    step(back_sum)
    step(down_sum)
    units_back(partner)
    step(back_sum)
    spread_out(1 - ylo, partner, grad_up, up_weight, back)
    step(back_sum)
    places = {}
    for h in range(2):
        for c in range(2):
            place_of = (up_weight, down_weight)[h].at[:, pl.ds(512 * c, 512)]
            places[h, c] = (place_of, fetched(out_hbm.at[c, h], place_of, load_sem.at[6 + 2 * h + c]))
    step(down_sum)
    weight_grad(ffn_in, grad_up, grad_up_weight, 0, 3)
    step(back_sum)
    step(down_sum)
    weight_grad(ffn_in, grad_up, grad_up_weight, 3, 6)
    step(down_sum)
    weight_grad(ffn_in, grad_up, grad_up_weight, 6, 8)
    writes = [fetched(grad_up_weight, grad_up_out, load_sem.at[0])]
    step(down_sum)
    finish(ahead_sum)
    loads[5].wait()

    def end(rows):
        layer_out[0, rows] = (middle[rows] + ahead_share[rows]).astype(bf16)

    some_rows(SHARE, 32, end)
    step(layer_move)
    finish(back_sum)
    gain = gains[pl.ds(2, 1)]
    small[...] = jnp.zeros_like(small)

    def back_norm(i, carry):
        at = pl.multiple_of(i * 32, 32)
        rows = pl.ds(at, 32)
        normed, inverse = standardize(middle[rows])
        value, grad_gain, grad_shift = norm_back(back_share[rows], normed, inverse, gain)
        here = pl.multiple_of(ylo * 512 + core * 256 + yhi * SHARE + at, 32)
        value += cot[pl.ds(here, 32)].astype(f32)
        grad_middle[rows] = value
        branch_share[rows] = value.astype(bf16)
        small[pl.ds(2, 1)] += grad_gain
        small[pl.ds(3, 1)] += grad_shift
        return carry

    lax.fori_loop(0, SHARE // 32, back_norm, 0)
    writes.append(fetched(grad_middle, grad_middle_out, load_sem.at[1]))
    for h in range(2):
        for c in range(2):
            place_of, load = places[h, c]
            load.wait()
            grad_tokens[:, pl.ds((h * 2 + c) * 512, 512)] = dot(branch_share[...], place_of[...]).astype(bf16)
    step(heads)
    step(layer_move)
    finish(down_sum, heads, layer_move)
    for write in writes:
        write.wait()


def feed_forward(ffn_in, cot, up, down, middle, out_weight, gains):
    return kernel_call(
        ffn_body,
        [share_sum(), share_sum(), weight_sum(), tokens_to_heads(), row_gather()],
        XZ + GROUP,
        [(ffn_in, ANY), (cot, ANY), (up, ANY), (down, ANY), (middle, ANY), (out_weight, ANY), (gains, VMEM)],
        [
            (shaped(bf16, 2, 64, PART), VMEM),
            (shaped(bf16, 2, 4, 4, 64, PART), ANY),
            (shaped(bf16, 1, 2, 2, SHARE, WIDTH), ANY),
            (shaped(f32, SHARE, WIDTH), ANY),
            (shaped(f32, 4, WIDTH), VMEM),
            (shaped(bf16, SHARE, WIDTH), VMEM),
            (shaped(bf16, 2, 2, 2, SHARE, 256), VMEM),
        ],
        [
            pltpu.VMEM((1, SHARE, WIDTH), bf16),
            pltpu.VMEM((SHARE, WIDTH), f32),
            pltpu.VMEM((2, 4, 4, 64, PART), bf16),
            pltpu.VMEM((SHARE, WIDTH), f32),
            pltpu.VMEM((SHARE, WIDTH), bf16),
            pltpu.VMEM((1024, WIDTH), bf16),
            pltpu.VMEM((1024, WIDTH), bf16),
            pltpu.VMEM((WIDTH, PART), bf16),
            pltpu.VMEM((WIDTH, PART), bf16),
            pltpu.VMEM((1024, PART), bf16),
            pltpu.VMEM((1024, PART), bf16),
            pltpu.VMEM((2, 2, 2, SHARE, WIDTH), bf16),
            pltpu.VMEM((2, 2, 2, SHARE, WIDTH), bf16),
            pltpu.VMEM((2, 4, 4, 64, PART), bf16),
            pltpu.VMEM((SHARE, WIDTH), f32),
            pltpu.VMEM((SHARE, WIDTH), f32),
            sems(10),
        ],
        2,
        62,
    )


def back_body(ins, outs, scratch, makers, ready):
    (
        attn_hbm,
        weight_hbm,
        up_hbm,
        projected_hbm,
        attended_hbm,
        mask_hbm,
        middle_hbm,
        inputs_hbm,
        branch_share,
        grad_heads,
        small_in,
        gains,
    ) = ins
    input_full, sum_up, sum_qkv, sum_out, small_out, branch_full = outs
    (
        projected,
        attended,
        mask,
        grad_middle,
        inputs_share,
        attn_in,
        weight,
        grad_up_weight,
        grad_qkv_weight,
        grad_out_weight,
        grad_branch,
        grad_projected,
        back,
        back_share,
        input_share,
        small,
        load_sem,
    ) = scratch
    make_up, make_qkv, make_out, make_branch, make_back, make_input, make_small = makers
    ylo, x, z, yhi, core = place()
    up_sum = make_up(grad_up_weight, sum_up)
    qkv_sum = make_qkv(grad_qkv_weight, sum_qkv)
    out_sum = make_out(grad_out_weight, sum_out)
    branch = make_branch(branch_share, branch_full)
    back_sum = make_back(back, back_share)
    input_move = make_input(input_share, input_full)
    small_sum = make_small(small, small_out)
    loads = [
        fetched(src, dst, load_sem.at[n])
        for n, (src, dst) in enumerate(
            (
                (projected_hbm, projected),
                (mask_hbm, mask),
                (up_hbm, grad_up_weight),
                (weight_hbm, weight),
                (attn_hbm, attn_in),
                (attended_hbm, attended),
                (inputs_hbm, inputs_share),
                (middle_hbm, grad_middle),
            )
        )
    ]

    def attend(r):
        for h in range(2):
            query = projected[r, :, pl.ds(h * HEAD, HEAD)]
            key = projected[r, :, pl.ds(256 + h * HEAD, HEAD)]
            value = projected[r, :, pl.ds(512 + h * HEAD, HEAD)]
            grad = grad_heads[r, :, :, :, pl.ds(h * HEAD, HEAD)].reshape(512, HEAD)
            scores = turned_dot(query, key) * HEAD ** (-0.5)
            scores = jnp.where(mask[r].astype(f32) > 0.5, scores, masked_score)
            expd = jnp.exp(scores - jnp.max(scores, axis=-1, keepdims=True))
            probs = expd / jnp.sum(expd, axis=-1, keepdims=True)
            grad_probs = turned_dot(grad, value)
            inner = jnp.sum(grad_probs * probs, axis=-1, keepdims=True)
            grad_scores = (probs * (grad_probs - inner)).astype(bf16)
            parts = (
                dot(grad_scores, key) * HEAD ** (-0.5),
                outer_dot(grad_scores, query) * HEAD ** (-0.5),
                outer_dot(probs.astype(bf16), grad),
            )
            for t in range(3):
                grad_projected[pl.ds(pl.multiple_of(r * 512, 512), 512), pl.ds(t * 256 + h * HEAD, HEAD)] = parts[
                    t
                ].astype(bf16)

    def spread_out(r):
        def one(n, carry):
            columns = pl.ds(pl.multiple_of(n * 512, 512), 512)
            rows = pl.ds(pl.multiple_of(r * 512, 512), 512)
            value = turned_dot(grad_projected[rows], weight[columns]).astype(bf16)
            for c in range(2):
                for u in range(2):
                    at = (2 * c + u) * SHARE
                    back[r, c, u, :, columns] = value[at : at + SHARE]
            return carry

        lax.fori_loop(0, WIDTH // 512, one, 0)

    def weight_grad(left, right, target):
        def one(n, carry):
            columns = pl.ds(pl.multiple_of(n * 256, 256), 256)
            value = outer_dot(left[..., columns].reshape(1024, 256), right).astype(bf16)
            for j in range(4):
                target[lax.div(n, 4), lax.rem(n, 4), j] = value[64 * j : 64 * j + 64]
            return carry

        lax.fori_loop(0, WIDTH // 256, one, 0)

    loads[0].wait()
    loads[1].wait()
    attend(ylo)
    ready()
    step(branch)
    loads[2].wait()
    step(up_sum)
    loads[3].wait()
    spread_out(ylo)
    step(back_sum)
    attend(1 - ylo)
    step(back_sum)
    step(up_sum)
    spread_out(1 - ylo)
    step(back_sum)
    step(up_sum)
    loads[4].wait()
    weight_grad(attn_in, grad_projected[...], grad_qkv_weight)
    step(branch)
    step(qkv_sum)
    step(back_sum)
    step(up_sum, up_sum)
    step(qkv_sum)
    finish(branch)
    gather_load = fetched(branch_full, grad_branch, load_sem.at[0])
    for load in loads[5:]:
        load.wait()
    step(qkv_sum, up_sum)
    gather_load.wait()
    weight_grad(grad_branch, attended[...].reshape(1024, 256), grad_out_weight)
    step(out_sum)
    finish(back_sum)
    gain = gains[pl.ds(0, 1)]
    small[...] = small_in[...]

    def back_norm(i, carry):
        rows = pl.ds(pl.multiple_of(i * 32, 32), 32)
        normed, inverse = standardize(inputs_share[rows])
        value, grad_gain, grad_shift = norm_back(back_share[rows], normed, inverse, gain)
        input_share[0, rows] = (grad_middle[rows] + value).astype(bf16)
        small[pl.ds(0, 1)] += grad_gain
        small[pl.ds(1, 1)] += grad_shift
        return carry

    lax.fori_loop(0, SHARE // 32, back_norm, 0)
    step(small_sum, input_move)
    step(up_sum, qkv_sum, out_sum, out_sum)
    step(small_sum, qkv_sum, out_sum, qkv_sum)
    step(small_sum, out_sum, qkv_sum, out_sum)
    step(qkv_sum, out_sum, input_move)
    finish(input_move, small_sum, up_sum, qkv_sum, out_sum)


def attention_back(
    attn_in,
    weight,
    grad_up_weight,
    projected,
    attended,
    mask,
    grad_middle,
    inputs_share,
    branch_share,
    grad_heads,
    small,
    gains,
):
    return kernel_call(
        back_body,
        [
            weight_sum(),
            weight_sum(768),
            weight_sum(256),
            share_gather(),
            share_sum(),
            row_gather(),
            small_reduce(),
        ],
        XZ + ["x2", "z2"] + GROUP,
        [
            (attn_in, ANY),
            (weight, ANY),
            (grad_up_weight, ANY),
            (projected, ANY),
            (attended, ANY),
            (mask, ANY),
            (grad_middle, ANY),
            (inputs_share, ANY),
            (branch_share, VMEM),
            (grad_heads, VMEM),
            (small, VMEM),
            (gains, VMEM),
        ],
        [
            (shaped(bf16, 1, 2, 2, SHARE, WIDTH), ANY),
            (shaped(bf16, 2, 64, PART), VMEM),
            (shaped(bf16, 2, 64, 768), VMEM),
            (shaped(bf16, 2, 64, 256), VMEM),
            (shaped(f32, 4, 128), VMEM),
            (shaped(bf16, 2, 2, 2, SHARE, WIDTH), ANY),
        ],
        [
            pltpu.VMEM((2, 512, 768), bf16),
            pltpu.VMEM((2, 2, 2, SHARE, 256), bf16),
            pltpu.VMEM((2, 512, 512), bf16),
            pltpu.VMEM((SHARE, WIDTH), f32),
            pltpu.VMEM((SHARE, WIDTH), f32),
            pltpu.VMEM((1024, WIDTH), bf16),
            pltpu.VMEM((WIDTH, 768), bf16),
            pltpu.VMEM((2, 4, 4, 64, PART), bf16),
            pltpu.VMEM((2, 4, 4, 64, 768), bf16),
            pltpu.VMEM((2, 4, 4, 64, 256), bf16),
            pltpu.VMEM((2, 2, 2, SHARE, WIDTH), bf16),
            pltpu.VMEM((1024, 768), bf16),
            pltpu.VMEM((2, 2, 2, SHARE, WIDTH), bf16),
            pltpu.VMEM((SHARE, WIDTH), f32),
            pltpu.VMEM((1, SHARE, WIDTH), bf16),
            pltpu.VMEM((4, WIDTH), f32),
            sems(8),
        ],
        3,
        62,
    )


def on_device(
    stream,
    code_ids,
    segment_ids,
    padding,
    codebook,
    norm1_gain,
    norm1_shift,
    w_qkv,
    w_out,
    norm2_gain,
    norm2_shift,
    w_up,
    w_down,
    cotangent,
):
    ylo, x, z, yhi, core = place()
    own_qkv = w_qkv.reshape(64, 3, 2, 256).transpose(2, 0, 1, 3).reshape(2, 64, 768)
    norms = jnp.stack([norm1_gain, norm1_shift, norm2_gain, norm2_shift] * 2)
    norms = jnp.concatenate([norms, norms], axis=1)
    (
        attn_in,
        qkv_full,
        out_full,
        cot,
        inputs_share,
        gains,
        allowed,
        projected,
        attended,
        middle,
        ffn_in,
        up_full,
        down_full,
    ) = forward(
        code_ids,
        segment_ids,
        padding,
        stream[0],
        cotangent[0],
        codebook,
        own_qkv,
        w_out,
        w_up,
        w_down,
        norms,
    )
    sum_down, grad_up_weight, layer_out, grad_middle, small, branch_share, grad_heads = feed_forward(
        ffn_in.reshape(1024, WIDTH),
        cot.reshape(1024, WIDTH),
        up_full.reshape(WIDTH, PART),
        down_full.reshape(WIDTH, PART),
        middle,
        out_full.reshape(2, 2, WIDTH, 512),
        gains,
    )
    input_grad, sum_up, sum_qkv, sum_out, small, _ = attention_back(
        attn_in.reshape(1024, WIDTH),
        qkv_full.reshape(WIDTH, 768),
        grad_up_weight,
        projected,
        attended,
        allowed,
        grad_middle,
        inputs_share,
        branch_share,
        grad_heads,
        small,
        gains,
    )

    sum_qkv, sum_out, sum_up, sum_down = (g.astype(f32) for g in (sum_qkv, sum_out, sum_up, sum_down))
    out_qkv = sum_qkv.reshape(2, 64, 3, 256).transpose(1, 2, 0, 3).reshape(64, 3, 512)
    out_out = sum_out.transpose(1, 0, 2).reshape(64, 512)
    out_up = sum_up.transpose(1, 0, 2).reshape(64, WIDTH)
    out_down = sum_down.transpose(1, 0, 2).reshape(64, WIDTH)
    odd = lax.rem(z, 2) == 1
    small = jnp.where(odd, small[:, 64:], small[:, :64])
    return (
        layer_out.reshape(1, 512, WIDTH).astype(f32),
        input_grad.reshape(1, 512, WIDTH).astype(f32),
        small[0],
        small[1],
        out_qkv,
        out_out,
        small[2],
        small[3],
        out_up,
        out_down,
    )


def solution(mesh):
    in_specs = (
        P("dp", None, None),
        P("dp", None),
        P("dp", None),
        P("dp", None),
        P(),
        P("dp"),
        P("dp"),
        P("dp", None, "mp"),
        P("dp", "mp"),
        P("dp"),
        P("dp"),
        P("dp", "mp"),
        P("dp", "mp"),
        P("dp", None, None),
    )
    out_specs = (
        P("dp", None, None),
        P("dp", None, None),
        P("dp"),
        P("dp"),
        P("dp", None, "mp"),
        P("dp", "mp"),
        P("dp"),
        P("dp"),
        P("dp", "mp"),
        P("dp", "mp"),
    )
    return jax.shard_map(
        on_device, mesh=mesh, in_specs=in_specs, out_specs=out_specs, check_vma=False
    )
```

```python
import functools

import jax
import jax.numpy as jnp
from jax import lax
from jax.experimental import pallas as pl
from jax.experimental.pallas import tpu as pltpu
from jax.sharding import PartitionSpec as P

HEAD = 128
WIDTH = 2048
SHARE = 128
PART = 1024
MESH = pl.DeviceIdType.MESH
ANY = pl.BlockSpec(memory_space=pl.ANY)
VMEM = pl.BlockSpec(memory_space=pltpu.VMEM)
masked_score = -1000000000.0
epsilon = 1e-05
f32 = jnp.float32
bf16 = jnp.bfloat16


def place():
    dp, mp = lax.axis_index("dp"), lax.axis_index("mp")
    return lax.div(dp, 16), lax.rem(lax.div(dp, 4), 4), lax.rem(dp, 4), lax.div(mp, 2), lax.rem(mp, 2)


def ring(position, step):
    return lax.rem(position + step + 4, 4)


def xz_neighbour(axis, step):
    ylo, x, z, yhi, core = place()
    if axis == 0:
        x = ring(x, step)
    else:
        z = ring(z, step)
    return (ylo * 16 + x * 4 + z, yhi * 2 + core)


def y_peer(step):
    ylo, x, z, yhi, core = place()
    y = ring(yhi * 2 + ylo, step)
    return (lax.rem(y, 2) * 16 + x * 4 + z, lax.div(y, 2) * 2 + core)


def lo_partner():
    ylo, x, z, yhi, core = place()
    return ((1 - ylo) * 16 + x * 4 + z, yhi * 2 + core)


def core_partner():
    ylo, x, z, yhi, core = place()
    return (ylo * 16 + x * 4 + z, yhi * 2 + 1 - core)


def greet(peers):
    barrier = pltpu.get_barrier_semaphore()
    for peer in peers:
        pl.semaphore_signal(barrier, inc=1, device_id=peer, device_id_type=MESH)
    return lambda: pl.semaphore_wait(barrier, len(peers))


def remote(src, dst, send_sem, recv_sem, peer):
    return pltpu.make_async_remote_copy(
        src_ref=src,
        dst_ref=dst,
        send_sem=send_sem,
        recv_sem=recv_sem,
        device_id=peer,
        device_id_type=MESH,
    )


def sems(*shape):
    return pltpu.SemaphoreType.DMA(shape)


def params(collective_id, mib=48):
    return pltpu.CompilerParams(
        collective_id=collective_id, has_side_effects=True, vmem_limit_bytes=mib << 20
    )


PEERS = {
    "core": core_partner,
    "x+": lambda: xz_neighbour(0, 1),
    "x-": lambda: xz_neighbour(0, -1),
    "z+": lambda: xz_neighbour(1, 1),
    "z-": lambda: xz_neighbour(1, -1),
    "x2": lambda: xz_neighbour(0, 2),
    "z2": lambda: xz_neighbour(1, 2),
    "y1": lambda: y_peer(1),
    "y2": lambda: y_peer(2),
    "y3": lambda: y_peer(3),
}


def diagonal_peer(step):
    dp, mp = y_peer(step)
    return (dp, mp + 1 - 2 * lax.rem(mp, 2))


PEERS.update({f"d{k}": functools.partial(diagonal_peer, k) for k in range(1, 4)})
GROUP = ["y1", "y2", "y3", "core", "d1", "d2", "d3"]


def kernel_call(body, jobs, peers, ins, outs, scratch, collective_id, mib=56):
    def kernel(*refs):
        taken = 0

        def take(count):
            nonlocal taken
            taken += count
            return refs[taken - count : taken]

        groups = [take(len(ins)), take(len(outs)), take(len(scratch))]
        makers = []
        for job in jobs:
            own = take(len(job["scratch"]))
            makers.append(lambda *given, job=job, own=own: job["steps"](*given, *own))
        ready = greet([PEERS[name]() for name in peers])
        body(*groups, makers, ready)

    return pl.pallas_call(
        kernel,
        out_shape=[shape for shape, _ in outs],
        in_specs=[spec for _, spec in ins],
        out_specs=[spec for _, spec in outs],
        scratch_shapes=scratch + [one for job in jobs for one in job["scratch"]],
        compiler_params=params(collective_id, mib),
    )(*[array for array, _ in ins])


def finish(*runs):
    for run in runs:
        for _ in run:
            pass


def step(*runs):
    for run in runs:
        next(run, None)


def shaped(dtype, *shape):
    return jax.ShapeDtypeStruct(shape, dtype)


def small_gather():
    def steps(own, everyone, send, recv):
        ylo, x, z, yhi, core = place()
        sent = []

        def go(here, n, peer):
            copy = remote(here, here, send.at[n], recv.at[n], peer)
            copy.start()
            sent.append(copy)

        def came(here, n):
            remote(here, here, send.at[n], recv.at[n], lo_partner()).wait_recv()

        everyone[ylo, x, z] = own[...]
        go(everyone.at[ylo, x, z], 0, lo_partner())
        yield
        came(everyone.at[1 - ylo, x, z], 0)
        for k in (1, 2, 3):
            go(everyone.at[:, x, z], k, xz_neighbour(0, k))
        yield
        for k in (1, 2, 3):
            came(everyone.at[:, ring(x, -k), z], k)
        for k in (1, 2, 3):
            go(everyone.at[:, :, z], 3 + k, xz_neighbour(1, k))
        yield
        for k in (1, 2, 3):
            came(everyone.at[:, :, ring(z, -k)], 3 + k)
        for copy in sent:
            copy.wait_send()

    return {"scratch": [sems(7), sems(7)], "steps": steps}


def small_reduce():
    def steps(rows, out, of_group, of_x, of_z, half, quarter, send, recv):
        ylo, x, z, yhi, core = place()
        y = yhi * 2 + ylo
        waits = []

        def go(src, dst, n, peer):
            copy = remote(src, dst, send.at[n], recv.at[n], peer)
            copy.start()
            waits.append(copy)

        def lanes(start, size):
            return pl.ds(pl.multiple_of(start, size), size)

        for n, (k, flip) in enumerate(((1, 0), (1, 1), (2, 0), (2, 1), (3, 0), (3, 1), (0, 1))):
            theirs = lanes(lax.rem(ring(y, k), 2) * 1024, 1024)
            go(rows.at[:, theirs], of_group.at[n], n, diagonal_peer(k) if flip else y_peer(k))
        yield
        for copy in waits:
            copy.wait_recv()
        total = rows[:, lanes(ylo * 1024, 1024)]
        for n in range(7):
            total += of_group[n]
        half[...] = total
        for k in (1, 2, 3):
            go(half.at[:, lanes(ring(x, k) * 256, 256)], of_x.at[k - 1], 6 + k, xz_neighbour(0, k))
        yield
        for copy in waits[7:]:
            copy.wait_recv()
        total = half[:, lanes(x * 256, 256)]
        for n in range(3):
            total += of_x[n]
        quarter[...] = total
        for k in (1, 2, 3):
            theirs = lanes(lax.div(ring(z, k), 2) * 128, 128)
            go(quarter.at[:, theirs], of_z.at[k - 1], 9 + k, xz_neighbour(1, k))
        yield
        for copy in waits[10:]:
            copy.wait_recv()
        total = quarter[:, lanes(lax.div(z, 2) * 128, 128)]
        for n in range(3):
            total += of_z[n]
        out[...] = total
        for copy in waits:
            copy.wait_send()

    return {
        "scratch": [
            pltpu.VMEM((7, 4, 1024), f32),
            pltpu.VMEM((3, 4, 256), f32),
            pltpu.VMEM((3, 4, 128), f32),
            pltpu.VMEM((4, 1024), f32),
            pltpu.VMEM((4, 256), f32),
            sems(13),
            sems(13),
        ],
        "steps": steps,
    }


def row_exchange(count=1):
    def steps(halves, full, local_sem, send, recv):
        ylo, x, z, yhi, core = place()
        up, down, other = y_peer(1), y_peer(3), core_partner()
        first = []
        for n in range(count):
            for u, peer in ((0, up), (1, down)):
                here = full.at[n, ylo, core, u]
                first.append(remote(halves.at[n, u], here, send.at[n, u], recv.at[n, u], peer))
        for n in range(count):
            here = full.at[n, ylo, core]
            first.append(remote(halves.at[n], here, send.at[n, 2], recv.at[n, 2], other))
        for copy in first:
            copy.start()
        local = [
            pltpu.make_async_copy(halves.at[n], full.at[n, ylo, core], local_sem.at[n])
            for n in range(count)
        ]
        for copy in local:
            copy.start()
        yield
        second = []
        for n in range(count):
            for u in range(2):
                here = full.at[n, 1 - ylo, core, u]
                remote(halves.at[n, u], here, send.at[n, u], recv.at[n, u], up).wait_recv()
                copy = remote(here, here, send.at[n, 3 + u], recv.at[n, 3 + u], other)
                copy.start()
                second.append(copy)
        yield
        for n in range(count):
            here = full.at[n, ylo, 1 - core]
            remote(halves.at[n], here, send.at[n, 2], recv.at[n, 2], other).wait_recv()
            for u in range(2):
                here = full.at[n, 1 - ylo, 1 - core, u]
                remote(here, here, send.at[n, 3 + u], recv.at[n, 3 + u], other).wait_recv()
        for copy in first + second:
            copy.wait_send()
        for copy in local:
            copy.wait()

    return {
        "scratch": [sems(count), sems(count, 5), sems(count, 5)],
        "steps": steps,
    }


def share_gather():
    def steps(share, full, local_sem, send, recv):
        ylo, x, z, yhi, core = place()
        y = yhi * 2 + ylo
        other = core_partner()
        half = SHARE // 2
        sent = []

        def of(step, half_core):
            source = ring(y, step)
            return full.at[lax.rem(source, 2), half_core, lax.div(source, 2)]

        def go(src, dst, n, peer):
            copy = remote(src, dst, send.at[n], recv.at[n], peer)
            copy.start()
            sent.append(copy)

        def came(dst, n):
            remote(dst, dst, send.at[n], recv.at[n], other).wait_recv()

        local = pltpu.make_async_copy(share, of(0, core), local_sem)
        go(share, of(0, core), 0, y_peer(1))
        go(share, of(0, core), 1, y_peer(3))
        go(share, of(0, core), 2, other)
        local.start()
        yield
        for n, step_back, rows, onward in ((0, 3, pl.ds(0, half), 1), (1, 1, pl.ds(half, half), 3)):
            here = of(step_back, core)
            came(here, n)
            go(here.at[rows], here.at[rows], 3 + n, y_peer(onward))
            go(here, here, 5 + n, other)
        yield
        far = of(2, core)
        came(far.at[pl.ds(0, half)], 3)
        came(far.at[pl.ds(half, half)], 4)
        go(far, far, 7, other)
        yield
        came(of(0, 1 - core), 2)
        came(of(3, 1 - core), 5)
        came(of(1, 1 - core), 6)
        came(of(2, 1 - core), 7)
        for copy in sent:
            copy.wait_send()
        local.wait()

    return {"scratch": [pltpu.SemaphoreType.DMA, sems(8), sems(8)], "steps": steps}


def add_rows(count, one):
    def body(i, carry):
        one(pl.ds(pl.multiple_of(i * 16, 16), 16))
        return carry

    lax.fori_loop(0, count // 16, body, 0)


def share_sum():
    def steps(partial, out, from_core, via, arrived, send, recv, send_two, recv_two):
        ylo, x, z, yhi, core = place()
        y = yhi * 2 + ylo
        other = core_partner()
        half = SHARE // 2

        def block(k, half_core):
            target = ring(y, k)
            return partial.at[lax.rem(target, 2), half_core, lax.div(target, 2)]

        first, second = {}, {}

        def to_core(order):
            for k in order:
                first[k] = remote(block(k, 1 - core), from_core.at[k], send.at[k], recv.at[k], other)
                first[k].start()

        to_core((2, 0))
        yield
        first[2].wait_recv()
        far = block(2, core)

        def add_far(rows):
            far[rows] = (far[rows].astype(f32) + from_core[2, rows].astype(f32)).astype(bf16)

        add_rows(SHARE, add_far)
        for n, k in ((0, 1), (1, 3)):
            second[n] = remote(
                far.at[pl.ds(half * n, half)], via.at[n], send_two.at[n], recv_two.at[n], y_peer(k)
            )
            second[n].start()
        yield
        to_core((1, 3))
        yield
        for n, k in ((0, 1), (1, 3)):
            first[k].wait_recv()
            second[n].wait_recv()
            near = block(k, core)

            def add_via(i, carry):
                at = pl.multiple_of(i * 16, 16)
                rows, with_via = pl.ds(at, 16), pl.ds(pl.multiple_of(half * n + at, 16), 16)
                value = near[with_via].astype(f32) + from_core[k, with_via].astype(f32)
                near[with_via] = (value + via[n, rows].astype(f32)).astype(bf16)
                plain = pl.ds(pl.multiple_of(half * (1 - n) + at, 16), 16)
                value = near[plain].astype(f32) + from_core[k, plain].astype(f32)
                near[plain] = value.astype(bf16)
                return carry

            lax.fori_loop(0, half // 16, add_via, 0)
            second[2 + n] = remote(near, arrived.at[n], send_two.at[2 + n], recv_two.at[2 + n], y_peer(k))
            second[2 + n].start()
        yield
        first[0].wait_recv()
        second[2].wait_recv()
        second[3].wait_recv()
        mine_own = block(0, core)

        def total(rows):
            value = mine_own[rows].astype(f32) + from_core[0, rows].astype(f32)
            out[rows] = value + arrived[0, rows].astype(f32) + arrived[1, rows].astype(f32)

        add_rows(SHARE, total)
        for k in range(4):
            first[k].wait_send()
            second[k].wait_send()

    return {
        "scratch": [
            pltpu.VMEM((4, SHARE, WIDTH), bf16),
            pltpu.VMEM((2, SHARE // 2, WIDTH), bf16),
            pltpu.VMEM((2, SHARE, WIDTH), bf16),
        ]
        + [sems(4)] * 4,
        "steps": steps,
    }


def feature_start(ylo, yhi, core):
    return pl.multiple_of((yhi * 2 + core) * 512 + ylo * 256, 256)


def heads_to_tokens():
    def steps(heads, tokens, send, recv):
        ylo, x, z, yhi, core = place()
        y = yhi * 2 + ylo
        mine = tokens.at[:, pl.ds(feature_start(ylo, yhi, core), 256)]
        sent = []

        def go(k, flip):
            target = ring(y, k)
            half = 1 - core if flip else core
            peer = diagonal_peer(k) if flip else y_peer(k)
            src = heads.at[lax.rem(target, 2), half, lax.div(target, 2)]
            copy = remote(src, mine, send.at[2 * k + flip], recv.at[2 * k + flip], peer)
            copy.start()
            sent.append(copy)

        for k in (1, 3):
            for flip in (0, 1):
                go(k, flip)
        yield
        for k, flip in ((2, 0), (2, 1), (0, 1)):
            go(k, flip)
        tokens[:, pl.ds(feature_start(ylo, yhi, core), 256)] = heads[ylo, core, yhi]
        yield
        for k, flip in ((1, 0), (1, 1), (3, 0), (3, 1), (2, 0), (2, 1), (0, 1)):
            source = ring(y, -k)
            half = 1 - core if flip else core
            start = feature_start(lax.rem(source, 2), lax.div(source, 2), half)
            here = tokens.at[:, pl.ds(start, 256)]
            remote(heads.at[0, 0, 0], here, send.at[2 * k + flip], recv.at[2 * k + flip], y_peer(1)).wait_recv()
        for copy in sent:
            copy.wait_send()

    return {"scratch": [sems(8), sems(8)], "steps": steps}


def tokens_to_heads():
    def steps(tokens, heads, send, recv):
        ylo, x, z, yhi, core = place()
        y = yhi * 2 + ylo
        mine = heads.at[ylo, core, yhi]
        sent = []
        order = ((1, 0), (1, 1), (3, 0), (3, 1), (2, 0), (2, 1), (0, 1))
        for k, flip in order:
            target = ring(y, k)
            half = 1 - core if flip else core
            peer = diagonal_peer(k) if flip else y_peer(k)
            start = feature_start(lax.rem(target, 2), lax.div(target, 2), half)
            src = tokens.at[:, pl.ds(start, 256)]
            copy = remote(src, mine, send.at[2 * k + flip], recv.at[2 * k + flip], peer)
            copy.start()
            sent.append(copy)
        heads[ylo, core, yhi] = tokens[:, pl.ds(feature_start(ylo, yhi, core), 256)]
        yield
        for k, flip in order:
            source = ring(y, -k)
            half = 1 - core if flip else core
            here = heads.at[lax.rem(source, 2), half, lax.div(source, 2)]
            remote(here, here, send.at[2 * k + flip], recv.at[2 * k + flip], y_peer(1)).wait_recv()
        for copy in sent:
            copy.wait_send()

    return {"scratch": [sems(8), sems(8)], "steps": steps}


def row_gather():
    def steps(share, full, local_sem, send, recv):
        ylo, x, z, yhi, core = place()
        across, other = y_peer(2), core_partner()
        mine = full.at[:, core, yhi]
        far = full.at[:, core, 1 - yhi]
        local = pltpu.make_async_copy(share, mine, local_sem)
        one = remote(share, mine, send.at[0], recv.at[0], across)
        two = remote(share, mine, send.at[1], recv.at[1], other)
        one.start()
        two.start()
        local.start()
        yield
        remote(share, far, send.at[0], recv.at[0], across).wait_recv()
        three = remote(far, far, send.at[2], recv.at[2], other)
        three.start()
        yield
        remote(share, full.at[:, 1 - core, yhi], send.at[1], recv.at[1], other).wait_recv()
        last = full.at[:, 1 - core, 1 - yhi]
        remote(last, last, send.at[2], recv.at[2], other).wait_recv()
        for copy in (one, two, three):
            copy.wait_send()
        local.wait()

    return {
        "scratch": [pltpu.SemaphoreType.DMA, sems(3), sems(3)],
        "steps": steps,
    }


SIGNS = (1, -1)
XZ = ["x+", "x-", "z+", "z-"]


def xz_near():
    return [[xz_neighbour(axis, d) for d in SIGNS] for axis in (0, 1)]


def weight_gather(columns, spread=False, flat=False, phases=(0, 1)):
    count = 4 if spread else 2

    def steps(own, full, local_sem, swap_send, swap_recv, send, recv):
        ylo, x, z, yhi, core = place()
        y = yhi * 2 + ylo
        near = xz_near()
        offsets = (0, -1, 1, 2)

        def move(src, dst, s, r, stage, d, axis):
            n = ((s * 2 + r) * 8 + stage) * 2 + d
            return remote(src, dst, send.at[n], recv.at[n], near[axis][d])

        def origin(s):
            if spread:
                return ring(y, offsets[s])
            return ylo if s == 0 else 1 - ylo

        def block(s, r, one, two, rows):
            if r == 0:
                return full.at[origin(s), ring(x, one), ring(z, two), rows]
            return full.at[origin(s), ring(x, two), ring(z, one), rows]

        def rows_of(r, d=None):
            return pl.ds(32 * r, 32) if d is None else pl.ds(32 * r + 16 * d, 16)

        def half(n):
            if flat:
                return own.at[:, pl.ds(pl.multiple_of(n * columns, columns), columns)]
            return own.at[n]

        sent = []

        def go(*args):
            copy = move(*args)
            copy.start()
            sent.append(copy)

        swaps = []
        if 0 in phases:
            mine = own if spread else half(ylo)
            here = full.at[origin(0), x, z]
            local = pltpu.make_async_copy(mine, here, local_sem)
            for s in range(1, count):
                peer = y_peer((4 - offsets[s]) % 4) if spread else lo_partner()
                src = own if spread else half(1 - ylo)
                swaps.append(remote(src, here, swap_send.at[s], swap_recv.at[s], peer))
            for swap in swaps:
                swap.start()
            def begin(s, source):
                for r in range(2):
                    for d in range(2):
                        src = source.at[rows_of(r)]
                        go(src, block(s, r, 0, 0, rows_of(r)), s, r, 0, d, r)
                for r in range(2):
                    for d in range(2):
                        src = source.at[rows_of(r)]
                        go(src, block(s, r, 0, 0, rows_of(r)), s, r, 2, d, 1 - r)

            begin(0, mine)
            local.start()
            yield
            for s in range(1, count):
                came = full.at[origin(s), x, z]
                remote(came, came, swap_send.at[s], swap_recv.at[s], lo_partner()).wait_recv()
                begin(s, came)
            yield
            for s in range(count):
                for r in range(2):
                    for d in range(2):
                        came = block(s, r, -SIGNS[d], 0, rows_of(r))
                        move(came, came, s, r, 0, d, r).wait_recv()
                        piece = block(s, r, -SIGNS[d], 0, rows_of(r, d))
                        go(piece, piece, s, r, 1, d, r)
                    for part in (1, 2):
                        for d in range(2):
                            came = block(s, r, offsets[part], 0, rows_of(r))
                            go(came, came, s, r, 2 + part, d, 1 - r)
                if s % 2:
                    yield
            for s in range(count):
                for r in range(2):
                    for d in range(2):
                        piece = block(s, r, 2, 0, rows_of(r, d))
                        move(piece, piece, s, r, 1, d, r).wait_recv()
                    for d in range(2):
                        came = block(s, r, 2, 0, rows_of(r))
                        go(came, came, s, r, 5, d, 1 - r)
                if s % 2:
                    yield

        def line_came(part, s, r, d):
            came = block(s, r, offsets[part], -SIGNS[d], rows_of(r))
            if 0 in phases:
                move(came, came, s, r, 2 + part, d, 1 - r).wait_recv()
            return came

        for part in (0, 2, 1, 3):
            d = part // 2
            for s in range(count):
                for r in range(2):
                    came = line_came(part, s, r, d)
                    if 1 in phases:
                        go(came, came, s, r, 6 + part % 2, d, 1 - r)
            if 0 in phases:
                yield
        for s in range(count):
            for r in range(2):
                for part in range(4):
                    line_came(part, s, r, 1 - part // 2)
        if 0 in phases:
            local.wait()
        yield
        if 1 in phases:
            for s in range(count):
                for r in range(2):
                    for part in range(4):
                        d = part // 2
                        came = block(s, r, offsets[part], 2, rows_of(r))
                        move(came, came, s, r, 6 + part % 2, d, 1 - r).wait_recv()
        for copy in sent + swaps:
            copy.wait_send()

    return {
        "scratch": [pltpu.SemaphoreType.DMA, sems(count), sems(count), sems(32 * count), sems(32 * count)],
        "steps": steps,
    }


def gathered(columns, count=2):
    return (shaped(bf16, count, 4, 4, 64, columns), ANY)


def weight_sum(columns=PART):
    def steps(grads, out, wide, thin, total, swap_send, swap_recv, send, recv):
        ylo, x, z, yhi, core = place()
        near = xz_near()
        partner = lo_partner()

        def move(src, dst, s, r, stage, d, axis):
            n = ((s * 2 + r) * 6 + stage) * 2 + d
            return remote(src, dst, send.at[n], recv.at[n], near[axis][d])

        def line(s, r, step, part):
            if r == 0:
                return grads.at[s, part, ring(z, step), pl.ds(0, 32)]
            return grads.at[s, ring(x, step), part, pl.ds(32, 32)]

        def block(s, r, step, rows):
            if r == 0:
                return grads.at[s, ring(x, step), z, rows]
            return grads.at[s, x, ring(z, step), rows]

        def wide_move(s, r, d, kind):
            if kind == 0:
                src = line(s, r, 2, pl.ds(2 * d, 2))
            elif kind == 1:
                src = line(s, r, SIGNS[d], pl.ds(2 - 2 * d, 2))
            else:
                src = line(s, r, SIGNS[d], pl.ds(2 * d, 2))
            return move(src, wide.at[s, r, kind, d], s, r, kind, d, 1 - r)

        def thin_move(s, r, d, kind):
            if kind == 0:
                src = block(s, r, 2, pl.ds(32 * r + 16 * d, 16))
            elif kind == 1:
                src = block(s, r, SIGNS[d], pl.ds(32 * r + 16 - 16 * d, 16))
            else:
                src = block(s, r, SIGNS[d], pl.ds(32 * r + 16 * d, 16))
            return move(src, thin.at[s, r, kind, d], s, r, 3 + kind, d, r)

        for s in range(2):
            for kind in range(2):
                for r in range(2):
                    for d in range(2):
                        wide_move(s, r, d, kind).start()
        yield

        for s in range(2):
            for r in range(2):
                for d in range(2):
                    wide_move(s, r, d, 0).wait_recv()
                    for p in range(2):
                        mine = line(s, r, SIGNS[d], 2 * d + p)

                        def one(rows):
                            value = mine[rows].astype(f32) + wide[s, r, 0, d, p, rows].astype(f32)
                            mine[rows] = value.astype(bf16)

                        add_rows(32, one)
                    wide_move(s, r, d, 2).start()
            yield

        for s in range(2):
            for r in range(2):
                for d in range(2):
                    wide_move(s, r, d, 1).wait_recv()
                    wide_move(s, r, d, 2).wait_recv()
                for p in range(4):
                    mine = line(s, r, 0, p)
                    d = p // 2

                    def one(rows):
                        value = mine[rows].astype(f32) + wide[s, r, 2, d, p % 2, rows].astype(f32)
                        value += wide[s, r, 1, 1 - d, p % 2, rows].astype(f32)
                        mine[rows] = value.astype(bf16)

                    add_rows(32, one)
                for kind in range(2):
                    for d in range(2):
                        thin_move(s, r, d, kind).start()
            yield

        for s in range(2):
            for r in range(2):
                for d in range(2):
                    thin_move(s, r, d, 0).wait_recv()
                    mine = block(s, r, SIGNS[d], pl.ds(32 * r + 16 * d, 16))
                    value = mine[...].astype(f32) + thin[s, r, 0, d].astype(f32)
                    mine[...] = value.astype(bf16)
                    thin_move(s, r, d, 2).start()
        yield

        for s in range(2):
            for r in range(2):
                for d in range(2):
                    thin_move(s, r, d, 1).wait_recv()
                    thin_move(s, r, d, 2).wait_recv()
                for d in range(2):
                    rows = pl.ds(32 * r + 16 * d, 16)
                    value = block(s, r, 0, rows)[...].astype(f32) + thin[s, r, 2, d].astype(f32)
                    value += thin[s, r, 1, 1 - d].astype(f32)
                    total[s, rows] = value.astype(bf16)
        swap = remote(total.at[1 - ylo], out.at[ylo], swap_send, swap_recv, partner)
        swap.start()
        out[ylo] = total[ylo]
        yield
        for s in range(2):
            for r in range(2):
                for d in range(2):
                    for kind in range(3):
                        wide_move(s, r, d, kind).wait_send()
                        thin_move(s, r, d, kind).wait_send()
        remote(total.at[0], out.at[1 - ylo], swap_send, swap_recv, partner).wait_recv()
        swap.wait_send()

    return {
        "scratch": [
            pltpu.VMEM((2, 2, 3, 2, 2, 32, columns), bf16),
            pltpu.VMEM((2, 2, 3, 2, 16, columns), bf16),
            pltpu.VMEM((2, 64, columns), bf16),
            pltpu.SemaphoreType.DMA,
            pltpu.SemaphoreType.DMA,
            sems(48),
            sems(48),
        ],
        "steps": steps,
    }


def standardize(value):
    mean = jnp.mean(value, axis=-1, keepdims=True)
    centered = value - mean
    scale_inv = lax.rsqrt(jnp.mean(centered * centered, axis=-1, keepdims=True) + epsilon)
    return (centered * scale_inv, scale_inv)


def norm_back(grad_normed_out, normed, scale_inv, gain):
    scaled = grad_normed_out * gain
    mean_one = jnp.mean(scaled, axis=-1, keepdims=True)
    mean_two = jnp.mean(scaled * normed, axis=-1, keepdims=True)
    grad_value = scale_inv * (scaled - mean_one - normed * mean_two)
    grad_gain = jnp.sum(grad_normed_out * normed, axis=0, keepdims=True)
    grad_shift = jnp.sum(grad_normed_out, axis=0, keepdims=True)
    return (grad_value, grad_gain, grad_shift)


def dot(a, b):
    return jnp.dot(a, b, preferred_element_type=f32)


def turned_dot(a, b):
    return lax.dot_general(a, b, (((1,), (1,)), ((), ())), preferred_element_type=f32)


def outer_dot(a, b):
    return lax.dot_general(a, b, (((0,), (0,)), ((), ())), preferred_element_type=f32)


def some_rows(count, size, one):
    def body(i, carry):
        one(pl.ds(pl.multiple_of(i * size, size), size))
        return carry

    lax.fori_loop(0, count // size, body, 0)


def fetched(src, dst, sem):
    copy = pltpu.make_async_copy(src, dst, sem)
    copy.start()
    return copy


CODES = 4096
CODE_CHUNK = 1024


def forward_body(ins, outs, scratch, makers, ready):
    ids, segments, padding, stream_hbm, cot_hbm, codebook, own_qkv, own_out, own_up, own_down, norms = ins
    (
        attn_out,
        qkv_out,
        out_weight_out,
        cot_full,
        inputs_out,
        gains,
        mask_out,
        projected_out,
        attended_out,
        middle_out,
        ffn_full,
        up_full,
        down_full,
    ) = outs
    (
        inputs_share,
        mask,
        projected,
        attended,
        middle,
        everyone,
        norm_tile,
        other_segments,
        other_padding,
        chunk,
        total,
        stream,
        cot_half,
        halves,
        attn_in,
        weight,
        out_weight,
        tokens,
        ffn_share,
        load_sem,
        swap_send,
        swap_recv,
    ) = scratch
    make_small, make_qkv, make_out, make_up, make_down, make_cot, make_attn, make_heads, make_share = makers
    ylo, x, z, yhi, core = place()
    small = make_small(norm_tile, everyone)
    qkv = make_qkv(own_qkv, weight)
    out = make_out(own_out, out_weight.at[core])
    up, down = make_up(own_up, up_full), make_down(own_down, down_full)
    cot_move = make_cot(cot_half, cot_full)
    attn_move = make_attn(halves, attn_in)
    heads = make_heads(attended, tokens)
    spread = make_share(ffn_share, ffn_full)

    def fetch(j):
        rows = pl.ds(j * CODE_CHUNK, CODE_CHUNK)
        return pltpu.make_async_copy(codebook.at[rows], chunk.at[j % 2], load_sem.at[j % 2])

    mine = pl.ds(pl.multiple_of(core * 256, 256), 256)
    loads = [fetched(stream_hbm.at[mine], stream, load_sem.at[2])]
    for u in range(2):
        rows = pl.ds(pl.multiple_of(core * 256 + u * SHARE, SHARE), SHARE)
        loads.append(fetched(cot_hbm.at[rows], cot_half.at[0, u], load_sem.at[3 + u]))
    fetch(0).start()
    lane = lax.broadcasted_iota(jnp.int32, (8, 128), 1)
    norm_tile[...] = jnp.where(lax.div(lane, 64) == lax.rem(z, 2), norms[...].astype(f32), 0.0)
    ready()
    step(small, qkv, out)
    row_swaps = [
        remote(segments, other_segments, swap_send.at[0], swap_recv.at[0], lo_partner()),
        remote(padding, other_padding, swap_send.at[1], swap_recv.at[1], lo_partner()),
    ]
    for swap in row_swaps:
        swap.start()
    for load in loads:
        load.wait()
    step(cot_move)
    total[...] = stream[...].astype(f32)
    my_ids = ids[:, mine]
    count = CODES // CODE_CHUNK
    for j in range(count):
        if j + 1 < count:
            fetch(j + 1).start()
        fetch(j).wait()
        code = lax.broadcasted_iota(jnp.int32, (CODE_CHUNK, 256), 0) + j * CODE_CHUNK
        pick = jnp.where(my_ids == code, 1.0, 0.0).astype(bf16)
        for part in range(2):
            columns = pl.ds(part * 1024, 1024)
            total[:, columns] += outer_dot(pick, chunk[j % 2, :, columns])
        step(small, (qkv, out, qkv, out)[j])
    finish(small)
    for t in range(16):
        at = (t // 8, t // 2 % 4, t % 2 * 2)
        pair = everyone[at] + everyone[at[0], at[1], at[2] + 1]
        gains[:, pl.ds(128 * t, 128)] = pair
    gain, shift = gains[pl.ds(0, 1)], gains[pl.ds(1, 1)]
    for u in range(2):

        def norm(rows):
            value = total[pl.ds(pl.multiple_of(u * SHARE + rows.start, 32), 32)]
            normed, _ = standardize(value)
            halves[0, u, rows] = (normed * gain + shift).astype(bf16)

        some_rows(SHARE, 32, norm)
    step(attn_move, qkv, out)

    def keep(rows):
        inputs_share[rows] = total[pl.ds(pl.multiple_of(yhi * SHARE + rows.start, 32), 32)]

    some_rows(SHARE, 32, keep)
    step(qkv, qkv)

    def see(r, segment_row, padding_row):
        turned = jnp.broadcast_to(segment_row.astype(f32), (SHARE, 512)).T[:, 0:1]
        query = lax.broadcasted_iota(jnp.int32, (512, 512), 0)
        key = lax.broadcasted_iota(jnp.int32, (512, 512), 1)
        same = turned == segment_row.astype(f32)
        live = (padding_row == 1) | (query == key)
        mask[r] = jnp.where(same & live & (key <= query), 1.0, 0.0).astype(bf16)

    for swap in row_swaps:
        swap.wait()
    see(ylo, segments[...], padding[...])
    see(1 - ylo, other_segments[...], other_padding[...])
    step(qkv, cot_move, qkv, out, out)
    step(attn_move)
    finish(qkv)
    step(out, out, up)
    finish(cot_move, attn_move)
    writes = [
        fetched(attn_in, attn_out, load_sem.at[0]),
        fetched(weight, qkv_out, load_sem.at[1]),
        fetched(inputs_share, inputs_out, load_sem.at[2]),
        fetched(mask, mask_out, load_sem.at[3]),
    ]

    def project(r):
        rows = attn_in[0, r].reshape(512, WIDTH)
        for t in range(3):
            columns = pl.ds(t * 256, 256)
            part = weight[:, :, :, :, columns].reshape(WIDTH, 256)
            projected[r, :, columns] = dot(rows, part).astype(bf16)

    def attend(r):
        for h in range(2):
            key = projected[r, :, pl.ds(256 + h * HEAD, HEAD)]
            value = projected[r, :, pl.ds(512 + h * HEAD, HEAD)]
            for c in range(2):
                rows = pl.ds(c * 256, 256)
                query = projected[r, rows, pl.ds(h * HEAD, HEAD)]
                scores = turned_dot(query, key) * HEAD ** (-0.5)
                scores = jnp.where(mask[r, rows].astype(f32) > 0.5, scores, masked_score)
                expd = jnp.exp(scores - jnp.max(scores, axis=-1, keepdims=True))
                probs = expd / jnp.sum(expd, axis=-1, keepdims=True)
                result = dot(probs.astype(bf16), value).astype(bf16)
                for u in range(2):
                    attended[r, c, u, :, pl.ds(h * HEAD, HEAD)] = result[u * SHARE : (u + 1) * SHARE]

    project(1 - ylo)
    step(out, down)
    attend(1 - ylo)
    step(heads)
    step(out, up)
    project(ylo)

    def swap(n, half_core):
        apart = (0, 1, -1, 2)[n // 2]
        if n % 2 == 0:
            here = out_weight.at[half_core, :, :, ring(z, apart), pl.ds(0, 32)]
        else:
            here = out_weight.at[half_core, :, ring(x, apart), :, pl.ds(32, 32)]
        return remote(here, here, swap_send.at[2 + n], swap_recv.at[2 + n], core_partner())

    step(out)
    for n in range(6):
        swap(n, core).start()
    step(down)
    attend(ylo)
    step(heads)
    finish(out)
    for n in (6, 7):
        swap(n, core).start()
    step(up, down)
    finish(heads)
    writes.append(fetched(projected, projected_out, load_sem.at[5]))
    writes.append(fetched(attended, attended_out, load_sem.at[6]))

    def branch(c, before):
        def one(n, carry):
            columns = pl.ds(pl.multiple_of(n * 512, 512), 512)
            value = before[:, columns]
            for h in range(2):
                features = pl.ds(pl.multiple_of((h * 2 + c) * 512, 512), 512)
                pair = pl.ds(lax.rem(n, 2) * 2, 2)
                part = out_weight[c, h * 2 + lax.div(n, 2), pair].reshape(512, 512)
                value += turned_dot(tokens[:, features], part)
            middle[:, columns] = value
            return carry

        lax.fori_loop(0, WIDTH // 512, one, 0)

    branch(core, inputs_share)
    for n in range(8):
        swap(n, 1 - core).wait_recv()
    writes.append(fetched(out_weight, out_weight_out, load_sem.at[4]))
    branch(1 - core, middle)
    gain_two, shift_two = gains[pl.ds(2, 1)], gains[pl.ds(3, 1)]

    def norm_two(rows):
        normed, _ = standardize(middle[rows])
        ffn_share[rows] = (normed * gain_two + shift_two).astype(bf16)

    some_rows(SHARE, 32, norm_two)
    step(spread)
    writes.append(fetched(middle, middle_out, load_sem.at[7]))
    step(up, down)
    step(up, down)
    step(up, down)
    step(spread)
    step(up, down)
    step(spread)
    step(up, down)
    finish(spread, up, down)
    for write in writes:
        write.wait()
    for n in range(8):
        swap(n, core).wait_send()


def forward(ids, segments, padding, stream, cot, codebook, own_qkv, own_out, own_up, own_down, norms):
    tokens_full = (shaped(bf16, 1, 2, 2, 2, SHARE, WIDTH), ANY)
    return kernel_call(
        forward_body,
        [
            small_gather(),
            weight_gather(768),
            weight_gather(512, spread=True),
            weight_gather(PART, flat=True),
            weight_gather(PART, flat=True),
            row_exchange(),
            row_exchange(),
            heads_to_tokens(),
            share_gather(),
        ],
        XZ + ["x2", "z2"] + GROUP,
        [
            (ids, VMEM),
            (segments, VMEM),
            (padding, VMEM),
            (stream, ANY),
            (cot, ANY),
            (codebook, ANY),
            (own_qkv, VMEM),
            (own_out, VMEM),
            (own_up, VMEM),
            (own_down, VMEM),
            (norms, VMEM),
        ],
        [
            tokens_full,
            gathered(768),
            (shaped(bf16, 2, 4, 4, 4, 64, 512), ANY),
            tokens_full,
            (shaped(f32, SHARE, WIDTH), ANY),
            (shaped(f32, 8, WIDTH), VMEM),
            (shaped(bf16, 2, 512, 512), ANY),
            (shaped(bf16, 2, 512, 768), ANY),
            (shaped(bf16, 2, 2, 2, SHARE, 256), ANY),
            (shaped(f32, SHARE, WIDTH), ANY),
            (shaped(bf16, 2, 2, 2, SHARE, WIDTH), ANY),
            gathered(PART),
            gathered(PART),
        ],
        [
            pltpu.VMEM((SHARE, WIDTH), f32),
            pltpu.VMEM((2, 512, 512), bf16),
            pltpu.VMEM((2, 512, 768), bf16),
            pltpu.VMEM((2, 2, 2, SHARE, 256), bf16),
            pltpu.VMEM((SHARE, WIDTH), f32),
            pltpu.VMEM((2, 4, 4, 8, 128), f32),
            pltpu.VMEM((8, 128), f32),
            pltpu.VMEM((1, 512), jnp.int32),
            pltpu.VMEM((1, 512), jnp.int32),
            pltpu.VMEM((2, CODE_CHUNK, WIDTH), bf16),
            pltpu.VMEM((256, WIDTH), f32),
            pltpu.VMEM((256, WIDTH), bf16),
            pltpu.VMEM((1, 2, SHARE, WIDTH), bf16),
            pltpu.VMEM((1, 2, SHARE, WIDTH), bf16),
            pltpu.VMEM((1, 2, 2, 2, SHARE, WIDTH), bf16),
            pltpu.VMEM((2, 4, 4, 64, 768), bf16),
            pltpu.VMEM((2, 4, 4, 4, 64, 512), bf16),
            pltpu.VMEM((SHARE, WIDTH), bf16),
            pltpu.VMEM((SHARE, WIDTH), bf16),
            sems(8),
            sems(10),
            sems(10),
        ],
        0,
    )


SLOPE = 0.7978845608028654
CUBIC = 0.044715


def ffn_body(ins, outs, scratch, makers, ready):
    ffn_hbm, cot_hbm, up_hbm, down_hbm, middle_hbm, out_hbm, gains = ins
    sum_down, grad_up_out, layer_full, grad_middle_out, small, branch_share, grad_heads = outs
    (
        layer_out,
        middle,
        grad_up_weight,
        grad_middle,
        grad_tokens,
        ffn_in,
        cot,
        up_weight,
        down_weight,
        hidden,
        grad_up,
        back,
        ahead,
        grad_down_weight,
        back_share,
        ahead_share,
        load_sem,
    ) = scratch
    make_back, make_ahead, make_down, make_heads, make_layer = makers
    ylo, x, z, yhi, core = place()
    back_sum = make_back(back, back_share)
    ahead_sum = make_ahead(ahead, ahead_share)
    down_sum = make_down(grad_down_weight, sum_down)
    heads = make_heads(grad_tokens, grad_heads)
    layer_move = make_layer(layer_out, layer_full)
    own, partner = (pl.ds(pl.multiple_of(r * 512, 512), 512) for r in (ylo, 1 - ylo))
    loads = [
        fetched(ffn_hbm.at[own], ffn_in.at[own], load_sem.at[0]),
        fetched(up_hbm, up_weight, load_sem.at[1]),
        fetched(ffn_hbm.at[partner], ffn_in.at[partner], load_sem.at[2]),
        fetched(down_hbm, down_weight, load_sem.at[3]),
        fetched(cot_hbm, cot, load_sem.at[4]),
        fetched(middle_hbm, middle, load_sem.at[5]),
    ]

    def units(rows):
        def one(n, carry):
            columns = pl.ds(pl.multiple_of(n * 512, 512), 512)
            value = dot(ffn_in[rows], up_weight[:, columns])
            square = value * value
            bend = jnp.tanh(SLOPE * value * (1.0 + CUBIC * square))
            half = 0.5 * (1.0 + bend)
            hidden[rows, columns] = (value * half).astype(bf16)
            slope = half + 0.5 * value * (1.0 - bend * bend) * SLOPE * (1.0 + 3.0 * CUBIC * square)
            grad_up[rows, columns] = slope.astype(bf16)
            return carry

        lax.fori_loop(0, PART // 512, one, 0)

    def units_back(rows):
        def one(n, carry):
            columns = pl.ds(pl.multiple_of(n * 512, 512), 512)
            grad = dot(cot[rows], down_weight[:, columns])
            grad_up[rows, columns] = (grad * grad_up[rows, columns].astype(f32)).astype(bf16)
            return carry

        lax.fori_loop(0, PART // 512, one, 0)

    def spread_out(r, rows, source, weight, target):
        def one(n, carry):
            columns = pl.ds(pl.multiple_of(n * 512, 512), 512)
            value = turned_dot(source[rows], weight[columns]).astype(bf16)
            for c in range(2):
                for u in range(2):
                    at = (2 * c + u) * SHARE
                    target[r, c, u, :, columns] = value[at : at + SHARE]
            return carry

        lax.fori_loop(0, WIDTH // 512, one, 0)

    def weight_grad(left, right, target, first=0, last=WIDTH // 256):
        def one(n, carry):
            columns = pl.ds(pl.multiple_of(n * 256, 256), 256)
            value = outer_dot(left[:, columns], right[...]).astype(bf16)
            for j in range(4):
                target[lax.div(n, 4), lax.rem(n, 4), j] = value[64 * j : 64 * j + 64]
            return carry

        lax.fori_loop(first, last, one, 0)

    loads[0].wait()
    loads[1].wait()
    units(own)
    loads[2].wait()
    units(partner)
    loads[3].wait()
    spread_out(ylo, own, hidden, down_weight, ahead)
    ready()
    step(ahead_sum)
    spread_out(1 - ylo, partner, hidden, down_weight, ahead)
    step(ahead_sum, ahead_sum)
    loads[4].wait()
    weight_grad(cot, hidden, grad_down_weight)
    step(down_sum)
    step(ahead_sum)
    units_back(own)
    step(down_sum)
    spread_out(ylo, own, grad_up, up_weight, back)
    step(back_sum)
    step(down_sum)
    units_back(partner)
    step(back_sum)
    spread_out(1 - ylo, partner, grad_up, up_weight, back)
    step(back_sum)
    places = {}
    for h in range(2):
        for c in range(2):
            place_of = (up_weight, down_weight)[h].at[:, pl.ds(512 * c, 512)]
            places[h, c] = (place_of, fetched(out_hbm.at[c, h], place_of, load_sem.at[6 + 2 * h + c]))
    step(down_sum)
    weight_grad(ffn_in, grad_up, grad_up_weight, 0, 3)
    step(back_sum)
    step(down_sum)
    weight_grad(ffn_in, grad_up, grad_up_weight, 3, 6)
    step(down_sum)
    weight_grad(ffn_in, grad_up, grad_up_weight, 6, 8)
    writes = [fetched(grad_up_weight, grad_up_out, load_sem.at[0])]
    step(down_sum)
    finish(ahead_sum)
    loads[5].wait()

    def end(rows):
        layer_out[0, rows] = (middle[rows] + ahead_share[rows]).astype(bf16)

    some_rows(SHARE, 32, end)
    step(layer_move)
    finish(back_sum)
    gain = gains[pl.ds(2, 1)]
    small[...] = jnp.zeros_like(small)

    def back_norm(i, carry):
        at = pl.multiple_of(i * 32, 32)
        rows = pl.ds(at, 32)
        normed, inverse = standardize(middle[rows])
        value, grad_gain, grad_shift = norm_back(back_share[rows], normed, inverse, gain)
        here = pl.multiple_of(ylo * 512 + core * 256 + yhi * SHARE + at, 32)
        value += cot[pl.ds(here, 32)].astype(f32)
        grad_middle[rows] = value
        branch_share[rows] = value.astype(bf16)
        small[pl.ds(2, 1)] += grad_gain
        small[pl.ds(3, 1)] += grad_shift
        return carry

    lax.fori_loop(0, SHARE // 32, back_norm, 0)
    writes.append(fetched(grad_middle, grad_middle_out, load_sem.at[1]))
    for h in range(2):
        for c in range(2):
            place_of, load = places[h, c]
            load.wait()
            grad_tokens[:, pl.ds((h * 2 + c) * 512, 512)] = dot(branch_share[...], place_of[...]).astype(bf16)
    step(heads)
    step(layer_move)
    finish(down_sum, heads, layer_move)
    for write in writes:
        write.wait()


def feed_forward(ffn_in, cot, up, down, middle, out_weight, gains):
    return kernel_call(
        ffn_body,
        [share_sum(), share_sum(), weight_sum(), tokens_to_heads(), row_gather()],
        XZ + GROUP,
        [(ffn_in, ANY), (cot, ANY), (up, ANY), (down, ANY), (middle, ANY), (out_weight, ANY), (gains, VMEM)],
        [
            (shaped(bf16, 2, 64, PART), VMEM),
            (shaped(bf16, 2, 4, 4, 64, PART), ANY),
            (shaped(bf16, 1, 2, 2, SHARE, WIDTH), ANY),
            (shaped(f32, SHARE, WIDTH), ANY),
            (shaped(f32, 4, WIDTH), VMEM),
            (shaped(bf16, SHARE, WIDTH), VMEM),
            (shaped(bf16, 2, 2, 2, SHARE, 256), VMEM),
        ],
        [
            pltpu.VMEM((1, SHARE, WIDTH), bf16),
            pltpu.VMEM((SHARE, WIDTH), f32),
            pltpu.VMEM((2, 4, 4, 64, PART), bf16),
            pltpu.VMEM((SHARE, WIDTH), f32),
            pltpu.VMEM((SHARE, WIDTH), bf16),
            pltpu.VMEM((1024, WIDTH), bf16),
            pltpu.VMEM((1024, WIDTH), bf16),
            pltpu.VMEM((WIDTH, PART), bf16),
            pltpu.VMEM((WIDTH, PART), bf16),
            pltpu.VMEM((1024, PART), bf16),
            pltpu.VMEM((1024, PART), bf16),
            pltpu.VMEM((2, 2, 2, SHARE, WIDTH), bf16),
            pltpu.VMEM((2, 2, 2, SHARE, WIDTH), bf16),
            pltpu.VMEM((2, 4, 4, 64, PART), bf16),
            pltpu.VMEM((SHARE, WIDTH), f32),
            pltpu.VMEM((SHARE, WIDTH), f32),
            sems(10),
        ],
        2,
        62,
    )


def back_body(ins, outs, scratch, makers, ready):
    (
        attn_hbm,
        weight_hbm,
        up_hbm,
        projected_hbm,
        attended_hbm,
        mask_hbm,
        middle_hbm,
        inputs_hbm,
        branch_share,
        grad_heads,
        small_in,
        gains,
    ) = ins
    input_full, sum_up, sum_qkv, sum_out, small_out, branch_full = outs
    (
        projected,
        attended,
        mask,
        grad_middle,
        inputs_share,
        attn_in,
        weight,
        grad_up_weight,
        grad_qkv_weight,
        grad_out_weight,
        grad_branch,
        grad_projected,
        back,
        back_share,
        input_share,
        small,
        load_sem,
    ) = scratch
    make_up, make_qkv, make_out, make_branch, make_back, make_input, make_small = makers
    ylo, x, z, yhi, core = place()
    up_sum = make_up(grad_up_weight, sum_up)
    qkv_sum = make_qkv(grad_qkv_weight, sum_qkv)
    out_sum = make_out(grad_out_weight, sum_out)
    branch = make_branch(branch_share, branch_full)
    back_sum = make_back(back, back_share)
    input_move = make_input(input_share, input_full)
    small_sum = make_small(small, small_out)
    loads = [
        fetched(src, dst, load_sem.at[n])
        for n, (src, dst) in enumerate(
            (
                (projected_hbm, projected),
                (mask_hbm, mask),
                (up_hbm, grad_up_weight),
                (weight_hbm, weight),
                (attn_hbm, attn_in),
                (attended_hbm, attended),
                (inputs_hbm, inputs_share),
                (middle_hbm, grad_middle),
            )
        )
    ]

    def attend(r):
        for h in range(2):
            query = projected[r, :, pl.ds(h * HEAD, HEAD)]
            key = projected[r, :, pl.ds(256 + h * HEAD, HEAD)]
            value = projected[r, :, pl.ds(512 + h * HEAD, HEAD)]
            grad = grad_heads[r, :, :, :, pl.ds(h * HEAD, HEAD)].reshape(512, HEAD)
            scores = turned_dot(query, key) * HEAD ** (-0.5)
            scores = jnp.where(mask[r].astype(f32) > 0.5, scores, masked_score)
            expd = jnp.exp(scores - jnp.max(scores, axis=-1, keepdims=True))
            probs = expd / jnp.sum(expd, axis=-1, keepdims=True)
            grad_probs = turned_dot(grad, value)
            inner = jnp.sum(grad_probs * probs, axis=-1, keepdims=True)
            grad_scores = (probs * (grad_probs - inner)).astype(bf16)
            parts = (
                dot(grad_scores, key) * HEAD ** (-0.5),
                outer_dot(grad_scores, query) * HEAD ** (-0.5),
                outer_dot(probs.astype(bf16), grad),
            )
            for t in range(3):
                grad_projected[pl.ds(pl.multiple_of(r * 512, 512), 512), pl.ds(t * 256 + h * HEAD, HEAD)] = parts[
                    t
                ].astype(bf16)

    def spread_out(r):
        def one(n, carry):
            columns = pl.ds(pl.multiple_of(n * 512, 512), 512)
            rows = pl.ds(pl.multiple_of(r * 512, 512), 512)
            value = turned_dot(grad_projected[rows], weight[columns]).astype(bf16)
            for c in range(2):
                for u in range(2):
                    at = (2 * c + u) * SHARE
                    back[r, c, u, :, columns] = value[at : at + SHARE]
            return carry

        lax.fori_loop(0, WIDTH // 512, one, 0)

    def weight_grad(left, right, target):
        def one(n, carry):
            columns = pl.ds(pl.multiple_of(n * 256, 256), 256)
            value = outer_dot(left[..., columns].reshape(1024, 256), right).astype(bf16)
            for j in range(4):
                target[lax.div(n, 4), lax.rem(n, 4), j] = value[64 * j : 64 * j + 64]
            return carry

        lax.fori_loop(0, WIDTH // 256, one, 0)

    loads[0].wait()
    loads[1].wait()
    attend(ylo)
    ready()
    step(branch)
    loads[2].wait()
    step(up_sum)
    loads[3].wait()
    spread_out(ylo)
    step(back_sum)
    attend(1 - ylo)
    step(back_sum)
    step(up_sum)
    spread_out(1 - ylo)
    step(back_sum)
    step(up_sum)
    loads[4].wait()
    weight_grad(attn_in, grad_projected[...], grad_qkv_weight)
    step(branch)
    step(qkv_sum)
    step(back_sum)
    step(up_sum, up_sum)
    step(qkv_sum)
    finish(branch)
    gather_load = fetched(branch_full, grad_branch, load_sem.at[0])
    for load in loads[5:]:
        load.wait()
    step(qkv_sum, up_sum)
    gather_load.wait()
    weight_grad(grad_branch, attended[...].reshape(1024, 256), grad_out_weight)
    step(out_sum)
    finish(back_sum)
    gain = gains[pl.ds(0, 1)]
    small[...] = small_in[...]

    def back_norm(i, carry):
        rows = pl.ds(pl.multiple_of(i * 32, 32), 32)
        normed, inverse = standardize(inputs_share[rows])
        value, grad_gain, grad_shift = norm_back(back_share[rows], normed, inverse, gain)
        input_share[0, rows] = (grad_middle[rows] + value).astype(bf16)
        small[pl.ds(0, 1)] += grad_gain
        small[pl.ds(1, 1)] += grad_shift
        return carry

    lax.fori_loop(0, SHARE // 32, back_norm, 0)
    step(small_sum, input_move)
    step(up_sum, qkv_sum, out_sum, out_sum)
    step(small_sum, qkv_sum, out_sum, qkv_sum)
    step(small_sum, out_sum, qkv_sum, out_sum)
    step(qkv_sum, out_sum, input_move)
    finish(input_move, small_sum, up_sum, qkv_sum, out_sum)


def attention_back(
    attn_in,
    weight,
    grad_up_weight,
    projected,
    attended,
    mask,
    grad_middle,
    inputs_share,
    branch_share,
    grad_heads,
    small,
    gains,
):
    return kernel_call(
        back_body,
        [
            weight_sum(),
            weight_sum(768),
            weight_sum(256),
            share_gather(),
            share_sum(),
            row_gather(),
            small_reduce(),
        ],
        XZ + ["x2", "z2"] + GROUP,
        [
            (attn_in, ANY),
            (weight, ANY),
            (grad_up_weight, ANY),
            (projected, ANY),
            (attended, ANY),
            (mask, ANY),
            (grad_middle, ANY),
            (inputs_share, ANY),
            (branch_share, VMEM),
            (grad_heads, VMEM),
            (small, VMEM),
            (gains, VMEM),
        ],
        [
            (shaped(bf16, 1, 2, 2, SHARE, WIDTH), ANY),
            (shaped(bf16, 2, 64, PART), VMEM),
            (shaped(bf16, 2, 64, 768), VMEM),
            (shaped(bf16, 2, 64, 256), VMEM),
            (shaped(f32, 4, 128), VMEM),
            (shaped(bf16, 2, 2, 2, SHARE, WIDTH), ANY),
        ],
        [
            pltpu.VMEM((2, 512, 768), bf16),
            pltpu.VMEM((2, 2, 2, SHARE, 256), bf16),
            pltpu.VMEM((2, 512, 512), bf16),
            pltpu.VMEM((SHARE, WIDTH), f32),
            pltpu.VMEM((SHARE, WIDTH), f32),
            pltpu.VMEM((1024, WIDTH), bf16),
            pltpu.VMEM((WIDTH, 768), bf16),
            pltpu.VMEM((2, 4, 4, 64, PART), bf16),
            pltpu.VMEM((2, 4, 4, 64, 768), bf16),
            pltpu.VMEM((2, 4, 4, 64, 256), bf16),
            pltpu.VMEM((2, 2, 2, SHARE, WIDTH), bf16),
            pltpu.VMEM((1024, 768), bf16),
            pltpu.VMEM((2, 2, 2, SHARE, WIDTH), bf16),
            pltpu.VMEM((SHARE, WIDTH), f32),
            pltpu.VMEM((1, SHARE, WIDTH), bf16),
            pltpu.VMEM((4, WIDTH), f32),
            sems(8),
        ],
        3,
        62,
    )


def on_device(
    stream,
    code_ids,
    segment_ids,
    padding,
    codebook,
    norm1_gain,
    norm1_shift,
    w_qkv,
    w_out,
    norm2_gain,
    norm2_shift,
    w_up,
    w_down,
    cotangent,
):
    ylo, x, z, yhi, core = place()
    own_qkv = w_qkv.reshape(64, 3, 2, 256).transpose(2, 0, 1, 3).reshape(2, 64, 768)
    norms = jnp.stack([norm1_gain, norm1_shift, norm2_gain, norm2_shift] * 2)
    norms = jnp.concatenate([norms, norms], axis=1)
    (
        attn_in,
        qkv_full,
        out_full,
        cot,
        inputs_share,
        gains,
        allowed,
        projected,
        attended,
        middle,
        ffn_in,
        up_full,
        down_full,
    ) = forward(
        code_ids,
        segment_ids,
        padding,
        stream[0],
        cotangent[0],
        codebook,
        own_qkv,
        w_out,
        w_up,
        w_down,
        norms,
    )
    sum_down, grad_up_weight, layer_out, grad_middle, small, branch_share, grad_heads = feed_forward(
        ffn_in.reshape(1024, WIDTH),
        cot.reshape(1024, WIDTH),
        up_full.reshape(WIDTH, PART),
        down_full.reshape(WIDTH, PART),
        middle,
        out_full.reshape(2, 2, WIDTH, 512),
        gains,
    )
    input_grad, sum_up, sum_qkv, sum_out, small, _ = attention_back(
        attn_in.reshape(1024, WIDTH),
        qkv_full.reshape(WIDTH, 768),
        grad_up_weight,
        projected,
        attended,
        allowed,
        grad_middle,
        inputs_share,
        branch_share,
        grad_heads,
        small,
        gains,
    )

    sum_qkv, sum_out, sum_up, sum_down = (g.astype(f32) for g in (sum_qkv, sum_out, sum_up, sum_down))
    out_qkv = sum_qkv.reshape(2, 64, 3, 256).transpose(1, 2, 0, 3).reshape(64, 3, 512)
    out_out = sum_out.transpose(1, 0, 2).reshape(64, 512)
    out_up = sum_up.transpose(1, 0, 2).reshape(64, WIDTH)
    out_down = sum_down.transpose(1, 0, 2).reshape(64, WIDTH)
    odd = lax.rem(z, 2) == 1
    small = jnp.where(odd, small[:, 64:], small[:, :64])
    return (
        layer_out.reshape(1, 512, WIDTH).astype(f32),
        input_grad.reshape(1, 512, WIDTH).astype(f32),
        small[0],
        small[1],
        out_qkv,
        out_out,
        small[2],
        small[3],
        out_up,
        out_down,
    )


def solution(mesh):
    in_specs = (
        P("dp", None, None),
        P("dp", None),
        P("dp", None),
        P("dp", None),
        P(),
        P("dp"),
        P("dp"),
        P("dp", None, "mp"),
        P("dp", "mp"),
        P("dp"),
        P("dp"),
        P("dp", "mp"),
        P("dp", "mp"),
        P("dp", None, None),
    )
    out_specs = (
        P("dp", None, None),
        P("dp", None, None),
        P("dp"),
        P("dp"),
        P("dp", None, "mp"),
        P("dp", "mp"),
        P("dp"),
        P("dp"),
        P("dp", "mp"),
        P("dp", "mp"),
    )
    return jax.shard_map(
        on_device, mesh=mesh, in_specs=in_specs, out_specs=out_specs, check_vma=False
    )
```

```python
import functools

import jax
import jax.numpy as jnp
from jax import lax
from jax.experimental import pallas as pl
from jax.experimental.pallas import tpu as pltpu
from jax.sharding import PartitionSpec as P

HEAD = 128
WIDTH = 2048
SHARE = 128
PART = 1024
MESH = pl.DeviceIdType.MESH
ANY = pl.BlockSpec(memory_space=pl.ANY)
VMEM = pl.BlockSpec(memory_space=pltpu.VMEM)
masked_score = -1000000000.0
epsilon = 1e-05
f32 = jnp.float32
bf16 = jnp.bfloat16


def place():
    dp, mp = lax.axis_index("dp"), lax.axis_index("mp")
    return lax.div(dp, 16), lax.rem(lax.div(dp, 4), 4), lax.rem(dp, 4), lax.div(mp, 2), lax.rem(mp, 2)


def ring(position, step):
    return lax.rem(position + step + 4, 4)


def xz_neighbour(axis, step):
    ylo, x, z, yhi, core = place()
    if axis == 0:
        x = ring(x, step)
    else:
        z = ring(z, step)
    return (ylo * 16 + x * 4 + z, yhi * 2 + core)


def y_peer(step):
    ylo, x, z, yhi, core = place()
    y = ring(yhi * 2 + ylo, step)
    return (lax.rem(y, 2) * 16 + x * 4 + z, lax.div(y, 2) * 2 + core)


def lo_partner():
    ylo, x, z, yhi, core = place()
    return ((1 - ylo) * 16 + x * 4 + z, yhi * 2 + core)


def core_partner():
    ylo, x, z, yhi, core = place()
    return (ylo * 16 + x * 4 + z, yhi * 2 + 1 - core)


def greet(peers):
    barrier = pltpu.get_barrier_semaphore()
    for peer in peers:
        pl.semaphore_signal(barrier, inc=1, device_id=peer, device_id_type=MESH)
    return lambda: pl.semaphore_wait(barrier, len(peers))


def remote(src, dst, send_sem, recv_sem, peer):
    return pltpu.make_async_remote_copy(
        src_ref=src,
        dst_ref=dst,
        send_sem=send_sem,
        recv_sem=recv_sem,
        device_id=peer,
        device_id_type=MESH,
    )


def sems(*shape):
    return pltpu.SemaphoreType.DMA(shape)


def params(collective_id, mib=48):
    return pltpu.CompilerParams(
        collective_id=collective_id, has_side_effects=True, vmem_limit_bytes=mib << 20
    )


PEERS = {
    "core": core_partner,
    "x+": lambda: xz_neighbour(0, 1),
    "x-": lambda: xz_neighbour(0, -1),
    "z+": lambda: xz_neighbour(1, 1),
    "z-": lambda: xz_neighbour(1, -1),
    "x2": lambda: xz_neighbour(0, 2),
    "z2": lambda: xz_neighbour(1, 2),
    "y1": lambda: y_peer(1),
    "y2": lambda: y_peer(2),
    "y3": lambda: y_peer(3),
}


def diagonal_peer(step):
    dp, mp = y_peer(step)
    return (dp, mp + 1 - 2 * lax.rem(mp, 2))


PEERS.update({f"d{k}": functools.partial(diagonal_peer, k) for k in range(1, 4)})
GROUP = ["y1", "y2", "y3", "core", "d1", "d2", "d3"]


def kernel_call(body, jobs, peers, ins, outs, scratch, collective_id, mib=56):
    def kernel(*refs):
        taken = 0

        def take(count):
            nonlocal taken
            taken += count
            return refs[taken - count : taken]

        groups = [take(len(ins)), take(len(outs)), take(len(scratch))]
        makers = []
        for job in jobs:
            own = take(len(job["scratch"]))
            makers.append(lambda *given, job=job, own=own: job["steps"](*given, *own))
        ready = greet([PEERS[name]() for name in peers])
        body(*groups, makers, ready)

    return pl.pallas_call(
        kernel,
        out_shape=[shape for shape, _ in outs],
        in_specs=[spec for _, spec in ins],
        out_specs=[spec for _, spec in outs],
        scratch_shapes=scratch + [one for job in jobs for one in job["scratch"]],
        compiler_params=params(collective_id, mib),
    )(*[array for array, _ in ins])


def finish(*runs):
    for run in runs:
        for _ in run:
            pass


def step(*runs):
    for run in runs:
        next(run, None)


def shaped(dtype, *shape):
    return jax.ShapeDtypeStruct(shape, dtype)


def small_gather():
    def steps(own, everyone, send, recv):
        ylo, x, z, yhi, core = place()
        sent = []

        def go(here, n, peer):
            copy = remote(here, here, send.at[n], recv.at[n], peer)
            copy.start()
            sent.append(copy)

        def came(here, n):
            remote(here, here, send.at[n], recv.at[n], lo_partner()).wait_recv()

        everyone[ylo, x, z] = own[...]
        go(everyone.at[ylo, x, z], 0, lo_partner())
        yield
        came(everyone.at[1 - ylo, x, z], 0)
        for k in (1, 2, 3):
            go(everyone.at[:, x, z], k, xz_neighbour(0, k))
        yield
        for k in (1, 2, 3):
            came(everyone.at[:, ring(x, -k), z], k)
        for k in (1, 2, 3):
            go(everyone.at[:, :, z], 3 + k, xz_neighbour(1, k))
        yield
        for k in (1, 2, 3):
            came(everyone.at[:, :, ring(z, -k)], 3 + k)
        for copy in sent:
            copy.wait_send()

    return {"scratch": [sems(7), sems(7)], "steps": steps}


def small_reduce():
    def steps(rows, out, of_group, of_x, of_z, half, quarter, send, recv):
        ylo, x, z, yhi, core = place()
        y = yhi * 2 + ylo
        waits = []

        def go(src, dst, n, peer):
            copy = remote(src, dst, send.at[n], recv.at[n], peer)
            copy.start()
            waits.append(copy)

        def lanes(start, size):
            return pl.ds(pl.multiple_of(start, size), size)

        for n, (k, flip) in enumerate(((1, 0), (1, 1), (2, 0), (2, 1), (3, 0), (3, 1), (0, 1))):
            theirs = lanes(lax.rem(ring(y, k), 2) * 1024, 1024)
            go(rows.at[:, theirs], of_group.at[n], n, diagonal_peer(k) if flip else y_peer(k))
        yield
        for copy in waits:
            copy.wait_recv()
        total = rows[:, lanes(ylo * 1024, 1024)]
        for n in range(7):
            total += of_group[n]
        half[...] = total
        for k in (1, 2, 3):
            go(half.at[:, lanes(ring(x, k) * 256, 256)], of_x.at[k - 1], 6 + k, xz_neighbour(0, k))
        yield
        for copy in waits[7:]:
            copy.wait_recv()
        total = half[:, lanes(x * 256, 256)]
        for n in range(3):
            total += of_x[n]
        quarter[...] = total
        for k in (1, 2, 3):
            theirs = lanes(lax.div(ring(z, k), 2) * 128, 128)
            go(quarter.at[:, theirs], of_z.at[k - 1], 9 + k, xz_neighbour(1, k))
        yield
        for copy in waits[10:]:
            copy.wait_recv()
        total = quarter[:, lanes(lax.div(z, 2) * 128, 128)]
        for n in range(3):
            total += of_z[n]
        out[...] = total
        for copy in waits:
            copy.wait_send()

    return {
        "scratch": [
            pltpu.VMEM((7, 4, 1024), f32),
            pltpu.VMEM((3, 4, 256), f32),
            pltpu.VMEM((3, 4, 128), f32),
            pltpu.VMEM((4, 1024), f32),
            pltpu.VMEM((4, 256), f32),
            sems(13),
            sems(13),
        ],
        "steps": steps,
    }


def row_exchange(count=1):
    def steps(halves, full, local_sem, send, recv):
        ylo, x, z, yhi, core = place()
        up, down, other = y_peer(1), y_peer(3), core_partner()
        first = []
        for n in range(count):
            for u, peer in ((0, up), (1, down)):
                here = full.at[n, ylo, core, u]
                first.append(remote(halves.at[n, u], here, send.at[n, u], recv.at[n, u], peer))
        for n in range(count):
            here = full.at[n, ylo, core]
            first.append(remote(halves.at[n], here, send.at[n, 2], recv.at[n, 2], other))
        for copy in first:
            copy.start()
        local = [
            pltpu.make_async_copy(halves.at[n], full.at[n, ylo, core], local_sem.at[n])
            for n in range(count)
        ]
        for copy in local:
            copy.start()
        yield
        second = []
        for n in range(count):
            for u in range(2):
                here = full.at[n, 1 - ylo, core, u]
                remote(halves.at[n, u], here, send.at[n, u], recv.at[n, u], up).wait_recv()
                copy = remote(here, here, send.at[n, 3 + u], recv.at[n, 3 + u], other)
                copy.start()
                second.append(copy)
        yield
        for n in range(count):
            here = full.at[n, ylo, 1 - core]
            remote(halves.at[n], here, send.at[n, 2], recv.at[n, 2], other).wait_recv()
            for u in range(2):
                here = full.at[n, 1 - ylo, 1 - core, u]
                remote(here, here, send.at[n, 3 + u], recv.at[n, 3 + u], other).wait_recv()
        for copy in first + second:
            copy.wait_send()
        for copy in local:
            copy.wait()

    return {
        "scratch": [sems(count), sems(count, 5), sems(count, 5)],
        "steps": steps,
    }


def share_gather():
    def steps(share, full, local_sem, send, recv):
        ylo, x, z, yhi, core = place()
        y = yhi * 2 + ylo
        other = core_partner()
        half = SHARE // 2
        sent = []

        def of(step, half_core):
            source = ring(y, step)
            return full.at[lax.rem(source, 2), half_core, lax.div(source, 2)]

        def go(src, dst, n, peer):
            copy = remote(src, dst, send.at[n], recv.at[n], peer)
            copy.start()
            sent.append(copy)

        def came(dst, n):
            remote(dst, dst, send.at[n], recv.at[n], other).wait_recv()

        local = pltpu.make_async_copy(share, of(0, core), local_sem)
        go(share, of(0, core), 0, y_peer(1))
        go(share, of(0, core), 1, y_peer(3))
        go(share, of(0, core), 2, other)
        local.start()
        yield
        for n, step_back, rows, onward in ((0, 3, pl.ds(0, half), 1), (1, 1, pl.ds(half, half), 3)):
            here = of(step_back, core)
            came(here, n)
            go(here.at[rows], here.at[rows], 3 + n, y_peer(onward))
            go(here, here, 5 + n, other)
        yield
        far = of(2, core)
        came(far.at[pl.ds(0, half)], 3)
        came(far.at[pl.ds(half, half)], 4)
        go(far, far, 7, other)
        yield
        came(of(0, 1 - core), 2)
        came(of(3, 1 - core), 5)
        came(of(1, 1 - core), 6)
        came(of(2, 1 - core), 7)
        for copy in sent:
            copy.wait_send()
        local.wait()

    return {"scratch": [pltpu.SemaphoreType.DMA, sems(8), sems(8)], "steps": steps}


def add_rows(count, one):
    def body(i, carry):
        one(pl.ds(pl.multiple_of(i * 16, 16), 16))
        return carry

    lax.fori_loop(0, count // 16, body, 0)


def share_sum():
    def steps(partial, out, from_core, via, arrived, send, recv, send_two, recv_two):
        ylo, x, z, yhi, core = place()
        y = yhi * 2 + ylo
        other = core_partner()
        half = SHARE // 2

        def block(k, half_core):
            target = ring(y, k)
            return partial.at[lax.rem(target, 2), half_core, lax.div(target, 2)]

        first, second = {}, {}

        def to_core(order):
            for k in order:
                first[k] = remote(block(k, 1 - core), from_core.at[k], send.at[k], recv.at[k], other)
                first[k].start()

        to_core((2, 0))
        yield
        first[2].wait_recv()
        far = block(2, core)

        def add_far(rows):
            far[rows] = (far[rows].astype(f32) + from_core[2, rows].astype(f32)).astype(bf16)

        add_rows(SHARE, add_far)
        for n, k in ((0, 1), (1, 3)):
            second[n] = remote(
                far.at[pl.ds(half * n, half)], via.at[n], send_two.at[n], recv_two.at[n], y_peer(k)
            )
            second[n].start()
        yield
        to_core((1, 3))
        yield
        for n, k in ((0, 1), (1, 3)):
            first[k].wait_recv()
            second[n].wait_recv()
            near = block(k, core)

            def add_via(i, carry):
                at = pl.multiple_of(i * 16, 16)
                rows, with_via = pl.ds(at, 16), pl.ds(pl.multiple_of(half * n + at, 16), 16)
                value = near[with_via].astype(f32) + from_core[k, with_via].astype(f32)
                near[with_via] = (value + via[n, rows].astype(f32)).astype(bf16)
                plain = pl.ds(pl.multiple_of(half * (1 - n) + at, 16), 16)
                value = near[plain].astype(f32) + from_core[k, plain].astype(f32)
                near[plain] = value.astype(bf16)
                return carry

            lax.fori_loop(0, half // 16, add_via, 0)
            second[2 + n] = remote(near, arrived.at[n], send_two.at[2 + n], recv_two.at[2 + n], y_peer(k))
            second[2 + n].start()
        yield
        first[0].wait_recv()
        second[2].wait_recv()
        second[3].wait_recv()
        mine_own = block(0, core)

        def total(rows):
            value = mine_own[rows].astype(f32) + from_core[0, rows].astype(f32)
            out[rows] = value + arrived[0, rows].astype(f32) + arrived[1, rows].astype(f32)

        add_rows(SHARE, total)
        for k in range(4):
            first[k].wait_send()
            second[k].wait_send()

    return {
        "scratch": [
            pltpu.VMEM((4, SHARE, WIDTH), bf16),
            pltpu.VMEM((2, SHARE // 2, WIDTH), bf16),
            pltpu.VMEM((2, SHARE, WIDTH), bf16),
        ]
        + [sems(4)] * 4,
        "steps": steps,
    }


def feature_start(ylo, yhi, core):
    return pl.multiple_of((yhi * 2 + core) * 512 + ylo * 256, 256)


def heads_to_tokens():
    def steps(heads, tokens, send, recv):
        ylo, x, z, yhi, core = place()
        y = yhi * 2 + ylo
        mine = tokens.at[:, pl.ds(feature_start(ylo, yhi, core), 256)]
        sent = []

        def go(k, flip):
            target = ring(y, k)
            half = 1 - core if flip else core
            peer = diagonal_peer(k) if flip else y_peer(k)
            src = heads.at[lax.rem(target, 2), half, lax.div(target, 2)]
            copy = remote(src, mine, send.at[2 * k + flip], recv.at[2 * k + flip], peer)
            copy.start()
            sent.append(copy)

        for k in (1, 3):
            for flip in (0, 1):
                go(k, flip)
        yield
        for k, flip in ((2, 0), (2, 1), (0, 1)):
            go(k, flip)
        tokens[:, pl.ds(feature_start(ylo, yhi, core), 256)] = heads[ylo, core, yhi]
        yield
        for k, flip in ((1, 0), (1, 1), (3, 0), (3, 1), (2, 0), (2, 1), (0, 1)):
            source = ring(y, -k)
            half = 1 - core if flip else core
            start = feature_start(lax.rem(source, 2), lax.div(source, 2), half)
            here = tokens.at[:, pl.ds(start, 256)]
            remote(heads.at[0, 0, 0], here, send.at[2 * k + flip], recv.at[2 * k + flip], y_peer(1)).wait_recv()
        for copy in sent:
            copy.wait_send()

    return {"scratch": [sems(8), sems(8)], "steps": steps}


def tokens_to_heads():
    def steps(tokens, heads, send, recv):
        ylo, x, z, yhi, core = place()
        y = yhi * 2 + ylo
        mine = heads.at[ylo, core, yhi]
        sent = []
        order = ((1, 0), (1, 1), (3, 0), (3, 1), (2, 0), (2, 1), (0, 1))
        for k, flip in order:
            target = ring(y, k)
            half = 1 - core if flip else core
            peer = diagonal_peer(k) if flip else y_peer(k)
            start = feature_start(lax.rem(target, 2), lax.div(target, 2), half)
            src = tokens.at[:, pl.ds(start, 256)]
            copy = remote(src, mine, send.at[2 * k + flip], recv.at[2 * k + flip], peer)
            copy.start()
            sent.append(copy)
        heads[ylo, core, yhi] = tokens[:, pl.ds(feature_start(ylo, yhi, core), 256)]
        yield
        for k, flip in order:
            source = ring(y, -k)
            half = 1 - core if flip else core
            here = heads.at[lax.rem(source, 2), half, lax.div(source, 2)]
            remote(here, here, send.at[2 * k + flip], recv.at[2 * k + flip], y_peer(1)).wait_recv()
        for copy in sent:
            copy.wait_send()

    return {"scratch": [sems(8), sems(8)], "steps": steps}


def row_gather():
    def steps(share, full, local_sem, send, recv):
        ylo, x, z, yhi, core = place()
        across, other = y_peer(2), core_partner()
        mine = full.at[:, core, yhi]
        far = full.at[:, core, 1 - yhi]
        local = pltpu.make_async_copy(share, mine, local_sem)
        one = remote(share, mine, send.at[0], recv.at[0], across)
        two = remote(share, mine, send.at[1], recv.at[1], other)
        one.start()
        two.start()
        local.start()
        yield
        remote(share, far, send.at[0], recv.at[0], across).wait_recv()
        three = remote(far, far, send.at[2], recv.at[2], other)
        three.start()
        yield
        remote(share, full.at[:, 1 - core, yhi], send.at[1], recv.at[1], other).wait_recv()
        last = full.at[:, 1 - core, 1 - yhi]
        remote(last, last, send.at[2], recv.at[2], other).wait_recv()
        for copy in (one, two, three):
            copy.wait_send()
        local.wait()

    return {
        "scratch": [pltpu.SemaphoreType.DMA, sems(3), sems(3)],
        "steps": steps,
    }


SIGNS = (1, -1)
XZ = ["x+", "x-", "z+", "z-"]


def xz_near():
    return [[xz_neighbour(axis, d) for d in SIGNS] for axis in (0, 1)]


def weight_gather(columns, spread=False, flat=False, phases=(0, 1)):
    count = 4 if spread else 2

    def steps(own, full, local_sem, swap_send, swap_recv, send, recv):
        ylo, x, z, yhi, core = place()
        y = yhi * 2 + ylo
        near = xz_near()
        offsets = (0, -1, 1, 2)

        def move(src, dst, s, r, stage, d, axis):
            n = ((s * 2 + r) * 8 + stage) * 2 + d
            return remote(src, dst, send.at[n], recv.at[n], near[axis][d])

        def origin(s):
            if spread:
                return ring(y, offsets[s])
            return ylo if s == 0 else 1 - ylo

        def block(s, r, one, two, rows):
            if r == 0:
                return full.at[origin(s), ring(x, one), ring(z, two), rows]
            return full.at[origin(s), ring(x, two), ring(z, one), rows]

        def rows_of(r, d=None):
            return pl.ds(32 * r, 32) if d is None else pl.ds(32 * r + 16 * d, 16)

        def half(n):
            if flat:
                return own.at[:, pl.ds(pl.multiple_of(n * columns, columns), columns)]
            return own.at[n]

        sent = []

        def go(*args):
            copy = move(*args)
            copy.start()
            sent.append(copy)

        swaps = []
        if 0 in phases:
            mine = own if spread else half(ylo)
            here = full.at[origin(0), x, z]
            local = pltpu.make_async_copy(mine, here, local_sem)
            for s in range(1, count):
                peer = y_peer((4 - offsets[s]) % 4) if spread else lo_partner()
                src = own if spread else half(1 - ylo)
                swaps.append(remote(src, here, swap_send.at[s], swap_recv.at[s], peer))
            for swap in swaps:
                swap.start()
            def begin(s, source):
                for r in range(2):
                    for d in range(2):
                        src = source.at[rows_of(r)]
                        go(src, block(s, r, 0, 0, rows_of(r)), s, r, 0, d, r)
                for r in range(2):
                    for d in range(2):
                        src = source.at[rows_of(r)]
                        go(src, block(s, r, 0, 0, rows_of(r)), s, r, 2, d, 1 - r)

            begin(0, mine)
            local.start()
            yield
            for s in range(1, count):
                came = full.at[origin(s), x, z]
                remote(came, came, swap_send.at[s], swap_recv.at[s], lo_partner()).wait_recv()
                begin(s, came)
            yield
            for s in range(count):
                for r in range(2):
                    for d in range(2):
                        came = block(s, r, -SIGNS[d], 0, rows_of(r))
                        move(came, came, s, r, 0, d, r).wait_recv()
                        piece = block(s, r, -SIGNS[d], 0, rows_of(r, d))
                        go(piece, piece, s, r, 1, d, r)
                    for part in (1, 2):
                        for d in range(2):
                            came = block(s, r, offsets[part], 0, rows_of(r))
                            go(came, came, s, r, 2 + part, d, 1 - r)
                if s % 2:
                    yield
            for s in range(count):
                for r in range(2):
                    for d in range(2):
                        piece = block(s, r, 2, 0, rows_of(r, d))
                        move(piece, piece, s, r, 1, d, r).wait_recv()
                    for d in range(2):
                        came = block(s, r, 2, 0, rows_of(r))
                        go(came, came, s, r, 5, d, 1 - r)
                if s % 2:
                    yield

        def line_came(part, s, r, d):
            came = block(s, r, offsets[part], -SIGNS[d], rows_of(r))
            if 0 in phases:
                move(came, came, s, r, 2 + part, d, 1 - r).wait_recv()
            return came

        for part in (0, 2, 1, 3):
            d = part // 2
            for s in range(count):
                for r in range(2):
                    came = line_came(part, s, r, d)
                    if 1 in phases:
                        go(came, came, s, r, 6 + part % 2, d, 1 - r)
            if 0 in phases:
                yield
        for s in range(count):
            for r in range(2):
                for part in range(4):
                    line_came(part, s, r, 1 - part // 2)
        if 0 in phases:
            local.wait()
        yield
        if 1 in phases:
            for s in range(count):
                for r in range(2):
                    for part in range(4):
                        d = part // 2
                        came = block(s, r, offsets[part], 2, rows_of(r))
                        move(came, came, s, r, 6 + part % 2, d, 1 - r).wait_recv()
        for copy in sent + swaps:
            copy.wait_send()

    return {
        "scratch": [pltpu.SemaphoreType.DMA, sems(count), sems(count), sems(32 * count), sems(32 * count)],
        "steps": steps,
    }


def gathered(columns, count=2):
    return (shaped(bf16, count, 4, 4, 64, columns), ANY)


def weight_sum(columns=PART):
    def steps(grads, out, wide, thin, total, swap_send, swap_recv, send, recv):
        ylo, x, z, yhi, core = place()
        near = xz_near()
        partner = lo_partner()

        def move(src, dst, s, r, stage, d, axis):
            n = ((s * 2 + r) * 6 + stage) * 2 + d
            return remote(src, dst, send.at[n], recv.at[n], near[axis][d])

        def line(s, r, step, part):
            if r == 0:
                return grads.at[s, part, ring(z, step), pl.ds(0, 32)]
            return grads.at[s, ring(x, step), part, pl.ds(32, 32)]

        def block(s, r, step, rows):
            if r == 0:
                return grads.at[s, ring(x, step), z, rows]
            return grads.at[s, x, ring(z, step), rows]

        def wide_move(s, r, d, kind):
            if kind == 0:
                src = line(s, r, 2, pl.ds(2 * d, 2))
            elif kind == 1:
                src = line(s, r, SIGNS[d], pl.ds(2 - 2 * d, 2))
            else:
                src = line(s, r, SIGNS[d], pl.ds(2 * d, 2))
            return move(src, wide.at[s, r, kind, d], s, r, kind, d, 1 - r)

        def thin_move(s, r, d, kind):
            if kind == 0:
                src = block(s, r, 2, pl.ds(32 * r + 16 * d, 16))
            elif kind == 1:
                src = block(s, r, SIGNS[d], pl.ds(32 * r + 16 - 16 * d, 16))
            else:
                src = block(s, r, SIGNS[d], pl.ds(32 * r + 16 * d, 16))
            return move(src, thin.at[s, r, kind, d], s, r, 3 + kind, d, r)

        for s in range(2):
            for kind in range(2):
                for r in range(2):
                    for d in range(2):
                        wide_move(s, r, d, kind).start()
        yield

        for s in range(2):
            for r in range(2):
                for d in range(2):
                    wide_move(s, r, d, 0).wait_recv()
                    for p in range(2):
                        mine = line(s, r, SIGNS[d], 2 * d + p)

                        def one(rows):
                            value = mine[rows].astype(f32) + wide[s, r, 0, d, p, rows].astype(f32)
                            mine[rows] = value.astype(bf16)

                        add_rows(32, one)
                    wide_move(s, r, d, 2).start()
            yield

        for s in range(2):
            for r in range(2):
                for d in range(2):
                    wide_move(s, r, d, 1).wait_recv()
                    wide_move(s, r, d, 2).wait_recv()
                for p in range(4):
                    mine = line(s, r, 0, p)
                    d = p // 2

                    def one(rows):
                        value = mine[rows].astype(f32) + wide[s, r, 2, d, p % 2, rows].astype(f32)
                        value += wide[s, r, 1, 1 - d, p % 2, rows].astype(f32)
                        mine[rows] = value.astype(bf16)

                    add_rows(32, one)
                for kind in range(2):
                    for d in range(2):
                        thin_move(s, r, d, kind).start()
            yield

        for s in range(2):
            for r in range(2):
                for d in range(2):
                    thin_move(s, r, d, 0).wait_recv()
                    mine = block(s, r, SIGNS[d], pl.ds(32 * r + 16 * d, 16))
                    value = mine[...].astype(f32) + thin[s, r, 0, d].astype(f32)
                    mine[...] = value.astype(bf16)
                    thin_move(s, r, d, 2).start()
        yield

        for s in range(2):
            for r in range(2):
                for d in range(2):
                    thin_move(s, r, d, 1).wait_recv()
                    thin_move(s, r, d, 2).wait_recv()
                for d in range(2):
                    rows = pl.ds(32 * r + 16 * d, 16)
                    value = block(s, r, 0, rows)[...].astype(f32) + thin[s, r, 2, d].astype(f32)
                    value += thin[s, r, 1, 1 - d].astype(f32)
                    total[s, rows] = value.astype(bf16)
        swap = remote(total.at[1 - ylo], out.at[ylo], swap_send, swap_recv, partner)
        swap.start()
        out[ylo] = total[ylo]
        yield
        for s in range(2):
            for r in range(2):
                for d in range(2):
                    for kind in range(3):
                        wide_move(s, r, d, kind).wait_send()
                        thin_move(s, r, d, kind).wait_send()
        remote(total.at[0], out.at[1 - ylo], swap_send, swap_recv, partner).wait_recv()
        swap.wait_send()

    return {
        "scratch": [
            pltpu.VMEM((2, 2, 3, 2, 2, 32, columns), bf16),
            pltpu.VMEM((2, 2, 3, 2, 16, columns), bf16),
            pltpu.VMEM((2, 64, columns), bf16),
            pltpu.SemaphoreType.DMA,
            pltpu.SemaphoreType.DMA,
            sems(48),
            sems(48),
        ],
        "steps": steps,
    }


def standardize(value):
    mean = jnp.mean(value, axis=-1, keepdims=True)
    centered = value - mean
    scale_inv = lax.rsqrt(jnp.mean(centered * centered, axis=-1, keepdims=True) + epsilon)
    return (centered * scale_inv, scale_inv)


def norm_back(grad_normed_out, normed, scale_inv, gain):
    scaled = grad_normed_out * gain
    mean_one = jnp.mean(scaled, axis=-1, keepdims=True)
    mean_two = jnp.mean(scaled * normed, axis=-1, keepdims=True)
    grad_value = scale_inv * (scaled - mean_one - normed * mean_two)
    grad_gain = jnp.sum(grad_normed_out * normed, axis=0, keepdims=True)
    grad_shift = jnp.sum(grad_normed_out, axis=0, keepdims=True)
    return (grad_value, grad_gain, grad_shift)


def dot(a, b):
    return jnp.dot(a, b, preferred_element_type=f32)


def turned_dot(a, b):
    return lax.dot_general(a, b, (((1,), (1,)), ((), ())), preferred_element_type=f32)


def outer_dot(a, b):
    return lax.dot_general(a, b, (((0,), (0,)), ((), ())), preferred_element_type=f32)


def some_rows(count, size, one):
    def body(i, carry):
        one(pl.ds(pl.multiple_of(i * size, size), size))
        return carry

    lax.fori_loop(0, count // size, body, 0)


def fetched(src, dst, sem):
    copy = pltpu.make_async_copy(src, dst, sem)
    copy.start()
    return copy


CODES = 4096
CODE_CHUNK = 1024


def forward_body(ins, outs, scratch, makers, ready):
    ids, segments, padding, stream_hbm, cot_hbm, codebook, own_qkv, own_out, own_up, own_down, norms = ins
    (
        attn_out,
        qkv_out,
        out_weight_out,
        cot_full,
        inputs_out,
        gains,
        mask_out,
        projected_out,
        attended_out,
        middle_out,
        ffn_full,
        up_full,
        down_full,
    ) = outs
    (
        inputs_share,
        mask,
        projected,
        attended,
        middle,
        everyone,
        norm_tile,
        other_segments,
        other_padding,
        chunk,
        total,
        stream,
        cot_half,
        halves,
        attn_in,
        weight,
        out_weight,
        tokens,
        ffn_share,
        load_sem,
        swap_send,
        swap_recv,
    ) = scratch
    make_small, make_qkv, make_out, make_up, make_down, make_cot, make_attn, make_heads, make_share = makers
    ylo, x, z, yhi, core = place()
    small = make_small(norm_tile, everyone)
    qkv = make_qkv(own_qkv, weight)
    out = make_out(own_out, out_weight.at[core])
    up, down = make_up(own_up, up_full), make_down(own_down, down_full)
    cot_move = make_cot(cot_half, cot_full)
    attn_move = make_attn(halves, attn_in)
    heads = make_heads(attended, tokens)
    spread = make_share(ffn_share, ffn_full)

    def fetch(j):
        rows = pl.ds(j * CODE_CHUNK, CODE_CHUNK)
        return pltpu.make_async_copy(codebook.at[rows], chunk.at[j % 2], load_sem.at[j % 2])

    mine = pl.ds(pl.multiple_of(core * 256, 256), 256)
    loads = [fetched(stream_hbm.at[mine], stream, load_sem.at[2])]
    for u in range(2):
        rows = pl.ds(pl.multiple_of(core * 256 + u * SHARE, SHARE), SHARE)
        loads.append(fetched(cot_hbm.at[rows], cot_half.at[0, u], load_sem.at[3 + u]))
    fetch(0).start()
    lane = lax.broadcasted_iota(jnp.int32, (8, 128), 1)
    norm_tile[...] = jnp.where(lax.div(lane, 64) == lax.rem(z, 2), norms[...].astype(f32), 0.0)
    ready()
    step(small, qkv, out)
    row_swaps = [
        remote(segments, other_segments, swap_send.at[0], swap_recv.at[0], lo_partner()),
        remote(padding, other_padding, swap_send.at[1], swap_recv.at[1], lo_partner()),
    ]
    for swap in row_swaps:
        swap.start()
    for load in loads:
        load.wait()
    step(cot_move)
    total[...] = stream[...].astype(f32)
    my_ids = ids[:, mine]
    count = CODES // CODE_CHUNK
    for j in range(count):
        if j + 1 < count:
            fetch(j + 1).start()
        fetch(j).wait()
        code = lax.broadcasted_iota(jnp.int32, (CODE_CHUNK, 256), 0) + j * CODE_CHUNK
        pick = jnp.where(my_ids == code, 1.0, 0.0).astype(bf16)
        for part in range(2):
            columns = pl.ds(part * 1024, 1024)
            total[:, columns] += outer_dot(pick, chunk[j % 2, :, columns])
        step(small, (qkv, out, qkv, out)[j])
    finish(small)
    for t in range(16):
        at = (t // 8, t // 2 % 4, t % 2 * 2)
        pair = everyone[at] + everyone[at[0], at[1], at[2] + 1]
        gains[:, pl.ds(128 * t, 128)] = pair
    gain, shift = gains[pl.ds(0, 1)], gains[pl.ds(1, 1)]
    for u in range(2):

        def norm(rows):
            value = total[pl.ds(pl.multiple_of(u * SHARE + rows.start, 32), 32)]
            normed, _ = standardize(value)
            halves[0, u, rows] = (normed * gain + shift).astype(bf16)

        some_rows(SHARE, 32, norm)
    step(attn_move, qkv, out)

    def keep(rows):
        inputs_share[rows] = total[pl.ds(pl.multiple_of(yhi * SHARE + rows.start, 32), 32)]

    some_rows(SHARE, 32, keep)
    step(qkv, qkv)

    def see(r, segment_row, padding_row):
        turned = jnp.broadcast_to(segment_row.astype(f32), (SHARE, 512)).T[:, 0:1]
        query = lax.broadcasted_iota(jnp.int32, (512, 512), 0)
        key = lax.broadcasted_iota(jnp.int32, (512, 512), 1)
        same = turned == segment_row.astype(f32)
        live = (padding_row == 1) | (query == key)
        mask[r] = jnp.where(same & live & (key <= query), 1.0, 0.0).astype(bf16)

    for swap in row_swaps:
        swap.wait()
    see(ylo, segments[...], padding[...])
    see(1 - ylo, other_segments[...], other_padding[...])
    step(qkv, cot_move, qkv, out, out)
    step(attn_move)
    finish(qkv)
    step(out, out, up)
    finish(cot_move, attn_move)
    writes = [
        fetched(attn_in, attn_out, load_sem.at[0]),
        fetched(weight, qkv_out, load_sem.at[1]),
        fetched(inputs_share, inputs_out, load_sem.at[2]),
        fetched(mask, mask_out, load_sem.at[3]),
    ]

    def project(r):
        rows = attn_in[0, r].reshape(512, WIDTH)
        for t in range(3):
            columns = pl.ds(t * 256, 256)
            part = weight[:, :, :, :, columns].reshape(WIDTH, 256)
            projected[r, :, columns] = dot(rows, part).astype(bf16)

    def attend(r):
        for h in range(2):
            key = projected[r, :, pl.ds(256 + h * HEAD, HEAD)]
            value = projected[r, :, pl.ds(512 + h * HEAD, HEAD)]
            for c in range(2):
                rows = pl.ds(c * 256, 256)
                query = projected[r, rows, pl.ds(h * HEAD, HEAD)]
                scores = turned_dot(query, key) * HEAD ** (-0.5)
                scores = jnp.where(mask[r, rows].astype(f32) > 0.5, scores, masked_score)
                expd = jnp.exp(scores - jnp.max(scores, axis=-1, keepdims=True))
                probs = expd / jnp.sum(expd, axis=-1, keepdims=True)
                result = dot(probs.astype(bf16), value).astype(bf16)
                for u in range(2):
                    attended[r, c, u, :, pl.ds(h * HEAD, HEAD)] = result[u * SHARE : (u + 1) * SHARE]

    project(1 - ylo)
    step(out, down)
    attend(1 - ylo)
    step(heads)
    step(out, up)
    project(ylo)

    def swap(n, half_core):
        apart = (0, 1, -1, 2)[n // 2]
        if n % 2 == 0:
            here = out_weight.at[half_core, :, :, ring(z, apart), pl.ds(0, 32)]
        else:
            here = out_weight.at[half_core, :, ring(x, apart), :, pl.ds(32, 32)]
        return remote(here, here, swap_send.at[2 + n], swap_recv.at[2 + n], core_partner())

    step(out)
    for n in range(6):
        swap(n, core).start()
    step(down)
    attend(ylo)
    step(heads)
    finish(out)
    for n in (6, 7):
        swap(n, core).start()
    step(up, down)
    finish(heads)
    writes.append(fetched(projected, projected_out, load_sem.at[5]))
    writes.append(fetched(attended, attended_out, load_sem.at[6]))

    def branch(c, before):
        def one(n, carry):
            columns = pl.ds(pl.multiple_of(n * 512, 512), 512)
            value = before[:, columns]
            for h in range(2):
                features = pl.ds(pl.multiple_of((h * 2 + c) * 512, 512), 512)
                pair = pl.ds(lax.rem(n, 2) * 2, 2)
                part = out_weight[c, h * 2 + lax.div(n, 2), pair].reshape(512, 512)
                value += turned_dot(tokens[:, features], part)
            middle[:, columns] = value
            return carry

        lax.fori_loop(0, WIDTH // 512, one, 0)

    branch(core, inputs_share)
    for n in range(8):
        swap(n, 1 - core).wait_recv()
    writes.append(fetched(out_weight, out_weight_out, load_sem.at[4]))
    branch(1 - core, middle)
    gain_two, shift_two = gains[pl.ds(2, 1)], gains[pl.ds(3, 1)]

    def norm_two(rows):
        normed, _ = standardize(middle[rows])
        ffn_share[rows] = (normed * gain_two + shift_two).astype(bf16)

    some_rows(SHARE, 32, norm_two)
    step(spread)
    writes.append(fetched(middle, middle_out, load_sem.at[7]))
    step(up, down)
    step(up, down)
    step(up, down)
    step(spread)
    step(up, down)
    step(spread)
    step(up, down)
    finish(spread, up, down)
    for write in writes:
        write.wait()
    for n in range(8):
        swap(n, core).wait_send()


def forward(ids, segments, padding, stream, cot, codebook, own_qkv, own_out, own_up, own_down, norms):
    tokens_full = (shaped(bf16, 1, 2, 2, 2, SHARE, WIDTH), ANY)
    return kernel_call(
        forward_body,
        [
            small_gather(),
            weight_gather(768),
            weight_gather(512, spread=True),
            weight_gather(PART, flat=True),
            weight_gather(PART, flat=True),
            row_exchange(),
            row_exchange(),
            heads_to_tokens(),
            share_gather(),
        ],
        XZ + ["x2", "z2"] + GROUP,
        [
            (ids, VMEM),
            (segments, VMEM),
            (padding, VMEM),
            (stream, ANY),
            (cot, ANY),
            (codebook, ANY),
            (own_qkv, VMEM),
            (own_out, VMEM),
            (own_up, VMEM),
            (own_down, VMEM),
            (norms, VMEM),
        ],
        [
            tokens_full,
            gathered(768),
            (shaped(bf16, 2, 4, 4, 4, 64, 512), ANY),
            tokens_full,
            (shaped(f32, SHARE, WIDTH), ANY),
            (shaped(f32, 8, WIDTH), VMEM),
            (shaped(bf16, 2, 512, 512), ANY),
            (shaped(bf16, 2, 512, 768), ANY),
            (shaped(bf16, 2, 2, 2, SHARE, 256), ANY),
            (shaped(f32, SHARE, WIDTH), ANY),
            (shaped(bf16, 2, 2, 2, SHARE, WIDTH), ANY),
            gathered(PART),
            gathered(PART),
        ],
        [
            pltpu.VMEM((SHARE, WIDTH), f32),
            pltpu.VMEM((2, 512, 512), bf16),
            pltpu.VMEM((2, 512, 768), bf16),
            pltpu.VMEM((2, 2, 2, SHARE, 256), bf16),
            pltpu.VMEM((SHARE, WIDTH), f32),
            pltpu.VMEM((2, 4, 4, 8, 128), f32),
            pltpu.VMEM((8, 128), f32),
            pltpu.VMEM((1, 512), jnp.int32),
            pltpu.VMEM((1, 512), jnp.int32),
            pltpu.VMEM((2, CODE_CHUNK, WIDTH), bf16),
            pltpu.VMEM((256, WIDTH), f32),
            pltpu.VMEM((256, WIDTH), bf16),
            pltpu.VMEM((1, 2, SHARE, WIDTH), bf16),
            pltpu.VMEM((1, 2, SHARE, WIDTH), bf16),
            pltpu.VMEM((1, 2, 2, 2, SHARE, WIDTH), bf16),
            pltpu.VMEM((2, 4, 4, 64, 768), bf16),
            pltpu.VMEM((2, 4, 4, 4, 64, 512), bf16),
            pltpu.VMEM((SHARE, WIDTH), bf16),
            pltpu.VMEM((SHARE, WIDTH), bf16),
            sems(8),
            sems(10),
            sems(10),
        ],
        0,
    )


SLOPE = 0.7978845608028654
CUBIC = 0.044715


def ffn_body(ins, outs, scratch, makers, ready):
    ffn_hbm, cot_hbm, up_hbm, down_hbm, middle_hbm, out_hbm, gains = ins
    sum_down, grad_up_out, layer_full, grad_middle_out, small, branch_share, grad_heads = outs
    (
        layer_out,
        middle,
        grad_up_weight,
        grad_middle,
        grad_tokens,
        ffn_in,
        cot,
        up_weight,
        down_weight,
        hidden,
        grad_up,
        back,
        ahead,
        grad_down_weight,
        back_share,
        ahead_share,
        load_sem,
    ) = scratch
    make_back, make_ahead, make_down, make_heads, make_layer = makers
    ylo, x, z, yhi, core = place()
    back_sum = make_back(back, back_share)
    ahead_sum = make_ahead(ahead, ahead_share)
    down_sum = make_down(grad_down_weight, sum_down)
    heads = make_heads(grad_tokens, grad_heads)
    layer_move = make_layer(layer_out, layer_full)
    own, partner = (pl.ds(pl.multiple_of(r * 512, 512), 512) for r in (ylo, 1 - ylo))
    loads = [
        fetched(ffn_hbm.at[own], ffn_in.at[own], load_sem.at[0]),
        fetched(up_hbm, up_weight, load_sem.at[1]),
        fetched(ffn_hbm.at[partner], ffn_in.at[partner], load_sem.at[2]),
        fetched(down_hbm, down_weight, load_sem.at[3]),
        fetched(cot_hbm, cot, load_sem.at[4]),
        fetched(middle_hbm, middle, load_sem.at[5]),
    ]

    def units(rows):
        def one(n, carry):
            columns = pl.ds(pl.multiple_of(n * 512, 512), 512)
            value = dot(ffn_in[rows], up_weight[:, columns])
            square = value * value
            bend = jnp.tanh(SLOPE * value * (1.0 + CUBIC * square))
            half = 0.5 * (1.0 + bend)
            hidden[rows, columns] = (value * half).astype(bf16)
            slope = half + 0.5 * value * (1.0 - bend * bend) * SLOPE * (1.0 + 3.0 * CUBIC * square)
            grad_up[rows, columns] = slope.astype(bf16)
            return carry

        lax.fori_loop(0, PART // 512, one, 0)

    def units_back(rows):
        def one(n, carry):
            columns = pl.ds(pl.multiple_of(n * 512, 512), 512)
            grad = dot(cot[rows], down_weight[:, columns])
            grad_up[rows, columns] = (grad * grad_up[rows, columns].astype(f32)).astype(bf16)
            return carry

        lax.fori_loop(0, PART // 512, one, 0)

    def spread_out(r, rows, source, weight, target):
        def one(n, carry):
            columns = pl.ds(pl.multiple_of(n * 512, 512), 512)
            value = turned_dot(source[rows], weight[columns]).astype(bf16)
            for c in range(2):
                for u in range(2):
                    at = (2 * c + u) * SHARE
                    target[r, c, u, :, columns] = value[at : at + SHARE]
            return carry

        lax.fori_loop(0, WIDTH // 512, one, 0)

    def weight_grad(left, right, target, first=0, last=WIDTH // 256):
        def one(n, carry):
            columns = pl.ds(pl.multiple_of(n * 256, 256), 256)
            value = outer_dot(left[:, columns], right[...]).astype(bf16)
            for j in range(4):
                target[lax.div(n, 4), lax.rem(n, 4), j] = value[64 * j : 64 * j + 64]
            return carry

        lax.fori_loop(first, last, one, 0)

    loads[0].wait()
    loads[1].wait()
    units(own)
    loads[2].wait()
    units(partner)
    loads[3].wait()
    spread_out(ylo, own, hidden, down_weight, ahead)
    ready()
    step(ahead_sum)
    spread_out(1 - ylo, partner, hidden, down_weight, ahead)
    step(ahead_sum, ahead_sum)
    loads[4].wait()
    weight_grad(cot, hidden, grad_down_weight)
    step(down_sum)
    step(ahead_sum)
    units_back(own)
    step(down_sum)
    spread_out(ylo, own, grad_up, up_weight, back)
    step(back_sum)
    step(down_sum)
    units_back(partner)
    step(back_sum)
    spread_out(1 - ylo, partner, grad_up, up_weight, back)
    step(back_sum)
    places = {}
    for h in range(2):
        for c in range(2):
            place_of = (up_weight, down_weight)[h].at[:, pl.ds(512 * c, 512)]
            places[h, c] = (place_of, fetched(out_hbm.at[c, h], place_of, load_sem.at[6 + 2 * h + c]))
    step(down_sum)
    weight_grad(ffn_in, grad_up, grad_up_weight, 0, 3)
    step(back_sum)
    step(down_sum)
    weight_grad(ffn_in, grad_up, grad_up_weight, 3, 6)
    step(down_sum)
    weight_grad(ffn_in, grad_up, grad_up_weight, 6, 8)
    writes = [fetched(grad_up_weight, grad_up_out, load_sem.at[0])]
    step(down_sum)
    finish(ahead_sum)
    loads[5].wait()

    def end(rows):
        layer_out[0, rows] = (middle[rows] + ahead_share[rows]).astype(bf16)

    some_rows(SHARE, 32, end)
    step(layer_move)
    finish(back_sum)
    gain = gains[pl.ds(2, 1)]
    small[...] = jnp.zeros_like(small)

    def back_norm(i, carry):
        at = pl.multiple_of(i * 32, 32)
        rows = pl.ds(at, 32)
        normed, inverse = standardize(middle[rows])
        value, grad_gain, grad_shift = norm_back(back_share[rows], normed, inverse, gain)
        here = pl.multiple_of(ylo * 512 + core * 256 + yhi * SHARE + at, 32)
        value += cot[pl.ds(here, 32)].astype(f32)
        grad_middle[rows] = value
        branch_share[rows] = value.astype(bf16)
        small[pl.ds(2, 1)] += grad_gain
        small[pl.ds(3, 1)] += grad_shift
        return carry

    lax.fori_loop(0, SHARE // 32, back_norm, 0)
    writes.append(fetched(grad_middle, grad_middle_out, load_sem.at[1]))
    for h in range(2):
        for c in range(2):
            place_of, load = places[h, c]
            load.wait()
            grad_tokens[:, pl.ds((h * 2 + c) * 512, 512)] = dot(branch_share[...], place_of[...]).astype(bf16)
    step(heads)
    step(layer_move)
    finish(down_sum, heads, layer_move)
    for write in writes:
        write.wait()


def feed_forward(ffn_in, cot, up, down, middle, out_weight, gains):
    return kernel_call(
        ffn_body,
        [share_sum(), share_sum(), weight_sum(), tokens_to_heads(), row_gather()],
        XZ + GROUP,
        [(ffn_in, ANY), (cot, ANY), (up, ANY), (down, ANY), (middle, ANY), (out_weight, ANY), (gains, VMEM)],
        [
            (shaped(bf16, 2, 64, PART), VMEM),
            (shaped(bf16, 2, 4, 4, 64, PART), ANY),
            (shaped(bf16, 1, 2, 2, SHARE, WIDTH), ANY),
            (shaped(f32, SHARE, WIDTH), ANY),
            (shaped(f32, 4, WIDTH), VMEM),
            (shaped(bf16, SHARE, WIDTH), VMEM),
            (shaped(bf16, 2, 2, 2, SHARE, 256), VMEM),
        ],
        [
            pltpu.VMEM((1, SHARE, WIDTH), bf16),
            pltpu.VMEM((SHARE, WIDTH), f32),
            pltpu.VMEM((2, 4, 4, 64, PART), bf16),
            pltpu.VMEM((SHARE, WIDTH), f32),
            pltpu.VMEM((SHARE, WIDTH), bf16),
            pltpu.VMEM((1024, WIDTH), bf16),
            pltpu.VMEM((1024, WIDTH), bf16),
            pltpu.VMEM((WIDTH, PART), bf16),
            pltpu.VMEM((WIDTH, PART), bf16),
            pltpu.VMEM((1024, PART), bf16),
            pltpu.VMEM((1024, PART), bf16),
            pltpu.VMEM((2, 2, 2, SHARE, WIDTH), bf16),
            pltpu.VMEM((2, 2, 2, SHARE, WIDTH), bf16),
            pltpu.VMEM((2, 4, 4, 64, PART), bf16),
            pltpu.VMEM((SHARE, WIDTH), f32),
            pltpu.VMEM((SHARE, WIDTH), f32),
            sems(10),
        ],
        2,
        62,
    )


def back_body(ins, outs, scratch, makers, ready):
    (
        attn_hbm,
        weight_hbm,
        up_hbm,
        projected_hbm,
        attended_hbm,
        mask_hbm,
        middle_hbm,
        inputs_hbm,
        branch_share,
        grad_heads,
        small_in,
        gains,
    ) = ins
    input_full, sum_up, sum_qkv, sum_out, small_out, branch_full = outs
    (
        projected,
        attended,
        mask,
        grad_middle,
        inputs_share,
        attn_in,
        weight,
        grad_up_weight,
        grad_qkv_weight,
        grad_out_weight,
        grad_branch,
        grad_projected,
        back,
        back_share,
        input_share,
        small,
        load_sem,
    ) = scratch
    make_up, make_qkv, make_out, make_branch, make_back, make_input, make_small = makers
    ylo, x, z, yhi, core = place()
    up_sum = make_up(grad_up_weight, sum_up)
    qkv_sum = make_qkv(grad_qkv_weight, sum_qkv)
    out_sum = make_out(grad_out_weight, sum_out)
    branch = make_branch(branch_share, branch_full)
    back_sum = make_back(back, back_share)
    input_move = make_input(input_share, input_full)
    small_sum = make_small(small, small_out)
    loads = [
        fetched(src, dst, load_sem.at[n])
        for n, (src, dst) in enumerate(
            (
                (projected_hbm, projected),
                (mask_hbm, mask),
                (up_hbm, grad_up_weight),
                (weight_hbm, weight),
                (attn_hbm, attn_in),
                (attended_hbm, attended),
                (inputs_hbm, inputs_share),
                (middle_hbm, grad_middle),
            )
        )
    ]

    def attend(r):
        for h in range(2):
            query = projected[r, :, pl.ds(h * HEAD, HEAD)]
            key = projected[r, :, pl.ds(256 + h * HEAD, HEAD)]
            value = projected[r, :, pl.ds(512 + h * HEAD, HEAD)]
            grad = grad_heads[r, :, :, :, pl.ds(h * HEAD, HEAD)].reshape(512, HEAD)
            scores = turned_dot(query, key) * HEAD ** (-0.5)
            scores = jnp.where(mask[r].astype(f32) > 0.5, scores, masked_score)
            expd = jnp.exp(scores - jnp.max(scores, axis=-1, keepdims=True))
            probs = expd / jnp.sum(expd, axis=-1, keepdims=True)
            grad_probs = turned_dot(grad, value)
            inner = jnp.sum(grad_probs * probs, axis=-1, keepdims=True)
            grad_scores = (probs * (grad_probs - inner)).astype(bf16)
            parts = (
                dot(grad_scores, key) * HEAD ** (-0.5),
                outer_dot(grad_scores, query) * HEAD ** (-0.5),
                outer_dot(probs.astype(bf16), grad),
            )
            for t in range(3):
                grad_projected[pl.ds(pl.multiple_of(r * 512, 512), 512), pl.ds(t * 256 + h * HEAD, HEAD)] = parts[
                    t
                ].astype(bf16)

    def spread_out(r):
        def one(n, carry):
            columns = pl.ds(pl.multiple_of(n * 512, 512), 512)
            rows = pl.ds(pl.multiple_of(r * 512, 512), 512)
            value = turned_dot(grad_projected[rows], weight[columns]).astype(bf16)
            for c in range(2):
                for u in range(2):
                    at = (2 * c + u) * SHARE
                    back[r, c, u, :, columns] = value[at : at + SHARE]
            return carry

        lax.fori_loop(0, WIDTH // 512, one, 0)

    def weight_grad(left, right, target):
        def one(n, carry):
            columns = pl.ds(pl.multiple_of(n * 256, 256), 256)
            value = outer_dot(left[..., columns].reshape(1024, 256), right).astype(bf16)
            for j in range(4):
                target[lax.div(n, 4), lax.rem(n, 4), j] = value[64 * j : 64 * j + 64]
            return carry

        lax.fori_loop(0, WIDTH // 256, one, 0)

    loads[0].wait()
    loads[1].wait()
    attend(ylo)
    ready()
    step(branch)
    loads[2].wait()
    step(up_sum)
    loads[3].wait()
    spread_out(ylo)
    step(back_sum)
    attend(1 - ylo)
    step(back_sum)
    step(up_sum)
    spread_out(1 - ylo)
    step(back_sum)
    step(up_sum)
    loads[4].wait()
    weight_grad(attn_in, grad_projected[...], grad_qkv_weight)
    step(branch)
    step(qkv_sum)
    step(back_sum)
    step(up_sum, up_sum)
    step(qkv_sum)
    finish(branch)
    gather_load = fetched(branch_full, grad_branch, load_sem.at[0])
    for load in loads[5:]:
        load.wait()
    step(qkv_sum, up_sum)
    gather_load.wait()
    weight_grad(grad_branch, attended[...].reshape(1024, 256), grad_out_weight)
    step(out_sum)
    finish(back_sum)
    gain = gains[pl.ds(0, 1)]
    small[...] = small_in[...]

    def back_norm(i, carry):
        rows = pl.ds(pl.multiple_of(i * 32, 32), 32)
        normed, inverse = standardize(inputs_share[rows])
        value, grad_gain, grad_shift = norm_back(back_share[rows], normed, inverse, gain)
        input_share[0, rows] = (grad_middle[rows] + value).astype(bf16)
        small[pl.ds(0, 1)] += grad_gain
        small[pl.ds(1, 1)] += grad_shift
        return carry

    lax.fori_loop(0, SHARE // 32, back_norm, 0)
    step(small_sum, input_move)
    step(up_sum, out_sum, qkv_sum, small_sum, out_sum, qkv_sum, out_sum, small_sum, qkv_sum)
    step(out_sum, qkv_sum, out_sum)
    step(out_sum, qkv_sum, input_move)
    finish(input_move, small_sum, up_sum, qkv_sum, out_sum)


def attention_back(
    attn_in,
    weight,
    grad_up_weight,
    projected,
    attended,
    mask,
    grad_middle,
    inputs_share,
    branch_share,
    grad_heads,
    small,
    gains,
):
    return kernel_call(
        back_body,
        [
            weight_sum(),
            weight_sum(768),
            weight_sum(256),
            share_gather(),
            share_sum(),
            row_gather(),
            small_reduce(),
        ],
        XZ + ["x2", "z2"] + GROUP,
        [
            (attn_in, ANY),
            (weight, ANY),
            (grad_up_weight, ANY),
            (projected, ANY),
            (attended, ANY),
            (mask, ANY),
            (grad_middle, ANY),
            (inputs_share, ANY),
            (branch_share, VMEM),
            (grad_heads, VMEM),
            (small, VMEM),
            (gains, VMEM),
        ],
        [
            (shaped(bf16, 1, 2, 2, SHARE, WIDTH), ANY),
            (shaped(bf16, 2, 64, PART), VMEM),
            (shaped(bf16, 2, 64, 768), VMEM),
            (shaped(bf16, 2, 64, 256), VMEM),
            (shaped(f32, 4, 128), VMEM),
            (shaped(bf16, 2, 2, 2, SHARE, WIDTH), ANY),
        ],
        [
            pltpu.VMEM((2, 512, 768), bf16),
            pltpu.VMEM((2, 2, 2, SHARE, 256), bf16),
            pltpu.VMEM((2, 512, 512), bf16),
            pltpu.VMEM((SHARE, WIDTH), f32),
            pltpu.VMEM((SHARE, WIDTH), f32),
            pltpu.VMEM((1024, WIDTH), bf16),
            pltpu.VMEM((WIDTH, 768), bf16),
            pltpu.VMEM((2, 4, 4, 64, PART), bf16),
            pltpu.VMEM((2, 4, 4, 64, 768), bf16),
            pltpu.VMEM((2, 4, 4, 64, 256), bf16),
            pltpu.VMEM((2, 2, 2, SHARE, WIDTH), bf16),
            pltpu.VMEM((1024, 768), bf16),
            pltpu.VMEM((2, 2, 2, SHARE, WIDTH), bf16),
            pltpu.VMEM((SHARE, WIDTH), f32),
            pltpu.VMEM((1, SHARE, WIDTH), bf16),
            pltpu.VMEM((4, WIDTH), f32),
            sems(8),
        ],
        3,
        62,
    )


def on_device(
    stream,
    code_ids,
    segment_ids,
    padding,
    codebook,
    norm1_gain,
    norm1_shift,
    w_qkv,
    w_out,
    norm2_gain,
    norm2_shift,
    w_up,
    w_down,
    cotangent,
):
    ylo, x, z, yhi, core = place()
    own_qkv = w_qkv.reshape(64, 3, 2, 256).transpose(2, 0, 1, 3).reshape(2, 64, 768)
    norms = jnp.stack([norm1_gain, norm1_shift, norm2_gain, norm2_shift] * 2)
    norms = jnp.concatenate([norms, norms], axis=1)
    (
        attn_in,
        qkv_full,
        out_full,
        cot,
        inputs_share,
        gains,
        allowed,
        projected,
        attended,
        middle,
        ffn_in,
        up_full,
        down_full,
    ) = forward(
        code_ids,
        segment_ids,
        padding,
        stream[0],
        cotangent[0],
        codebook,
        own_qkv,
        w_out,
        w_up,
        w_down,
        norms,
    )
    sum_down, grad_up_weight, layer_out, grad_middle, small, branch_share, grad_heads = feed_forward(
        ffn_in.reshape(1024, WIDTH),
        cot.reshape(1024, WIDTH),
        up_full.reshape(WIDTH, PART),
        down_full.reshape(WIDTH, PART),
        middle,
        out_full.reshape(2, 2, WIDTH, 512),
        gains,
    )
    input_grad, sum_up, sum_qkv, sum_out, small, _ = attention_back(
        attn_in.reshape(1024, WIDTH),
        qkv_full.reshape(WIDTH, 768),
        grad_up_weight,
        projected,
        attended,
        allowed,
        grad_middle,
        inputs_share,
        branch_share,
        grad_heads,
        small,
        gains,
    )

    sum_qkv, sum_out, sum_up, sum_down = (g.astype(f32) for g in (sum_qkv, sum_out, sum_up, sum_down))
    out_qkv = sum_qkv.reshape(2, 64, 3, 256).transpose(1, 2, 0, 3).reshape(64, 3, 512)
    out_out = sum_out.transpose(1, 0, 2).reshape(64, 512)
    out_up = sum_up.transpose(1, 0, 2).reshape(64, WIDTH)
    out_down = sum_down.transpose(1, 0, 2).reshape(64, WIDTH)
    odd = lax.rem(z, 2) == 1
    small = jnp.where(odd, small[:, 64:], small[:, :64])
    return (
        layer_out.reshape(1, 512, WIDTH).astype(f32),
        input_grad.reshape(1, 512, WIDTH).astype(f32),
        small[0],
        small[1],
        out_qkv,
        out_out,
        small[2],
        small[3],
        out_up,
        out_down,
    )


def solution(mesh):
    in_specs = (
        P("dp", None, None),
        P("dp", None),
        P("dp", None),
        P("dp", None),
        P(),
        P("dp"),
        P("dp"),
        P("dp", None, "mp"),
        P("dp", "mp"),
        P("dp"),
        P("dp"),
        P("dp", "mp"),
        P("dp", "mp"),
        P("dp", None, None),
    )
    out_specs = (
        P("dp", None, None),
        P("dp", None, None),
        P("dp"),
        P("dp"),
        P("dp", None, "mp"),
        P("dp", "mp"),
        P("dp"),
        P("dp"),
        P("dp", "mp"),
        P("dp", "mp"),
    )
    return jax.shard_map(
        on_device, mesh=mesh, in_specs=in_specs, out_specs=out_specs, check_vma=False
    )
```
